128 devices in a mesh: tm: 8 (over x_lo, z), space: 16 (over y, x_hi, core).
Axes of the slice: x: 4 (x_hi: 2, x_lo: 2; x = x_hi * 2 + x_lo), y: 4, z: 4, core: 2. Of those that a mesh axis runs over, the one named last changes fastest.
Arguments:
- fine_nodes: float32 [8, 3, 53, 256, 256], P('tm', None, None, 'space'), may hold values from -6 to 6
- fine_rates: float32 [53, 53], replicated, may hold values from -3 to 3
- fine_pairs: float32 [53, 53], replicated, may hold values from -0.4 to 0.4
- fine_diff: float32 [53], replicated, may hold values from 0.1 to 0.8
- coarse_rates: float32 [21, 21], replicated, may hold values from -4 to 4
- coarse_pairs: float32 [21, 21], replicated, may hold values from -0.8 to 0.8
- coarse_diff: float32 [21], replicated, may hold values from 0.1 to 0.8
- species_map: int32 [53, 1], replicated, may hold values from 0 to 20
Outputs:
- new_nodes: float32 [8, 3, 53, 256, 256], P('tm', None, None, 'space')
The draws below stay inside these ranges and needn't reach their ends.
Inputs may be any that keep to these rules, and one draw needn't show every extreme that they name: `species_map`: every one of the 21 lumped species is named by at least one detailed species.
All inputs are finite; a program needn't handle non-finite values.
Results may differ from the reference program's by a relative error of at most 0.00011.
Values sent between devices are 32-bit elements; how exact they have to be, the bound alone decides.
No kernel may reach another device: no remote copies, remote signals or barrier semaphores. Data moves between devices by JAX's collectives and lax.ppermute only.
A program may use at most 128 MiB of HBM per device.

```python
import math
import jax
import jax.numpy as jnp
from jax import lax

SPECIES = 53
COARSE = 21
NODES = 3
NY = 256
SLICES = 8
NX = 256


def shard_levels(stream_key, dims, shards, smallest, largest):
    loudness = 1.0
    for axis_at, blocks in shards:
        heights = jax.random.uniform(jax.random.fold_in(jax.random.fold_in(stream_key, 6), axis_at), (blocks,), jnp.float32, smallest / len(shards), largest / len(shards))
        loudness = loudness * jnp.repeat(jnp.exp(heights), dims[axis_at] // blocks).reshape((-1,) + (1,) * (len(dims) - 1 - axis_at))
    return loudness


def different_ones(own_key, rows, amount, top, lift):
    sequence = jax.random.permutation(jax.random.fold_in(own_key, 1), amount)
    pull = sequence
    for power in range(3):
        pull = pull * pull // amount
    pull = pull * lift // amount
    chance = jax.random.randint(jax.random.fold_in(own_key, 2), (rows, amount), 0, 4096) + pull
    fixed_rows = jax.random.permutation(jax.random.fold_in(own_key, 3), rows)[jnp.arange(amount) % rows]
    chance = jnp.where(jnp.arange(rows)[:, None] == fixed_rows[None, :], 1 << 14, chance)
    priority = chance * amount + jnp.arange(amount)
    return lax.top_k(priority.astype(jnp.int32), top)[1].astype(jnp.int32)


def normal_values(key, dims, width, limit, pieces=(), held_as=jnp.bfloat16):
    factor_of = shard_levels(key, dims, pieces, -0.22, 0.18) if pieces else 1.0
    result = jax.random.normal(key, dims, jnp.float32) * width * factor_of
    return jnp.minimum(jnp.maximum(result, -limit), limit).astype(held_as)


def setup_inputs(seed: int = 0) -> dict:
    seeds = jax.random.split(jax.random.key(seed), 9)
    fine_nodes = normal_values(seeds[0], (SLICES, NODES, SPECIES, NX, NY), 1.0, 6.0, ((0, 8), (3, 16)), jnp.float32)
    fine_rates = normal_values(seeds[1], (SPECIES, SPECIES), 0.41, 3.0, (), jnp.float32)
    fine_pairs = normal_values(seeds[2], (SPECIES, SPECIES), 0.05, 0.4, (), jnp.float32)
    fine_diff = jnp.clip(jnp.exp(jax.random.uniform(seeds[3], (SPECIES,), jnp.float32, math.log(0.1), math.log(0.8))), 0.1, 0.8)
    coarse_rates = normal_values(seeds[4], (COARSE, COARSE), 0.65, 4.0, (), jnp.float32)
    coarse_pairs = normal_values(seeds[5], (COARSE, COARSE), 0.1, 0.8, (), jnp.float32)
    coarse_diff = jnp.clip(jnp.exp(jax.random.uniform(seeds[6], (COARSE,), jnp.float32, math.log(0.1), math.log(0.8))), 0.1, 0.8)
    species_map = different_ones(seeds[7], SPECIES, COARSE, 1, 0)
    return dict(fine_nodes=fine_nodes, fine_rates=fine_rates, fine_pairs=fine_pairs, fine_diff=fine_diff, coarse_rates=coarse_rates, coarse_pairs=coarse_pairs, coarse_diff=coarse_diff, species_map=species_map)


step_length = 0.1
relaxation = 3.0
weights_first = (5.0 / 24.0, 1.0 / 3.0, -1.0 / 24.0)
weights_second = (-1.0 / 24.0, 1.0 / 3.0, 5.0 / 24.0)


def second_first(padded):
    return (16.0 * (padded[..., 1:-3, :] + padded[..., 3:-1, :]) - (padded[..., :-4, :] + padded[..., 4:, :]) - 30.0 * padded[..., 2:-2, :]) / 12.0


def second_other(state_field):
    near = jnp.roll(state_field, 1, -1) + jnp.roll(state_field, -1, -1)
    far = jnp.roll(state_field, 2, -1) + jnp.roll(state_field, -2, -1)
    return (16.0 * near - far - 30.0 * state_field) / 12.0


def pad_first(state_field):
    widths = [(0, 0)] * (state_field.ndim - 2) + [(2, 2), (0, 0)]
    return jnp.pad(state_field, widths)


def tendency(state_field, padded, diffusion, rate_matrix, pair_matrix):
    laplace = second_first(padded) + second_other(state_field)
    linear = jnp.einsum("st,...txy->...sxy", rate_matrix, state_field, precision=lax.Precision.HIGHEST)
    square = jnp.einsum("st,...txy->...sxy", pair_matrix, state_field * state_field, precision=lax.Precision.HIGHEST)
    return diffusion[:, None, None] * laplace + linear - relaxation * state_field + square


def combine(weights, values):
    return step_length * (weights[0] * values[0] + weights[1] * values[1] + weights[2] * values[2])


def reference(fine_nodes, fine_rates, fine_pairs, fine_diff, coarse_rates, coarse_pairs, coarse_diff, species_map):
    lumping = (species_map[:, 0][None, :] == jnp.arange(COARSE, dtype=jnp.int32)[:, None]).astype(jnp.float32)
    counts = jnp.sum(lumping, axis=1)
    spreading = (lumping / counts[:, None]).T
    half_step = 0.5 * step_length

    def fine_eval(values):
        return tendency(values, pad_first(values), fine_diff, fine_rates, fine_pairs)

    def coarse_eval(values):
        return tendency(values, pad_first(values), coarse_diff, coarse_rates, coarse_pairs)

    def restrict(values):
        return jnp.einsum("cs,...sxy->...cxy", lumping, values, precision=lax.Precision.HIGHEST)

    def prolong(values):
        return jnp.einsum("sc,...cxy->...sxy", spreading, values, precision=lax.Precision.HIGHEST)

    outputs = []
    carried_end = None
    chain_value = None
    for slice_number in range(SLICES):
        node_values = fine_nodes[slice_number]
        old_terms = fine_eval(node_values)
        swept_zero = node_values[0]
        swept_one = swept_zero + combine(weights_first, old_terms)
        fresh_one = fine_eval(swept_one)
        swept_two = swept_one + half_step * (fresh_one - old_terms[1]) + combine(weights_second, old_terms)
        fresh_two = fine_eval(swept_two)
        fresh = (old_terms[0], fresh_one, fresh_two)
        source_zero = restrict(combine(weights_first, fresh))
        source_one = restrict(combine(weights_second, fresh))
        lumped = restrict(jnp.stack([swept_zero, swept_one, swept_two]))
        lumped_terms = coarse_eval(lumped)
        if slice_number == 0:
            chain_begin = lumped[0]
        else:
            chain_begin = chain_value
        chain_one = chain_begin + half_step * (coarse_eval(chain_begin) - lumped_terms[0]) + source_zero
        chain_two = chain_one + half_step * (coarse_eval(chain_one) - lumped_terms[1]) + source_one
        if slice_number == 0:
            node_zero = node_values[0]
        else:
            node_zero = carried_end
        node_one = swept_one + prolong(chain_one - lumped[1])
        node_two = swept_two + prolong(chain_two - lumped[2])
        outputs.append(jnp.stack([node_zero, node_one, node_two]))
        carried_end = swept_two + prolong(chain_two - restrict(swept_two))
        chain_value = chain_two
    return jnp.stack(outputs)
```

```python
import functools

import jax
import jax.numpy as jnp
from jax import lax
from jax.experimental import pallas as pl
from jax.experimental.pallas import tpu as pltpu
from jax.sharding import PartitionSpec as P

SPECIES, COARSE = 53, 21
SP, CP = 56, 24
ROWS, COLS = 16, 256
SLICES, SLABS = 8, 16
STEP, HALF, RELAX = 0.1, 0.05, 3.0
W0 = (5.0 / 24.0, 1.0 / 3.0, -1.0 / 24.0)
W1 = (-1.0 / 24.0, 1.0 / 3.0, 5.0 / 24.0)
F32, BF16 = jnp.float32, jnp.bfloat16
VMEM_LIMIT = 48 * 1024 * 1024


def split(x):
    hi = x.astype(BF16)
    lo = (x - hi.astype(F32)).astype(BF16)
    return jnp.concatenate([hi, lo], axis=0)


def dot(w, x):
    return jnp.dot(w, x, preferred_element_type=F32)


def with_squares(x):
    return split(jnp.concatenate([x, x * x], axis=0))


def lap_y(x):
    near = pltpu.roll(x, 1, 1) + pltpu.roll(x, COLS - 1, 1)
    far = pltpu.roll(x, 2, 1) + pltpu.roll(x, COLS - 2, 1)
    return 16.0 * near - far - 60.0 * x


def lap_x(row, x, low, high):
    total = None
    for offset, factor in ((-1, 16.0), (1, 16.0), (-2, -1.0), (2, -1.0)):
        if low <= x + offset < high:
            term = factor * row(x + offset)
            total = term if total is None else total + term
    return total


def first_kernel(core, u, out, outer, inner):
    at_top = core[0] == 0
    for m in range(3):
        for x in range(ROWS):
            out[m, x, SP - 8 :, :] = jnp.zeros((8, COLS), F32)
            out[m, x, :SPECIES, :] = u[m, :, x, :]
        for r in range(2):
            first, last = out[m, r], out[m, ROWS - 2 + r]
            outer[m, r] = jnp.where(at_top, first, last)
            inner[m, r] = jnp.where(at_top, last, first)


def restricted(y):
    return y[0:24] + y[24:48], y[48:72], y[72:96] + y[96:120]


def old_kernel(u, wf, wr, wc, d12, dc12, n1, s, r0, e0, c0, p0s, pss, v0s):
    w0 = [STEP * w for w in W0]
    ws = [STEP * W1[0], STEP * W1[1] - HALF, STEP * W1[2]]
    for x in range(ROWS):
        us = [u[m, x] for m in range(3)]
        qs = [v * v for v in us]
        p0 = w0[0] * us[0] + w0[1] * us[1] + w0[2] * us[2]
        p0q = w0[0] * qs[0] + w0[1] * qs[1] + w0[2] * qs[2]
        ps = ws[0] * us[0] + ws[1] * us[1] + ws[2] * us[2]
        psq = ws[0] * qs[0] + ws[1] * qs[1] + ws[2] * qs[2]
        y = dot(wf[...], split(jnp.concatenate([p0, p0q], axis=0)))
        n1[x] = us[0] + (y[:SP] + y[SP:]) + d12[...] * lap_y(p0)
        y = dot(wf[...], split(jnp.concatenate([ps, psq], axis=0)))
        s[x] = (y[:SP] + y[SP:]) + d12[...] * lap_y(ps)
        r, c, v = restricted(dot(wr[...], split(jnp.concatenate([us[0], qs[0]], axis=0))))
        r0[x] = r + lap_y(v) * (1.0 / 12.0)
        y = dot(wc[...], with_squares(c))
        e0[x] = (y[:CP] + y[CP:]) + dc12[...] * lap_y(c)
        p0s[x], pss[x], v0s[x], c0[x] = p0, ps, v, c
    for x in range(ROWS):
        n1[x] += d12[...] * lap_x(lambda i: p0s[i], x, 0, ROWS)
        s[x] += d12[...] * lap_x(lambda i: pss[i], x, 0, ROWS)
        r0[x] += lap_x(lambda i: v0s[i], x, 0, ROWS) * (1.0 / 12.0)
        e0[x] += dc12[...] * lap_x(lambda i: c0[i], x, 0, ROWS)


def edge_terms(side, halo):
    top = side == 0
    near, far = jnp.where(top, halo[1], halo[0]), jnp.where(top, halo[0], halo[1])
    beside, next_one = 16.0 * near - far, -near
    return jnp.where(top, beside, next_one), jnp.where(top, next_one, beside)


def received(side, core, outer, inner):
    take = side == core
    return [jnp.where(take, outer[r], inner[r]) for r in range(2)]


def send(side, core, outer, inner, rows):
    @pl.when(side == core)
    def _():
        for r, row in enumerate(rows):
            outer[r] = row

    @pl.when(side != core)
    def _():
        for r, row in enumerate(rows):
            inner[r] = row


def old_edge_kernel(core_ref, uo, ui, lv, d12, dc12, n1i, si, r0i, e0i, n1, s, r0, e0, outer, inner):
    side, core = pl.program_id(0), core_ref[0]
    take = side == core
    w0 = [STEP * w for w in W0]
    ws = [STEP * W1[0], STEP * W1[1] - HALF, STEP * W1[2]]
    p0, ps, c, v = [], [], [], []
    for r in range(2):
        us = [jnp.where(take, uo[m, r], ui[m, r]) for m in range(3)]
        p0.append(w0[0] * us[0] + w0[1] * us[1] + w0[2] * us[2])
        ps.append(ws[0] * us[0] + ws[1] * us[1] + ws[2] * us[2])
        y = dot(lv[...], split(us[0]))
        c.append(y[0:24])
        v.append(y[24:48] + y[48:72])
    p0, ps, c, v = (edge_terms(side, h) for h in (p0, ps, c, v))
    rows = []
    for r in range(2):
        rows.append(n1i[r] + d12[...] * p0[r])
        n1[r] = rows[r]
        s[r] = si[r] + d12[...] * ps[r]
        r0[r] = r0i[r] + v[r] * (1.0 / 12.0)
        e0[r] = e0i[r] + dc12[...] * c[r]
    send(side, core, outer, inner, rows)


def mid_kernel(n1, s, wfr, wc, d12, dc12, n2, r1, e1, c1, v1s):
    for x in range(ROWS):
        n = n1[x]
        y = dot(wfr[...], with_squares(n))
        lap = lap_y(n) + lap_x(lambda i: n1[i], x, 0, ROWS)
        n2[x] = n + HALF * ((y[:SP] + y[SP : 2 * SP]) + d12[...] * lap) + s[x]
        r, c, v = restricted(y[2 * SP :])
        r1[x] = r + lap_y(v) * (1.0 / 12.0)
        y = dot(wc[...], with_squares(c))
        e1[x] = (y[:CP] + y[CP:]) + dc12[...] * lap_y(c)
        v1s[x], c1[x] = v, c
    for x in range(ROWS):
        r1[x] += lap_x(lambda i: v1s[i], x, 0, ROWS) * (1.0 / 12.0)
        e1[x] += dc12[...] * lap_x(lambda i: c1[i], x, 0, ROWS)


def lumped_old(first, c0, e0):
    return jnp.where(first, c0, -HALF * e0)


def mid_edge_kernel(
    core_ref, no, ni, lv, wr, d12, dc12, r0, e0, c0, n2i, r1i, e1i, n2, r1, e1, outer, inner
):
    side, core, first = pl.program_id(0), core_ref[0], core_ref[1] == 0
    top = side == 0
    halo = received(side, core, no, ni)
    c, v = [], []
    for r in range(2):
        y = dot(lv[...], split(halo[r]))
        c.append(y[0:24])
        v.append(y[24:48] + y[48:72])
    n, c, v = (edge_terms(side, h) for h in (halo, c, v))
    zero, zero_c = jnp.zeros((SP, COLS), F32), jnp.zeros((CP, COLS), F32)
    terms = []
    for r in range(4):
        on_top, on_bottom = r < 2, r >= 2

        def pick(pair, zero):
            return jnp.where(top, pair[r] if on_top else zero, pair[r - 2] if on_bottom else zero)

        n2[r] = n2i[r] + (HALF * d12[...]) * pick(n, zero)
        r1[r] = r1i[r] + pick(v, zero_c) * (1.0 / 12.0)
        e1[r] = e1i[r] + dc12[...] * pick(c, zero_c)
        terms.append(restricted(dot(wr[...], with_squares(n2[r]))))
    vs = [t[2] for t in terms]
    rows = []
    for r in range(2):
        near_top = 16.0 * vs[1] - vs[2] if r == 0 else 16.0 * (vs[0] + vs[2]) - vs[3]
        near_bottom = 16.0 * (vs[1] + vs[3]) - vs[0] if r == 0 else 16.0 * vs[2] - vs[1]
        value = jnp.where(top, vs[r], vs[r + 2])
        lap = lap_y(value) + jnp.where(top, near_top, near_bottom)
        g2 = jnp.where(top, terms[r][0], terms[r + 2][0]) + lap * (1.0 / 12.0)
        old, mid = jnp.where(top, r0[r], r0[r + 2]), jnp.where(top, r1[r], r1[r + 2])
        base = lumped_old(first, jnp.where(top, c0[r], c0[r + 2]), jnp.where(top, e0[r], e0[r + 2]))
        rows.append((STEP * W0[0]) * old + (STEP * W0[1]) * mid + (STEP * W0[2]) * g2 + base)
    rows += [jnp.where(top, vs[r], vs[r + 2]) for r in range(2)]
    send(side, core, outer, inner, rows)


def row_a(x):
    return x + 2 if x < 2 else (x + 4 if x < 14 else x + 16)


def row_b(x):
    return x + 4 if x < 2 else (x + 16 if x < 14 else x + 20)


def last_kernel(tm, n2, wr, r0, r1, e0, e1, c0, ab, c2, v2s):
    first = tm[0] == 0
    gs = []
    for x in range(ROWS):
        r, c, v = restricted(dot(wr[...], with_squares(n2[x])))
        gs.append(r + lap_y(v) * (1.0 / 12.0))
        v2s[x], c2[x] = v, c
    for x in range(ROWS):
        g2 = gs[x] + lap_x(lambda i: v2s[i], x, 0, ROWS) * (1.0 / 12.0)
        ab[row_a(x)] = (
            (STEP * W0[0]) * r0[x]
            + (STEP * W0[1]) * r1[x]
            + (STEP * W0[2]) * g2
            + lumped_old(first, c0[x], e0[x])
        )
        ab[row_b(x)] = (
            (STEP * W1[0]) * r0[x] + (STEP * W1[1]) * r1[x] + (STEP * W1[2]) * g2 - HALF * e1[x]
        )
    for x in (-2, -1, ROWS, ROWS + 1):
        ab[row_a(x)] = jnp.zeros((CP, COLS), F32)


def last_edge_kernel(core_ref, mo, mi, ho, hi, abi, ab):
    side, core, slab = pl.program_id(0), core_ref[0], core_ref[2]
    top, take = side == 0, side == core
    own = [jnp.where(take, mo[r], mi[r]) for r in range(4)]
    halo = [jnp.where(take, ho[r], hi[r]) for r in range(4)]
    inside = jnp.where(top, slab > 0, slab < SLABS - 1)
    fix = edge_terms(side, halo[2:])
    theirs = edge_terms(1 - side, own[2:])
    ka, kb = STEP * W0[2] / 12.0, STEP * W1[2] / 12.0
    a = [jnp.where(top, abi[2 + r], abi[r]) + ka * fix[r] for r in range(2)]
    b = [abi[4 + r] + kb * fix[r] for r in range(2)]
    h = [jnp.where(inside, halo[r] + ka * theirs[r], 0.0) for r in range(2)]
    for r in range(2):
        ab[r] = jnp.where(top, h[r], a[r])
        ab[2 + r] = jnp.where(top, a[r], h[r])
        ab[4 + r] = b[r]


def lumped_rate(z, x, wc, dc12, low, high):
    y = dot(wc[...], with_squares(z(x)))
    return (y[:CP] + y[CP:]) + dc12[...] * (lap_y(z(x)) + lap_x(z, x, low, high))


def chain_kernel(first, info, *refs):
    if first:
        ab, wc, dc12, z12, z2, up, down, z1 = refs
    else:
        before, above, below, ab, wc, dc12, z12, z2, up, down, z1 = refs

    @pl.when(info[3] == 1)
    def _():
        slab = info[2]
        keep_top, keep_bottom = slab > 0, slab < SLABS - 1

        def start(x):
            if x < 0:
                return above[x + 4]
            return below[x - ROWS] if x >= ROWS else before[x]

        for x in range(-2, ROWS + 2):
            value = ab[row_a(x)]
            if not first:
                value = value + start(x) + HALF * lumped_rate(start, x, wc, dc12, -4, ROWS + 4)
                if x < 0:
                    value = jnp.where(keep_top, value, 0.0)
                elif x >= ROWS:
                    value = jnp.where(keep_bottom, value, 0.0)
            z1[x + 2] = value
        for x in range(ROWS):
            row = lambda i: z1[i + 2]
            value = row(x) + HALF * lumped_rate(row, x, wc, dc12, -2, ROWS + 2) + ab[row_b(x)]
            z12[x] = row(x)
            z12[ROWS + x] = value
            z2[x] = value
            if x < 4:
                up[x] = value
            if x >= ROWS - 4:
                down[x - ROWS + 4] = value


def thirds(x):
    hi = x.astype(BF16)
    rest = x - hi.astype(F32)
    mid = rest.astype(BF16)
    return jnp.concatenate([hi, mid, (rest - mid.astype(F32)).astype(BF16)], axis=0)


def spread(pro, share, value):
    return dot(pro[...], thirds(jnp.concatenate([share[...] * value, jnp.zeros((8, COLS), F32)], axis=0)))


def base_kernel(n1, n2, c1, c2, pro, share, b1, b2):
    for x in range(ROWS):
        b1[x] = n1[x] - spread(pro, share, c1[x])
        b2[x] = n2[x] - spread(pro, share, c2[x])


def out_kernel(info, u, b0, b1, b2, pro, share, *refs):
    z0s, z12s = refs[: SLICES - 1], refs[SLICES - 1 : 2 * SLICES - 1]
    out, z, sem = refs[2 * SLICES - 1 :]
    for p in range(SLICES):

        @pl.when(info[1] == p)
        def _():
            copies = [pltpu.make_async_copy(z12s[p], z.at[pl.ds(ROWS, 2 * ROWS)], sem.at[0])]
            if p:
                copies.append(pltpu.make_async_copy(z0s[p - 1], z.at[pl.ds(0, ROWS)], sem.at[1]))
            for copy in copies:
                copy.start()
            for copy in copies:
                copy.wait()

    first = info[1] == 0
    for x in range(ROWS):
        value = jnp.where(first, u[x], b0[x] + spread(pro, share, z[x]))
        out[0, :, x, :] = value[:SPECIES]
        out[1, :, x, :] = (b1[x] + spread(pro, share, z[ROWS + x]))[:SPECIES]
        out[2, :, x, :] = (b2[x] + spread(pro, share, z[2 * ROWS + x]))[:SPECIES]


def field(rows, species):
    return jax.ShapeDtypeStruct((rows, species, COLS), F32)


SMEM = pl.BlockSpec(memory_space=pltpu.SMEM)
PARAMS = dict(compiler_params=pltpu.CompilerParams(vmem_limit_bytes=VMEM_LIMIT))


def halves(w):
    hi = lax.reduce_precision(w, 8, 7)
    lo = w - hi
    return hi.astype(BF16), lo.astype(BF16)


def doubled(w):
    return jnp.concatenate([w, w], axis=1)


def padded(w, rows, columns):
    return jnp.pad(w, ((0, rows - w.shape[0]), (0, columns - w.shape[1])))


def weights(fine_rates, fine_pairs, fine_diff, coarse_rates, coarse_pairs, coarse_diff, species_map):
    lumping = padded(
        (species_map[:, 0][None, :] == jnp.arange(COARSE, dtype=jnp.int32)[:, None]).astype(F32), CP, SP
    )
    eye = jnp.eye(SPECIES, dtype=F32)
    fine = jnp.concatenate(
        [padded(fine_rates - RELAX * eye, SP, SP), padded(fine_pairs, SP, SP)], axis=1
    )
    coarse = jnp.concatenate(
        [padded(coarse_rates - RELAX * jnp.eye(COARSE, dtype=F32), CP, CP), padded(coarse_pairs, CP, CP)], axis=1
    )
    diff = jnp.pad(fine_diff, (0, SP - SPECIES))
    lumped_fine = jnp.dot(lumping, fine, precision=lax.Precision.HIGHEST)
    lumped_diff = lumping * diff[None, :]
    none = jnp.zeros((CP, SP), F32)
    fh, fl = halves(fine)
    rh, rl = halves(lumped_fine)
    ch, cl = halves(coarse)
    dh, dl = halves(lumped_diff)
    lum, none = lumping.astype(BF16), none.astype(BF16)
    wf = doubled(jnp.concatenate([fh, fl], axis=0))
    side = [jnp.concatenate([part, none], axis=1) for part in (lum, dh, dl)]
    wr = doubled(jnp.concatenate([rh, rl] + side + [jnp.zeros((8, 2 * SP), BF16)], axis=0))
    lv = doubled(jnp.concatenate([lum, dh, dl, jnp.zeros((8, SP), BF16)], axis=0))
    wc = doubled(jnp.concatenate([ch, cl], axis=0))
    d12 = jnp.broadcast_to((diff / 12.0)[:, None], (SP, COLS))
    dc12 = jnp.broadcast_to((jnp.pad(coarse_diff, (0, CP - COARSE)) / 12.0)[:, None], (CP, COLS))
    counts = jnp.maximum(jnp.sum(lumping, axis=1), 1.0)
    share = jnp.broadcast_to((1.0 / counts)[:, None], (CP, COLS))
    pro = padded(lumping.T, SP, CP + 8).astype(BF16)
    pro = jnp.concatenate([pro, pro, pro], axis=1)
    return dict(wf=wf, wr=wr, wfr=jnp.concatenate([wf, wr], axis=0), lv=lv, wc=wc, d12=d12, dc12=dc12, share=share, pro=pro)


AXES = ("tm", "space")


def device(slice_at, slab):
    return slice_at * SLABS + slab


def host(slab):
    return device((slab % 2) * 4, slab)


OUTER = [(s, s + 1) for s in range(1, SLABS - 1, 2)] + [(s + 1, s) for s in range(1, SLABS - 1, 2)]
INNER = [(s, s ^ 1) for s in range(SLABS)]


def swap(outer, inner):
    got_inner = lax.ppermute(inner, "space", INNER)
    got_outer = lax.ppermute(outer, "space", OUTER)
    return got_outer, got_inner


def after(value, *others):
    return lax.optimization_barrier((value,) + others)[0]


def local(fine_nodes, fine_rates, fine_pairs, fine_diff, coarse_rates, coarse_pairs, coarse_diff, species_map):
    slice_at, slab = lax.axis_index("tm"), lax.axis_index("space")
    hosting = slice_at == (slab % 2) * 4
    info = jnp.stack([slab % 2, slice_at, slab, hosting.astype(jnp.int32)]).astype(jnp.int32)
    w = weights(fine_rates, fine_pairs, fine_diff, coarse_rates, coarse_pairs, coarse_diff, species_map)
    nodes = fine_nodes[0]
    message = jax.ShapeDtypeStruct((3, 2, SP, COLS), F32)
    u, outer, inner = pl.pallas_call(
        first_kernel,
        out_shape=[jax.ShapeDtypeStruct((3, ROWS, SP, COLS), F32), message, message],
        in_specs=[SMEM, pl.BlockSpec(memory_space=pltpu.VMEM)],
        name="first",
        **PARAMS,
    )(info, nodes)
    uo, ui = swap(outer, inner)

    fine, coarse = field(ROWS, SP), field(ROWS, CP)
    n1, s, r0, e0, c0 = pl.pallas_call(
        old_kernel,
        out_shape=[fine, fine, coarse, coarse, coarse],
        scratch_shapes=[pltpu.VMEM(f.shape, F32) for f in (fine, fine, coarse)],
        name="old",
        **PARAMS,
    )(u, w["wf"], w["wr"], w["wc"], w["d12"], w["dc12"])

    def edge(rows, species, at):
        return pl.BlockSpec((rows, species, COLS), lambda i: (at * i, 0, 0))

    def whole(array):
        return pl.BlockSpec(array.shape, lambda i: (0,) * array.ndim)

    two = field(2, SP)
    n1, s, r0, e0, outer, inner = pl.pallas_call(
        old_edge_kernel,
        grid=(2,),
        out_shape=[fine, fine, coarse, coarse, two, two],
        in_specs=[SMEM, whole(uo), whole(ui), whole(w["lv"]), whole(w["d12"]), whole(w["dc12"])]
        + [edge(2, SP, 7), edge(2, SP, 7), edge(2, CP, 7), edge(2, CP, 7)],
        out_specs=[edge(2, SP, 7), edge(2, SP, 7), edge(2, CP, 7), edge(2, CP, 7), whole(two), whole(two)],
        input_output_aliases={6: 0, 7: 1, 8: 2, 9: 3},
        name="old_edge",
        **PARAMS,
    )(info, uo, ui, w["lv"], w["d12"], w["dc12"], n1, s, r0, e0)
    no, ni = swap(outer, inner)

    n2, r1, e1, c1 = pl.pallas_call(
        mid_kernel,
        out_shape=[fine, coarse, coarse, coarse],
        scratch_shapes=[pltpu.VMEM(coarse.shape, F32)],
        name="mid",
        **PARAMS,
    )(n1, s, w["wfr"], w["wc"], w["d12"], w["dc12"])

    four = field(4, CP)
    n2, r1, e1, outer, inner = pl.pallas_call(
        mid_edge_kernel,
        grid=(2,),
        out_shape=[fine, coarse, coarse, four, four],
        in_specs=[SMEM, whole(no), whole(ni), whole(w["lv"]), whole(w["wr"]), whole(w["d12"]), whole(w["dc12"])]
        + [edge(4, CP, 3)] * 3
        + [edge(4, SP, 3), edge(4, CP, 3), edge(4, CP, 3)],
        out_specs=[edge(4, SP, 3), edge(4, CP, 3), edge(4, CP, 3), whole(four), whole(four)],
        input_output_aliases={10: 0, 11: 1, 12: 2},
        name="mid_edge",
        **PARAMS,
    )(info, no, ni, w["lv"], w["wr"], w["d12"], w["dc12"], r0, e0, c0, n2, r1, e1)
    ho, hi = swap(outer, inner)

    pieces = field(36, CP)
    ab, c2 = pl.pallas_call(
        last_kernel,
        out_shape=[pieces, coarse],
        in_specs=[SMEM] + [pl.BlockSpec(memory_space=pltpu.VMEM)] * 7,
        scratch_shapes=[pltpu.VMEM(coarse.shape, F32)],
        name="last",
        **PARAMS,
    )(info[1:2], n2, w["wr"], r0, r1, e0, e1, c0)
    ab = pl.pallas_call(
        last_edge_kernel,
        grid=(2,),
        out_shape=pieces,
        in_specs=[SMEM, whole(four), whole(four), whole(four), whole(four), edge(6, CP, 5)],
        out_specs=edge(6, CP, 5),
        input_output_aliases={5: 0},
        name="last_edge",
        **PARAMS,
    )(info, outer, inner, ho, hi, ab)

    slabs = range(SLABS)
    brought = [
        lax.ppermute(ab, AXES, [(device(p, s), host(s)) for s in slabs]) for p in range(SLICES)
    ]
    z0s, z12s = [], []
    z2 = above = below = None
    for p in range(SLICES):
        first = p == 0
        operands = [info] + ([] if first else [z2, above, below]) + [brought[p], w["wc"], w["dc12"]]
        z12, z2, up, down = pl.pallas_call(
            functools.partial(chain_kernel, first),
            out_shape=[field(2 * ROWS, CP), coarse, four, four],
            in_specs=[SMEM] + [pl.BlockSpec(memory_space=pltpu.VMEM)] * (len(operands) - 1),
            scratch_shapes=[pltpu.VMEM((ROWS + 4, CP, COLS), F32)],
            name="chain",
            **PARAMS,
        )(*operands)
        if p < SLICES - 1:
            above = lax.ppermute(down, AXES, [(host(s), host(s + 1)) for s in range(SLABS - 1)])
            below = lax.ppermute(up, AXES, [(host(s + 1), host(s)) for s in range(SLABS - 1)])
            z0s.append(lax.ppermute(z2, AXES, [(host(s), device(p + 1, s)) for s in slabs]))
        z12s.append(lax.ppermute(z12, AXES, [(host(s), device(p, s)) for s in slabs]))

    b1, b2 = pl.pallas_call(
        base_kernel, out_shape=[fine, fine], name="base", **PARAMS
    )(n1, n2, c1, c2, w["pro"], w["share"])
    b0 = lax.ppermute(b2, "tm", [(i, i + 1) for i in range(SLICES - 1)])
    vmem, hbm = pl.BlockSpec(memory_space=pltpu.VMEM), pl.BlockSpec(memory_space=pl.ANY)
    out = pl.pallas_call(
        out_kernel,
        out_shape=jax.ShapeDtypeStruct((3, SPECIES, ROWS, COLS), F32),
        in_specs=[SMEM] + [vmem] * 6 + [hbm] * (2 * SLICES - 1),
        scratch_shapes=[pltpu.VMEM((3 * ROWS, CP, COLS), F32), pltpu.SemaphoreType.DMA((2,))],
        name="out",
        **PARAMS,
    )(info, u[0], b0, b1, b2, w["pro"], w["share"], *z0s, *z12s)
    return out[None]


def solution(mesh):
    in_specs = (P("tm", None, None, "space", None), P(), P(), P(), P(), P(), P(), P())
    out_specs = P("tm", None, None, "space", None)
    return jax.shard_map(local, mesh=mesh, in_specs=in_specs, out_specs=out_specs, check_vma=False)
```

```python
import functools

import jax
import jax.numpy as jnp
from jax import lax
from jax.experimental import pallas as pl
from jax.experimental.pallas import tpu as pltpu
from jax.sharding import PartitionSpec as P

SPECIES, COARSE = 53, 21
SP, CP = 56, 24
ROWS, COLS = 16, 256
SLICES, SLABS = 8, 16
STEP, HALF, RELAX = 0.1, 0.05, 3.0
W0 = (5.0 / 24.0, 1.0 / 3.0, -1.0 / 24.0)
W1 = (-1.0 / 24.0, 1.0 / 3.0, 5.0 / 24.0)
F32, BF16 = jnp.float32, jnp.bfloat16
VMEM_LIMIT = 48 * 1024 * 1024


def split(x):
    hi = x.astype(BF16)
    lo = (x - hi.astype(F32)).astype(BF16)
    return jnp.concatenate([hi, lo], axis=0)


def thirds(x):
    hi = x.astype(BF16)
    rest = x - hi.astype(F32)
    mid = rest.astype(BF16)
    return jnp.concatenate([hi, mid, (rest - mid.astype(F32)).astype(BF16)], axis=0)


def zeros(rows):
    return jnp.zeros((rows, COLS), F32)


def dot(w, x):
    return jnp.dot(w, x, preferred_element_type=F32)


def stacked(x, squares):
    return split(jnp.concatenate([x, squares, zeros(16)], axis=0))


def lap_y(x):
    near = pltpu.roll(x, 1, 1) + pltpu.roll(x, COLS - 1, 1)
    far = pltpu.roll(x, 2, 1) + pltpu.roll(x, COLS - 2, 1)
    return 16.0 * near - far - 60.0 * x


def lap_x(row, x, low, high):
    total = None
    for offset, factor in ((-1, 16.0), (1, 16.0), (-2, -1.0), (2, -1.0)):
        if low <= x + offset < high:
            term = factor * row(x + offset)
            total = term if total is None else total + term
    return total


def beside(near, far):
    return 16.0 * near - far, -near


def prep_kernel(rates, pairs, diff, crates, cpairs, cdiff, smap, wf, wr, wfr, lv, wc, pro, d12, dc12, share, a, mi):
    row = lax.broadcasted_iota(jnp.int32, (SP, 128), 0)
    lane = lax.broadcasted_iota(jnp.int32, (SP, 128), 1)

    def framed(ref, rows, columns, height):
        a[...] = jnp.zeros((SP, 128), F32)
        a[:rows, :columns] = ref[...]
        return a[:height, :]

    def halves(x):
        hi = x.astype(BF16).astype(F32)
        return hi, (x - hi).astype(BF16).astype(F32)

    def column(values, height):
        return jnp.sum(jnp.where(row == lane, values, 0.0), axis=1, keepdims=True)[:height]

    eye = jnp.where(row == lane, RELAX, 0.0)
    fine = framed(rates, SPECIES, SPECIES, SP) - jnp.where(row < SPECIES, eye, 0.0)
    fine = fine + pltpu.roll(framed(pairs, SPECIES, SPECIES, SP), SP, 1)
    coarse = framed(crates, COARSE, COARSE, CP) - jnp.where(row < COARSE, eye, 0.0)[:CP]
    coarse = coarse + pltpu.roll(framed(cpairs, COARSE, COARSE, CP), CP, 1)
    diff_row = framed(diff, 1, SPECIES, 8)[0:1]
    d12[...] = jnp.broadcast_to(column(diff_row, SP) / 12.0, (SP, COLS))
    dc12[...] = jnp.broadcast_to(column(framed(cdiff, 1, COARSE, 8)[0:1], CP) / 12.0, (CP, COLS))
    mi[...] = jnp.full((SP, 128), -1, jnp.int32)
    mi[:SPECIES, 0:1] = smap[...]
    map_column = mi[:, 0:1]
    map_row = jnp.sum(jnp.where(row == lane, map_column, 0), axis=0, keepdims=True)
    lum = jnp.where((map_row == row[:CP]) & (lane[:CP] < SPECIES), 1.0, 0.0)
    counts = jnp.sum(lum, axis=1, keepdims=True)
    share[...] = jnp.broadcast_to(1.0 / jnp.maximum(counts, 1.0), (CP, COLS))
    lumped = jnp.dot(lum[:, :SP], fine, precision=lax.Precision.HIGHEST, preferred_element_type=F32)
    fh, fl = halves(fine)
    rh, rl = halves(lumped)
    dh, dl = halves(lum * diff_row)
    ch, cl = halves(coarse)
    f = jnp.concatenate([fh, fl], axis=0).astype(BF16)
    r = jnp.concatenate([rh, rl, lum, dh, dl, jnp.zeros((8, 128), F32)], axis=0).astype(BF16)
    for at in (0, 128):
        wf[:, at : at + 128] = f
        wr[:, at : at + 128] = r
        wfr[: 2 * SP, at : at + 128] = f
        wfr[2 * SP :, at : at + 128] = r
    v = jnp.concatenate([lum, dh, dl, jnp.zeros((8, 128), F32)], axis=0)
    lv[...] = (v + pltpu.roll(v, 64, 1)).astype(BF16)
    c = jnp.concatenate([ch, cl], axis=0)
    wc[...] = (c + pltpu.roll(c, 64, 1)).astype(BF16)
    lane96 = lax.broadcasted_iota(jnp.int32, (SP, 96), 1)
    pro[...] = jnp.where(map_column == lane96 % 32, 1.0, 0.0).astype(BF16)


def first_kernel(info, u, outer, inner):
    at_top = info[0] == 0
    for m in range(3):
        for r in range(2):
            first, last = u[m, :, r, :], u[m, :, ROWS - 2 + r, :]
            for out, value in ((outer, jnp.where(at_top, first, last)), (inner, jnp.where(at_top, last, first))):
                out[m, r, SP - 8 :, :] = zeros(8)
                out[m, r, :SPECIES, :] = value


def restricted(y):
    return y[0:24] + y[24:48], y[48:72], y[72:96] + y[96:120]


MIX0 = [STEP * w for w in W0]
MIXS = [STEP * W1[0], STEP * W1[1] - HALF, STEP * W1[2]]


def mixed(factors, values):
    return factors[0] * values[0] + factors[1] * values[1] + factors[2] * values[2]


def old_kernel(u, wf, wr, wc, d12, dc12, n1, s, r0, e0, c0, ut, p0s, pss, v0s):
    for x in range(ROWS):
        for m in range(3):
            ut[x, m, SP - 8 :, :] = zeros(8)
            ut[x, m, :SPECIES, :] = u[m, :, x, :]
        us = [ut[x, m] for m in range(3)]
        qs = [v * v for v in us]
        p0, ps = mixed(MIX0, us), mixed(MIXS, us)
        y = dot(wf[...], stacked(p0, mixed(MIX0, qs)))
        n1[x] = us[0] + (y[:SP] + y[SP:]) + d12[...] * lap_y(p0)
        y = dot(wf[...], stacked(ps, mixed(MIXS, qs)))
        s[x] = (y[:SP] + y[SP:]) + d12[...] * lap_y(ps)
        r, c, v = restricted(dot(wr[...], stacked(us[0], qs[0])))
        r0[x] = r + lap_y(v) * (1.0 / 12.0)
        y = dot(wc[...], stacked(c, c * c))
        e0[x] = (y[:CP] + y[CP:]) + dc12[...] * lap_y(c)
        p0s[x], pss[x], v0s[x], c0[x] = p0, ps, v, c
    for x in range(ROWS):
        n1[x] += d12[...] * lap_x(lambda i: p0s[i], x, 0, ROWS)
        s[x] += d12[...] * lap_x(lambda i: pss[i], x, 0, ROWS)
        r0[x] += lap_x(lambda i: v0s[i], x, 0, ROWS) * (1.0 / 12.0)
        e0[x] += dc12[...] * lap_x(lambda i: c0[i], x, 0, ROWS)


def lumped_halo(lv, row):
    y = dot(lv[...], split(jnp.concatenate([row, zeros(8)], axis=0)))
    return y[0:24], y[24:48] + y[48:72]


SIDES = (((0, 1), (1, 0)), ((ROWS - 1, ROWS - 2), (0, 1)))


def pick_halo(info, side, outer, inner):
    take = info[0] == side
    return lambda *at: jnp.where(take, outer[at], inner[at])


def send(info, outer, inner, tops, bottoms):
    at_top = info[0] == 0
    for r, (top, bottom) in enumerate(zip(tops, bottoms)):
        outer[r] = jnp.where(at_top, top, bottom)
        inner[r] = jnp.where(at_top, bottom, top)


def old_edge_kernel(info, uo, ui, lv, d12, dc12, n1i, si, r0i, e0i, n1, s, r0, e0, outer, inner):
    for side, (rows, order) in enumerate(SIDES):
        halo = pick_halo(info, side, uo, ui)
        us = [[halo(m, r) for m in range(3)] for r in order]
        p0 = beside(*[mixed(MIX0, v) for v in us])
        ps = beside(*[mixed(MIXS, v) for v in us])
        lumped = [lumped_halo(lv, v[0]) for v in us]
        c = beside(lumped[0][0], lumped[1][0])
        v = beside(lumped[0][1], lumped[1][1])
        for i, x in enumerate(rows):
            n1[x] = n1i[x] + d12[...] * p0[i]
            s[x] = si[x] + d12[...] * ps[i]
            r0[x] = r0i[x] + v[i] * (1.0 / 12.0)
            e0[x] = e0i[x] + dc12[...] * c[i]
    send(info, outer, inner, [n1[0], n1[1]], [n1[ROWS - 2], n1[ROWS - 1]])


def mid_kernel(n1, s, wfr, wc, d12, dc12, n2, r1, e1, c1, v1s):
    for x in range(ROWS):
        n = n1[x]
        y = dot(wfr[...], stacked(n, n * n))
        lap = lap_y(n) + lap_x(lambda i: n1[i], x, 0, ROWS)
        n2[x] = n + HALF * ((y[:SP] + y[SP : 2 * SP]) + d12[...] * lap) + s[x]
        r, c, v = restricted(y[2 * SP :])
        r1[x] = r + lap_y(v) * (1.0 / 12.0)
        y = dot(wc[...], stacked(c, c * c))
        e1[x] = (y[:CP] + y[CP:]) + dc12[...] * lap_y(c)
        v1s[x], c1[x] = v, c
    for x in range(ROWS):
        r1[x] += lap_x(lambda i: v1s[i], x, 0, ROWS) * (1.0 / 12.0)
        e1[x] += dc12[...] * lap_x(lambda i: c1[i], x, 0, ROWS)


def lumped_old(first, c0, e0):
    return jnp.where(first, c0, -HALF * e0)


def piece_a(first, x, g2, r0, r1, e0, c0):
    return mixed(MIX0, (r0[x], r1[x], g2)) + lumped_old(first, c0[x], e0[x])


def mid_edge_kernel(info, no, ni, lv, wr, d12, dc12, r0, e0, c0, n2i, r1i, e1i, n2, r1, e1, outer, inner):
    first = info[1] == 0
    messages = []
    for side, (rows, order) in enumerate(SIDES):
        halo = pick_halo(info, side, no, ni)
        ns = [halo(r) for r in order]
        lumped = [lumped_halo(lv, v) for v in ns]
        c = beside(lumped[0][0], lumped[1][0])
        v = beside(lumped[0][1], lumped[1][1])
        n = beside(*ns)
        for i, x in enumerate(rows):
            n2[x] = n2i[x] + (HALF * d12[...]) * n[i]
            r1[x] = r1i[x] + v[i] * (1.0 / 12.0)
            e1[x] = e1i[x] + dc12[...] * c[i]
        step = 1 if side == 0 else -1
        near = [rows[0] + step * i for i in range(4)]
        terms = [restricted(dot(wr[...], stacked(n2[x], n2[x] * n2[x]))) for x in near[:2]]
        terms += [restricted(dot(wr[...], stacked(n2i[x], n2i[x] * n2i[x]))) for x in near[2:]]
        vs = [t[2] for t in terms]
        laps = [16.0 * vs[1] - vs[2], 16.0 * (vs[0] + vs[2]) - vs[3]]
        pieces = [
            piece_a(first, x, terms[i][0] + (lap_y(vs[i]) + laps[i]) * (1.0 / 12.0), r0, r1, e0, c0)
            for i, x in enumerate(rows)
        ]
        messages.append(pieces[::step] + vs[:2][::step])
    send(info, outer, inner, *messages)


def row_a(x):
    return x + 2


def row_b(x):
    return x + 4 + ROWS


def last_kernel(info, n2, wr, r0, r1, e0, e1, c0, ab, c2, v2s):
    first = info[1] == 0
    gs = []
    for x in range(ROWS):
        r, c, v = restricted(dot(wr[...], stacked(n2[x], n2[x] * n2[x])))
        gs.append(r + lap_y(v) * (1.0 / 12.0))
        v2s[x], c2[x] = v, c
    for x in range(ROWS):
        g2 = gs[x] + lap_x(lambda i: v2s[i], x, 0, ROWS) * (1.0 / 12.0)
        ab[row_a(x)] = piece_a(first, x, g2, r0, r1, e0, c0)
        ab[row_b(x)] = (
            (STEP * W1[0]) * r0[x] + (STEP * W1[1]) * r1[x] + (STEP * W1[2]) * g2 - HALF * e1[x]
        )


def last_edge_kernel(info, mo, mi, ho, hi, abi, ab, outer, inner):
    ka, kb = STEP * W0[2] / 12.0, STEP * W1[2] / 12.0
    for side, (rows, order) in enumerate(SIDES):
        inside = info[2] > 0 if side == 0 else info[2] < SLABS - 1
        own, halo = pick_halo(info, side, mo, mi), pick_halo(info, side, ho, hi)
        fix = beside(*[halo(2 + r) for r in order])
        theirs = beside(*[own(2 + r) for r in order[::-1]])
        step = 1 if side == 0 else -1
        for i, x in enumerate(rows):
            ab[row_a(x)] = abi[row_a(x)] + ka * fix[i]
            ab[row_b(x)] = abi[row_b(x)] + kb * fix[i]
            ab[row_a(rows[0] - step * (i + 1))] = jnp.where(inside, halo(order[i]) + ka * theirs[i], 0.0)
    tops = [abi[row_a(x)] for x in range(2, 6)] + [ab[row_b(x)] for x in (0, 1)] + [abi[row_b(x)] for x in (2, 3)]
    bottoms = [abi[row_a(x)] for x in range(10, 14)] + [abi[row_b(x)] for x in (12, 13)]
    bottoms += [ab[row_b(x)] for x in (14, 15)]
    send(info, outer, inner, tops, bottoms)


AB_ROWS, EXT_ROWS = 2 * ROWS + 4, 2 * ROWS + 20


def extend_kernel(info, ab, eo, ei, ext):
    for x in range(AB_ROWS):
        ext[x] = ab[x]
    for side in range(2):
        halo = pick_halo(info, side, eo, ei)
        for r in range(8):
            ext[AB_ROWS + 8 * side + r] = halo(r)


def ext_a(ext, x):
    if -2 <= x < ROWS + 2:
        return ext[row_a(x)]
    return ext[AB_ROWS + x + 6] if x < 0 else ext[AB_ROWS + 8 + x - (ROWS + 2)]


def ext_b(ext, x):
    if 0 <= x < ROWS:
        return ext[row_b(x)]
    return ext[AB_ROWS + 4 + x + 4] if x < 0 else ext[AB_ROWS + 12 + x - ROWS]


def swept(info, z, x, reach, add, wc, dc12):
    value = z(x)
    y = dot(wc[...], stacked(value, value * value))
    lap = lap_y(value) + lap_x(z, x, -reach, ROWS + reach)
    value = value + HALF * ((y[:CP] + y[CP:]) + dc12[...] * lap) + add
    if x < 0:
        value = jnp.where(info[2] > 0, value, 0.0)
    elif x >= ROWS:
        value = jnp.where(info[2] < SLABS - 1, value, 0.0)
    return value


def begin(info, z0, zo, zi, depth):
    top, bottom = pick_halo(info, 0, zo, zi), pick_halo(info, 1, zo, zi)

    def row(x):
        if x < 0:
            return top(x + depth)
        return bottom(x - ROWS) if x >= ROWS else z0[x]

    return row


def from_scratch(ref, reach):
    return lambda x: ref[x + reach]


def give(info, depth, message, outer, inner, value):
    for x in range(ROWS):
        message[x] = value(x)
    send(info, outer, inner, [value(x) for x in range(depth)], [value(x) for x in range(ROWS - depth, ROWS)])


def start_kernel(info, ab, wc, dc12, result, message, outer, inner):
    @pl.when(info[1] == 0)
    def _():
        z1 = lambda x: ab[row_a(x)]
        for x in range(ROWS):
            result[x] = zeros(CP)
            result[ROWS + x] = z1(x)
            result[2 * ROWS + x] = swept(info, z1, x, 2, ab[row_b(x)], wc, dc12)
        give(info, 8, message, outer, inner, lambda x: result[2 * ROWS + x])


def pair_kernel(at, depth, info, z0, zo, zi, exta, abb, wc, dc12, ra, rb, message, outer, inner, za, zb, zc):
    @pl.when(info[1] == at)
    def _():
        z = begin(info, z0, zo, zi, 8)
        for x in range(-6, ROWS + 6):
            za[x + 6] = swept(info, z, x, 8, ext_a(exta, x), wc, dc12)
        z = from_scratch(za, 6)
        for x in range(-4, ROWS + 4):
            zb[x + 4] = swept(info, z, x, 6, ext_b(exta, x), wc, dc12)
        z = from_scratch(zb, 4)
        for x in range(-2, ROWS + 2):
            zc[x + 2] = swept(info, z, x, 4, abb[row_a(x)], wc, dc12)
        z = from_scratch(zc, 2)
        for x in range(ROWS):
            ra[x], ra[ROWS + x], ra[2 * ROWS + x] = z0[x], za[x + 6], zb[x + 4]
            rb[x], rb[ROWS + x] = zb[x + 4], zc[x + 2]
            rb[2 * ROWS + x] = swept(info, z, x, 2, abb[row_b(x)], wc, dc12)
        give(info, depth, message, outer, inner, lambda x: rb[2 * ROWS + x])


def single_kernel(at, info, z0, zo, zi, ab, wc, dc12, result, za):
    @pl.when(info[1] == at)
    def _():
        z = begin(info, z0, zo, zi, 4)
        for x in range(-2, ROWS + 2):
            za[x + 2] = swept(info, z, x, 4, ab[row_a(x)], wc, dc12)
        z = from_scratch(za, 2)
        for x in range(ROWS):
            result[x], result[ROWS + x] = z0[x], za[x + 2]
            result[2 * ROWS + x] = swept(info, z, x, 2, ab[row_b(x)], wc, dc12)


def base_kernel(n1, n2, c1, c2, pro, share, b1, b2):
    for x in range(ROWS):
        for n, c, b in ((n1, c1, b1), (n2, c2, b2)):
            value = thirds(jnp.concatenate([share[...] * c[x], zeros(8)], axis=0))
            b[:, x, :] = (n[x] - dot(pro[...], value))[:SPECIES]


def out_kernel(info, where, u, b0, b1, b2, share, *refs):
    results, (out, z, spread, sem) = refs[:SLICES], refs[SLICES:]
    for p in range(SLICES):

        @pl.when(info[1] == p)
        def _():
            copy = pltpu.make_async_copy(results[p], z, sem)
            copy.start()
            copy.wait()

    for m in range(3):
        for x in range(ROWS):
            spread[m, :, x, :] = share[...] * z[m * ROWS + x]
    first = info[1] == 0
    for s in range(SPECIES):
        to = where[s]
        out[0, s] = jnp.where(first, u[0, s], b0[s]) + spread[0, to]
        out[1, s] = b1[s] + spread[1, to]
        out[2, s] = b2[s] + spread[2, to]


def field(*shape):
    return jax.ShapeDtypeStruct(shape + (COLS,), F32)


SMEM = pl.BlockSpec(memory_space=pltpu.SMEM)
VMEM = pl.BlockSpec(memory_space=pltpu.VMEM)
ANY = pl.BlockSpec(memory_space=pl.ANY)


def call(kernel, name, outs, *args, specs=None, scratch=(), alias=None):
    specs = specs or [SMEM if a.dtype == jnp.int32 and a.ndim == 1 else VMEM for a in args]
    return pl.pallas_call(
        kernel,
        out_shape=outs,
        in_specs=specs,
        scratch_shapes=[pltpu.VMEM(f.shape, f.dtype) if isinstance(f, jax.ShapeDtypeStruct) else f for f in scratch],
        input_output_aliases=alias or {},
        compiler_params=pltpu.CompilerParams(vmem_limit_bytes=VMEM_LIMIT),
        name=name,
    )(*args)


AXES = ("tm", "space")
OUTER = [(s, s + 1) for s in range(1, SLABS - 1, 2)] + [(s + 1, s) for s in range(1, SLABS - 1, 2)]
INNER = [(s, s ^ 1) for s in range(SLABS)]
SAME = [(s, s) for s in range(SLABS)]


def moved(value, slices, slabs):
    route = [(p * SLABS + s, q * SLABS + t) for p, q in slices for s, t in slabs]
    return lax.ppermute(value, AXES, route)


def swap(outer, inner, slices=tuple(range(SLICES))):
    pairs = [(p, p) for p in slices]
    got_inner = moved(inner, pairs, INNER)
    got_outer = moved(outer, pairs, OUTER)
    return got_outer, got_inner


def hop(message, outer, inner, p, q):
    return moved(message, [(p, q)], SAME), moved(outer, [(p, q)], OUTER), moved(inner, [(p, q)], INNER)


def after(value, other):
    return lax.optimization_barrier((value, other))[0]


def local(fine_nodes, fine_rates, fine_pairs, fine_diff, coarse_rates, coarse_pairs, coarse_diff, species_map):
    slice_at, slab = lax.axis_index("tm"), lax.axis_index("space")
    info = jnp.stack([slab % 2, slice_at, slab]).astype(jnp.int32)
    nodes = fine_nodes[0]
    fine, coarse = field(ROWS, SP), field(ROWS, CP)
    message = field(3, 2, SP)
    outer, inner = call(first_kernel, "first", [message, message], info, nodes)
    uo, ui = swap(outer, inner)

    def bf16(*shape):
        return jax.ShapeDtypeStruct(shape, BF16)

    wf, wr, wfr, lv, wc, pro, d12, dc12, share = call(
        prep_kernel,
        "prep",
        [bf16(2 * SP, 256), bf16(128, 256), bf16(2 * SP + 128, 256), bf16(80, 128), bf16(2 * CP, 128), bf16(SP, 96)]
        + [field(SP), field(CP), field(CP)],
        fine_rates,
        fine_pairs,
        fine_diff.reshape(1, SPECIES),
        coarse_rates,
        coarse_pairs,
        coarse_diff.reshape(1, COARSE),
        species_map,
        scratch=[pltpu.VMEM((SP, 128), F32), pltpu.VMEM((SP, 128), jnp.int32)],
    )
    n1, s, r0, e0, c0 = call(
        old_kernel,
        "old",
        [fine, fine, coarse, coarse, coarse],
        *(nodes, wf, wr, wc, d12, dc12),
        scratch=[field(ROWS, 3, SP), fine, fine, coarse],
    )
    two, four, eight = field(2, SP), field(4, CP), field(8, CP)
    n1, s, r0, e0, outer, inner = call(
        old_edge_kernel,
        "old_edge",
        [fine, fine, coarse, coarse, two, two],
        *(info, uo, ui, lv, d12, dc12, n1, s, r0, e0),
        alias={6: 0, 7: 1, 8: 2, 9: 3},
    )
    no, ni = swap(outer, inner)
    n2, r1, e1, c1 = call(
        mid_kernel, "mid", [fine, coarse, coarse, coarse], n1, s, wfr, wc, d12, dc12, scratch=[coarse]
    )
    n2, r1, e1, outer, inner = call(
        mid_edge_kernel,
        "mid_edge",
        [fine, coarse, coarse, four, four],
        *(info, no, ni, lv, wr, d12, dc12, r0, e0, c0, n2, r1, e1),
        alias={10: 0, 11: 1, 12: 2},
    )
    ho, hi = swap(outer, inner)
    pieces, extended = field(AB_ROWS, CP), field(EXT_ROWS, CP)
    ab, c2 = call(
        last_kernel, "last", [pieces, coarse], *(info, n2, wr, r0, r1, e0, e1, c0), scratch=[coarse]
    )
    ab, ext_outer, ext_inner = call(
        last_edge_kernel, "last_edge", [pieces, eight, eight], info, outer, inner, ho, hi, ab, alias={5: 0}
    )

    result = field(3 * ROWS, CP)
    result0, *sent = call(start_kernel, "start", [result, coarse, eight, eight], info, ab, wc, dc12)
    z = hop(*sent, 0, 1)
    ext_outer, ext_inner = after(ext_outer, sent[0]), after(ext_inner, sent[0])
    eo, ei = swap(ext_outer, ext_inner, (1, 3, 5))
    ext = call(extend_kernel, "extend", extended, info, ab, eo, ei)
    ab_two = moved(after(ab, sent[0]), [(2, 1)], SAME)
    ext_odd = moved(ext, [(3, 4), (5, 6)], SAME)

    def pair(at, depth, z, exta, abb):
        return call(
            functools.partial(pair_kernel, at, depth),
            "pair",
            [result, result, coarse, field(depth, CP), field(depth, CP)],
            *(info, *z, exta, abb, wc, dc12),
            scratch=[field(ROWS + 12, CP), field(ROWS + 8, CP), field(ROWS + 4, CP)],
        )

    result1, rb, *sent = pair(1, 8, z, ext, ab_two)
    z = hop(*sent, 1, 4)
    result2 = moved(rb, [(1, 2)], SAME)
    b1, b2 = call(base_kernel, "base", [field(SPECIES, ROWS)] * 2, after(n1, result0), n2, c1, c2, pro, share)
    b0 = moved(b2, [(p, p + 1) for p in range(SLICES - 1)], SAME)
    ra, result4, *sent = pair(4, 8, z, ext_odd, ab)
    z = hop(*sent, 4, 6)
    result3 = moved(ra, [(4, 3)], SAME)
    ra, result6, *sent = pair(6, 4, z, ext_odd, ab)
    z = hop(*sent, 6, 7)
    result5 = moved(ra, [(6, 5)], SAME)
    result7 = call(
        functools.partial(single_kernel, 7),
        "single",
        result,
        *(info, *z, ab, wc, dc12),
        scratch=[field(ROWS + 4, CP)],
    )
    results = [result0, result1, result2, result3, result4, result5, result6, result7]
    out = call(
        out_kernel,
        "out",
        field(3, SPECIES, ROWS),
        *(info, species_map[:, 0], nodes, b0, b1, b2, share, *results),
        specs=[SMEM, SMEM] + [VMEM] * 5 + [ANY] * SLICES,
        scratch=[result, field(3, CP, ROWS), pltpu.SemaphoreType.DMA],
    )
    return out[None]


def solution(mesh):
    in_specs = (P("tm", None, None, "space", None), P(), P(), P(), P(), P(), P(), P())
    out_specs = P("tm", None, None, "space", None)
    return jax.shard_map(local, mesh=mesh, in_specs=in_specs, out_specs=out_specs, check_vma=False)
```

```python
import functools

import jax
import jax.numpy as jnp
from jax import lax
from jax.experimental import pallas as pl
from jax.experimental.pallas import tpu as pltpu
from jax.sharding import PartitionSpec as P

SPECIES, COARSE = 53, 21
SP, CP = 56, 24
ROWS, COLS = 16, 256
SLICES, SLABS = 8, 16
STEP, HALF, RELAX = 0.1, 0.05, 3.0
W0 = (5.0 / 24.0, 1.0 / 3.0, -1.0 / 24.0)
W1 = (-1.0 / 24.0, 1.0 / 3.0, 5.0 / 24.0)
F32, BF16 = jnp.float32, jnp.bfloat16
VMEM_LIMIT = 48 * 1024 * 1024


def split(x):
    hi = x.astype(BF16)
    lo = (x - hi.astype(F32)).astype(BF16)
    return jnp.concatenate([hi, lo], axis=0)


def thirds(x):
    hi = x.astype(BF16)
    rest = x - hi.astype(F32)
    mid = rest.astype(BF16)
    return jnp.concatenate([hi, mid, (rest - mid.astype(F32)).astype(BF16)], axis=0)


def zeros(rows):
    return jnp.zeros((rows, COLS), F32)


def dot(w, x):
    return jnp.dot(w, x, preferred_element_type=F32)


def stacked(x, squares):
    return split(jnp.concatenate([x, squares, zeros(16)], axis=0))


def lap_y(x):
    near = pltpu.roll(x, 1, 1) + pltpu.roll(x, COLS - 1, 1)
    far = pltpu.roll(x, 2, 1) + pltpu.roll(x, COLS - 2, 1)
    return 16.0 * near - far - 60.0 * x


def lap_x(row, x, low, high):
    total = None
    for offset, factor in ((-1, 16.0), (1, 16.0), (-2, -1.0), (2, -1.0)):
        if low <= x + offset < high:
            term = factor * row(x + offset)
            total = term if total is None else total + term
    return total


def beside(near, far):
    return 16.0 * near - far, -near


def prep_kernel(rates, pairs, diff, crates, cpairs, cdiff, smap, wf, wr, wfr, lv, wc, pro, d12, dc12, share, a, mi):
    row = lax.broadcasted_iota(jnp.int32, (SP, 128), 0)
    lane = lax.broadcasted_iota(jnp.int32, (SP, 128), 1)

    def framed(ref, rows, columns, height):
        a[...] = jnp.zeros((SP, 128), F32)
        a[:rows, :columns] = ref[...]
        return a[:height, :]

    def halves(x):
        hi = x.astype(BF16).astype(F32)
        return hi, (x - hi).astype(BF16).astype(F32)

    def column(values, height):
        return jnp.sum(jnp.where(row == lane, values, 0.0), axis=1, keepdims=True)[:height]

    eye = jnp.where(row == lane, RELAX, 0.0)
    fine = framed(rates, SPECIES, SPECIES, SP) - jnp.where(row < SPECIES, eye, 0.0)
    fine = fine + pltpu.roll(framed(pairs, SPECIES, SPECIES, SP), SP, 1)
    coarse = framed(crates, COARSE, COARSE, CP) - jnp.where(row < COARSE, eye, 0.0)[:CP]
    coarse = coarse + pltpu.roll(framed(cpairs, COARSE, COARSE, CP), CP, 1)
    diff_row = framed(diff, 1, SPECIES, 8)[0:1]
    d12[...] = jnp.broadcast_to(column(diff_row, SP) / 12.0, (SP, COLS))
    dc12[...] = jnp.broadcast_to(column(framed(cdiff, 1, COARSE, 8)[0:1], CP) / 12.0, (CP, COLS))
    mi[...] = jnp.full((SP, 128), -1, jnp.int32)
    mi[:SPECIES, 0:1] = smap[...]
    map_column = mi[:, 0:1]
    map_row = jnp.sum(jnp.where(row == lane, map_column, 0), axis=0, keepdims=True)
    lum = jnp.where((map_row == row[:CP]) & (lane[:CP] < SPECIES), 1.0, 0.0)
    counts = jnp.sum(lum, axis=1, keepdims=True)
    share[...] = jnp.broadcast_to(1.0 / jnp.maximum(counts, 1.0), (CP, COLS))
    lumped = jnp.dot(lum[:, :SP], fine, precision=lax.Precision.HIGHEST, preferred_element_type=F32)
    fh, fl = halves(fine)
    rh, rl = halves(lumped)
    dh, dl = halves(lum * diff_row)
    ch, cl = halves(coarse)
    f = jnp.concatenate([fh, fl], axis=0).astype(BF16)
    r = jnp.concatenate([rh, rl, lum, dh, dl, jnp.zeros((8, 128), F32)], axis=0).astype(BF16)
    for at in (0, 128):
        wf[:, at : at + 128] = f
        wr[:, at : at + 128] = r
        wfr[: 2 * SP, at : at + 128] = f
        wfr[2 * SP :, at : at + 128] = r
    v = jnp.concatenate([lum, dh, dl, jnp.zeros((8, 128), F32)], axis=0)
    lv[...] = (v + pltpu.roll(v, 64, 1)).astype(BF16)
    c = jnp.concatenate([ch, cl], axis=0)
    wc[...] = (c + pltpu.roll(c, 64, 1)).astype(BF16)
    lane96 = lax.broadcasted_iota(jnp.int32, (SP, 96), 1)
    pro[...] = jnp.where(map_column == lane96 % 32, 1.0, 0.0).astype(BF16)


def first_kernel(info, u, outer, inner):
    at_top = info[0] == 0
    for m in range(3):
        for r in range(2):
            first, last = u[m, :, r, :], u[m, :, ROWS - 2 + r, :]
            for out, value in ((outer, jnp.where(at_top, first, last)), (inner, jnp.where(at_top, last, first))):
                out[m, r, SP - 8 :, :] = zeros(8)
                out[m, r, :SPECIES, :] = value


def restricted(y):
    return y[0:24] + y[24:48], y[48:72], y[72:96] + y[96:120]


MIX0 = [STEP * w for w in W0]
MIXS = [STEP * W1[0], STEP * W1[1] - HALF, STEP * W1[2]]


def mixed(factors, values):
    return factors[0] * values[0] + factors[1] * values[1] + factors[2] * values[2]


def old_kernel(u, wf, wr, wc, d12, dc12, n1, s, r0, e0, c0, ut, p0s, pss, v0s):
    for x in range(ROWS):
        for m in range(3):
            ut[x, m, SP - 8 :, :] = zeros(8)
            ut[x, m, :SPECIES, :] = u[m, :, x, :]
        us = [ut[x, m] for m in range(3)]
        qs = [v * v for v in us]
        p0, ps = mixed(MIX0, us), mixed(MIXS, us)
        y = dot(wf[...], stacked(p0, mixed(MIX0, qs)))
        n1[x] = us[0] + (y[:SP] + y[SP:]) + d12[...] * lap_y(p0)
        y = dot(wf[...], stacked(ps, mixed(MIXS, qs)))
        s[x] = (y[:SP] + y[SP:]) + d12[...] * lap_y(ps)
        r, c, v = restricted(dot(wr[...], stacked(us[0], qs[0])))
        r0[x] = r + lap_y(v) * (1.0 / 12.0)
        y = dot(wc[...], stacked(c, c * c))
        e0[x] = (y[:CP] + y[CP:]) + dc12[...] * lap_y(c)
        p0s[x], pss[x], v0s[x], c0[x] = p0, ps, v, c
    for x in range(ROWS):
        n1[x] += d12[...] * lap_x(lambda i: p0s[i], x, 0, ROWS)
        s[x] += d12[...] * lap_x(lambda i: pss[i], x, 0, ROWS)
        r0[x] += lap_x(lambda i: v0s[i], x, 0, ROWS) * (1.0 / 12.0)
        e0[x] += dc12[...] * lap_x(lambda i: c0[i], x, 0, ROWS)


def lumped_halo(lv, row):
    y = dot(lv[...], split(jnp.concatenate([row, zeros(8)], axis=0)))
    return y[0:24], y[24:48] + y[48:72]


SIDES = (((0, 1), (1, 0)), ((ROWS - 1, ROWS - 2), (0, 1)))


def pick_halo(info, side, outer, inner):
    take = info[0] == side
    return lambda *at: jnp.where(take, outer[at], inner[at])


def send(info, outer, inner, tops, bottoms):
    at_top = info[0] == 0
    for r, (top, bottom) in enumerate(zip(tops, bottoms)):
        outer[r] = jnp.where(at_top, top, bottom)
        inner[r] = jnp.where(at_top, bottom, top)


def old_edge_kernel(info, uo, ui, lv, d12, dc12, n1i, si, r0i, e0i, n1, s, r0, e0, outer, inner):
    for side, (rows, order) in enumerate(SIDES):
        halo = pick_halo(info, side, uo, ui)
        us = [[halo(m, r) for m in range(3)] for r in order]
        p0 = beside(*[mixed(MIX0, v) for v in us])
        ps = beside(*[mixed(MIXS, v) for v in us])
        lumped = [lumped_halo(lv, v[0]) for v in us]
        c = beside(lumped[0][0], lumped[1][0])
        v = beside(lumped[0][1], lumped[1][1])
        for i, x in enumerate(rows):
            n1[x] = n1i[x] + d12[...] * p0[i]
            s[x] = si[x] + d12[...] * ps[i]
            r0[x] = r0i[x] + v[i] * (1.0 / 12.0)
            e0[x] = e0i[x] + dc12[...] * c[i]
    send(info, outer, inner, [n1[0], n1[1]], [n1[ROWS - 2], n1[ROWS - 1]])


def mid_kernel(n1, s, wfr, wc, d12, dc12, n2, r1, e1, c1, v1s):
    for x in range(ROWS):
        n = n1[x]
        y = dot(wfr[...], stacked(n, n * n))
        lap = lap_y(n) + lap_x(lambda i: n1[i], x, 0, ROWS)
        n2[x] = n + HALF * ((y[:SP] + y[SP : 2 * SP]) + d12[...] * lap) + s[x]
        r, c, v = restricted(y[2 * SP :])
        r1[x] = r + lap_y(v) * (1.0 / 12.0)
        y = dot(wc[...], stacked(c, c * c))
        e1[x] = (y[:CP] + y[CP:]) + dc12[...] * lap_y(c)
        v1s[x], c1[x] = v, c
    for x in range(ROWS):
        r1[x] += lap_x(lambda i: v1s[i], x, 0, ROWS) * (1.0 / 12.0)
        e1[x] += dc12[...] * lap_x(lambda i: c1[i], x, 0, ROWS)


def lumped_old(first, c0, e0):
    return jnp.where(first, c0, -HALF * e0)


def row_a(x):
    return x + 2


def row_b(x):
    return x + 4 + ROWS


AB_ROWS, EXT_ROWS = 2 * ROWS + 4, 2 * ROWS + 20


def ext_a(x):
    if -2 <= x < ROWS + 2:
        return row_a(x)
    return AB_ROWS + x + 6 if x < 0 else AB_ROWS + 8 + x - (ROWS + 2)


def ext_b(x):
    if 0 <= x < ROWS:
        return row_b(x)
    return AB_ROWS + 4 + x + 4 if x < 0 else AB_ROWS + 12 + x - ROWS


def mid_edge_kernel(info, no, ni, lv, wr, d12, dc12, r0, e0, c0, n2i, r1i, e1i, n2, r1, e1, ab, c2, outer, inner, v2s):
    first = info[1] == 0
    for side, (rows, order) in enumerate(SIDES):
        halo = pick_halo(info, side, no, ni)
        ns = [halo(r) for r in order]
        lumped = [lumped_halo(lv, v) for v in ns]
        c = beside(lumped[0][0], lumped[1][0])
        v = beside(lumped[0][1], lumped[1][1])
        n = beside(*ns)
        for i, x in enumerate(rows):
            n2[x] = n2i[x] + (HALF * d12[...]) * n[i]
            r1[x] = r1i[x] + v[i] * (1.0 / 12.0)
            e1[x] = e1i[x] + dc12[...] * c[i]
    gs = []
    for x in range(ROWS):
        value = n2[x] if x in (0, 1, ROWS - 2, ROWS - 1) else n2i[x]
        r, c2[x], v2s[x] = restricted(dot(wr[...], stacked(value, value * value)))
        gs.append(r)
    for x in range(ROWS):
        edge = x in (0, 1, ROWS - 2, ROWS - 1)
        mid, late = (r1[x], e1[x]) if edge else (r1i[x], e1i[x])
        g2 = gs[x] + (lap_y(v2s[x]) + lap_x(lambda i: v2s[i], x, 0, ROWS)) * (1.0 / 12.0)
        ab[row_a(x)] = mixed(MIX0, (r0[x], mid, g2)) + lumped_old(first, c0[x], e0[x])
        ab[row_b(x)] = mixed([STEP * w for w in W1], (r0[x], mid, g2)) - HALF * late
    top = [ab[row_a(x)] for x in range(6)] + [ab[row_b(x)] for x in range(4)] + [v2s[x] for x in range(2)]
    bottom = [ab[row_a(x)] for x in range(ROWS - 6, ROWS)] + [ab[row_b(x)] for x in range(ROWS - 4, ROWS)]
    send(info, outer, inner, top, bottom + [v2s[x] for x in range(ROWS - 2, ROWS)])


def last_edge_kernel(info, mo, mi, ho, hi, abi, ab, short):
    ka, kb = STEP * W0[2] / 12.0, STEP * W1[2] / 12.0
    done = {}
    for side, (rows, order) in enumerate(SIDES):
        inside = info[2] > 0 if side == 0 else info[2] < SLABS - 1
        own, halo = pick_halo(info, side, mo, mi), pick_halo(info, side, ho, hi)
        fix = beside(*[halo(10 + r) for r in order])
        theirs = beside(*[own(10 + r) for r in order[::-1]])
        for i, x in enumerate(rows):
            done[row_a(x)] = abi[row_a(x)] + ka * fix[i]
            done[row_b(x)] = abi[row_b(x)] + kb * fix[i]
        for depth, at, to, factor in ((6, 0, ext_a, ka), (4, 6, ext_b, kb)):
            for i in range(depth):
                x = -1 - i if side == 0 else ROWS + i
                value = halo(at + (depth - 1 - i if side == 0 else i))
                if i < 2:
                    value = value + factor * theirs[i]
                done[to(x)] = jnp.where(inside, value, 0.0)
    for at, value in done.items():
        ab[at] = value
    for at in range(AB_ROWS):
        short[at] = done[at] if at in done else abi[at]


def swept(info, z, x, reach, add, wc, dc12):
    value = z(x)
    y = dot(wc[...], stacked(value, value * value))
    lap = lap_y(value) + lap_x(z, x, -reach, ROWS + reach)
    value = value + HALF * ((y[:CP] + y[CP:]) + dc12[...] * lap) + add
    if x < 0:
        value = jnp.where(info[2] > 0, value, 0.0)
    elif x >= ROWS:
        value = jnp.where(info[2] < SLABS - 1, value, 0.0)
    return value


def begin(info, z0, zo, zi, depth):
    top, bottom = pick_halo(info, 0, zo, zi), pick_halo(info, 1, zo, zi)

    def row(x):
        if x < 0:
            return top(x + depth)
        return bottom(x - ROWS) if x >= ROWS else z0[x]

    return row


def from_scratch(ref, reach):
    return lambda x: ref[x + reach]


def give(info, depth, message, outer, inner, value):
    for x in range(ROWS):
        message[x] = value(x)
    send(info, outer, inner, [value(x) for x in range(depth)], [value(x) for x in range(ROWS - depth, ROWS)])


def hosting(info, hosts):
    return info[1] == jnp.where(info[0] == 0, hosts[0], hosts[1])


def start_kernel(hosts, info, ab, wc, dc12, rb, message, outer, inner):
    @pl.when(hosting(info, hosts))
    def _():
        z1 = lambda x: ab[row_a(x)]
        for x in range(ROWS):
            rb[x] = zeros(CP)
            rb[ROWS + x] = z1(x)
            rb[2 * ROWS + x] = swept(info, z1, x, 2, ab[row_b(x)], wc, dc12)
        give(info, 8, message, outer, inner, lambda x: rb[2 * ROWS + x])


def pair_kernel(
    hosts, depth, info, z0, zo, zi, mine, short, long, wc, dc12, rai, rbi, ra, rb, message, outer, inner, za, zb, zc
):
    def sweep(exta, abb):
        z = begin(info, z0, zo, zi, 8)
        for x in range(-6, ROWS + 6):
            za[x + 6] = swept(info, z, x, 8, exta[ext_a(x)], wc, dc12)
        z = from_scratch(za, 6)
        for x in range(-4, ROWS + 4):
            zb[x + 4] = swept(info, z, x, 6, exta[ext_b(x)], wc, dc12)
        z = from_scratch(zb, 4)
        for x in range(-2, ROWS + 2):
            zc[x + 2] = swept(info, z, x, 4, abb[row_a(x)], wc, dc12)
        z = from_scratch(zc, 2)
        for x in range(ROWS):
            ra[x], ra[ROWS + x], ra[2 * ROWS + x] = z0[x], za[x + 6], zb[x + 4]
            rb[x], rb[ROWS + x] = zb[x + 4], zc[x + 2]
            rb[2 * ROWS + x] = swept(info, z, x, 2, abb[row_b(x)], wc, dc12)
        give(info, depth, message, outer, inner, lambda x: rb[2 * ROWS + x])

    active, odd = hosting(info, hosts), info[1] % 2 == 1
    if hosts[0] % 2 or hosts[1] % 2:
        pl.when(active & odd)(lambda: sweep(mine, short))
    if not (hosts[0] % 2 and hosts[1] % 2):

        pl.when(active & (info[1] % 2 == 0))(lambda: sweep(long, mine))


def base_kernel(n1, n2, c1, c2, pro, share, b1, b2):
    for x in range(ROWS):
        for n, c, b in ((n1, c1, b1), (n2, c2, b2)):
            value = thirds(jnp.concatenate([share[...] * c[x], zeros(8)], axis=0))
            b[:, x, :] = (n[x] - dot(pro[...], value))[:SPECIES]


def out_kernel(
    info, where, u, b0, b1, b2, share, z0, zo, zi, ab, wc, dc12, ra, rb, out, z, za, spread, node, sem
):
    last = info[1] == SLICES - 1
    for parity, result in enumerate((rb, ra)):

        @pl.when((info[1] % 2 == parity) & (info[1] < SLICES - 1))
        def _():
            for x in range(3 * ROWS):
                z[x] = result[x]

    @pl.when(last)
    def _():
        for x in range(ROWS):
            z[x] = z0[x]

    def finish(m, base):
        for x in range(ROWS):
            spread[m, :, x, :] = share[...] * z[m * ROWS + x]
        for s in range(SPECIES):
            node[m, s] = base(s) + spread[m, where[s]]
        copy = pltpu.make_async_copy(node.at[m], out.at[m], sem.at[m])
        copy.start()
        return copy

    first = info[1] == 0
    copies = [finish(0, lambda s: jnp.where(first, u[0, s], b0[s]))]

    @pl.when(last)
    def _():
        row = begin(info, z0, zo, zi, 4)
        for x in range(-2, ROWS + 2):
            za[x + 2] = swept(info, row, x, 4, ab[row_a(x)], wc, dc12)
        row = from_scratch(za, 2)
        for x in range(ROWS):
            z[ROWS + x] = za[x + 2]
            z[2 * ROWS + x] = swept(info, row, x, 2, ab[row_b(x)], wc, dc12)

    copies += [finish(1, lambda s: b1[s]), finish(2, lambda s: b2[s])]
    for copy in copies:
        copy.wait()


def field(*shape):
    return jax.ShapeDtypeStruct(shape + (COLS,), F32)


SMEM = pl.BlockSpec(memory_space=pltpu.SMEM)
VMEM = pl.BlockSpec(memory_space=pltpu.VMEM)
ANY = pl.BlockSpec(memory_space=pl.ANY)


def call(kernel, name, outs, *args, scratch=(), alias=None, out_specs=None):
    specs = [SMEM if a.dtype == jnp.int32 and a.ndim == 1 else VMEM for a in args]
    return pl.pallas_call(
        kernel,
        out_shape=outs,
        in_specs=specs,
        **({"out_specs": out_specs} if out_specs else {}),
        scratch_shapes=[pltpu.VMEM(f.shape, f.dtype) if isinstance(f, jax.ShapeDtypeStruct) else f for f in scratch],
        input_output_aliases=alias or {},
        compiler_params=pltpu.CompilerParams(vmem_limit_bytes=VMEM_LIMIT),
        name=name,
    )(*args)


AXES = ("tm", "space")
OUTER = [(s, s + 1) for s in range(1, SLABS - 1, 2)] + [(s + 1, s) for s in range(1, SLABS - 1, 2)]
INNER = [(s, s ^ 1) for s in range(SLABS)]
SAME = [(s, s) for s in range(SLABS)]
GROUPS = (((0,), (0, 0)), ((1, 2), (1, 1)), ((3, 4), (3, 4)), ((5, 6), (6, 5)), ((7,), (7, 7)))


def moved(value, *routes):
    pairs = [
        (source[s % 2] * SLABS + s, target[t % 2] * SLABS + t) for source, target, slabs in routes for s, t in slabs
    ]
    return lax.ppermute(value, AXES, pairs)


def both(p):
    return (p, p)


def swap(outer, inner):
    got_inner = moved(inner, *[(both(p), both(p), INNER) for p in range(SLICES)])
    got_outer = moved(outer, *[(both(p), both(p), OUTER) for p in range(SLICES)])
    return got_outer, got_inner


def hop(message, outer, inner, source, target):
    return [moved(value, (source, target, slabs)) for value, slabs in ((message, SAME), (outer, OUTER), (inner, INNER))]


def after(value, other):
    return lax.optimization_barrier((value, other))[0]


def local(fine_nodes, fine_rates, fine_pairs, fine_diff, coarse_rates, coarse_pairs, coarse_diff, species_map):
    slice_at, slab = lax.axis_index("tm"), lax.axis_index("space")
    info = jnp.stack([slab % 2, slice_at, slab]).astype(jnp.int32)
    nodes = fine_nodes[0]
    fine, coarse = field(ROWS, SP), field(ROWS, CP)
    message = field(3, 2, SP)
    outer, inner = call(first_kernel, "first", [message, message], info, nodes)
    uo, ui = swap(outer, inner)

    def bf16(*shape):
        return jax.ShapeDtypeStruct(shape, BF16)

    wf, wr, wfr, lv, wc, pro, d12, dc12, share = call(
        prep_kernel,
        "prep",
        [bf16(2 * SP, 256), bf16(128, 256), bf16(2 * SP + 128, 256), bf16(80, 128), bf16(2 * CP, 128), bf16(SP, 96)]
        + [field(SP), field(CP), field(CP)],
        fine_rates,
        fine_pairs,
        fine_diff.reshape(1, SPECIES),
        coarse_rates,
        coarse_pairs,
        coarse_diff.reshape(1, COARSE),
        species_map,
        scratch=[pltpu.VMEM((SP, 128), F32), pltpu.VMEM((SP, 128), jnp.int32)],
    )
    n1, s, r0, e0, c0 = call(
        old_kernel,
        "old",
        [fine, fine, coarse, coarse, coarse],
        *(nodes, wf, wr, wc, d12, dc12),
        scratch=[field(ROWS, 3, SP), fine, fine, coarse],
    )
    two, twelve, eight = field(2, SP), field(12, CP), field(8, CP)
    n1, s, r0, e0, outer, inner = call(
        old_edge_kernel,
        "old_edge",
        [fine, fine, coarse, coarse, two, two],
        *(info, uo, ui, lv, d12, dc12, n1, s, r0, e0),
        alias={6: 0, 7: 1, 8: 2, 9: 3},
    )
    no, ni = swap(outer, inner)
    n2, r1, e1, c1 = call(
        mid_kernel, "mid", [fine, coarse, coarse, coarse], n1, s, wfr, wc, d12, dc12, scratch=[coarse]
    )
    extended, short = field(EXT_ROWS, CP), field(AB_ROWS, CP)
    n2, r1, e1, abx, c2, outer, inner = call(
        mid_edge_kernel,
        "mid_edge",
        [fine, coarse, coarse, extended, coarse, twelve, twelve],
        *(info, no, ni, lv, wr, d12, dc12, r0, e0, c0, n2, r1, e1),
        alias={10: 0, 11: 1, 12: 2},
        scratch=[coarse],
    )
    ho, hi = swap(outer, inner)
    b1, b2 = call(base_kernel, "base", [field(SPECIES, ROWS)] * 2, n1, n2, c1, c2, pro, share)
    abx, ab = call(last_edge_kernel, "last_edge", [extended, short], info, outer, inner, ho, hi, abx, alias={5: 0})

    ab, abx = after(ab, b1), after(abx, b1)
    result = field(3 * ROWS, CP)
    pairs = [(slices, hosts) for slices, hosts in GROUPS if len(slices) == 2]
    short, long = [], []
    for slices, hosts in pairs:
        for core, host in enumerate(hosts):
            slabs = [(t, t) for t in range(core, SLABS, 2)]
            if host == slices[0]:
                short.append((both(slices[1]), both(host), slabs))
            else:
                long.append((both(slices[0]), both(host), slabs))
    short, long = moved(ab, *short), moved(abx, *long)
    rb, *sent = call(
        functools.partial(start_kernel, GROUPS[0][1]), "start", [result, coarse, eight, eight], info, ab, wc, dc12
    )
    ra = rb
    for at, (slices, hosts) in enumerate(GROUPS[1:], 1):
        z = hop(*sent, GROUPS[at - 1][1], hosts)
        if at == 1:
            *z, short, long = lax.optimization_barrier((*z, short, long))
            b0 = moved(after(b2, z[0]), *[(both(p), both(p + 1), SAME) for p in range(3, SLICES - 1)])
        elif at == 2:
            *z, b0 = lax.optimization_barrier((*z, b0))
            late = moved(after(b2, z[0]), *[(both(p), both(p + 1), SAME) for p in range(3)])
        elif at == 3:
            *z, late = lax.optimization_barrier((*z, late))
        else:
            ra = moved(ra, *[(hosts, both(slices[0]), SAME) for slices, hosts in pairs])
            rb = moved(rb, (both(0), both(0), SAME), *[(hosts, both(slices[1]), SAME) for slices, hosts in pairs])
            *z, ra, rb = lax.optimization_barrier((*z, ra, rb))
        if len(slices) == 2:
            depth = 4 * len(GROUPS[at + 1][0])
            ra, rb, *sent = call(
                functools.partial(pair_kernel, hosts, depth),
                "pair",
                [result, result, coarse, field(depth, CP), field(depth, CP)],
                *(info, *z, abx, short, long, wc, dc12, ra, rb),
                scratch=[field(ROWS + 12, CP), field(ROWS + 8, CP), field(ROWS + 4, CP)],
                alias={9: 0, 10: 1},
            )
    out = call(
        out_kernel,
        "out",
        field(3, SPECIES, ROWS),
        *(info, species_map[:, 0], nodes, b0 + late, b1, b2, share, *z, ab, wc, dc12, ra, rb),
        out_specs=ANY,
        scratch=[result, field(ROWS + 4, CP), field(3, CP, ROWS), field(3, SPECIES, ROWS), pltpu.SemaphoreType.DMA((3,))],
    )
    return out[None]


def solution(mesh):
    in_specs = (P("tm", None, None, "space", None), P(), P(), P(), P(), P(), P(), P())
    out_specs = P("tm", None, None, "space", None)
    return jax.shard_map(local, mesh=mesh, in_specs=in_specs, out_specs=out_specs, check_vma=False)
```

```python
import functools

import jax
import jax.numpy as jnp
from jax import lax
from jax.experimental import pallas as pl
from jax.experimental.pallas import tpu as pltpu
from jax.sharding import PartitionSpec as P

SPECIES, COARSE = 53, 21
SP, CP = 56, 24
ROWS, COLS = 16, 256
SLICES, SLABS = 8, 16
STEP, HALF, RELAX = 0.1, 0.05, 3.0
W0 = (5.0 / 24.0, 1.0 / 3.0, -1.0 / 24.0)
W1 = (-1.0 / 24.0, 1.0 / 3.0, 5.0 / 24.0)
F32, BF16 = jnp.float32, jnp.bfloat16
GROUPS = (((0,), (0, 0)), ((1, 2), (1, 1)), ((3, 4), (3, 4)), ((5, 6), (6, 5)), ((7,), (7, 7)))
VMEM_LIMIT = 24 * 1024 * 1024


def split(x):
    hi = x.astype(BF16)
    lo = (x - hi.astype(F32)).astype(BF16)
    return jnp.concatenate([hi, lo], axis=0)


def thirds(x):
    hi = x.astype(BF16)
    rest = x - hi.astype(F32)
    mid = rest.astype(BF16)
    return jnp.concatenate([hi, mid, (rest - mid.astype(F32)).astype(BF16)], axis=0)


def zeros(rows):
    return jnp.zeros((rows, COLS), F32)


def dot(w, x):
    return jnp.dot(w, x, preferred_element_type=F32)


def stacked(x, squares):
    return split(jnp.concatenate([x, squares, zeros(16)], axis=0))


def lap_y(x):
    near = pltpu.roll(x, 1, 1) + pltpu.roll(x, COLS - 1, 1)
    far = pltpu.roll(x, 2, 1) + pltpu.roll(x, COLS - 2, 1)
    return 16.0 * near - far - 60.0 * x


def lap_x(row, x, low, high):
    total = None
    for offset, factor in ((-1, 16.0), (1, 16.0), (-2, -1.0), (2, -1.0)):
        if low <= x + offset < high:
            term = factor * row(x + offset)
            total = term if total is None else total + term
    return total


def beside(near, far):
    return 16.0 * near - far, -near


def prep_kernel(rates, pairs, diff, crates, cpairs, cdiff, smap, wf, wr, wfr, lv, wc, pro, d12, dc12, share, a, mi):
    row = lax.broadcasted_iota(jnp.int32, (SP, 128), 0)
    lane = lax.broadcasted_iota(jnp.int32, (SP, 128), 1)

    def framed(ref, rows, columns, height):
        a[...] = jnp.zeros((SP, 128), F32)
        a[:rows, :columns] = ref[...]
        return a[:height, :]

    def halves(x):
        hi = x.astype(BF16).astype(F32)
        return hi, (x - hi).astype(BF16).astype(F32)

    def column(values, height):
        return jnp.sum(jnp.where(row == lane, values, 0.0), axis=1, keepdims=True)[:height]

    eye = jnp.where(row == lane, RELAX, 0.0)
    fine = framed(rates, SPECIES, SPECIES, SP) - jnp.where(row < SPECIES, eye, 0.0)
    fine = fine + pltpu.roll(framed(pairs, SPECIES, SPECIES, SP), SP, 1)
    coarse = framed(crates, COARSE, COARSE, CP) - jnp.where(row < COARSE, eye, 0.0)[:CP]
    coarse = coarse + pltpu.roll(framed(cpairs, COARSE, COARSE, CP), CP, 1)
    diff_row = framed(diff, 1, SPECIES, 8)[0:1]
    d12[...] = jnp.broadcast_to(column(diff_row, SP) / 12.0, (SP, COLS))
    dc12[...] = jnp.broadcast_to(column(framed(cdiff, 1, COARSE, 8)[0:1], CP) / 12.0, (CP, COLS))
    mi[...] = jnp.full((SP, 128), -1, jnp.int32)
    mi[:SPECIES, 0:1] = smap[...]
    map_column = mi[:, 0:1]
    map_row = jnp.sum(jnp.where(row == lane, map_column, 0), axis=0, keepdims=True)
    lum = jnp.where((map_row == row[:CP]) & (lane[:CP] < SPECIES), 1.0, 0.0)
    counts = jnp.sum(lum, axis=1, keepdims=True)
    share[...] = jnp.broadcast_to(1.0 / jnp.maximum(counts, 1.0), (CP, COLS))
    lumped = jnp.dot(lum[:, :SP], fine, precision=lax.Precision.HIGHEST, preferred_element_type=F32)
    fh, fl = halves(fine)
    rh, rl = halves(lumped)
    dh, dl = halves(lum * diff_row)
    ch, cl = halves(coarse)
    f = jnp.concatenate([fh, fl], axis=0).astype(BF16)
    r = jnp.concatenate([rh, rl, lum, dh, dl, jnp.zeros((8, 128), F32)], axis=0).astype(BF16)
    for at in (0, 128):
        wf[:, at : at + 128] = f
        wr[:, at : at + 128] = r
        wfr[: 2 * SP, at : at + 128] = f
        wfr[2 * SP :, at : at + 128] = r
    v = jnp.concatenate([lum, dh, dl, jnp.zeros((8, 128), F32)], axis=0)
    lv[...] = (v + pltpu.roll(v, 64, 1)).astype(BF16)
    c = jnp.concatenate([ch, cl], axis=0)
    wc[...] = (c + pltpu.roll(c, 64, 1)).astype(BF16)
    lane96 = lax.broadcasted_iota(jnp.int32, (SP, 96), 1)
    pro[...] = jnp.where(map_column == lane96 % 32, 1.0, 0.0).astype(BF16)


def first_kernel(info, u, outer, inner):
    at_top = info[0] == 0
    for m in range(3):
        for r in range(2):
            first, last = u[m, :, r, :], u[m, :, ROWS - 2 + r, :]
            for out, value in ((outer, jnp.where(at_top, first, last)), (inner, jnp.where(at_top, last, first))):
                out[m, r, SP - 8 :, :] = zeros(8)
                out[m, r, :SPECIES, :] = value


def restricted(y):
    return y[0:24] + y[24:48], y[48:72], y[72:96] + y[96:120]


MIX0 = [STEP * w for w in W0]
MIXS = [STEP * W1[0], STEP * W1[1] - HALF, STEP * W1[2]]


def mixed(factors, values):
    return factors[0] * values[0] + factors[1] * values[1] + factors[2] * values[2]


def old_kernel(u, wf, wr, wc, d12, dc12, n1, s, r0, e0, c0, ut, p0s, pss, v0s):
    for x in range(ROWS):
        for m in range(3):
            ut[x, m, SP - 8 :, :] = zeros(8)
            ut[x, m, :SPECIES, :] = u[m, :, x, :]
        us = [ut[x, m] for m in range(3)]
        qs = [v * v for v in us]
        p0, ps = mixed(MIX0, us), mixed(MIXS, us)
        y = dot(wf[...], stacked(p0, mixed(MIX0, qs)))
        n1[x] = us[0] + (y[:SP] + y[SP:]) + d12[...] * lap_y(p0)
        y = dot(wf[...], stacked(ps, mixed(MIXS, qs)))
        s[x] = (y[:SP] + y[SP:]) + d12[...] * lap_y(ps)
        r, c, v = restricted(dot(wr[...], stacked(us[0], qs[0])))
        r0[x] = r + lap_y(v) * (1.0 / 12.0)
        y = dot(wc[...], stacked(c, c * c))
        e0[x] = (y[:CP] + y[CP:]) + dc12[...] * lap_y(c)
        p0s[x], pss[x], v0s[x], c0[x] = p0, ps, v, c
    for x in range(ROWS):
        n1[x] += d12[...] * lap_x(lambda i: p0s[i], x, 0, ROWS)
        s[x] += d12[...] * lap_x(lambda i: pss[i], x, 0, ROWS)
        r0[x] += lap_x(lambda i: v0s[i], x, 0, ROWS) * (1.0 / 12.0)
        e0[x] += dc12[...] * lap_x(lambda i: c0[i], x, 0, ROWS)


def lumped_halo(lv, row):
    y = dot(lv[...], split(jnp.concatenate([row, zeros(8)], axis=0)))
    return y[0:24], y[24:48] + y[48:72]


SIDES = (((0, 1), (1, 0)), ((ROWS - 1, ROWS - 2), (0, 1)))


def pick_halo(info, side, outer, inner):
    take = info[0] == side
    return lambda *at: jnp.where(take, outer[at], inner[at])


def send(info, outer, inner, tops, bottoms):
    at_top = info[0] == 0
    for r, (top, bottom) in enumerate(zip(tops, bottoms)):
        outer[r] = jnp.where(at_top, top, bottom)
        inner[r] = jnp.where(at_top, bottom, top)


def old_edge_kernel(info, uo, ui, lv, d12, dc12, n1i, si, r0i, e0i, n1, s, r0, e0, outer, inner):
    for side, (rows, order) in enumerate(SIDES):
        halo = pick_halo(info, side, uo, ui)
        us = [[halo(m, r) for m in range(3)] for r in order]
        p0 = beside(*[mixed(MIX0, v) for v in us])
        ps = beside(*[mixed(MIXS, v) for v in us])
        lumped = [lumped_halo(lv, v[0]) for v in us]
        c = beside(lumped[0][0], lumped[1][0])
        v = beside(lumped[0][1], lumped[1][1])
        for i, x in enumerate(rows):
            n1[x] = n1i[x] + d12[...] * p0[i]
            s[x] = si[x] + d12[...] * ps[i]
            r0[x] = r0i[x] + v[i] * (1.0 / 12.0)
            e0[x] = e0i[x] + dc12[...] * c[i]
    send(info, outer, inner, [n1[0], n1[1]], [n1[ROWS - 2], n1[ROWS - 1]])


def mid_kernel(n1, s, wfr, wc, d12, dc12, n2, r1, e1, c1, v1s):
    for x in range(ROWS):
        n = n1[x]
        y = dot(wfr[...], stacked(n, n * n))
        lap = lap_y(n) + lap_x(lambda i: n1[i], x, 0, ROWS)
        n2[x] = n + HALF * ((y[:SP] + y[SP : 2 * SP]) + d12[...] * lap) + s[x]
        r, c, v = restricted(y[2 * SP :])
        r1[x] = r + lap_y(v) * (1.0 / 12.0)
        y = dot(wc[...], stacked(c, c * c))
        e1[x] = (y[:CP] + y[CP:]) + dc12[...] * lap_y(c)
        v1s[x], c1[x] = v, c
    for x in range(ROWS):
        r1[x] += lap_x(lambda i: v1s[i], x, 0, ROWS) * (1.0 / 12.0)
        e1[x] += dc12[...] * lap_x(lambda i: c1[i], x, 0, ROWS)


def lumped_old(first, c0, e0):
    return jnp.where(first, c0, -HALF * e0)


def row_a(x):
    return x + 2


def row_b(x):
    return x + 4 + ROWS


AB_ROWS, EXT_ROWS = 2 * ROWS + 4, 2 * ROWS + 20


def ext_a(x):
    if -2 <= x < ROWS + 2:
        return row_a(x)
    return AB_ROWS + x + 6 if x < 0 else AB_ROWS + 8 + x - (ROWS + 2)


def ext_b(x):
    if 0 <= x < ROWS:
        return row_b(x)
    return AB_ROWS + 4 + x + 4 if x < 0 else AB_ROWS + 12 + x - ROWS


def mid_edge_kernel(info, no, ni, lv, wr, d12, dc12, r0, e0, c0, n2i, r1i, e1i, n2, r1, e1, ab, c2, outer, inner, v2s):
    first = info[1] == 0
    for side, (rows, order) in enumerate(SIDES):
        halo = pick_halo(info, side, no, ni)
        ns = [halo(r) for r in order]
        lumped = [lumped_halo(lv, v) for v in ns]
        c = beside(lumped[0][0], lumped[1][0])
        v = beside(lumped[0][1], lumped[1][1])
        n = beside(*ns)
        for i, x in enumerate(rows):
            n2[x] = n2i[x] + (HALF * d12[...]) * n[i]
            r1[x] = r1i[x] + v[i] * (1.0 / 12.0)
            e1[x] = e1i[x] + dc12[...] * c[i]
    gs = []
    for x in range(ROWS):
        value = n2[x] if x in (0, 1, ROWS - 2, ROWS - 1) else n2i[x]
        r, c2[x], v2s[x] = restricted(dot(wr[...], stacked(value, value * value)))
        gs.append(r)
    for x in range(ROWS):
        edge = x in (0, 1, ROWS - 2, ROWS - 1)
        mid, late = (r1[x], e1[x]) if edge else (r1i[x], e1i[x])
        g2 = gs[x] + (lap_y(v2s[x]) + lap_x(lambda i: v2s[i], x, 0, ROWS)) * (1.0 / 12.0)
        ab[row_a(x)] = mixed(MIX0, (r0[x], mid, g2)) + lumped_old(first, c0[x], e0[x])
        ab[row_b(x)] = mixed([STEP * w for w in W1], (r0[x], mid, g2)) - HALF * late
    top = [ab[row_a(x)] for x in range(6)] + [ab[row_b(x)] for x in range(4)] + [v2s[x] for x in range(2)]
    bottom = [ab[row_a(x)] for x in range(ROWS - 6, ROWS)] + [ab[row_b(x)] for x in range(ROWS - 4, ROWS)]
    send(info, outer, inner, top, bottom + [v2s[x] for x in range(ROWS - 2, ROWS)])


def last_edge_kernel(info, mo, mi, ho, hi, abi, ab, short):
    ka, kb = STEP * W0[2] / 12.0, STEP * W1[2] / 12.0
    done = {}
    for side, (rows, order) in enumerate(SIDES):
        inside = info[2] > 0 if side == 0 else info[2] < SLABS - 1
        own, halo = pick_halo(info, side, mo, mi), pick_halo(info, side, ho, hi)
        fix = beside(*[halo(10 + r) for r in order])
        theirs = beside(*[own(10 + r) for r in order[::-1]])
        for i, x in enumerate(rows):
            done[row_a(x)] = abi[row_a(x)] + ka * fix[i]
            done[row_b(x)] = abi[row_b(x)] + kb * fix[i]
        for depth, at, to, factor in ((6, 0, ext_a, ka), (4, 6, ext_b, kb)):
            for i in range(depth):
                x = -1 - i if side == 0 else ROWS + i
                value = halo(at + (depth - 1 - i if side == 0 else i))
                if i < 2:
                    value = value + factor * theirs[i]
                done[to(x)] = jnp.where(inside, value, 0.0)
    for at, value in done.items():
        ab[at] = value
    for at in range(AB_ROWS):
        short[at] = done[at] if at in done else abi[at]


def swept(info, z, x, reach, add, wc, dc12):
    value = z(x)
    y = dot(wc[...], stacked(value, value * value))
    lap = lap_y(value) + lap_x(z, x, -reach, ROWS + reach)
    value = value + HALF * ((y[:CP] + y[CP:]) + dc12[...] * lap) + add
    if x < 0:
        value = jnp.where(info[2] > 0, value, 0.0)
    elif x >= ROWS:
        value = jnp.where(info[2] < SLABS - 1, value, 0.0)
    return value


def begin(info, z0, zo, zi, depth):
    top, bottom = pick_halo(info, 0, zo, zi), pick_halo(info, 1, zo, zi)

    def row(x):
        if x < 0:
            return top(x + depth)
        return bottom(x - ROWS) if x >= ROWS else z0[x]

    return row


def from_scratch(ref, reach):
    return lambda x: ref[x + reach]


def give(info, depth, outer, inner, value):
    send(info, outer, inner, [value(x) for x in range(depth)], [value(x) for x in range(ROWS - depth, ROWS)])


def hosting(info, hosts):
    return info[1] == jnp.where(info[0] == 0, hosts[0], hosts[1])


def start_kernel(hosts, info, ab, wc, dc12, rb, message, outer, inner):
    @pl.when(hosting(info, hosts))
    def _():
        z1 = lambda x: ab[row_a(x)]
        for x in range(ROWS):
            rb[x] = zeros(CP)
            rb[ROWS + x] = z1(x)
            message[x] = swept(info, z1, x, 2, ab[row_b(x)], wc, dc12)
            rb[2 * ROWS + x] = message[x]
        give(info, 8, outer, inner, lambda x: message[x])


def pair_kernel(
    hosts, depth, info, z0, zo, zi, mine, short, long, wc, dc12, message, outer, inner, za, zb, zc
):
    def sweep(exta, abb):
        z = begin(info, z0, zo, zi, 8)
        for x in range(-6, ROWS + 6):
            za[x + 6] = swept(info, z, x, 8, exta[ext_a(x)], wc, dc12)
        z = from_scratch(za, 6)
        for x in range(-4, ROWS + 4):
            zb[x + 4] = swept(info, z, x, 6, exta[ext_b(x)], wc, dc12)
        z = from_scratch(zb, 4)
        for x in range(-2, ROWS + 2):
            zc[x + 2] = swept(info, z, x, 4, abb[row_a(x)], wc, dc12)
        z = from_scratch(zc, 2)
        for x in range(ROWS):
            message[x] = swept(info, z, x, 2, abb[row_b(x)], wc, dc12)
        give(info, depth, outer, inner, lambda x: message[x])

    active, odd = hosting(info, hosts), info[1] % 2 == 1
    if hosts[0] % 2 or hosts[1] % 2:
        pl.when(active & odd)(lambda: sweep(mine, short))
    if not (hosts[0] % 2 and hosts[1] % 2):

        pl.when(active & (info[1] % 2 == 0))(lambda: sweep(long, mine))


def gather_kernel(hosts, info, z0, za, zb, zc, z2, home_in, away_in, home, away):
    def fill(one, two):
        for x in range(ROWS):
            one[x], one[ROWS + x], one[2 * ROWS + x] = z0[x], za[x + 6], zb[x + 4]
            two[x], two[ROWS + x], two[2 * ROWS + x] = zb[x + 4], zc[x + 2], z2[x]

    active, odd = hosting(info, hosts), info[1] % 2 == 1
    pl.when(active & odd)(lambda: fill(home, away))
    pl.when(active & ~odd)(lambda: fill(away, home))


def base_kernel(n1, n2, c1, c2, pro, share, b1, b2):
    for x in range(ROWS):
        for n, c, b in ((n1, c1, b1), (n2, c2, b2)):
            value = thirds(jnp.concatenate([share[...] * c[x], zeros(8)], axis=0))
            b[:, x, :] = (n[x] - dot(pro[...], value))[:SPECIES]


def out_kernel(
    info, where, u, b0, b1, b2, share, z0, zo, zi, ab, wc, dc12, home, early, other, out, z, za, spread, node, sem
):
    last = info[1] == SLICES - 1
    hosts = hosting(info, GROUPS[0][1])
    for slices, at in GROUPS[1:]:
        hosts = hosts | (hosting(info, at) & ~last)
    second = info[1] == GROUPS[1][0][1]
    for here, result in ((hosts, home), (second, early), (~hosts & ~second & ~last, other)):

        @pl.when(here)
        def _():
            for x in range(3 * ROWS):
                z[x] = result[x]

    @pl.when(last)
    def _():
        for x in range(ROWS):
            z[x] = z0[x]

    def finish(m, base):
        for x in range(ROWS):
            spread[m, :, x, :] = share[...] * z[m * ROWS + x]
        for s in range(SPECIES):
            node[m, s] = base(s) + spread[m, where[s]]
        copy = pltpu.make_async_copy(node.at[m], out.at[m], sem.at[m])
        copy.start()
        return copy

    first = info[1] == 0
    copies = [finish(0, lambda s: jnp.where(first, u[0, s], b0[s]))]

    @pl.when(last)
    def _():
        row = begin(info, z0, zo, zi, 4)
        for x in range(-2, ROWS + 2):
            za[x + 2] = swept(info, row, x, 4, ab[row_a(x)], wc, dc12)
        row = from_scratch(za, 2)
        for x in range(ROWS):
            z[ROWS + x] = za[x + 2]
            z[2 * ROWS + x] = swept(info, row, x, 2, ab[row_b(x)], wc, dc12)

    copies += [finish(1, lambda s: b1[s]), finish(2, lambda s: b2[s])]
    for copy in copies:
        copy.wait()


def field(*shape):
    return jax.ShapeDtypeStruct(shape + (COLS,), F32)


SMEM = pl.BlockSpec(memory_space=pltpu.SMEM)
VMEM = pl.BlockSpec(memory_space=pltpu.VMEM)
ANY = pl.BlockSpec(memory_space=pl.ANY)


def call(kernel, name, outs, *args, scratch=(), alias=None, out_specs=None):
    specs = [SMEM if a.dtype == jnp.int32 and a.ndim == 1 else VMEM for a in args]
    return pl.pallas_call(
        kernel,
        out_shape=outs,
        in_specs=specs,
        **({"out_specs": out_specs} if out_specs else {}),
        scratch_shapes=[pltpu.VMEM(f.shape, f.dtype) if isinstance(f, jax.ShapeDtypeStruct) else f for f in scratch],
        input_output_aliases=alias or {},
        compiler_params=pltpu.CompilerParams(vmem_limit_bytes=VMEM_LIMIT),
        name=name,
    )(*args)


AXES = ("tm", "space")
OUTER = [(s, s + 1) for s in range(1, SLABS - 1, 2)] + [(s + 1, s) for s in range(1, SLABS - 1, 2)]
INNER = [(s, s ^ 1) for s in range(SLABS)]
SAME = [(s, s) for s in range(SLABS)]


def moved(value, *routes):
    pairs = [
        (source[s % 2] * SLABS + s, target[t % 2] * SLABS + t) for source, target, slabs in routes for s, t in slabs
    ]
    return lax.ppermute(value, AXES, pairs)


def both(p):
    return (p, p)


def swap(outer, inner):
    got_inner = moved(inner, *[(both(p), both(p), INNER) for p in range(SLICES)])
    got_outer = moved(outer, *[(both(p), both(p), OUTER) for p in range(SLICES)])
    return got_outer, got_inner


def hop(message, outer, inner, source, target):
    return [moved(value, (source, target, slabs)) for value, slabs in ((message, SAME), (outer, OUTER), (inner, INNER))]


def after(value, other):
    return lax.optimization_barrier((value, other))[0]


def local(fine_nodes, fine_rates, fine_pairs, fine_diff, coarse_rates, coarse_pairs, coarse_diff, species_map):
    slice_at, slab = lax.axis_index("tm"), lax.axis_index("space")
    info = jnp.stack([slab % 2, slice_at, slab]).astype(jnp.int32)
    nodes = fine_nodes[0]
    fine, coarse = field(ROWS, SP), field(ROWS, CP)
    message = field(3, 2, SP)
    outer, inner = call(first_kernel, "first", [message, message], info, nodes)
    uo, ui = swap(outer, inner)

    def bf16(*shape):
        return jax.ShapeDtypeStruct(shape, BF16)

    wf, wr, wfr, lv, wc, pro, d12, dc12, share = call(
        prep_kernel,
        "prep",
        [bf16(2 * SP, 256), bf16(128, 256), bf16(2 * SP + 128, 256), bf16(80, 128), bf16(2 * CP, 128), bf16(SP, 96)]
        + [field(SP), field(CP), field(CP)],
        fine_rates,
        fine_pairs,
        fine_diff.reshape(1, SPECIES),
        coarse_rates,
        coarse_pairs,
        coarse_diff.reshape(1, COARSE),
        species_map,
        scratch=[pltpu.VMEM((SP, 128), F32), pltpu.VMEM((SP, 128), jnp.int32)],
    )
    n1, s, r0, e0, c0 = call(
        old_kernel,
        "old",
        [fine, fine, coarse, coarse, coarse],
        *(nodes, wf, wr, wc, d12, dc12),
        scratch=[field(ROWS, 3, SP), fine, fine, coarse],
    )
    two, twelve, eight = field(2, SP), field(12, CP), field(8, CP)
    n1, s, r0, e0, outer, inner = call(
        old_edge_kernel,
        "old_edge",
        [fine, fine, coarse, coarse, two, two],
        *(info, uo, ui, lv, d12, dc12, n1, s, r0, e0),
        alias={6: 0, 7: 1, 8: 2, 9: 3},
    )
    no, ni = swap(outer, inner)
    n2, r1, e1, c1 = call(
        mid_kernel, "mid", [fine, coarse, coarse, coarse], n1, s, wfr, wc, d12, dc12, scratch=[coarse]
    )
    extended, short = field(EXT_ROWS, CP), field(AB_ROWS, CP)
    n2, r1, e1, abx, c2, outer, inner = call(
        mid_edge_kernel,
        "mid_edge",
        [fine, coarse, coarse, extended, coarse, twelve, twelve],
        *(info, no, ni, lv, wr, d12, dc12, r0, e0, c0, n2, r1, e1),
        alias={10: 0, 11: 1, 12: 2},
        scratch=[coarse],
    )
    ho, hi = swap(outer, inner)
    b1, b2 = call(base_kernel, "base", [field(SPECIES, ROWS)] * 2, n1, n2, c1, c2, pro, share)
    abx, ab = call(last_edge_kernel, "last_edge", [extended, short], info, outer, inner, ho, hi, abx, alias={5: 0})

    ab, abx = after(ab, b1), after(abx, b1)
    result = field(3 * ROWS, CP)
    pairs = [(slices, hosts) for slices, hosts in GROUPS if len(slices) == 2]
    short, long, back = [], [], []
    for slices, hosts in pairs:
        for core, host in enumerate(hosts):
            slabs = [(t, t) for t in range(core, SLABS, 2)]
            other = slices[1] if host == slices[0] else slices[0]
            (short if host == slices[0] else long).append((both(other), both(host), slabs))
            back.append((both(host), both(other), slabs))
    short = moved(ab, *short)
    forward = [(both(p), both(p + 1), SAME) for p in range(SLICES - 1)]
    b0 = moved(after(b2, ab), *forward[1:])
    home, *sent = call(
        functools.partial(start_kernel, GROUPS[0][1]), "start", [result, coarse, eight, eight], info, ab, wc, dc12
    )
    away = home
    for at, (slices, hosts) in enumerate(GROUPS[1:], 1):
        z = hop(*sent, GROUPS[at - 1][1], hosts)
        if at == 1:
            *z, short, b0 = lax.optimization_barrier((*z, short, b0))
            long = moved(after(abx, z[0]), *long)
        elif at == 2:
            *z, long = lax.optimization_barrier((*z, long))
            late = moved(after(b2, z[0]), forward[0])
            early = moved(after(away, z[0]), *back[:2])
        elif at == 3:
            *z, late, early, home, away = lax.optimization_barrier((*z, late, early, home, away))
        else:
            other = moved(away, *back[2:])
            *z, other, home = lax.optimization_barrier((*z, other, home))
        if len(slices) == 2:
            depth = 4 * len(GROUPS[at + 1][0])
            *sent, za, zb, zc = call(
                functools.partial(pair_kernel, hosts, depth),
                "pair",
                [coarse, field(depth, CP), field(depth, CP), field(ROWS + 12, CP), field(ROWS + 8, CP), field(ROWS + 4, CP)],
                *(info, *z, abx, short, long, wc, dc12),
            )
            home, away = call(
                functools.partial(gather_kernel, hosts),
                "gather",
                [result, result],
                *(info, z[0], za, zb, zc, sent[0], home, away),
                alias={6: 0, 7: 1},
            )
    out = call(
        out_kernel,
        "out",
        field(3, SPECIES, ROWS),
        *(info, species_map[:, 0], nodes, b0 + late, b1, b2, share, *z, ab, wc, dc12, home, early, other),
        out_specs=ANY,
        scratch=[result, field(ROWS + 4, CP), field(3, CP, ROWS), field(3, SPECIES, ROWS), pltpu.SemaphoreType.DMA((3,))],
    )
    return out[None]


def solution(mesh):
    in_specs = (P("tm", None, None, "space", None), P(), P(), P(), P(), P(), P(), P())
    out_specs = P("tm", None, None, "space", None)
    return jax.shard_map(local, mesh=mesh, in_specs=in_specs, out_specs=out_specs, check_vma=False)
```

```python
import functools

import jax
import jax.numpy as jnp
from jax import lax
from jax.experimental import pallas as pl
from jax.experimental.pallas import tpu as pltpu
from jax.sharding import PartitionSpec as P

SPECIES, COARSE = 53, 21
SP, CP = 56, 24
ROWS, COLS = 16, 256
SLICES, SLABS = 8, 16
STEP, HALF, RELAX = 0.1, 0.05, 3.0
W0 = (5.0 / 24.0, 1.0 / 3.0, -1.0 / 24.0)
W1 = (-1.0 / 24.0, 1.0 / 3.0, 5.0 / 24.0)
F32, BF16 = jnp.float32, jnp.bfloat16
GROUPS = (((0,), (0, 0)), ((1, 2), (1, 5)), ((3, 4), (3, 4)), ((5, 6), (5, 6)), ((7,), (7, 7)))
VMEM_LIMIT = 24 * 1024 * 1024


def split(x):
    hi = x.astype(BF16)
    lo = (x - hi.astype(F32)).astype(BF16)
    return jnp.concatenate([hi, lo], axis=0)


def thirds(x):
    hi = x.astype(BF16)
    rest = x - hi.astype(F32)
    mid = rest.astype(BF16)
    return jnp.concatenate([hi, mid, (rest - mid.astype(F32)).astype(BF16)], axis=0)


def zeros(rows):
    return jnp.zeros((rows, COLS), F32)


def dot(w, x):
    return jnp.dot(w, x, preferred_element_type=F32)


def stacked(x, squares):
    return split(jnp.concatenate([x, squares, zeros(16)], axis=0))


def lap_y(x):
    near = pltpu.roll(x, 1, 1) + pltpu.roll(x, COLS - 1, 1)
    far = pltpu.roll(x, 2, 1) + pltpu.roll(x, COLS - 2, 1)
    return 16.0 * near - far - 60.0 * x


def lap_rows(ref, x):
    return 16.0 * (ref[x - 1] + ref[x + 1]) - (ref[x - 2] + ref[x + 2])


def beside(near, far):
    return 16.0 * near - far, -near


def prep_kernel(rates, pairs, diff, crates, cpairs, cdiff, smap, wf, wr, wfr, lv, wc, pro, d12, dc12, share, a, mi):
    row = lax.broadcasted_iota(jnp.int32, (SP, 128), 0)
    lane = lax.broadcasted_iota(jnp.int32, (SP, 128), 1)

    def framed(ref, rows, columns, height):
        a[...] = jnp.zeros((SP, 128), F32)
        a[:rows, :columns] = ref[...]
        return a[:height, :]

    def halves(x):
        hi = x.astype(BF16).astype(F32)
        return hi, (x - hi).astype(BF16).astype(F32)

    def column(values, height):
        return jnp.sum(jnp.where(row == lane, values, 0.0), axis=1, keepdims=True)[:height]

    eye = jnp.where(row == lane, RELAX, 0.0)
    fine = framed(rates, SPECIES, SPECIES, SP) - jnp.where(row < SPECIES, eye, 0.0)
    fine = fine + pltpu.roll(framed(pairs, SPECIES, SPECIES, SP), SP, 1)
    coarse = framed(crates, COARSE, COARSE, CP) - jnp.where(row < COARSE, eye, 0.0)[:CP]
    coarse = coarse + pltpu.roll(framed(cpairs, COARSE, COARSE, CP), CP, 1)
    diff_row = framed(diff, 1, SPECIES, 8)[0:1]
    d12[...] = jnp.broadcast_to(column(diff_row, SP) / 12.0, (SP, COLS))
    dc12[...] = jnp.broadcast_to(column(framed(cdiff, 1, COARSE, 8)[0:1], CP) / 12.0, (CP, COLS))
    mi[...] = jnp.full((SP, 128), -1, jnp.int32)
    mi[:SPECIES, 0:1] = smap[...]
    map_column = mi[:, 0:1]
    map_row = jnp.sum(jnp.where(row == lane, map_column, 0), axis=0, keepdims=True)
    lum = jnp.where((map_row == row[:CP]) & (lane[:CP] < SPECIES), 1.0, 0.0)
    counts = jnp.sum(lum, axis=1, keepdims=True)
    share[...] = jnp.broadcast_to(1.0 / jnp.maximum(counts, 1.0), (CP, COLS))
    lumped = jnp.dot(lum[:, :SP], fine, precision=lax.Precision.HIGHEST, preferred_element_type=F32)
    fh, fl = halves(fine)
    rh, rl = halves(lumped)
    dh, dl = halves(lum * diff_row)
    ch, cl = halves(coarse)
    f = jnp.concatenate([fh, fl], axis=0).astype(BF16)
    r = jnp.concatenate([rh, rl, lum, dh, dl, jnp.zeros((8, 128), F32)], axis=0).astype(BF16)
    for at in (0, 128):
        wf[:, at : at + 128] = f
        wr[:, at : at + 128] = r
        wfr[: 2 * SP, at : at + 128] = f
        wfr[2 * SP :, at : at + 128] = r
    v = jnp.concatenate([lum, dh, dl, jnp.zeros((8, 128), F32)], axis=0)
    lv[...] = (v + pltpu.roll(v, 64, 1)).astype(BF16)
    c = jnp.concatenate([ch, cl], axis=0)
    wc[...] = (c + pltpu.roll(c, 64, 1)).astype(BF16)
    lane96 = lax.broadcasted_iota(jnp.int32, (SP, 96), 1)
    pro[...] = jnp.where(map_column == lane96 % 32, 1.0, 0.0).astype(BF16)


class Position:
    def __init__(self):
        self.slice_at, self.slab = lax.axis_index("tm"), lax.axis_index("space")

    def __getitem__(self, at):
        return (self.slab % 2, self.slice_at, self.slab)[at]


def blocks(rows, body):
    @pl.loop(0, rows // 4)
    def _(i):
        body(4 * i)


def first_kernel(u, outer, inner):
    info = Position()
    at_top = info[0] == 0
    for m in range(3):
        for r in range(2):
            first, last = u[m, :, r, :], u[m, :, ROWS - 2 + r, :]
            for out, value in ((outer, jnp.where(at_top, first, last)), (inner, jnp.where(at_top, last, first))):
                out[m, r, SP - 8 :, :] = zeros(8)
                out[m, r, :SPECIES, :] = value


def restricted(y):
    return y[0:24] + y[24:48], y[48:72], y[72:96] + y[96:120]


MIX0 = [STEP * w for w in W0]
MIXS = [STEP * W1[0], STEP * W1[1] - HALF, STEP * W1[2]]


def mixed(factors, values):
    return factors[0] * values[0] + factors[1] * values[1] + factors[2] * values[2]


def old_kernel(u, wf, wr, wc, d12, dc12, n1, s, r0, e0, c0, ut, p0s, pss, v0s, c0s):
    for k in range(4):
        for m in range(3):
            ut[k, m, SP - 8 :, :] = zeros(8)
    for x in (0, 1, ROWS + 2, ROWS + 3):
        p0s[x], pss[x], v0s[x], c0s[x] = zeros(SP), zeros(SP), zeros(CP), zeros(CP)

    def terms(x0):
        for k in range(4):
            for m in range(3):
                ut[k, m, :SPECIES, :] = u[m, :, x0 + k, :]
        for k in range(4):
            x = x0 + k
            us = [ut[k, m] for m in range(3)]
            qs = [v * v for v in us]
            p0, ps = mixed(MIX0, us), mixed(MIXS, us)
            y = dot(wf[...], stacked(p0, mixed(MIX0, qs)))
            n1[x] = us[0] + (y[:SP] + y[SP:]) + d12[...] * lap_y(p0)
            y = dot(wf[...], stacked(ps, mixed(MIXS, qs)))
            s[x] = (y[:SP] + y[SP:]) + d12[...] * lap_y(ps)
            r, c, v = restricted(dot(wr[...], stacked(us[0], qs[0])))
            r0[x] = r + lap_y(v) * (1.0 / 12.0)
            y = dot(wc[...], stacked(c, c * c))
            e0[x] = (y[:CP] + y[CP:]) + dc12[...] * lap_y(c)
            p0s[x + 2], pss[x + 2], v0s[x + 2], c0s[x + 2], c0[x] = p0, ps, v, c, c

    blocks(ROWS, terms)

    def laps(x0):
        for k in range(4):
            x = x0 + k
            n1[x] += d12[...] * lap_rows(p0s, x + 2)
            s[x] += d12[...] * lap_rows(pss, x + 2)
            r0[x] += lap_rows(v0s, x + 2) * (1.0 / 12.0)
            e0[x] += dc12[...] * lap_rows(c0s, x + 2)

    blocks(ROWS, laps)


def lumped_halo(lv, row):
    y = dot(lv[...], split(jnp.concatenate([row, zeros(8)], axis=0)))
    return y[0:24], y[24:48] + y[48:72]


SIDES = (((0, 1), (1, 0)), ((ROWS - 1, ROWS - 2), (0, 1)))


def pick_halo(info, side, outer, inner):
    take = info[0] == side
    return lambda *at: jnp.where(take, outer[at], inner[at])


def send(info, outer, inner, tops, bottoms):
    at_top = info[0] == 0
    for r, (top, bottom) in enumerate(zip(tops, bottoms)):
        outer[r] = jnp.where(at_top, top, bottom)
        inner[r] = jnp.where(at_top, bottom, top)


def old_edge_kernel(uo, ui, lv, d12, dc12, n1i, si, r0i, e0i, n1, s, r0, e0, outer, inner):
    info = Position()
    for side, (rows, order) in enumerate(SIDES):
        halo = pick_halo(info, side, uo, ui)
        us = [[halo(m, r) for m in range(3)] for r in order]
        p0 = beside(*[mixed(MIX0, v) for v in us])
        ps = beside(*[mixed(MIXS, v) for v in us])
        lumped = [lumped_halo(lv, v[0]) for v in us]
        c = beside(lumped[0][0], lumped[1][0])
        v = beside(lumped[0][1], lumped[1][1])
        for i, x in enumerate(rows):
            n1[x] = n1i[x] + d12[...] * p0[i]
            s[x] = si[x] + d12[...] * ps[i]
            r0[x] = r0i[x] + v[i] * (1.0 / 12.0)
            e0[x] = e0i[x] + dc12[...] * c[i]
    send(info, outer, inner, [n1[0], n1[1]], [n1[ROWS - 2], n1[ROWS - 1]])


def mid_kernel(n1, s, wfr, wc, d12, dc12, n2, r1, e1, c1, n1s, v1s, c1s):
    for x in (0, 1, ROWS + 2, ROWS + 3):
        n1s[x], v1s[x], c1s[x] = zeros(SP), zeros(CP), zeros(CP)

    def terms(x0):
        for k in range(4):
            x = x0 + k
            n = n1[x]
            y = dot(wfr[...], stacked(n, n * n))
            n2[x] = n + HALF * ((y[:SP] + y[SP : 2 * SP]) + d12[...] * lap_y(n)) + s[x]
            r, c, v = restricted(y[2 * SP :])
            r1[x] = r + lap_y(v) * (1.0 / 12.0)
            y = dot(wc[...], stacked(c, c * c))
            e1[x] = (y[:CP] + y[CP:]) + dc12[...] * lap_y(c)
            n1s[x + 2], v1s[x + 2], c1s[x + 2], c1[x] = n, v, c, c

    blocks(ROWS, terms)

    def laps(x0):
        for k in range(4):
            x = x0 + k
            n2[x] += (HALF * d12[...]) * lap_rows(n1s, x + 2)
            r1[x] += lap_rows(v1s, x + 2) * (1.0 / 12.0)
            e1[x] += dc12[...] * lap_rows(c1s, x + 2)

    blocks(ROWS, laps)


def lumped_old(first, c0, e0):
    return jnp.where(first, c0, -HALF * e0)


AB_ROWS, EXT_ROWS = 2 * ROWS + 4, 2 * ROWS + 20
A0, B0 = 2, ROWS + 4
XA0, XB0 = 6, ROWS + 16


def mid_edge_kernel(no, ni, lv, wr, d12, dc12, r0, e0, c0, n2i, r1i, e1i, n2, r1, e1, ab, c2, outer, inner, v2s, gs):
    info = Position()
    first = info[1] == 0
    for side, (rows, order) in enumerate(SIDES):
        halo = pick_halo(info, side, no, ni)
        ns = [halo(r) for r in order]
        lumped = [lumped_halo(lv, v) for v in ns]
        c = beside(lumped[0][0], lumped[1][0])
        v = beside(lumped[0][1], lumped[1][1])
        n = beside(*ns)
        for i, x in enumerate(rows):
            n2[x] = n2i[x] + (HALF * d12[...]) * n[i]
            r1[x] = r1i[x] + v[i] * (1.0 / 12.0)
            e1[x] = e1i[x] + dc12[...] * c[i]
    for x in (0, 1, ROWS + 2, ROWS + 3):
        v2s[x] = zeros(CP)

    def lumped(x, value):
        gs[x], c2[x], v2s[x + 2] = restricted(dot(wr[...], stacked(value, value * value)))

    def pieces(x, mid, late):
        v = v2s[x + 2]
        g2 = gs[x] + (lap_y(v) + lap_rows(v2s, x + 2)) * (1.0 / 12.0)
        ab[x + XA0] = mixed(MIX0, (r0[x], mid, g2)) + lumped_old(first, c0[x], e0[x])
        ab[x + XB0] = mixed([STEP * w for w in W1], (r0[x], mid, g2)) - HALF * late

    edges = (0, 1, ROWS - 2, ROWS - 1)
    for x in edges:
        lumped(x, n2[x])
    blocks(ROWS - 4, lambda x0: [lumped(x, n2i[x]) for x in (x0 + 2, x0 + 3, x0 + 4, x0 + 5)])
    for x in edges:
        pieces(x, r1[x], e1[x])
    blocks(ROWS - 4, lambda x0: [pieces(x, r1i[x], e1i[x]) for x in (x0 + 2, x0 + 3, x0 + 4, x0 + 5)])
    top = [ab[x + XA0] for x in range(6)] + [ab[x + XB0] for x in range(4)] + [v2s[x + 2] for x in range(2)]
    bottom = [ab[x + XA0] for x in range(ROWS - 6, ROWS)] + [ab[x + XB0] for x in range(ROWS - 4, ROWS)]
    send(info, outer, inner, top, bottom + [v2s[x] for x in range(ROWS, ROWS + 2)])


def last_edge_kernel(mo, mi, ho, hi, abi, ab, short):
    info = Position()
    ka, kb = STEP * W0[2] / 12.0, STEP * W1[2] / 12.0
    done = {}
    for side, (rows, order) in enumerate(SIDES):
        inside = info[2] > 0 if side == 0 else info[2] < SLABS - 1
        own, halo = pick_halo(info, side, mo, mi), pick_halo(info, side, ho, hi)
        fix = beside(*[halo(10 + r) for r in order])
        theirs = beside(*[own(10 + r) for r in order[::-1]])
        for i, x in enumerate(rows):
            done[x + XA0] = abi[x + XA0] + ka * fix[i]
            done[x + XB0] = abi[x + XB0] + kb * fix[i]
        for depth, at, to, factor in ((6, 0, XA0, ka), (4, 6, XB0, kb)):
            for i in range(depth):
                x = -1 - i if side == 0 else ROWS + i
                value = halo(at + (depth - 1 - i if side == 0 else i))
                if i < 2:
                    value = value + factor * theirs[i]
                done[x + to] = jnp.where(inside, value, 0.0)
    for at, value in done.items():
        ab[at] = value
    for x in range(-2, ROWS + 2):
        short[x + A0] = done[x + XA0] if x + XA0 in done else abi[x + XA0]
    for x in range(ROWS):
        short[x + B0] = done[x + XB0] if x + XB0 in done else abi[x + XB0]


def sweep(info, z, z0, add, add0, out, out0, low, rows, wc, dc12):
    def body(i):
        x0 = i + low
        z8 = [z[x0 + z0 + k] for k in range(-2, 6)]
        for k in range(4):
            x, value = x0 + k, z8[k + 2]
            y = dot(wc[...], stacked(value, value * value))
            lap = lap_y(value) + 16.0 * (z8[k + 1] + z8[k + 3]) - (z8[k] + z8[k + 4])
            value = value + HALF * ((y[:CP] + y[CP:]) + dc12[...] * lap) + add[x + add0]
            if low < 0:
                inside = ((x >= 0) | (info[2] > 0)) & ((x < ROWS) | (info[2] < SLABS - 1))
                value = jnp.where(inside, value, 0.0)
            out[x + out0] = value

    blocks(rows, body)


def begin(info, z0, zo, zi, depth, zs):
    top, bottom = pick_halo(info, 0, zo, zi), pick_halo(info, 1, zo, zi)
    for r in range(depth):
        zs[r], zs[depth + ROWS + r] = top(r), bottom(r)

    def body(x):
        for k in range(4):
            zs[depth + x + k] = z0[x + k]

    blocks(ROWS, body)


def give(info, depth, outer, inner, value):
    send(info, outer, inner, [value(x) for x in range(depth)], [value(x) for x in range(ROWS - depth, ROWS)])


def hosting(info, hosts):
    return info[1] == jnp.where(info[0] == 0, hosts[0], hosts[1])


def start_kernel(hosts, ab, wc, dc12, result, message, outer, inner):
    info = Position()

    @pl.when(hosting(info, hosts))
    def _():
        sweep(info, ab, A0, ab, B0, message, 0, 0, ROWS, wc, dc12)
        give(info, 8, outer, inner, lambda x: message[x])

        def body(x0):
            for x in (x0, x0 + 1, x0 + 2, x0 + 3):
                result[x], result[ROWS + x], result[2 * ROWS + x] = zeros(CP), ab[x + A0], message[x]

        blocks(ROWS, body)


def pair_kernel(
    slices, hosts, depth, z0, zo, zi, mine, short, long, wc, dc12, message, outer, inner, za, zb, zc, zs
):
    info = Position()

    def sweeps(one, two):
        begin(info, z0, zo, zi, 8, zs)
        sweep(info, zs, 8, one, XA0, za, 6, -6, ROWS + 12, wc, dc12)
        sweep(info, za, 6, one, XB0, zb, 4, -4, ROWS + 8, wc, dc12)
        if two is mine:
            sweep(info, zb, 4, two, XA0, zc, 2, -2, ROWS + 4, wc, dc12)
            sweep(info, zc, 2, two, XB0, message, 0, 0, ROWS, wc, dc12)
        else:
            sweep(info, zb, 4, two, A0, zc, 2, -2, ROWS + 4, wc, dc12)
            sweep(info, zc, 2, two, B0, message, 0, 0, ROWS, wc, dc12)
        give(info, depth, outer, inner, lambda x: message[x])

    for host in sorted(set(hosts)):
        one = mine if host == slices[0] else long
        two = mine if host == slices[1] else short
        pl.when(hosting(info, hosts) & (info[1] == host))(functools.partial(sweeps, one, two))


def gather(z0, za, zb, zc, z2, one, two):
    def body(x0):
        for x in (x0, x0 + 1, x0 + 2, x0 + 3):
            one[x], one[ROWS + x], one[2 * ROWS + x] = z0[x], za[x + 6], zb[x + 4]
            two[x], two[ROWS + x], two[2 * ROWS + x] = zb[x + 4], zc[x + 2], z2[x]

    blocks(ROWS, body)


def gather_kernel(slices, hosts, z0, za, zb, zc, z2, home_in, away_in, home, away):
    info = Position()
    active, second = hosting(info, hosts), info[1] == slices[1]
    pl.when(active & ~second)(lambda: gather(z0, za, zb, zc, z2, home, away))
    pl.when(active & second)(lambda: gather(z0, za, zb, zc, z2, away, home))


def base_kernel(n1, n2, c1, c2, pro, share, b1, b2):
    def body(x0):
        for x in (x0, x0 + 1, x0 + 2, x0 + 3):
            for n, c, b in ((n1, c1, b1), (n2, c2, b2)):
                value = thirds(jnp.concatenate([share[...] * c[x], zeros(8)], axis=0))
                b[:, x, :] = (n[x] - dot(pro[...], value))[:SPECIES]

    blocks(ROWS, body)


def out_kernel(
    where, u, b0, b1, b2, share, z0, zo, zi, ab, wc, dc12, home, one, other, out, z, za, zs, spread, node, sem
):
    info = Position()
    last = info[1] == SLICES - 1
    at_home = hosting(info, GROUPS[0][1])
    for slices, hosts in GROUPS[1:-1]:
        at_home = at_home | (hosting(info, hosts) & ((info[1] == slices[0]) | (info[1] == slices[1])))
    first = info[1] == GROUPS[1][0][0]
    for here, result in ((at_home, home), (first & ~at_home, one), (~at_home & ~first & ~last, other)):

        @pl.when(here)
        def _():

            def body(x0):
                for x in (x0, x0 + 1, x0 + 2, x0 + 3):
                    z[x] = result[x]

            blocks(3 * ROWS, body)

    @pl.when(last)
    def _():
        begin(info, z0, zo, zi, 4, zs)

        def body(x0):
            for x in (x0, x0 + 1, x0 + 2, x0 + 3):
                z[x] = z0[x]

        blocks(ROWS, body)

    def finish(m, base):
        def body(x0):
            for x in (x0, x0 + 1, x0 + 2, x0 + 3):
                spread[m, :, x, :] = share[...] * z[m * ROWS + x]

        blocks(ROWS, body)

        def add(s):
            node[m, s] = base(s) + spread[m, where[s]]

        blocks(SPECIES, lambda s: [add(s + k) for k in range(4)])
        for s in range(SPECIES - SPECIES % 4, SPECIES):
            add(s)
        copy = pltpu.make_async_copy(node.at[m], out.at[m], sem.at[m])
        copy.start()
        return copy

    first = info[1] == 0
    copies = [finish(0, lambda s: jnp.where(first, u[0, s], b0[s]))]

    @pl.when(last)
    def _():
        sweep(info, zs, 4, ab, A0, za, 2, -2, ROWS + 4, wc, dc12)
        sweep(info, za, 2, ab, B0, z.at[pl.ds(2 * ROWS, ROWS)], 0, 0, ROWS, wc, dc12)

        def body(x0):
            for x in (x0, x0 + 1, x0 + 2, x0 + 3):
                z[ROWS + x] = za[x + 2]

        blocks(ROWS, body)

    copies += [finish(1, lambda s: b1[s]), finish(2, lambda s: b2[s])]
    for copy in copies:
        copy.wait()


def field(*shape):
    return jax.ShapeDtypeStruct(shape + (COLS,), F32)


SMEM = pl.BlockSpec(memory_space=pltpu.SMEM)
VMEM = pl.BlockSpec(memory_space=pltpu.VMEM)
ANY = pl.BlockSpec(memory_space=pl.ANY)


def call(kernel, name, outs, *args, scratch=(), alias=None, out_specs=None):
    specs = [SMEM if a.dtype == jnp.int32 and a.ndim == 1 else VMEM for a in args]
    return pl.pallas_call(
        kernel,
        out_shape=outs,
        in_specs=specs,
        **({"out_specs": out_specs} if out_specs else {}),
        scratch_shapes=[pltpu.VMEM(f.shape, f.dtype) if isinstance(f, jax.ShapeDtypeStruct) else f for f in scratch],
        input_output_aliases=alias or {},
        compiler_params=pltpu.CompilerParams(vmem_limit_bytes=VMEM_LIMIT),
        name=name,
    )(*args)


AXES = ("tm", "space")
OUTER = [(s, s + 1) for s in range(1, SLABS - 1, 2)] + [(s + 1, s) for s in range(1, SLABS - 1, 2)]
INNER = [(s, s ^ 1) for s in range(SLABS)]
SAME = [(s, s) for s in range(SLABS)]


def moved(value, *routes):
    pairs = [
        (source[s % 2] * SLABS + s, target[t % 2] * SLABS + t) for source, target, slabs in routes for s, t in slabs
    ]
    return lax.ppermute(value, AXES, pairs)


def both(p):
    return (p, p)


def swap(outer, inner):
    got_inner = moved(inner, *[(both(p), both(p), INNER) for p in range(SLICES)])
    got_outer = moved(outer, *[(both(p), both(p), OUTER) for p in range(SLICES)])
    return got_outer, got_inner


def hop(message, outer, inner, source, target):
    parts = ((outer, OUTER), (inner, INNER), (message, SAME))
    zo, zi, z = [moved(value, (source, target, slabs)) for value, slabs in parts]
    return [z, zo, zi]


def after(value, other):
    return lax.optimization_barrier((value, other))[0]


def local(fine_nodes, fine_rates, fine_pairs, fine_diff, coarse_rates, coarse_pairs, coarse_diff, species_map):
    nodes = fine_nodes[0]
    fine, coarse = field(ROWS, SP), field(ROWS, CP)
    message = field(3, 2, SP)
    outer, inner = call(first_kernel, "first", [message, message], nodes)
    uo, ui = swap(outer, inner)

    def bf16(*shape):
        return jax.ShapeDtypeStruct(shape, BF16)

    wf, wr, wfr, lv, wc, pro, d12, dc12, share = call(
        prep_kernel,
        "prep",
        [bf16(2 * SP, 256), bf16(128, 256), bf16(2 * SP + 128, 256), bf16(80, 128), bf16(2 * CP, 128), bf16(SP, 96)]
        + [field(SP), field(CP), field(CP)],
        fine_rates,
        fine_pairs,
        fine_diff.reshape(1, SPECIES),
        coarse_rates,
        coarse_pairs,
        coarse_diff.reshape(1, COARSE),
        species_map,
        scratch=[pltpu.VMEM((SP, 128), F32), pltpu.VMEM((SP, 128), jnp.int32)],
    )
    n1, s, r0, e0, c0 = call(
        old_kernel,
        "old",
        [fine, fine, coarse, coarse, coarse],
        *(nodes, wf, wr, wc, d12, dc12),
        scratch=[field(4, 3, SP), field(ROWS + 4, SP), field(ROWS + 4, SP), field(ROWS + 4, CP), field(ROWS + 4, CP)],
    )
    two, twelve, eight = field(2, SP), field(12, CP), field(8, CP)
    n1, s, r0, e0, outer, inner = call(
        old_edge_kernel,
        "old_edge",
        [fine, fine, coarse, coarse, two, two],
        *(uo, ui, lv, d12, dc12, n1, s, r0, e0),
        alias={5: 0, 6: 1, 7: 2, 8: 3},
    )
    no, ni = swap(outer, inner)
    n2, r1, e1, c1 = call(
        mid_kernel, "mid", [fine, coarse, coarse, coarse], n1, s, wfr, wc, d12, dc12, scratch=[field(ROWS + 4, SP), field(ROWS + 4, CP), field(ROWS + 4, CP)]
    )
    extended, short = field(EXT_ROWS, CP), field(AB_ROWS, CP)
    n2, r1, e1, abx, c2, outer, inner = call(
        mid_edge_kernel,
        "mid_edge",
        [fine, coarse, coarse, extended, coarse, twelve, twelve],
        *(no, ni, lv, wr, d12, dc12, r0, e0, c0, n2, r1, e1),
        alias={9: 0, 10: 1, 11: 2},
        scratch=[field(ROWS + 4, CP), coarse],
    )
    ho, hi = swap(outer, inner)
    b1, b2 = call(base_kernel, "base", [field(SPECIES, ROWS)] * 2, n1, n2, c1, c2, pro, share)
    abx, ab = call(last_edge_kernel, "last_edge", [extended, short], outer, inner, ho, hi, abx, alias={4: 0})

    ab, abx = after(ab, b1), after(abx, b1)
    result = field(3 * ROWS, CP)
    pairs = [(slices, hosts) for slices, hosts in GROUPS if len(slices) == 2]
    short, long, back, first = [], [], [], []
    for slices, hosts in pairs:
        for core, host in enumerate(hosts):
            slabs = [(t, t) for t in range(core, SLABS, 2)]
            if host != slices[0]:
                long.append((both(slices[0]), both(host), slabs))
            if host != slices[1]:
                short.append((both(slices[1]), both(host), slabs))
            back.append((both(host), both(slices[0] if host == slices[1] else slices[1]), slabs))
            if host not in slices:
                first.append((both(host), both(slices[0]), slabs))
    short, long = moved(ab, *short), moved(abx, *long)
    forward = [(both(p), both(p + 1), SAME) for p in range(SLICES - 1)]
    home, *sent = call(
        functools.partial(start_kernel, GROUPS[0][1]), "start", [result, coarse, eight, eight], ab, wc, dc12
    )
    away = home
    for at, (slices, hosts) in enumerate(GROUPS[1:], 1):
        z = hop(*sent, GROUPS[at - 1][1], hosts)
        if at == 1:
            *z, short, long = lax.optimization_barrier((*z, short, long))
            b0 = moved(after(b2, z[0]), *forward)
        elif at == 2:
            *z, b0 = lax.optimization_barrier((*z, b0))
            one = moved(after(home, z[0]), *first)
        elif at == 3:
            *z, one, home, away = lax.optimization_barrier((*z, one, home, away))
        else:
            other = moved(away, *back)
            *z, other, home = lax.optimization_barrier((*z, other, home))
        if len(slices) == 2:
            depth = 4 * len(GROUPS[at + 1][0])
            *sent, za, zb, zc = call(
                functools.partial(pair_kernel, slices, hosts, depth),
                "pair",
                [coarse, field(depth, CP), field(depth, CP), field(ROWS + 12, CP), field(ROWS + 8, CP), field(ROWS + 4, CP)],
                *(*z, abx, short, long, wc, dc12),
                scratch=[field(ROWS + 16, CP)],
            )
            home, away = call(
                functools.partial(gather_kernel, slices, hosts),
                "gather",
                [result, result],
                *(z[0], za, zb, zc, sent[0], home, away),
                alias={5: 0, 6: 1},
            )
    out = call(
        out_kernel,
        "out",
        field(3, SPECIES, ROWS),
        *(species_map[:, 0], nodes, b0, b1, b2, share, *z, ab, wc, dc12, home, one, other),
        out_specs=ANY,
        scratch=[result, field(ROWS + 4, CP), field(ROWS + 8, CP), field(3, CP, ROWS), field(3, SPECIES, ROWS), pltpu.SemaphoreType.DMA((3,))],
    )
    return out[None]


def solution(mesh):
    in_specs = (P("tm", None, None, "space", None), P(), P(), P(), P(), P(), P(), P())
    out_specs = P("tm", None, None, "space", None)
    return jax.shard_map(local, mesh=mesh, in_specs=in_specs, out_specs=out_specs, check_vma=False)
```

```python
import functools

import jax
import jax.numpy as jnp
from jax import lax
from jax.experimental import pallas as pl
from jax.experimental.pallas import tpu as pltpu
from jax.sharding import PartitionSpec as P

SPECIES, COARSE = 53, 21
SP, CP = 56, 24
ROWS, COLS = 16, 256
SLICES, SLABS = 8, 16
STEP, HALF, RELAX = 0.1, 0.05, 3.0
W0 = (5.0 / 24.0, 1.0 / 3.0, -1.0 / 24.0)
W1 = (-1.0 / 24.0, 1.0 / 3.0, 5.0 / 24.0)
F32, BF16 = jnp.float32, jnp.bfloat16
GROUPS = (((0,), (0, 0)), ((1, 2), (1, 5)), ((3, 4), (3, 4)), ((5, 6), (5, 6)), ((7,), (7, 7)))
VMEM_LIMIT = 24 * 1024 * 1024


def split(x):
    hi = x.astype(BF16)
    lo = (x - hi.astype(F32)).astype(BF16)
    return jnp.concatenate([hi, lo], axis=0)


def thirds(x):
    hi = x.astype(BF16)
    rest = x - hi.astype(F32)
    mid = rest.astype(BF16)
    return jnp.concatenate([hi, mid, (rest - mid.astype(F32)).astype(BF16)], axis=0)


def zeros(rows):
    return jnp.zeros((rows, COLS), F32)


def dot(w, x):
    return jnp.dot(w, x, preferred_element_type=F32)


def stacked(x, squares):
    return split(jnp.concatenate([x, squares, zeros(16)], axis=0))


def lap_y(x):
    near = pltpu.roll(x, 1, 1) + pltpu.roll(x, COLS - 1, 1)
    far = pltpu.roll(x, 2, 1) + pltpu.roll(x, COLS - 2, 1)
    return 16.0 * near - far - 60.0 * x


def lap_rows(ref, x):
    return 16.0 * (ref[x - 1] + ref[x + 1]) - (ref[x - 2] + ref[x + 2])


def beside(near, far):
    return 16.0 * near - far, -near


RATES, PAIRS, CRATES, CPAIRS, DIFF, CDIFF, MAP, RAW = 0, 56, 112, 136, 160, 161, 162, 168


def prep_kernel(raw, wf, wr, wfr, lv, wc, pro, d12, dc12, share):
    row = lax.broadcasted_iota(jnp.int32, (SP, 128), 0)
    lane = lax.broadcasted_iota(jnp.int32, (SP, 128), 1)

    def halves(x):
        hi = x.astype(BF16).astype(F32)
        return hi, (x - hi).astype(BF16).astype(F32)

    def column(values, height):
        return jnp.sum(jnp.where(row == lane, values, 0.0), axis=1, keepdims=True)[:height]

    eye = jnp.where(row == lane, RELAX, 0.0)
    fine = raw[RATES : RATES + SP, :] - jnp.where(row < SPECIES, eye, 0.0)
    fine = fine + pltpu.roll(raw[PAIRS : PAIRS + SP, :], SP, 1)
    coarse = raw[CRATES : CRATES + CP, :] - jnp.where(row < COARSE, eye, 0.0)[:CP]
    coarse = coarse + pltpu.roll(raw[CPAIRS : CPAIRS + CP, :], CP, 1)
    vectors = raw[DIFF : DIFF + 8, :]
    diff_row = vectors[0:1]
    d12[...] = jnp.broadcast_to(column(diff_row, SP) / 12.0, (SP, COLS))
    dc12[...] = jnp.broadcast_to(column(vectors[1:2], CP) / 12.0, (CP, COLS))
    map_row = jnp.where(lane[0:1] < SPECIES, vectors[2:3].astype(jnp.int32), -1)
    map_column = jnp.sum(jnp.where(row == lane, map_row, 0), axis=1, keepdims=True)
    map_column = jnp.where(row[:, 0:1] < SPECIES, map_column, -1)
    lum = jnp.where((map_row == row[:CP]) & (lane[:CP] < SPECIES), 1.0, 0.0)
    counts = jnp.sum(lum, axis=1, keepdims=True)
    share[...] = jnp.broadcast_to(1.0 / jnp.maximum(counts, 1.0), (CP, COLS))
    lumped = jnp.dot(lum[:, :SP], fine, precision=lax.Precision.HIGHEST, preferred_element_type=F32)
    fh, fl = halves(fine)
    rh, rl = halves(lumped)
    dh, dl = halves(lum * diff_row)
    ch, cl = halves(coarse)
    f = jnp.concatenate([fh, fl], axis=0).astype(BF16)
    r = jnp.concatenate([rh, rl, lum, dh, dl, jnp.zeros((8, 128), F32)], axis=0).astype(BF16)
    for at in (0, 128):
        wf[:, at : at + 128] = f
        wr[:, at : at + 128] = r
        wfr[: 2 * SP, at : at + 128] = f
        wfr[2 * SP :, at : at + 128] = r
    v = jnp.concatenate([lum, dh, dl, jnp.zeros((8, 128), F32)], axis=0)
    lv[...] = (v + pltpu.roll(v, 64, 1)).astype(BF16)
    c = jnp.concatenate([ch, cl], axis=0)
    wc[...] = (c + pltpu.roll(c, 64, 1)).astype(BF16)
    lane96 = lax.broadcasted_iota(jnp.int32, (SP, 96), 1)
    pro[...] = jnp.where(map_column == lane96 % 32, 1.0, 0.0).astype(BF16)


class Position:
    def __init__(self):
        self.slice_at, self.slab = lax.axis_index("tm"), lax.axis_index("space")

    def __getitem__(self, at):
        return (self.slab % 2, self.slice_at, self.slab)[at]


def blocks(rows, body, size=4):
    @pl.loop(0, rows // size)
    def _(i):
        body([size * i + k for k in range(size)])


def first_kernel(u, weights_made, outer, inner):
    info = Position()
    at_top = info[0] == 0
    for m in range(3):
        for r in range(2):
            first, last = u[m, :, r, :], u[m, :, ROWS - 2 + r, :]
            for out, value in ((outer, jnp.where(at_top, first, last)), (inner, jnp.where(at_top, last, first))):
                out[m, r, SP - 8 :, :] = zeros(8)
                out[m, r, :SPECIES, :] = value


def restricted(y):
    return y[0:24] + y[24:48], y[48:72], y[72:96] + y[96:120]


MIX0 = [STEP * w for w in W0]
MIXS = [STEP * W1[0], STEP * W1[1] - HALF, STEP * W1[2]]


def mixed(factors, values):
    return factors[0] * values[0] + factors[1] * values[1] + factors[2] * values[2]


def old_kernel(u, wf, wr, wc, d12, dc12, n1, s, r0, e0, c0, ut, p0s, pss, v0s, c0s):
    for k in range(4):
        for m in range(3):
            ut[k, m, SP - 8 :, :] = zeros(8)
    for x in (0, 1, ROWS + 2, ROWS + 3):
        p0s[x], pss[x], v0s[x], c0s[x] = zeros(SP), zeros(SP), zeros(CP), zeros(CP)

    def terms(xs):
        for k, x in enumerate(xs):
            for m in range(3):
                ut[k, m, :SPECIES, :] = u[m, :, x, :]
        for k, x in enumerate(xs):
            us = [ut[k, m] for m in range(3)]
            qs = [v * v for v in us]
            p0, ps = mixed(MIX0, us), mixed(MIXS, us)
            y = dot(wf[...], stacked(p0, mixed(MIX0, qs)))
            n1[x] = us[0] + (y[:SP] + y[SP:]) + d12[...] * lap_y(p0)
            y = dot(wf[...], stacked(ps, mixed(MIXS, qs)))
            s[x] = (y[:SP] + y[SP:]) + d12[...] * lap_y(ps)
            r, c, v = restricted(dot(wr[...], stacked(us[0], qs[0])))
            r0[x] = r + lap_y(v) * (1.0 / 12.0)
            y = dot(wc[...], stacked(c, c * c))
            e0[x] = (y[:CP] + y[CP:]) + dc12[...] * lap_y(c)
            p0s[x + 2], pss[x + 2], v0s[x + 2], c0s[x + 2], c0[x] = p0, ps, v, c, c

    blocks(ROWS, terms)

    def laps(xs):
        for x in xs:
            n1[x] += d12[...] * lap_rows(p0s, x + 2)
            s[x] += d12[...] * lap_rows(pss, x + 2)
            r0[x] += lap_rows(v0s, x + 2) * (1.0 / 12.0)
            e0[x] += dc12[...] * lap_rows(c0s, x + 2)

    blocks(ROWS, laps)


def lumped_halo(lv, row):
    y = dot(lv[...], split(jnp.concatenate([row, zeros(8)], axis=0)))
    return y[0:24], y[24:48] + y[48:72]


SIDES = (((0, 1), (1, 0)), ((ROWS - 1, ROWS - 2), (0, 1)))


def pick_halo(info, side, outer, inner):
    take = info[0] == side
    return lambda *at: jnp.where(take, outer[at], inner[at])


def send(info, outer, inner, tops, bottoms):
    at_top = info[0] == 0
    for r, (top, bottom) in enumerate(zip(tops, bottoms)):
        outer[r] = jnp.where(at_top, top, bottom)
        inner[r] = jnp.where(at_top, bottom, top)


def old_edge_kernel(uo, ui, lv, d12, dc12, n1i, si, r0i, e0i, n1, s, r0, e0, outer, inner):
    info = Position()
    for side, (rows, order) in enumerate(SIDES):
        halo = pick_halo(info, side, uo, ui)
        us = [[halo(m, r) for m in range(3)] for r in order]
        p0 = beside(*[mixed(MIX0, v) for v in us])
        ps = beside(*[mixed(MIXS, v) for v in us])
        lumped = [lumped_halo(lv, v[0]) for v in us]
        c = beside(lumped[0][0], lumped[1][0])
        v = beside(lumped[0][1], lumped[1][1])
        for i, x in enumerate(rows):
            n1[x] = n1i[x] + d12[...] * p0[i]
            s[x] = si[x] + d12[...] * ps[i]
            r0[x] = r0i[x] + v[i] * (1.0 / 12.0)
            e0[x] = e0i[x] + dc12[...] * c[i]
    send(info, outer, inner, [n1[0], n1[1]], [n1[ROWS - 2], n1[ROWS - 1]])


def mid_kernel(n1, s, wfr, wc, d12, dc12, n2, r1, e1, c1, n1s, v1s, c1s):
    for x in (0, 1, ROWS + 2, ROWS + 3):
        n1s[x], v1s[x], c1s[x] = zeros(SP), zeros(CP), zeros(CP)

    def terms(xs):
        for x in xs:
            n = n1[x]
            y = dot(wfr[...], stacked(n, n * n))
            n2[x] = n + HALF * ((y[:SP] + y[SP : 2 * SP]) + d12[...] * lap_y(n)) + s[x]
            r, c, v = restricted(y[2 * SP :])
            r1[x] = r + lap_y(v) * (1.0 / 12.0)
            y = dot(wc[...], stacked(c, c * c))
            e1[x] = (y[:CP] + y[CP:]) + dc12[...] * lap_y(c)
            n1s[x + 2], v1s[x + 2], c1s[x + 2], c1[x] = n, v, c, c

    blocks(ROWS, terms)

    def laps(xs):
        for x in xs:
            n2[x] += (HALF * d12[...]) * lap_rows(n1s, x + 2)
            r1[x] += lap_rows(v1s, x + 2) * (1.0 / 12.0)
            e1[x] += dc12[...] * lap_rows(c1s, x + 2)

    blocks(ROWS, laps)


def lumped_old(first, c0, e0):
    return jnp.where(first, c0, -HALF * e0)


AB_ROWS, EXT_ROWS = 2 * ROWS + 4, 2 * ROWS + 20
A0, B0 = 2, ROWS + 4
XA0, XB0 = 6, ROWS + 16


def mid_edge_kernel(no, ni, lv, wr, d12, dc12, r0, e0, c0, n2i, r1i, e1i, n2, r1, e1, ab, c2, outer, inner, v2s, gs):
    info = Position()
    first = info[1] == 0
    for side, (rows, order) in enumerate(SIDES):
        halo = pick_halo(info, side, no, ni)
        ns = [halo(r) for r in order]
        lumped = [lumped_halo(lv, v) for v in ns]
        c = beside(lumped[0][0], lumped[1][0])
        v = beside(lumped[0][1], lumped[1][1])
        n = beside(*ns)
        for i, x in enumerate(rows):
            n2[x] = n2i[x] + (HALF * d12[...]) * n[i]
            r1[x] = r1i[x] + v[i] * (1.0 / 12.0)
            e1[x] = e1i[x] + dc12[...] * c[i]
    for x in (0, 1, ROWS + 2, ROWS + 3):
        v2s[x] = zeros(CP)

    def lumped(x, value):
        gs[x], c2[x], v2s[x + 2] = restricted(dot(wr[...], stacked(value, value * value)))

    def pieces(x, mid, late):
        v = v2s[x + 2]
        g2 = gs[x] + (lap_y(v) + lap_rows(v2s, x + 2)) * (1.0 / 12.0)
        ab[x + XA0] = mixed(MIX0, (r0[x], mid, g2)) + lumped_old(first, c0[x], e0[x])
        ab[x + XB0] = mixed([STEP * w for w in W1], (r0[x], mid, g2)) - HALF * late

    edges = (0, 1, ROWS - 2, ROWS - 1)
    for x in edges:
        lumped(x, n2[x])
    blocks(ROWS - 4, lambda xs: [lumped(x + 2, n2i[x + 2]) for x in xs], ROWS - 4)
    for x in edges:
        pieces(x, r1[x], e1[x])
    blocks(ROWS - 4, lambda xs: [pieces(x + 2, r1i[x + 2], e1i[x + 2]) for x in xs], ROWS - 4)
    top = [ab[x + XA0] for x in range(6)] + [ab[x + XB0] for x in range(4)] + [v2s[x + 2] for x in range(2)]
    bottom = [ab[x + XA0] for x in range(ROWS - 6, ROWS)] + [ab[x + XB0] for x in range(ROWS - 4, ROWS)]
    send(info, outer, inner, top, bottom + [v2s[x] for x in range(ROWS, ROWS + 2)])


def last_edge_kernel(mo, mi, ho, hi, abi, ab, short):
    info = Position()
    ka, kb = STEP * W0[2] / 12.0, STEP * W1[2] / 12.0
    done = {}
    for side, (rows, order) in enumerate(SIDES):
        inside = info[2] > 0 if side == 0 else info[2] < SLABS - 1
        own, halo = pick_halo(info, side, mo, mi), pick_halo(info, side, ho, hi)
        fix = beside(*[halo(10 + r) for r in order])
        theirs = beside(*[own(10 + r) for r in order[::-1]])
        for i, x in enumerate(rows):
            done[x + XA0] = abi[x + XA0] + ka * fix[i]
            done[x + XB0] = abi[x + XB0] + kb * fix[i]
        for depth, at, to, factor in ((6, 0, XA0, ka), (4, 6, XB0, kb)):
            for i in range(depth):
                x = -1 - i if side == 0 else ROWS + i
                value = halo(at + (depth - 1 - i if side == 0 else i))
                if i < 2:
                    value = value + factor * theirs[i]
                done[x + to] = jnp.where(inside, value, 0.0)
    for at, value in done.items():
        ab[at] = value
    for x in range(-2, ROWS + 2):
        short[x + A0] = done[x + XA0] if x + XA0 in done else abi[x + XA0]
    for x in range(ROWS):
        short[x + B0] = done[x + XB0] if x + XB0 in done else abi[x + XB0]


def sweep(info, z, z0, add, add0, out, out0, low, rows, wc, dc12):
    size = rows // 2

    def body(xs):
        zr = [z[xs[0] + (low + z0 + k)] for k in range(-2, size + 2)]
        for k in range(size):
            x, value = xs[k] + low, zr[k + 2]
            y = dot(wc[...], stacked(value, value * value))
            lap = lap_y(value) + 16.0 * (zr[k + 1] + zr[k + 3]) - (zr[k] + zr[k + 4])
            value = value + HALF * ((y[:CP] + y[CP:]) + dc12[...] * lap) + add[x + add0]
            if low < 0:
                inside = ((x >= 0) | (info[2] > 0)) & ((x < ROWS) | (info[2] < SLABS - 1))
                value = jnp.where(inside, value, 0.0)
            out[x + out0] = value

    blocks(rows, body, size)


def begin(info, z0, zo, zi, depth, zs):
    top, bottom = pick_halo(info, 0, zo, zi), pick_halo(info, 1, zo, zi)
    for r in range(depth):
        zs[r], zs[depth + ROWS + r] = top(r), bottom(r)

    def body(xs):
        for x in xs:
            zs[depth + x] = z0[x]

    blocks(ROWS, body)


def give(info, depth, outer, inner, value):
    send(info, outer, inner, [value(x) for x in range(depth)], [value(x) for x in range(ROWS - depth, ROWS)])


def hosting(info, hosts):
    return info[1] == jnp.where(info[0] == 0, hosts[0], hosts[1])


def start_kernel(hosts, ab, wc, dc12, result, unused, message, outer, inner):
    info = Position()

    @pl.when(hosting(info, hosts))
    def _():
        sweep(info, ab, A0, ab, B0, message, 0, 0, ROWS, wc, dc12)
        give(info, 8, outer, inner, lambda x: message[x])

        def body(xs):
            for x in xs:
                result[x], result[ROWS + x], result[2 * ROWS + x] = zeros(CP), ab[x + A0], message[x]

        blocks(ROWS, body)


def pair_kernel(
    slices, hosts, depth, z0, zo, zi, mine, short, long, wc, dc12, message, outer, inner, za, zb, zc, zs
):
    info = Position()

    def sweeps(one, two):
        begin(info, z0, zo, zi, 8, zs)
        sweep(info, zs, 8, one, XA0, za, 6, -6, ROWS + 12, wc, dc12)
        sweep(info, za, 6, one, XB0, zb, 4, -4, ROWS + 8, wc, dc12)
        if two is mine:
            sweep(info, zb, 4, two, XA0, zc, 2, -2, ROWS + 4, wc, dc12)
            sweep(info, zc, 2, two, XB0, message, 0, 0, ROWS, wc, dc12)
        else:
            sweep(info, zb, 4, two, A0, zc, 2, -2, ROWS + 4, wc, dc12)
            sweep(info, zc, 2, two, B0, message, 0, 0, ROWS, wc, dc12)
        give(info, depth, outer, inner, lambda x: message[x])

    for host in sorted(set(hosts)):
        one = mine if host == slices[0] else long
        two = mine if host == slices[1] else short
        pl.when(hosting(info, hosts) & (info[1] == host))(functools.partial(sweeps, one, two))


def gather(z0, za, zb, zc, z2, one, two):
    def body(xs):
        for x in xs:
            one[x], one[ROWS + x], one[2 * ROWS + x] = z0[x], za[x + 6], zb[x + 4]
            two[x], two[ROWS + x], two[2 * ROWS + x] = zb[x + 4], zc[x + 2], z2[x]

    blocks(ROWS, body)


def gather_kernel(slices, hosts, z0, za, zb, zc, z2, home_in, away_in, home, away):
    info = Position()
    active, second = hosting(info, hosts), info[1] == slices[1]
    pl.when(active & ~second)(lambda: gather(z0, za, zb, zc, z2, home, away))
    pl.when(active & second)(lambda: gather(z0, za, zb, zc, z2, away, home))


def base_kernel(n1, n2, c1, c2, pro, share, b1, b2):
    def body(xs):
        for x in xs:
            for n, c, b in ((n1, c1, b1), (n2, c2, b2)):
                value = thirds(jnp.concatenate([share[...] * c[x], zeros(8)], axis=0))
                b[:, x, :] = (n[x] - dot(pro[...], value))[:SPECIES]

    blocks(ROWS, body)


def out_kernel(
    where, u, b0, b1, b2, share, z0, zo, zi, ab, wc, dc12, home, one, other, out, z, za, zs, spread, node, sem
):
    info = Position()
    last = info[1] == SLICES - 1
    at_home = hosting(info, GROUPS[0][1])
    for slices, hosts in GROUPS[1:-1]:
        at_home = at_home | (hosting(info, hosts) & ((info[1] == slices[0]) | (info[1] == slices[1])))
    first = info[1] == GROUPS[1][0][0]
    for here, result in ((at_home, home), (first & ~at_home, one), (~at_home & ~first & ~last, other)):

        @pl.when(here)
        def _():

            def body(xs):
                for x in xs:
                    z[x] = result[x]

            blocks(3 * ROWS, body)

    @pl.when(last)
    def _():
        begin(info, z0, zo, zi, 4, zs)

        def body(xs):
            for x in xs:
                z[x] = z0[x]

        blocks(ROWS, body)

    def finish(m, base):
        def body(xs):
            for x in xs:
                spread[m, :, x, :] = share[...] * z[m * ROWS + x]

        blocks(ROWS, body, ROWS)

        def add(s):
            node[m, s] = base(s) + spread[m, where[s]]

        blocks(SPECIES, lambda at: [add(s) for s in at], 13)
        add(SPECIES - 1)
        copy = pltpu.make_async_copy(node.at[m], out.at[m], sem.at[m])
        copy.start()
        return copy

    first = info[1] == 0
    copies = [finish(0, lambda s: jnp.where(first, u[0, s], b0[s]))]

    @pl.when(last)
    def _():
        sweep(info, zs, 4, ab, A0, za, 2, -2, ROWS + 4, wc, dc12)
        sweep(info, za, 2, ab, B0, z.at[pl.ds(2 * ROWS, ROWS)], 0, 0, ROWS, wc, dc12)

        def body(xs):
            for x in xs:
                z[ROWS + x] = za[x + 2]

        blocks(ROWS, body)

    copies += [finish(1, lambda s: b1[s]), finish(2, lambda s: b2[s])]
    for copy in copies:
        copy.wait()


def field(*shape):
    return jax.ShapeDtypeStruct(shape + (COLS,), F32)


SMEM = pl.BlockSpec(memory_space=pltpu.SMEM)
VMEM = pl.BlockSpec(memory_space=pltpu.VMEM)
ANY = pl.BlockSpec(memory_space=pl.ANY)


def call(kernel, name, outs, *args, scratch=(), alias=None, out_specs=None, specs=None):
    specs = specs or [SMEM if a.dtype == jnp.int32 and a.ndim == 1 else VMEM for a in args]
    return pl.pallas_call(
        kernel,
        out_shape=outs,
        in_specs=specs,
        **({"out_specs": out_specs} if out_specs else {}),
        scratch_shapes=[pltpu.VMEM(f.shape, f.dtype) if isinstance(f, jax.ShapeDtypeStruct) else f for f in scratch],
        input_output_aliases=alias or {},
        compiler_params=pltpu.CompilerParams(vmem_limit_bytes=VMEM_LIMIT),
        name=name,
    )(*args)


AXES = ("tm", "space")
OUTER = [(s, s + 1) for s in range(1, SLABS - 1, 2)] + [(s + 1, s) for s in range(1, SLABS - 1, 2)]
INNER = [(s, s ^ 1) for s in range(SLABS)]
SAME = [(s, s) for s in range(SLABS)]


def moved(value, *routes):
    pairs = [
        (source[s % 2] * SLABS + s, target[t % 2] * SLABS + t) for source, target, slabs in routes for s, t in slabs
    ]
    return lax.ppermute(value, AXES, pairs)


def both(p):
    return (p, p)


def swap(outer, inner):
    got_inner = moved(inner, *[(both(p), both(p), INNER) for p in range(SLICES)])
    got_outer = moved(outer, *[(both(p), both(p), OUTER) for p in range(SLICES)])
    return got_outer, got_inner


def hop(message, outer, inner, source, target):
    parts = ((outer, OUTER), (inner, INNER), (message, SAME))
    zo, zi, z = [moved(value, (source, target, slabs)) for value, slabs in parts]
    return [z, zo, zi]


def after(value, other):
    return lax.optimization_barrier((value, other))[0]


def local(fine_nodes, fine_rates, fine_pairs, fine_diff, coarse_rates, coarse_pairs, coarse_diff, species_map):
    nodes = fine_nodes[0]
    fine, coarse = field(ROWS, SP), field(ROWS, CP)
    message = field(3, 2, SP)
    def bf16(*shape):
        return jax.ShapeDtypeStruct(shape, BF16)

    raw = sum(
        jnp.pad(v.astype(F32), ((at, RAW - at - v.shape[0]), (0, 128 - v.shape[1])))
        for at, v in (
            (RATES, fine_rates),
            (PAIRS, fine_pairs),
            (CRATES, coarse_rates),
            (CPAIRS, coarse_pairs),
            (DIFF, fine_diff.reshape(1, SPECIES)),
            (CDIFF, coarse_diff.reshape(1, COARSE)),
            (MAP, species_map.reshape(1, SPECIES)),
        )
    )
    wf, wr, wfr, lv, wc, pro, d12, dc12, share = call(
        prep_kernel,
        "prep",
        [bf16(2 * SP, 256), bf16(128, 256), bf16(2 * SP + 128, 256), bf16(80, 128), bf16(2 * CP, 128), bf16(SP, 96)]
        + [field(SP), field(CP), field(CP)],
        raw,
    )
    outer, inner = call(first_kernel, "first", [message, message], nodes, wc)
    uo, ui = swap(outer, inner)

    n1, s, r0, e0, c0 = call(
        old_kernel,
        "old",
        [fine, fine, coarse, coarse, coarse],
        *(nodes, wf, wr, wc, d12, dc12),
        scratch=[field(4, 3, SP), field(ROWS + 4, SP), field(ROWS + 4, SP), field(ROWS + 4, CP), field(ROWS + 4, CP)],
    )
    two, twelve, eight = field(2, SP), field(12, CP), field(8, CP)
    n1, s, r0, e0, outer, inner = call(
        old_edge_kernel,
        "old_edge",
        [fine, fine, coarse, coarse, two, two],
        *(uo, ui, lv, d12, dc12, n1, s, r0, e0),
        alias={5: 0, 6: 1, 7: 2, 8: 3},
    )
    no, ni = swap(outer, inner)
    n2, r1, e1, c1 = call(
        mid_kernel, "mid", [fine, coarse, coarse, coarse], n1, s, wfr, wc, d12, dc12, scratch=[field(ROWS + 4, SP), field(ROWS + 4, CP), field(ROWS + 4, CP)]
    )
    extended, short = field(EXT_ROWS, CP), field(AB_ROWS, CP)
    n2, r1, e1, abx, c2, outer, inner = call(
        mid_edge_kernel,
        "mid_edge",
        [fine, coarse, coarse, extended, coarse, twelve, twelve],
        *(no, ni, lv, wr, d12, dc12, r0, e0, c0, n2, r1, e1),
        alias={9: 0, 10: 1, 11: 2},
        scratch=[field(ROWS + 4, CP), coarse],
    )
    ho, hi = swap(outer, inner)
    b1, b2 = call(base_kernel, "base", [field(SPECIES, ROWS)] * 2, n1, n2, c1, c2, pro, share)
    abx, ab = call(last_edge_kernel, "last_edge", [extended, short], outer, inner, ho, hi, abx, alias={4: 0})

    ab, abx = after(ab, b1), after(abx, b1)
    result = field(3 * ROWS, CP)
    pairs = [(slices, hosts) for slices, hosts in GROUPS if len(slices) == 2]
    short, long, back, first = [], [], [], []
    for slices, hosts in pairs:
        for core, host in enumerate(hosts):
            slabs = [(t, t) for t in range(core, SLABS, 2)]
            if host != slices[0]:
                long.append((both(slices[0]), both(host), slabs))
            if host != slices[1]:
                short.append((both(slices[1]), both(host), slabs))
            back.append((both(host), both(slices[0] if host == slices[1] else slices[1]), slabs))
            if host not in slices:
                first.append((both(host), both(slices[0]), slabs))
    short, long, long_last = moved(ab, *short), moved(abx, *long[:-1]), long[-1:]
    forward = [(both(p), both(p + 1), SAME) for p in range(SLICES - 1)]
    home, away, *sent = call(
        functools.partial(start_kernel, GROUPS[0][1]), "start", [result, result, coarse, eight, eight], ab, wc, dc12
    )
    for at, (slices, hosts) in enumerate(GROUPS[1:], 1):
        z = hop(*sent, GROUPS[at - 1][1], hosts)
        if at == 1:
            *z, short, long = lax.optimization_barrier((*z, short, long))
            b0, long_last = moved(after(b2, z[0]), *forward), moved(after(abx, z[0]), *long_last)
        elif at == 2:
            *z, b0, long_last = lax.optimization_barrier((*z, b0, long_last))
        elif at == 3:
            *z, home, away = lax.optimization_barrier((*z, home, away))
        else:
            other, one = moved(away, *back), moved(home, *first)
            *z, other, one, home = lax.optimization_barrier((*z, other, one, home))
        if len(slices) == 2:
            depth = 4 * len(GROUPS[at + 1][0])
            *sent, za, zb, zc = call(
                functools.partial(pair_kernel, slices, hosts, depth),
                "pair",
                [coarse, field(depth, CP), field(depth, CP), field(ROWS + 12, CP), field(ROWS + 8, CP), field(ROWS + 4, CP)],
                *(*z, abx, short, long_last if at == 3 else long, wc, dc12),
                scratch=[field(ROWS + 16, CP)],
            )
            home, away = call(
                functools.partial(gather_kernel, slices, hosts),
                "gather",
                [result, result],
                *(z[0], za, zb, zc, sent[0], home, away),
                alias={5: 0, 6: 1},
            )
    out = call(
        out_kernel,
        "out",
        field(3, SPECIES, ROWS),
        *(species_map[:, 0], nodes, b0, b1, b2, share, *z, ab, wc, dc12, home, one, other),
        out_specs=ANY,
        scratch=[result, field(ROWS + 4, CP), field(ROWS + 8, CP), field(3, CP, ROWS), field(3, SPECIES, ROWS), pltpu.SemaphoreType.DMA((3,))],
    )
    return out[None]


def solution(mesh):
    in_specs = (P("tm", None, None, "space", None), P(), P(), P(), P(), P(), P(), P())
    out_specs = P("tm", None, None, "space", None)
    return jax.shard_map(local, mesh=mesh, in_specs=in_specs, out_specs=out_specs, check_vma=False)
```

```python
import functools

import jax
import jax.numpy as jnp
from jax import lax
from jax.experimental import pallas as pl
from jax.experimental.pallas import tpu as pltpu
from jax.sharding import PartitionSpec as P

SPECIES, COARSE = 53, 21
SP, CP = 56, 24
ROWS, COLS = 16, 256
SLICES, SLABS = 8, 16
STEP, HALF, RELAX = 0.1, 0.05, 3.0
W0 = (5.0 / 24.0, 1.0 / 3.0, -1.0 / 24.0)
W1 = (-1.0 / 24.0, 1.0 / 3.0, 5.0 / 24.0)
F32, BF16 = jnp.float32, jnp.bfloat16
GROUPS = (((0,), (0, 0)), ((1, 2), (1, 5)), ((3, 4), (3, 4)), ((5, 6), (5, 6)), ((7,), (7, 7)))
VMEM_LIMIT = 24 * 1024 * 1024


def split(x):
    hi = x.astype(BF16)
    lo = (x - hi.astype(F32)).astype(BF16)
    return jnp.concatenate([hi, lo], axis=0)


def thirds(x):
    hi = x.astype(BF16)
    rest = x - hi.astype(F32)
    mid = rest.astype(BF16)
    return jnp.concatenate([hi, mid, (rest - mid.astype(F32)).astype(BF16)], axis=0)


def zeros(rows):
    return jnp.zeros((rows, COLS), F32)


def dot(w, x):
    return jnp.dot(w, x, preferred_element_type=F32)


def stacked(x, squares):
    return split(jnp.concatenate([x, squares, zeros(16)], axis=0))


def lap_y(x):
    near = pltpu.roll(x, 1, 1) + pltpu.roll(x, COLS - 1, 1)
    far = pltpu.roll(x, 2, 1) + pltpu.roll(x, COLS - 2, 1)
    return 16.0 * near - far - 60.0 * x


def lap_rows(ref, x):
    return 16.0 * (ref[x - 1] + ref[x + 1]) - (ref[x - 2] + ref[x + 2])


def beside(near, far):
    return 16.0 * near - far, -near


RATES, PAIRS, CRATES, CPAIRS, DIFF, CDIFF, MAP, RAW = 0, 56, 112, 136, 160, 161, 162, 168


def prep_kernel(raw, wf, wr, wfr, lv, wc, pro, d12, dc12, share):
    row = lax.broadcasted_iota(jnp.int32, (SP, 128), 0)
    lane = lax.broadcasted_iota(jnp.int32, (SP, 128), 1)

    def halves(x):
        hi = x.astype(BF16).astype(F32)
        return hi, (x - hi).astype(BF16).astype(F32)

    def column(values, height):
        return jnp.sum(jnp.where(row == lane, values, 0.0), axis=1, keepdims=True)[:height]

    eye = jnp.where(row == lane, RELAX, 0.0)
    fine = raw[RATES : RATES + SP, :] - jnp.where(row < SPECIES, eye, 0.0)
    fine = fine + pltpu.roll(raw[PAIRS : PAIRS + SP, :], SP, 1)
    coarse = raw[CRATES : CRATES + CP, :] - jnp.where(row < COARSE, eye, 0.0)[:CP]
    coarse = coarse + pltpu.roll(raw[CPAIRS : CPAIRS + CP, :], CP, 1)
    vectors = raw[DIFF : DIFF + 8, :]
    diff_row = vectors[0:1]
    d12[...] = jnp.broadcast_to(column(diff_row, SP) / 12.0, (SP, COLS))
    dc12[...] = jnp.broadcast_to(column(vectors[1:2], CP) / 12.0, (CP, COLS))
    map_row = jnp.where(lane[0:1] < SPECIES, vectors[2:3].astype(jnp.int32), -1)
    map_column = jnp.sum(jnp.where(row == lane, map_row, 0), axis=1, keepdims=True)
    map_column = jnp.where(row[:, 0:1] < SPECIES, map_column, -1)
    lum = jnp.where((map_row == row[:CP]) & (lane[:CP] < SPECIES), 1.0, 0.0)
    counts = jnp.sum(lum, axis=1, keepdims=True)
    share[...] = jnp.broadcast_to(1.0 / jnp.maximum(counts, 1.0), (CP, COLS))
    lumped = jnp.dot(lum[:, :SP], fine, precision=lax.Precision.HIGHEST, preferred_element_type=F32)
    fh, fl = halves(fine)
    rh, rl = halves(lumped)
    dh, dl = halves(lum * diff_row)
    ch, cl = halves(coarse)
    f = jnp.concatenate([fh, fl], axis=0).astype(BF16)
    r = jnp.concatenate([rh, rl, lum, dh, dl, jnp.zeros((8, 128), F32)], axis=0).astype(BF16)
    for at in (0, 128):
        wf[:, at : at + 128] = f
        wr[:, at : at + 128] = r
        wfr[: 2 * SP, at : at + 128] = f
        wfr[2 * SP :, at : at + 128] = r
    v = jnp.concatenate([lum, dh, dl, jnp.zeros((8, 128), F32)], axis=0)
    lv[...] = (v + pltpu.roll(v, 64, 1)).astype(BF16)
    c = jnp.concatenate([ch, cl], axis=0)
    wc[...] = (c + pltpu.roll(c, 64, 1)).astype(BF16)
    lane96 = lax.broadcasted_iota(jnp.int32, (SP, 96), 1)
    pro[...] = jnp.where(map_column == lane96 % 32, 1.0, 0.0).astype(BF16)


class Position:
    def __init__(self):
        self.slice_at, self.slab = lax.axis_index("tm"), lax.axis_index("space")

    def __getitem__(self, at):
        return (self.slab % 2, self.slice_at, self.slab)[at]


def blocks(rows, body, size=4):
    @pl.loop(0, rows // size)
    def _(i):
        body([size * i + k for k in range(size)])


def first_kernel(u, weights_made, outer, inner):
    info = Position()
    at_top = info[0] == 0
    for m in range(3):
        for r in range(2):
            first, last = u[m, :, r, :], u[m, :, ROWS - 2 + r, :]
            for out, value in ((outer, jnp.where(at_top, first, last)), (inner, jnp.where(at_top, last, first))):
                out[m, r, SP - 8 :, :] = zeros(8)
                out[m, r, :SPECIES, :] = value


def restricted(y):
    return y[0:24] + y[24:48], y[48:72], y[72:96] + y[96:120]


MIX0 = [STEP * w for w in W0]
MIXS = [STEP * W1[0], STEP * W1[1] - HALF, STEP * W1[2]]


def mixed(factors, values):
    return factors[0] * values[0] + factors[1] * values[1] + factors[2] * values[2]


def old_kernel(u, wf, wr, wc, d12, dc12, n1, s, r0, e0, c0, ut, p0s, pss, v0s, c0s):
    for k in range(4):
        for m in range(3):
            ut[k, m, SP - 8 :, :] = zeros(8)
    for x in (0, 1, ROWS + 2, ROWS + 3):
        p0s[x], pss[x], v0s[x], c0s[x] = zeros(SP), zeros(SP), zeros(CP), zeros(CP)

    def terms(xs):
        for k, x in enumerate(xs):
            for m in range(3):
                ut[k, m, :SPECIES, :] = u[m, :, x, :]
        for k, x in enumerate(xs):
            us = [ut[k, m] for m in range(3)]
            qs = [v * v for v in us]
            p0, ps = mixed(MIX0, us), mixed(MIXS, us)
            y = dot(wf[...], stacked(p0, mixed(MIX0, qs)))
            n1[x] = us[0] + (y[:SP] + y[SP:]) + d12[...] * lap_y(p0)
            y = dot(wf[...], stacked(ps, mixed(MIXS, qs)))
            s[x] = (y[:SP] + y[SP:]) + d12[...] * lap_y(ps)
            r, c, v = restricted(dot(wr[...], stacked(us[0], qs[0])))
            r0[x] = r + lap_y(v) * (1.0 / 12.0)
            y = dot(wc[...], stacked(c, c * c))
            e0[x] = (y[:CP] + y[CP:]) + dc12[...] * lap_y(c)
            p0s[x + 2], pss[x + 2], v0s[x + 2], c0s[x + 2], c0[x] = p0, ps, v, c, c

    blocks(ROWS, terms)

    def laps(xs):
        for x in xs:
            n1[x] += d12[...] * lap_rows(p0s, x + 2)
            s[x] += d12[...] * lap_rows(pss, x + 2)
            r0[x] += lap_rows(v0s, x + 2) * (1.0 / 12.0)
            e0[x] += dc12[...] * lap_rows(c0s, x + 2)

    blocks(ROWS, laps)


def lumped_halo(lv, row):
    y = dot(lv[...], split(jnp.concatenate([row, zeros(8)], axis=0)))
    return y[0:24], y[24:48] + y[48:72]


SIDES = (((0, 1), (1, 0)), ((ROWS - 1, ROWS - 2), (0, 1)))


def pick_halo(info, side, outer, inner):
    take = info[0] == side
    return lambda *at: jnp.where(take, outer[at], inner[at])


def send(info, outer, inner, tops, bottoms):
    at_top = info[0] == 0
    for r, (top, bottom) in enumerate(zip(tops, bottoms)):
        outer[r] = jnp.where(at_top, top, bottom)
        inner[r] = jnp.where(at_top, bottom, top)


def old_edge_kernel(uo, ui, lv, d12, dc12, n1i, si, r0i, e0i, n1, s, r0, e0, outer, inner):
    info = Position()
    for side, (rows, order) in enumerate(SIDES):
        halo = pick_halo(info, side, uo, ui)
        us = [[halo(m, r) for m in range(3)] for r in order]
        p0 = beside(*[mixed(MIX0, v) for v in us])
        ps = beside(*[mixed(MIXS, v) for v in us])
        lumped = [lumped_halo(lv, v[0]) for v in us]
        c = beside(lumped[0][0], lumped[1][0])
        v = beside(lumped[0][1], lumped[1][1])
        for i, x in enumerate(rows):
            n1[x] = n1i[x] + d12[...] * p0[i]
            s[x] = si[x] + d12[...] * ps[i]
            r0[x] = r0i[x] + v[i] * (1.0 / 12.0)
            e0[x] = e0i[x] + dc12[...] * c[i]
    send(info, outer, inner, [n1[0], n1[1]], [n1[ROWS - 2], n1[ROWS - 1]])


def mid_kernel(n1, s, wfr, wc, d12, dc12, n2, r1, e1, c1, n1s, v1s, c1s):
    for x in (0, 1, ROWS + 2, ROWS + 3):
        n1s[x], v1s[x], c1s[x] = zeros(SP), zeros(CP), zeros(CP)

    def terms(xs):
        for x in xs:
            n = n1[x]
            y = dot(wfr[...], stacked(n, n * n))
            n2[x] = n + HALF * ((y[:SP] + y[SP : 2 * SP]) + d12[...] * lap_y(n)) + s[x]
            r, c, v = restricted(y[2 * SP :])
            r1[x] = r + lap_y(v) * (1.0 / 12.0)
            y = dot(wc[...], stacked(c, c * c))
            e1[x] = (y[:CP] + y[CP:]) + dc12[...] * lap_y(c)
            n1s[x + 2], v1s[x + 2], c1s[x + 2], c1[x] = n, v, c, c

    blocks(ROWS, terms)

    def laps(xs):
        for x in xs:
            n2[x] += (HALF * d12[...]) * lap_rows(n1s, x + 2)
            r1[x] += lap_rows(v1s, x + 2) * (1.0 / 12.0)
            e1[x] += dc12[...] * lap_rows(c1s, x + 2)

    blocks(ROWS, laps)


def lumped_old(first, c0, e0):
    return jnp.where(first, c0, -HALF * e0)


AB_ROWS, EXT_ROWS = 2 * ROWS + 4, 2 * ROWS + 20
A0, B0 = 2, ROWS + 4
XA0, XB0 = 6, ROWS + 16


def mid_edge_kernel(no, ni, lv, wr, d12, dc12, r0, e0, c0, n2i, r1i, e1i, n2, r1, e1, ab, c2, outer, inner, v2s, gs):
    info = Position()
    first = info[1] == 0
    for side, (rows, order) in enumerate(SIDES):
        halo = pick_halo(info, side, no, ni)
        ns = [halo(r) for r in order]
        lumped = [lumped_halo(lv, v) for v in ns]
        c = beside(lumped[0][0], lumped[1][0])
        v = beside(lumped[0][1], lumped[1][1])
        n = beside(*ns)
        for i, x in enumerate(rows):
            n2[x] = n2i[x] + (HALF * d12[...]) * n[i]
            r1[x] = r1i[x] + v[i] * (1.0 / 12.0)
            e1[x] = e1i[x] + dc12[...] * c[i]
    for x in (0, 1, ROWS + 2, ROWS + 3):
        v2s[x] = zeros(CP)

    def lumped(x, value):
        gs[x], c2[x], v2s[x + 2] = restricted(dot(wr[...], stacked(value, value * value)))

    def pieces(x, mid, late):
        v = v2s[x + 2]
        g2 = gs[x] + (lap_y(v) + lap_rows(v2s, x + 2)) * (1.0 / 12.0)
        ab[x + XA0] = mixed(MIX0, (r0[x], mid, g2)) + lumped_old(first, c0[x], e0[x])
        ab[x + XB0] = mixed([STEP * w for w in W1], (r0[x], mid, g2)) - HALF * late

    edges = (0, 1, ROWS - 2, ROWS - 1)
    for x in edges:
        lumped(x, n2[x])
    blocks(ROWS - 4, lambda xs: [lumped(x + 2, n2i[x + 2]) for x in xs], ROWS - 4)
    for x in edges:
        pieces(x, r1[x], e1[x])
    blocks(ROWS - 4, lambda xs: [pieces(x + 2, r1i[x + 2], e1i[x + 2]) for x in xs], ROWS - 4)
    top = [ab[x + XA0] for x in range(6)] + [ab[x + XB0] for x in range(4)] + [v2s[x + 2] for x in range(2)]
    bottom = [ab[x + XA0] for x in range(ROWS - 6, ROWS)] + [ab[x + XB0] for x in range(ROWS - 4, ROWS)]
    send(info, outer, inner, top, bottom + [v2s[x] for x in range(ROWS, ROWS + 2)])


def last_edge_kernel(mo, mi, ho, hi, abi, ab, short):
    info = Position()
    ka, kb = STEP * W0[2] / 12.0, STEP * W1[2] / 12.0
    done = {}
    for side, (rows, order) in enumerate(SIDES):
        inside = info[2] > 0 if side == 0 else info[2] < SLABS - 1
        own, halo = pick_halo(info, side, mo, mi), pick_halo(info, side, ho, hi)
        fix = beside(*[halo(10 + r) for r in order])
        theirs = beside(*[own(10 + r) for r in order[::-1]])
        for i, x in enumerate(rows):
            done[x + XA0] = abi[x + XA0] + ka * fix[i]
            done[x + XB0] = abi[x + XB0] + kb * fix[i]
        for depth, at, to, factor in ((6, 0, XA0, ka), (4, 6, XB0, kb)):
            for i in range(depth):
                x = -1 - i if side == 0 else ROWS + i
                value = halo(at + (depth - 1 - i if side == 0 else i))
                if i < 2:
                    value = value + factor * theirs[i]
                done[x + to] = jnp.where(inside, value, 0.0)
    for at, value in done.items():
        ab[at] = value
    for x in range(-2, ROWS + 2):
        short[x + A0] = done[x + XA0] if x + XA0 in done else abi[x + XA0]
    for x in range(ROWS):
        short[x + B0] = done[x + XB0] if x + XB0 in done else abi[x + XB0]


def sweep(info, z, z0, add, add0, out, out0, low, rows, wc, dc12):
    size = rows // 2

    def body(xs):
        zr = [z[xs[0] + (low + z0 + k)] for k in range(-2, size + 2)]
        for k in range(size):
            x, value = xs[k] + low, zr[k + 2]
            y = dot(wc[...], stacked(value, value * value))
            lap = lap_y(value) + 16.0 * (zr[k + 1] + zr[k + 3]) - (zr[k] + zr[k + 4])
            value = value + HALF * ((y[:CP] + y[CP:]) + dc12[...] * lap) + add[x + add0]
            if low < 0:
                inside = ((x >= 0) | (info[2] > 0)) & ((x < ROWS) | (info[2] < SLABS - 1))
                value = jnp.where(inside, value, 0.0)
            out[x + out0] = value

    blocks(rows, body, size)


def begin(info, z0, zo, zi, depth, zs):
    top, bottom = pick_halo(info, 0, zo, zi), pick_halo(info, 1, zo, zi)
    for r in range(depth):
        zs[r], zs[depth + ROWS + r] = top(r), bottom(r)

    def body(xs):
        for x in xs:
            zs[depth + x] = z0[x]

    blocks(ROWS, body)


def give(info, depth, outer, inner, value):
    send(info, outer, inner, [value(x) for x in range(depth)], [value(x) for x in range(ROWS - depth, ROWS)])


def hosting(info, hosts):
    return info[1] == jnp.where(info[0] == 0, hosts[0], hosts[1])


def start_kernel(hosts, ab, wc, dc12, result, unused, message, outer, inner):
    info = Position()

    @pl.when(hosting(info, hosts))
    def _():
        sweep(info, ab, A0, ab, B0, message, 0, 0, ROWS, wc, dc12)
        give(info, 8, outer, inner, lambda x: message[x])

        def body(xs):
            for x in xs:
                result[x], result[ROWS + x], result[2 * ROWS + x] = zeros(CP), ab[x + A0], message[x]

        blocks(ROWS, body)


def pair_kernel(
    slices, hosts, depth, z0, zo, zi, mine, short, long, wc, dc12, message, outer, inner, za, zb, zc, zs
):
    info = Position()

    def sweeps(one, two):
        begin(info, z0, zo, zi, 8, zs)
        sweep(info, zs, 8, one, XA0, za, 6, -6, ROWS + 12, wc, dc12)
        sweep(info, za, 6, one, XB0, zb, 4, -4, ROWS + 8, wc, dc12)
        if two is mine:
            sweep(info, zb, 4, two, XA0, zc, 2, -2, ROWS + 4, wc, dc12)
            sweep(info, zc, 2, two, XB0, message, 0, 0, ROWS, wc, dc12)
        else:
            sweep(info, zb, 4, two, A0, zc, 2, -2, ROWS + 4, wc, dc12)
            sweep(info, zc, 2, two, B0, message, 0, 0, ROWS, wc, dc12)
        give(info, depth, outer, inner, lambda x: message[x])

    for host in sorted(set(hosts)):
        one = mine if host == slices[0] else long
        two = mine if host == slices[1] else short
        pl.when(hosting(info, hosts) & (info[1] == host))(functools.partial(sweeps, one, two))


def gather(z0, za, zb, zc, z2, one, two):
    def body(xs):
        for x in xs:
            one[x], one[ROWS + x], one[2 * ROWS + x] = z0[x], za[x + 6], zb[x + 4]
            two[x], two[ROWS + x], two[2 * ROWS + x] = zb[x + 4], zc[x + 2], z2[x]

    blocks(ROWS, body)


def gather_kernel(slices, hosts, z0, za, zb, zc, z2, home_in, away_in, home, away):
    info = Position()
    active, second = hosting(info, hosts), info[1] == slices[1]
    pl.when(active & ~second)(lambda: gather(z0, za, zb, zc, z2, home, away))
    pl.when(active & second)(lambda: gather(z0, za, zb, zc, z2, away, home))


def base_kernel(n1, n2, c1, c2, pro, share, b1, b2):
    def body(xs):
        for x in xs:
            for n, c, b in ((n1, c1, b1), (n2, c2, b2)):
                value = thirds(jnp.concatenate([share[...] * c[x], zeros(8)], axis=0))
                b[:, x, :] = (n[x] - dot(pro[...], value))[:SPECIES]

    blocks(ROWS, body)


def out_kernel(
    where, u, b0, b1, b2, share, z0, zo, zi, ab, wc, dc12, home, one, other, out, z, za, zs, spread, node, sem
):
    info = Position()
    last = info[1] == SLICES - 1
    at_home = hosting(info, GROUPS[0][1])
    for slices, hosts in GROUPS[1:-1]:
        at_home = at_home | (hosting(info, hosts) & ((info[1] == slices[0]) | (info[1] == slices[1])))
    first = info[1] == GROUPS[1][0][0]
    for here, result in ((at_home, home), (first & ~at_home, one), (~at_home & ~first & ~last, other)):

        @pl.when(here)
        def _():

            def body(xs):
                for x in xs:
                    z[x] = result[x]

            blocks(3 * ROWS, body)

    @pl.when(last)
    def _():
        begin(info, z0, zo, zi, 4, zs)

        def body(xs):
            for x in xs:
                z[x] = z0[x]

        blocks(ROWS, body)

    def finish(m, base):
        def body(xs):
            for x in xs:
                spread[m, :, x, :] = share[...] * z[m * ROWS + x]

        blocks(ROWS, body, ROWS)

        def add(s):
            node[m, s] = base(s) + spread[m, where[s]]

        blocks(SPECIES, lambda at: [add(s) for s in at], 13)
        add(SPECIES - 1)
        copy = pltpu.make_async_copy(node.at[m], out.at[m], sem.at[m])
        copy.start()
        return copy

    first = info[1] == 0
    copies = [finish(0, lambda s: jnp.where(first, u[0, s], b0[s]))]

    @pl.when(last)
    def _():
        sweep(info, zs, 4, ab, A0, za, 2, -2, ROWS + 4, wc, dc12)
        sweep(info, za, 2, ab, B0, z.at[pl.ds(2 * ROWS, ROWS)], 0, 0, ROWS, wc, dc12)

        def body(xs):
            for x in xs:
                z[ROWS + x] = za[x + 2]

        blocks(ROWS, body)

    copies += [finish(1, lambda s: b1[s]), finish(2, lambda s: b2[s])]
    for copy in copies:
        copy.wait()


def field(*shape):
    return jax.ShapeDtypeStruct(shape + (COLS,), F32)


SMEM = pl.BlockSpec(memory_space=pltpu.SMEM)
VMEM = pl.BlockSpec(memory_space=pltpu.VMEM)
ANY = pl.BlockSpec(memory_space=pl.ANY)


def call(kernel, name, outs, *args, scratch=(), alias=None, out_specs=None, specs=None):
    specs = specs or [SMEM if a.dtype == jnp.int32 and a.ndim == 1 else VMEM for a in args]
    return pl.pallas_call(
        kernel,
        out_shape=outs,
        in_specs=specs,
        **({"out_specs": out_specs} if out_specs else {}),
        scratch_shapes=[pltpu.VMEM(f.shape, f.dtype) if isinstance(f, jax.ShapeDtypeStruct) else f for f in scratch],
        input_output_aliases=alias or {},
        compiler_params=pltpu.CompilerParams(vmem_limit_bytes=VMEM_LIMIT),
        name=name,
    )(*args)


AXES = ("tm", "space")
OUTER = [(s, s + 1) for s in range(1, SLABS - 1, 2)] + [(s + 1, s) for s in range(1, SLABS - 1, 2)]
INNER = [(s, s ^ 1) for s in range(SLABS)]
SAME = [(s, s) for s in range(SLABS)]


def moved(value, *routes):
    pairs = [
        (source[s % 2] * SLABS + s, target[t % 2] * SLABS + t) for source, target, slabs in routes for s, t in slabs
    ]
    return lax.ppermute(value, AXES, pairs)


def both(p):
    return (p, p)


def swap(outer, inner):
    got_inner = moved(inner, *[(both(p), both(p), INNER) for p in range(SLICES)])
    got_outer = moved(outer, *[(both(p), both(p), OUTER) for p in range(SLICES)])
    return got_outer, got_inner


def hop(message, outer, inner, source, target):
    parts = ((outer, OUTER), (inner, INNER), (message, SAME))
    zo, zi, z = [moved(value, (source, target, slabs)) for value, slabs in parts]
    return [z, zo, zi]


def after(value, other):
    return lax.optimization_barrier((value, other))[0]


def local(fine_nodes, fine_rates, fine_pairs, fine_diff, coarse_rates, coarse_pairs, coarse_diff, species_map):
    nodes = fine_nodes[0]
    fine, coarse = field(ROWS, SP), field(ROWS, CP)
    message = field(3, 2, SP)
    def bf16(*shape):
        return jax.ShapeDtypeStruct(shape, BF16)

    raw = sum(
        jnp.pad(v.astype(F32), ((at, RAW - at - v.shape[0]), (0, 128 - v.shape[1])))
        for at, v in (
            (RATES, fine_rates),
            (PAIRS, fine_pairs),
            (CRATES, coarse_rates),
            (CPAIRS, coarse_pairs),
            (DIFF, fine_diff.reshape(1, SPECIES)),
            (CDIFF, coarse_diff.reshape(1, COARSE)),
            (MAP, species_map.reshape(1, SPECIES)),
        )
    )
    wf, wr, wfr, lv, wc, pro, d12, dc12, share = call(
        prep_kernel,
        "prep",
        [bf16(2 * SP, 256), bf16(128, 256), bf16(2 * SP + 128, 256), bf16(80, 128), bf16(2 * CP, 128), bf16(SP, 96)]
        + [field(SP), field(CP), field(CP)],
        raw,
    )
    outer, inner = call(first_kernel, "first", [message, message], nodes, wc)
    uo, ui = swap(outer, inner)

    n1, s, r0, e0, c0 = call(
        old_kernel,
        "old",
        [fine, fine, coarse, coarse, coarse],
        *(nodes, wf, wr, wc, d12, dc12),
        scratch=[field(4, 3, SP), field(ROWS + 4, SP), field(ROWS + 4, SP), field(ROWS + 4, CP), field(ROWS + 4, CP)],
    )
    two, twelve, eight = field(2, SP), field(12, CP), field(8, CP)
    n1, s, r0, e0, outer, inner = call(
        old_edge_kernel,
        "old_edge",
        [fine, fine, coarse, coarse, two, two],
        *(uo, ui, lv, d12, dc12, n1, s, r0, e0),
        alias={5: 0, 6: 1, 7: 2, 8: 3},
    )
    no, ni = swap(outer, inner)
    n2, r1, e1, c1 = call(
        mid_kernel, "mid", [fine, coarse, coarse, coarse], n1, s, wfr, wc, d12, dc12, scratch=[field(ROWS + 4, SP), field(ROWS + 4, CP), field(ROWS + 4, CP)]
    )
    extended, short = field(EXT_ROWS, CP), field(AB_ROWS, CP)
    n2, r1, e1, abx, c2, outer, inner = call(
        mid_edge_kernel,
        "mid_edge",
        [fine, coarse, coarse, extended, coarse, twelve, twelve],
        *(no, ni, lv, wr, d12, dc12, r0, e0, c0, n2, r1, e1),
        alias={9: 0, 10: 1, 11: 2},
        scratch=[field(ROWS + 4, CP), coarse],
    )
    ho, hi = swap(outer, inner)
    b1, b2 = call(base_kernel, "base", [field(SPECIES, ROWS)] * 2, n1, n2, c1, c2, pro, share)
    abx, ab = call(last_edge_kernel, "last_edge", [extended, short], outer, inner, ho, hi, abx, alias={4: 0})

    ab, abx = after(ab, b1), after(abx, b1)
    result = field(3 * ROWS, CP)
    pairs = [(slices, hosts) for slices, hosts in GROUPS if len(slices) == 2]
    short, long, back, first = [], [], [], []
    for slices, hosts in pairs:
        for core, host in enumerate(hosts):
            slabs = [(t, t) for t in range(core, SLABS, 2)]
            if host != slices[0]:
                long.append((both(slices[0]), both(host), slabs))
            if host != slices[1]:
                short.append((both(slices[1]), both(host), slabs))
            back.append((both(host), both(slices[0] if host == slices[1] else slices[1]), slabs))
            if host not in slices:
                first.append((both(host), both(slices[0]), slabs))
    short, long = moved(ab, *short), moved(abx, *long)
    forward = [(both(p), both(p + 1), SAME) for p in range(SLICES - 1)]
    home, away, *sent = call(
        functools.partial(start_kernel, GROUPS[0][1]), "start", [result, result, coarse, eight, eight], ab, wc, dc12
    )
    for at, (slices, hosts) in enumerate(GROUPS[1:], 1):
        z = hop(*sent, GROUPS[at - 1][1], hosts)
        if at == 1:
            z = list(lax.optimization_barrier(tuple(z)))
            b0 = moved(after(b2, z[0]), *forward)
        elif at == 2:
            *z, b0 = lax.optimization_barrier((*z, b0))
        elif at == 3:
            *z, home, away = lax.optimization_barrier((*z, home, away))
        else:
            other, one = moved(away, *back), moved(home, *first)
            *z, other, one, home = lax.optimization_barrier((*z, other, one, home))
        if len(slices) == 2:
            depth = 4 * len(GROUPS[at + 1][0])
            *sent, za, zb, zc = call(
                functools.partial(pair_kernel, slices, hosts, depth),
                "pair",
                [coarse, field(depth, CP), field(depth, CP), field(ROWS + 12, CP), field(ROWS + 8, CP), field(ROWS + 4, CP)],
                *(*z, abx, short, long, wc, dc12),
                scratch=[field(ROWS + 16, CP)],
            )
            home, away = call(
                functools.partial(gather_kernel, slices, hosts),
                "gather",
                [result, result],
                *(z[0], za, zb, zc, sent[0], home, away),
                alias={5: 0, 6: 1},
            )
    out = call(
        out_kernel,
        "out",
        field(3, SPECIES, ROWS),
        *(species_map[:, 0], nodes, b0, b1, b2, share, *z, ab, wc, dc12, home, one, other),
        out_specs=ANY,
        scratch=[result, field(ROWS + 4, CP), field(ROWS + 8, CP), field(3, CP, ROWS), field(3, SPECIES, ROWS), pltpu.SemaphoreType.DMA((3,))],
    )
    return out[None]


def solution(mesh):
    in_specs = (P("tm", None, None, "space", None), P(), P(), P(), P(), P(), P(), P())
    out_specs = P("tm", None, None, "space", None)
    return jax.shard_map(local, mesh=mesh, in_specs=in_specs, out_specs=out_specs, check_vma=False)
```

```python
import functools

import jax
import jax.numpy as jnp
from jax import lax
from jax.experimental import pallas as pl
from jax.experimental.pallas import tpu as pltpu
from jax.sharding import PartitionSpec as P

SPECIES, COARSE = 53, 21
SP, CP = 56, 24
ROWS, COLS = 16, 256
SLICES, SLABS = 8, 16
STEP, HALF, RELAX = 0.1, 0.05, 3.0
W0 = (5.0 / 24.0, 1.0 / 3.0, -1.0 / 24.0)
W1 = (-1.0 / 24.0, 1.0 / 3.0, 5.0 / 24.0)
F32, BF16 = jnp.float32, jnp.bfloat16
GROUPS = (((0,), (0, 0)), ((1, 2), (1, 1)), ((3, 4), (3, 4)), ((5, 6), (5, 6)), ((7,), (7, 7)))
VMEM_LIMIT = 24 * 1024 * 1024


def split(x):
    hi = x.astype(BF16)
    lo = (x - hi.astype(F32)).astype(BF16)
    return jnp.concatenate([hi, lo], axis=0)


def thirds(x):
    hi = x.astype(BF16)
    rest = x - hi.astype(F32)
    mid = rest.astype(BF16)
    return jnp.concatenate([hi, mid, (rest - mid.astype(F32)).astype(BF16)], axis=0)


def zeros(rows):
    return jnp.zeros((rows, COLS), F32)


def dot(w, x):
    return jnp.dot(w, x, preferred_element_type=F32)


def stacked(x, squares):
    return split(jnp.concatenate([x, squares, zeros(16)], axis=0))


def lap_y(x):
    near = pltpu.roll(x, 1, 1) + pltpu.roll(x, COLS - 1, 1)
    far = pltpu.roll(x, 2, 1) + pltpu.roll(x, COLS - 2, 1)
    return 16.0 * near - far - 60.0 * x


def lap_rows(ref, x):
    return 16.0 * (ref[x - 1] + ref[x + 1]) - (ref[x - 2] + ref[x + 2])


def beside(near, far):
    return 16.0 * near - far, -near


RATES, PAIRS, CRATES, CPAIRS, DIFF, CDIFF, MAP, RAW = 0, 56, 112, 136, 160, 161, 162, 168


def prep_kernel(raw, wf, wr, wfr, lv, wc, pro, d12, dc12, share):
    row = lax.broadcasted_iota(jnp.int32, (SP, 128), 0)
    lane = lax.broadcasted_iota(jnp.int32, (SP, 128), 1)

    def halves(x):
        hi = x.astype(BF16).astype(F32)
        return hi, (x - hi).astype(BF16).astype(F32)

    def column(values, height):
        return jnp.sum(jnp.where(row == lane, values, 0.0), axis=1, keepdims=True)[:height]

    eye = jnp.where(row == lane, RELAX, 0.0)
    fine = raw[RATES : RATES + SP, :] - jnp.where(row < SPECIES, eye, 0.0)
    fine = fine + pltpu.roll(raw[PAIRS : PAIRS + SP, :], SP, 1)
    coarse = raw[CRATES : CRATES + CP, :] - jnp.where(row < COARSE, eye, 0.0)[:CP]
    coarse = coarse + pltpu.roll(raw[CPAIRS : CPAIRS + CP, :], CP, 1)
    vectors = raw[DIFF : DIFF + 8, :]
    diff_row = vectors[0:1]
    d12[...] = jnp.broadcast_to(column(diff_row, SP) / 12.0, (SP, COLS))
    dc12[...] = jnp.broadcast_to(column(vectors[1:2], CP) / 12.0, (CP, COLS))
    map_row = jnp.where(lane[0:1] < SPECIES, vectors[2:3].astype(jnp.int32), -1)
    map_column = jnp.sum(jnp.where(row == lane, map_row, 0), axis=1, keepdims=True)
    map_column = jnp.where(row[:, 0:1] < SPECIES, map_column, -1)
    lum = jnp.where((map_row == row[:CP]) & (lane[:CP] < SPECIES), 1.0, 0.0)
    counts = jnp.sum(lum, axis=1, keepdims=True)
    share[...] = jnp.broadcast_to(1.0 / jnp.maximum(counts, 1.0), (CP, COLS))
    lumped = jnp.dot(lum[:, :SP], fine, precision=lax.Precision.HIGHEST, preferred_element_type=F32)
    fh, fl = halves(fine)
    rh, rl = halves(lumped)
    dh, dl = halves(lum * diff_row)
    ch, cl = halves(coarse)
    f = jnp.concatenate([fh, fl], axis=0).astype(BF16)
    r = jnp.concatenate([rh, rl, lum, dh, dl, jnp.zeros((8, 128), F32)], axis=0).astype(BF16)
    for at in (0, 128):
        wf[:, at : at + 128] = f
        wr[:, at : at + 128] = r
        wfr[: 2 * SP, at : at + 128] = f
        wfr[2 * SP :, at : at + 128] = r
    v = jnp.concatenate([lum, dh, dl, jnp.zeros((8, 128), F32)], axis=0)
    lv[...] = (v + pltpu.roll(v, 64, 1)).astype(BF16)
    c = jnp.concatenate([ch, cl], axis=0)
    wc[...] = (c + pltpu.roll(c, 64, 1)).astype(BF16)
    lane96 = lax.broadcasted_iota(jnp.int32, (SP, 96), 1)
    pro[...] = jnp.where(map_column == lane96 % 32, 1.0, 0.0).astype(BF16)


class Position:
    def __init__(self):
        self.slice_at, self.slab = lax.axis_index("tm"), lax.axis_index("space")

    def __getitem__(self, at):
        return (self.slab % 2, self.slice_at, self.slab)[at]


def blocks(rows, body, size=4):
    @pl.loop(0, rows // size)
    def _(i):
        body([size * i + k for k in range(size)])


def first_kernel(u, weights_made, outer, inner):
    info = Position()
    at_top = info[0] == 0
    for m in range(3):
        for r in range(2):
            first, last = u[m, :, r, :], u[m, :, ROWS - 2 + r, :]
            for out, value in ((outer, jnp.where(at_top, first, last)), (inner, jnp.where(at_top, last, first))):
                out[m, r, SP - 8 :, :] = zeros(8)
                out[m, r, :SPECIES, :] = value


def restricted(y):
    return y[0:24] + y[24:48], y[48:72], y[72:96] + y[96:120]


MIX0 = [STEP * w for w in W0]
MIXS = [STEP * W1[0], STEP * W1[1] - HALF, STEP * W1[2]]


def mixed(factors, values):
    return factors[0] * values[0] + factors[1] * values[1] + factors[2] * values[2]


def old_kernel(u, wf, wr, wc, d12, dc12, n1, s, r0, e0, c0, ut, p0s, pss, v0s, c0s):
    for k in range(4):
        for m in range(3):
            ut[k, m, SP - 8 :, :] = zeros(8)
    for x in (0, 1, ROWS + 2, ROWS + 3):
        p0s[x], pss[x], v0s[x], c0s[x] = zeros(SP), zeros(SP), zeros(CP), zeros(CP)

    def terms(xs):
        for k, x in enumerate(xs):
            for m in range(3):
                ut[k, m, :SPECIES, :] = u[m, :, x, :]
        for k, x in enumerate(xs):
            us = [ut[k, m] for m in range(3)]
            qs = [v * v for v in us]
            p0, ps = mixed(MIX0, us), mixed(MIXS, us)
            y = dot(wf[...], stacked(p0, mixed(MIX0, qs)))
            n1[x] = us[0] + (y[:SP] + y[SP:]) + d12[...] * lap_y(p0)
            y = dot(wf[...], stacked(ps, mixed(MIXS, qs)))
            s[x] = (y[:SP] + y[SP:]) + d12[...] * lap_y(ps)
            r, c, v = restricted(dot(wr[...], stacked(us[0], qs[0])))
            r0[x] = r + lap_y(v) * (1.0 / 12.0)
            y = dot(wc[...], stacked(c, c * c))
            e0[x] = (y[:CP] + y[CP:]) + dc12[...] * lap_y(c)
            p0s[x + 2], pss[x + 2], v0s[x + 2], c0s[x + 2], c0[x] = p0, ps, v, c, c

    blocks(ROWS, terms)

    def laps(xs):
        for x in xs:
            n1[x] += d12[...] * lap_rows(p0s, x + 2)
            s[x] += d12[...] * lap_rows(pss, x + 2)
            r0[x] += lap_rows(v0s, x + 2) * (1.0 / 12.0)
            e0[x] += dc12[...] * lap_rows(c0s, x + 2)

    blocks(ROWS, laps)


def lumped_halo(lv, row):
    y = dot(lv[...], split(jnp.concatenate([row, zeros(8)], axis=0)))
    return y[0:24], y[24:48] + y[48:72]


SIDES = (((0, 1), (1, 0)), ((ROWS - 1, ROWS - 2), (0, 1)))


def pick_halo(info, side, outer, inner):
    take = info[0] == side
    return lambda *at: jnp.where(take, outer[at], inner[at])


def send(info, outer, inner, tops, bottoms):
    at_top = info[0] == 0
    for r, (top, bottom) in enumerate(zip(tops, bottoms)):
        outer[r] = jnp.where(at_top, top, bottom)
        inner[r] = jnp.where(at_top, bottom, top)


def old_edge_kernel(uo, ui, lv, d12, dc12, n1i, si, r0i, e0i, n1, s, r0, e0, outer, inner):
    info = Position()
    for side, (rows, order) in enumerate(SIDES):
        halo = pick_halo(info, side, uo, ui)
        us = [[halo(m, r) for m in range(3)] for r in order]
        p0 = beside(*[mixed(MIX0, v) for v in us])
        ps = beside(*[mixed(MIXS, v) for v in us])
        lumped = [lumped_halo(lv, v[0]) for v in us]
        c = beside(lumped[0][0], lumped[1][0])
        v = beside(lumped[0][1], lumped[1][1])
        for i, x in enumerate(rows):
            n1[x] = n1i[x] + d12[...] * p0[i]
            s[x] = si[x] + d12[...] * ps[i]
            r0[x] = r0i[x] + v[i] * (1.0 / 12.0)
            e0[x] = e0i[x] + dc12[...] * c[i]
    send(info, outer, inner, [n1[0], n1[1]], [n1[ROWS - 2], n1[ROWS - 1]])


def mid_kernel(n1, s, wfr, wc, d12, dc12, n2, r1, e1, c1, n1s, v1s, c1s):
    for x in (0, 1, ROWS + 2, ROWS + 3):
        n1s[x], v1s[x], c1s[x] = zeros(SP), zeros(CP), zeros(CP)

    def terms(xs):
        for x in xs:
            n = n1[x]
            y = dot(wfr[...], stacked(n, n * n))
            n2[x] = n + HALF * ((y[:SP] + y[SP : 2 * SP]) + d12[...] * lap_y(n)) + s[x]
            r, c, v = restricted(y[2 * SP :])
            r1[x] = r + lap_y(v) * (1.0 / 12.0)
            y = dot(wc[...], stacked(c, c * c))
            e1[x] = (y[:CP] + y[CP:]) + dc12[...] * lap_y(c)
            n1s[x + 2], v1s[x + 2], c1s[x + 2], c1[x] = n, v, c, c

    blocks(ROWS, terms)

    def laps(xs):
        for x in xs:
            n2[x] += (HALF * d12[...]) * lap_rows(n1s, x + 2)
            r1[x] += lap_rows(v1s, x + 2) * (1.0 / 12.0)
            e1[x] += dc12[...] * lap_rows(c1s, x + 2)

    blocks(ROWS, laps)


def lumped_old(first, c0, e0):
    return jnp.where(first, c0, -HALF * e0)


AB_ROWS, EXT_ROWS = 2 * ROWS + 4, 2 * ROWS + 20
A0, B0 = 2, ROWS + 4
XA0, XB0 = 6, ROWS + 16


def mid_edge_kernel(no, ni, lv, wr, d12, dc12, r0, e0, c0, n2i, r1i, e1i, n2, r1, e1, ab, c2, outer, inner, v2s, gs):
    info = Position()
    first = info[1] == 0
    for side, (rows, order) in enumerate(SIDES):
        halo = pick_halo(info, side, no, ni)
        ns = [halo(r) for r in order]
        lumped = [lumped_halo(lv, v) for v in ns]
        c = beside(lumped[0][0], lumped[1][0])
        v = beside(lumped[0][1], lumped[1][1])
        n = beside(*ns)
        for i, x in enumerate(rows):
            n2[x] = n2i[x] + (HALF * d12[...]) * n[i]
            r1[x] = r1i[x] + v[i] * (1.0 / 12.0)
            e1[x] = e1i[x] + dc12[...] * c[i]
    for x in (0, 1, ROWS + 2, ROWS + 3):
        v2s[x] = zeros(CP)

    def lumped(x, value):
        gs[x], c2[x], v2s[x + 2] = restricted(dot(wr[...], stacked(value, value * value)))

    def pieces(x, mid, late):
        v = v2s[x + 2]
        g2 = gs[x] + (lap_y(v) + lap_rows(v2s, x + 2)) * (1.0 / 12.0)
        ab[x + XA0] = mixed(MIX0, (r0[x], mid, g2)) + lumped_old(first, c0[x], e0[x])
        ab[x + XB0] = mixed([STEP * w for w in W1], (r0[x], mid, g2)) - HALF * late

    edges = (0, 1, ROWS - 2, ROWS - 1)
    for x in edges:
        lumped(x, n2[x])
    blocks(ROWS - 4, lambda xs: [lumped(x + 2, n2i[x + 2]) for x in xs], ROWS - 4)
    for x in edges:
        pieces(x, r1[x], e1[x])
    blocks(ROWS - 4, lambda xs: [pieces(x + 2, r1i[x + 2], e1i[x + 2]) for x in xs], ROWS - 4)
    top = [ab[x + XA0] for x in range(6)] + [ab[x + XB0] for x in range(4)] + [v2s[x + 2] for x in range(2)]
    bottom = [ab[x + XA0] for x in range(ROWS - 6, ROWS)] + [ab[x + XB0] for x in range(ROWS - 4, ROWS)]
    send(info, outer, inner, top, bottom + [v2s[x] for x in range(ROWS, ROWS + 2)])


def last_edge_kernel(mo, mi, ho, hi, abi, ab, short):
    info = Position()
    ka, kb = STEP * W0[2] / 12.0, STEP * W1[2] / 12.0
    done = {}
    for side, (rows, order) in enumerate(SIDES):
        inside = info[2] > 0 if side == 0 else info[2] < SLABS - 1
        own, halo = pick_halo(info, side, mo, mi), pick_halo(info, side, ho, hi)
        fix = beside(*[halo(10 + r) for r in order])
        theirs = beside(*[own(10 + r) for r in order[::-1]])
        for i, x in enumerate(rows):
            done[x + XA0] = abi[x + XA0] + ka * fix[i]
            done[x + XB0] = abi[x + XB0] + kb * fix[i]
        for depth, at, to, factor in ((6, 0, XA0, ka), (4, 6, XB0, kb)):
            for i in range(depth):
                x = -1 - i if side == 0 else ROWS + i
                value = halo(at + (depth - 1 - i if side == 0 else i))
                if i < 2:
                    value = value + factor * theirs[i]
                done[x + to] = jnp.where(inside, value, 0.0)
    for at, value in done.items():
        ab[at] = value
    for x in range(-2, ROWS + 2):
        short[x + A0] = done[x + XA0] if x + XA0 in done else abi[x + XA0]
    for x in range(ROWS):
        short[x + B0] = done[x + XB0] if x + XB0 in done else abi[x + XB0]


def sweep(info, z, z0, add, add0, out, out0, low, rows, wc, dc12):
    size = rows // 2

    def body(xs):
        zr = [z[xs[0] + (low + z0 + k)] for k in range(-2, size + 2)]
        for k in range(size):
            x, value = xs[k] + low, zr[k + 2]
            y = dot(wc[...], stacked(value, value * value))
            lap = lap_y(value) + 16.0 * (zr[k + 1] + zr[k + 3]) - (zr[k] + zr[k + 4])
            value = value + HALF * ((y[:CP] + y[CP:]) + dc12[...] * lap) + add[x + add0]
            if low < 0:
                inside = ((x >= 0) | (info[2] > 0)) & ((x < ROWS) | (info[2] < SLABS - 1))
                value = jnp.where(inside, value, 0.0)
            out[x + out0] = value

    blocks(rows, body, size)


def begin(info, z0, zo, zi, depth, zs):
    top, bottom = pick_halo(info, 0, zo, zi), pick_halo(info, 1, zo, zi)
    for r in range(depth):
        zs[r], zs[depth + ROWS + r] = top(r), bottom(r)

    def body(xs):
        for x in xs:
            zs[depth + x] = z0[x]

    blocks(ROWS, body)


def give(info, depth, outer, inner, value):
    send(info, outer, inner, [value(x) for x in range(depth)], [value(x) for x in range(ROWS - depth, ROWS)])


def hosting(info, hosts):
    return info[1] == jnp.where(info[0] == 0, hosts[0], hosts[1])


def start_kernel(hosts, ab, wc, dc12, result, unused, message, outer, inner):
    info = Position()

    @pl.when(hosting(info, hosts))
    def _():
        sweep(info, ab, A0, ab, B0, message, 0, 0, ROWS, wc, dc12)
        give(info, 8, outer, inner, lambda x: message[x])

        def body(xs):
            for x in xs:
                result[x], result[ROWS + x], result[2 * ROWS + x] = zeros(CP), ab[x + A0], message[x]

        blocks(ROWS, body)


def pair_kernel(
    slices, hosts, depth, z0, zo, zi, mine, short, long, wc, dc12, message, outer, inner, za, zb, zc, zs
):
    info = Position()

    def sweeps(one, two):
        begin(info, z0, zo, zi, 8, zs)
        sweep(info, zs, 8, one, XA0, za, 6, -6, ROWS + 12, wc, dc12)
        sweep(info, za, 6, one, XB0, zb, 4, -4, ROWS + 8, wc, dc12)
        if two is mine:
            sweep(info, zb, 4, two, XA0, zc, 2, -2, ROWS + 4, wc, dc12)
            sweep(info, zc, 2, two, XB0, message, 0, 0, ROWS, wc, dc12)
        else:
            sweep(info, zb, 4, two, A0, zc, 2, -2, ROWS + 4, wc, dc12)
            sweep(info, zc, 2, two, B0, message, 0, 0, ROWS, wc, dc12)
        give(info, depth, outer, inner, lambda x: message[x])

    for host in sorted(set(hosts)):
        one = mine if host == slices[0] else long
        two = mine if host == slices[1] else short
        pl.when(hosting(info, hosts) & (info[1] == host))(functools.partial(sweeps, one, two))


def inner_kernel(z, inner):
    info = Position()
    for r in range(8):
        inner[r] = jnp.where(info[0] == 0, z[ROWS - 8 + r], z[r])


def gather(z0, za, zb, zc, z2, one, two):
    def body(xs):
        for x in xs:
            one[x], one[ROWS + x], one[2 * ROWS + x] = z0[x], za[x + 6], zb[x + 4]
            two[x], two[ROWS + x], two[2 * ROWS + x] = zb[x + 4], zc[x + 2], z2[x]

    blocks(ROWS, body)


def gather_kernel(slices, hosts, z0, za, zb, zc, z2, home_in, away_in, home, away):
    info = Position()
    active, second = hosting(info, hosts), info[1] == slices[1]
    pl.when(active & ~second)(lambda: gather(z0, za, zb, zc, z2, home, away))
    pl.when(active & second)(lambda: gather(z0, za, zb, zc, z2, away, home))


def base_kernel(n1, n2, c1, c2, pro, share, b1, b2):
    def body(xs):
        for x in xs:
            for n, c, b in ((n1, c1, b1), (n2, c2, b2)):
                value = thirds(jnp.concatenate([share[...] * c[x], zeros(8)], axis=0))
                b[:, x, :] = (n[x] - dot(pro[...], value))[:SPECIES]

    blocks(ROWS, body)


def out_kernel(
    where, u, b0, late, b1, b2, share, z0, zo, zi, ab, wc, dc12, home, other, out, z, za, zs, spread, node, sem
):
    info = Position()
    last = info[1] == SLICES - 1
    at_home = hosting(info, GROUPS[0][1])
    for slices, hosts in GROUPS[1:-1]:
        at_home = at_home | (hosting(info, hosts) & ((info[1] == slices[0]) | (info[1] == slices[1])))
    for here, result in ((at_home, home), (~at_home & ~last, other)):

        @pl.when(here)
        def _():

            def body(xs):
                for x in xs:
                    z[x] = result[x]

            blocks(3 * ROWS, body)

    @pl.when(last)
    def _():
        begin(info, z0, zo, zi, 4, zs)

        def body(xs):
            for x in xs:
                z[x] = z0[x]

        blocks(ROWS, body)

    def finish(m, base):
        def body(xs):
            for x in xs:
                spread[m, :, x, :] = share[...] * z[m * ROWS + x]

        blocks(ROWS, body, ROWS)

        def add(s):
            node[m, s] = base(s) + spread[m, where[s]]

        blocks(SPECIES, lambda at: [add(s) for s in at], 13)
        add(SPECIES - 1)
        copy = pltpu.make_async_copy(node.at[m], out.at[m], sem.at[m])
        copy.start()
        return copy

    first = info[1] == 0
    copies = [finish(0, lambda s: jnp.where(first, u[0, s], b0[s] + late[s]))]

    @pl.when(last)
    def _():
        sweep(info, zs, 4, ab, A0, za, 2, -2, ROWS + 4, wc, dc12)
        sweep(info, za, 2, ab, B0, z.at[pl.ds(2 * ROWS, ROWS)], 0, 0, ROWS, wc, dc12)

        def body(xs):
            for x in xs:
                z[ROWS + x] = za[x + 2]

        blocks(ROWS, body)

    copies += [finish(1, lambda s: b1[s]), finish(2, lambda s: b2[s])]
    for copy in copies:
        copy.wait()


def field(*shape):
    return jax.ShapeDtypeStruct(shape + (COLS,), F32)


SMEM = pl.BlockSpec(memory_space=pltpu.SMEM)
VMEM = pl.BlockSpec(memory_space=pltpu.VMEM)
ANY = pl.BlockSpec(memory_space=pl.ANY)


def call(kernel, name, outs, *args, scratch=(), alias=None, out_specs=None, specs=None):
    specs = specs or [SMEM if a.dtype == jnp.int32 and a.ndim == 1 else VMEM for a in args]
    return pl.pallas_call(
        kernel,
        out_shape=outs,
        in_specs=specs,
        **({"out_specs": out_specs} if out_specs else {}),
        scratch_shapes=[pltpu.VMEM(f.shape, f.dtype) if isinstance(f, jax.ShapeDtypeStruct) else f for f in scratch],
        input_output_aliases=alias or {},
        compiler_params=pltpu.CompilerParams(vmem_limit_bytes=VMEM_LIMIT),
        name=name,
    )(*args)


AXES = ("tm", "space")
OUTER = [(s, s + 1) for s in range(1, SLABS - 1, 2)] + [(s + 1, s) for s in range(1, SLABS - 1, 2)]
INNER = [(s, s ^ 1) for s in range(SLABS)]
SAME = [(s, s) for s in range(SLABS)]


def moved(value, *routes):
    pairs = [
        (source[s % 2] * SLABS + s, target[t % 2] * SLABS + t) for source, target, slabs in routes for s, t in slabs
    ]
    return lax.ppermute(value, AXES, pairs)


def both(p):
    return (p, p)


def swap(outer, inner):
    got_inner = moved(inner, *[(both(p), both(p), INNER) for p in range(SLICES)])
    got_outer = moved(outer, *[(both(p), both(p), OUTER) for p in range(SLICES)])
    return got_outer, got_inner


def hop(message, outer, inner, source, target):
    parts = ((outer, OUTER), (inner, INNER), (message, SAME))
    zo, zi, z = [moved(value, (source, target, slabs)) for value, slabs in parts]
    return [z, zo, zi]


def after(value, other):
    return lax.optimization_barrier((value, other))[0]


def local(fine_nodes, fine_rates, fine_pairs, fine_diff, coarse_rates, coarse_pairs, coarse_diff, species_map):
    nodes = fine_nodes[0]
    fine, coarse = field(ROWS, SP), field(ROWS, CP)
    message = field(3, 2, SP)
    def bf16(*shape):
        return jax.ShapeDtypeStruct(shape, BF16)

    raw = sum(
        jnp.pad(v.astype(F32), ((at, RAW - at - v.shape[0]), (0, 128 - v.shape[1])))
        for at, v in (
            (RATES, fine_rates),
            (PAIRS, fine_pairs),
            (CRATES, coarse_rates),
            (CPAIRS, coarse_pairs),
            (DIFF, fine_diff.reshape(1, SPECIES)),
            (CDIFF, coarse_diff.reshape(1, COARSE)),
            (MAP, species_map.reshape(1, SPECIES)),
        )
    )
    wf, wr, wfr, lv, wc, pro, d12, dc12, share = call(
        prep_kernel,
        "prep",
        [bf16(2 * SP, 256), bf16(128, 256), bf16(2 * SP + 128, 256), bf16(80, 128), bf16(2 * CP, 128), bf16(SP, 96)]
        + [field(SP), field(CP), field(CP)],
        raw,
    )
    outer, inner = call(first_kernel, "first", [message, message], nodes, wc)
    uo, ui = swap(outer, inner)

    n1, s, r0, e0, c0 = call(
        old_kernel,
        "old",
        [fine, fine, coarse, coarse, coarse],
        *(nodes, wf, wr, wc, d12, dc12),
        scratch=[field(4, 3, SP), field(ROWS + 4, SP), field(ROWS + 4, SP), field(ROWS + 4, CP), field(ROWS + 4, CP)],
    )
    two, twelve, eight = field(2, SP), field(12, CP), field(8, CP)
    n1, s, r0, e0, outer, inner = call(
        old_edge_kernel,
        "old_edge",
        [fine, fine, coarse, coarse, two, two],
        *(uo, ui, lv, d12, dc12, n1, s, r0, e0),
        alias={5: 0, 6: 1, 7: 2, 8: 3},
    )
    no, ni = swap(outer, inner)
    n2, r1, e1, c1 = call(
        mid_kernel, "mid", [fine, coarse, coarse, coarse], n1, s, wfr, wc, d12, dc12, scratch=[field(ROWS + 4, SP), field(ROWS + 4, CP), field(ROWS + 4, CP)]
    )
    extended, short = field(EXT_ROWS, CP), field(AB_ROWS, CP)
    n2, r1, e1, abx, c2, outer, inner = call(
        mid_edge_kernel,
        "mid_edge",
        [fine, coarse, coarse, extended, coarse, twelve, twelve],
        *(no, ni, lv, wr, d12, dc12, r0, e0, c0, n2, r1, e1),
        alias={9: 0, 10: 1, 11: 2},
        scratch=[field(ROWS + 4, CP), coarse],
    )
    ho, hi = swap(outer, inner)
    b1, b2 = call(base_kernel, "base", [field(SPECIES, ROWS)] * 2, n1, n2, c1, c2, pro, share)
    abx, ab = call(last_edge_kernel, "last_edge", [extended, short], outer, inner, ho, hi, abx, alias={4: 0})

    forward = [(both(p), both(p + 1), SAME) for p in range(SLICES - 1)]
    b0 = moved(b2, *forward[1:])
    ab, abx = after(ab, b1), after(abx, b1)
    result = field(3 * ROWS, CP)
    pairs = [(slices, hosts) for slices, hosts in GROUPS if len(slices) == 2]
    short, long, back = [], [], []
    for slices, hosts in pairs:
        for core, host in enumerate(hosts):
            slabs = [(t, t) for t in range(core, SLABS, 2)]
            if host != slices[0]:
                long.append((both(slices[0]), both(host), slabs))
            if host != slices[1]:
                short.append((both(slices[1]), both(host), slabs))
            back.append((both(host), both(slices[0] if host == slices[1] else slices[1]), slabs))
    short, long = moved(ab, *short), moved(abx, *long)
    home, away, *sent = call(
        functools.partial(start_kernel, GROUPS[0][1]), "start", [result, result, coarse, eight, eight], ab, wc, dc12
    )
    for at, (slices, hosts) in enumerate(GROUPS[1:], 1):
        if at > 1:
            z = hop(*sent, GROUPS[at - 1][1], hosts)
        if at == 1:
            zo, zm = lax.optimization_barrier(
                (moved(sent[1], (both(0), hosts, OUTER)), moved(sent[0], (both(0), hosts, SAME)))
            )
            zi = moved(call(inner_kernel, "inner", eight, zm), (hosts, hosts, INNER))
            z = [zm, zo, zi]
        elif at == 2:
            *z, b0 = lax.optimization_barrier((*z, b0))
            late = moved(after(b2, z[0]), forward[0])
        elif at == 3:
            *z, late, home, away = lax.optimization_barrier((*z, late, home, away))
        else:
            other = moved(away, *back)
            *z, other, home = lax.optimization_barrier((*z, other, home))
        if len(slices) == 2:
            depth = 4 * len(GROUPS[at + 1][0])
            *sent, za, zb, zc = call(
                functools.partial(pair_kernel, slices, hosts, depth),
                "pair",
                [coarse, field(depth, CP), field(depth, CP), field(ROWS + 12, CP), field(ROWS + 8, CP), field(ROWS + 4, CP)],
                *(*z, abx, short, long, wc, dc12),
                scratch=[field(ROWS + 16, CP)],
            )
            home, away = call(
                functools.partial(gather_kernel, slices, hosts),
                "gather",
                [result, result],
                *(z[0], za, zb, zc, sent[0], home, away),
                alias={5: 0, 6: 1},
            )
    out = call(
        out_kernel,
        "out",
        field(3, SPECIES, ROWS),
        *(species_map[:, 0], nodes, b0, late, b1, b2, share, *z, ab, wc, dc12, home, other),
        out_specs=ANY,
        scratch=[result, field(ROWS + 4, CP), field(ROWS + 8, CP), field(3, CP, ROWS), field(3, SPECIES, ROWS), pltpu.SemaphoreType.DMA((3,))],
    )
    return out[None]


def solution(mesh):
    in_specs = (P("tm", None, None, "space", None), P(), P(), P(), P(), P(), P(), P())
    out_specs = P("tm", None, None, "space", None)
    return jax.shard_map(local, mesh=mesh, in_specs=in_specs, out_specs=out_specs, check_vma=False)
```

```python
import functools

import jax
import jax.numpy as jnp
from jax import lax
from jax.experimental import pallas as pl
from jax.experimental.pallas import tpu as pltpu
from jax.sharding import PartitionSpec as P

SPECIES, COARSE = 53, 21
SP, CP = 56, 24
ROWS, COLS = 16, 256
SLICES, SLABS = 8, 16
STEP, HALF, RELAX = 0.1, 0.05, 3.0
W0 = (5.0 / 24.0, 1.0 / 3.0, -1.0 / 24.0)
W1 = (-1.0 / 24.0, 1.0 / 3.0, 5.0 / 24.0)
F32, BF16 = jnp.float32, jnp.bfloat16
GROUPS = (((0,), (0, 0)), ((1, 2), (1, 5)), ((3, 4), (3, 4)), ((5, 6), (5, 6)), ((7,), (7, 7)))
VMEM_LIMIT = 24 * 1024 * 1024


def split(x):
    hi = x.astype(BF16)
    lo = (x - hi.astype(F32)).astype(BF16)
    return jnp.concatenate([hi, lo], axis=0)


def thirds(x):
    hi = x.astype(BF16)
    rest = x - hi.astype(F32)
    mid = rest.astype(BF16)
    return jnp.concatenate([hi, mid, (rest - mid.astype(F32)).astype(BF16)], axis=0)


def zeros(rows):
    return jnp.zeros((rows, COLS), F32)


def dot(w, x):
    return jnp.dot(w, x, preferred_element_type=F32)


def stacked(x, squares):
    return split(jnp.concatenate([x, squares, zeros(16)], axis=0))


def lap_y(x):
    near = pltpu.roll(x, 1, 1) + pltpu.roll(x, COLS - 1, 1)
    far = pltpu.roll(x, 2, 1) + pltpu.roll(x, COLS - 2, 1)
    return 16.0 * near - far - 60.0 * x


def lap_rows(ref, x):
    return 16.0 * (ref[x - 1] + ref[x + 1]) - (ref[x - 2] + ref[x + 2])


def beside(near, far):
    return 16.0 * near - far, -near


RATES, PAIRS, CRATES, CPAIRS, DIFF, CDIFF, MAP, RAW = 0, 56, 112, 136, 160, 161, 162, 168


def prep_kernel(raw, wf, wr, wfr, lv, wc, pro, d12, dc12, share):
    row = lax.broadcasted_iota(jnp.int32, (SP, 128), 0)
    lane = lax.broadcasted_iota(jnp.int32, (SP, 128), 1)

    def halves(x):
        hi = x.astype(BF16).astype(F32)
        return hi, (x - hi).astype(BF16).astype(F32)

    def column(values, height):
        return jnp.sum(jnp.where(row == lane, values, 0.0), axis=1, keepdims=True)[:height]

    eye = jnp.where(row == lane, RELAX, 0.0)
    fine = raw[RATES : RATES + SP, :] - jnp.where(row < SPECIES, eye, 0.0)
    fine = fine + pltpu.roll(raw[PAIRS : PAIRS + SP, :], SP, 1)
    coarse = raw[CRATES : CRATES + CP, :] - jnp.where(row < COARSE, eye, 0.0)[:CP]
    coarse = coarse + pltpu.roll(raw[CPAIRS : CPAIRS + CP, :], CP, 1)
    vectors = raw[DIFF : DIFF + 8, :]
    diff_row = vectors[0:1]
    d12[...] = jnp.broadcast_to(column(diff_row, SP) / 12.0, (SP, COLS))
    dc12[...] = jnp.broadcast_to(column(vectors[1:2], CP) / 12.0, (CP, COLS))
    map_row = jnp.where(lane[0:1] < SPECIES, vectors[2:3].astype(jnp.int32), -1)
    map_column = jnp.sum(jnp.where(row == lane, map_row, 0), axis=1, keepdims=True)
    map_column = jnp.where(row[:, 0:1] < SPECIES, map_column, -1)
    lum = jnp.where((map_row == row[:CP]) & (lane[:CP] < SPECIES), 1.0, 0.0)
    counts = jnp.sum(lum, axis=1, keepdims=True)
    share[...] = jnp.broadcast_to(1.0 / jnp.maximum(counts, 1.0), (CP, COLS))
    lumped = jnp.dot(lum[:, :SP], fine, precision=lax.Precision.HIGHEST, preferred_element_type=F32)
    fh, fl = halves(fine)
    rh, rl = halves(lumped)
    dh, dl = halves(lum * diff_row)
    ch, cl = halves(coarse)
    f = jnp.concatenate([fh, fl], axis=0).astype(BF16)
    r = jnp.concatenate([rh, rl, lum, dh, dl, jnp.zeros((8, 128), F32)], axis=0).astype(BF16)
    for at in (0, 128):
        wf[:, at : at + 128] = f
        wr[:, at : at + 128] = r
        wfr[: 2 * SP, at : at + 128] = f
        wfr[2 * SP :, at : at + 128] = r
    v = jnp.concatenate([lum, dh, dl, jnp.zeros((8, 128), F32)], axis=0)
    lv[...] = (v + pltpu.roll(v, 64, 1)).astype(BF16)
    c = jnp.concatenate([ch, cl], axis=0)
    wc[...] = (c + pltpu.roll(c, 64, 1)).astype(BF16)
    lane96 = lax.broadcasted_iota(jnp.int32, (SP, 96), 1)
    pro[...] = jnp.where(map_column == lane96 % 32, 1.0, 0.0).astype(BF16)


class Position:
    def __init__(self):
        self.slice_at, self.slab = lax.axis_index("tm"), lax.axis_index("space")

    def __getitem__(self, at):
        return (self.slab % 2, self.slice_at, self.slab)[at]


def blocks(rows, body, size=4):
    @pl.loop(0, rows // size)
    def _(i):
        body([size * i + k for k in range(size)])


def first_kernel(u, weights_made, outer, inner):
    info = Position()
    at_top = info[0] == 0
    for m in range(3):
        for r in range(2):
            first, last = u[m, :, r, :], u[m, :, ROWS - 2 + r, :]
            for out, value in ((outer, jnp.where(at_top, first, last)), (inner, jnp.where(at_top, last, first))):
                out[m, r, SP - 8 :, :] = zeros(8)
                out[m, r, :SPECIES, :] = value


def restricted(y):
    return y[0:24] + y[24:48], y[48:72], y[72:96] + y[96:120]


MIX0 = [STEP * w for w in W0]
MIXS = [STEP * W1[0], STEP * W1[1] - HALF, STEP * W1[2]]


def mixed(factors, values):
    return factors[0] * values[0] + factors[1] * values[1] + factors[2] * values[2]


def old_kernel(u, wf, wr, wc, d12, dc12, n1, s, r0, e0, c0, ut, p0s, pss, v0s, c0s):
    for k in range(4):
        for m in range(3):
            ut[k, m, SP - 8 :, :] = zeros(8)
    for x in (0, 1, ROWS + 2, ROWS + 3):
        p0s[x], pss[x], v0s[x], c0s[x] = zeros(SP), zeros(SP), zeros(CP), zeros(CP)

    def terms(xs):
        for k, x in enumerate(xs):
            for m in range(3):
                ut[k, m, :SPECIES, :] = u[m, :, x, :]
        for k, x in enumerate(xs):
            us = [ut[k, m] for m in range(3)]
            qs = [v * v for v in us]
            p0, ps = mixed(MIX0, us), mixed(MIXS, us)
            y = dot(wf[...], stacked(p0, mixed(MIX0, qs)))
            n1[x] = us[0] + (y[:SP] + y[SP:]) + d12[...] * lap_y(p0)
            y = dot(wf[...], stacked(ps, mixed(MIXS, qs)))
            s[x] = (y[:SP] + y[SP:]) + d12[...] * lap_y(ps)
            r, c, v = restricted(dot(wr[...], stacked(us[0], qs[0])))
            r0[x] = r + lap_y(v) * (1.0 / 12.0)
            y = dot(wc[...], stacked(c, c * c))
            e0[x] = (y[:CP] + y[CP:]) + dc12[...] * lap_y(c)
            p0s[x + 2], pss[x + 2], v0s[x + 2], c0s[x + 2], c0[x] = p0, ps, v, c, c

    blocks(ROWS, terms)

    def laps(xs):
        for x in xs:
            n1[x] += d12[...] * lap_rows(p0s, x + 2)
            s[x] += d12[...] * lap_rows(pss, x + 2)
            r0[x] += lap_rows(v0s, x + 2) * (1.0 / 12.0)
            e0[x] += dc12[...] * lap_rows(c0s, x + 2)

    blocks(ROWS, laps)


def lumped_halo(lv, row):
    y = dot(lv[...], split(jnp.concatenate([row, zeros(8)], axis=0)))
    return y[0:24], y[24:48] + y[48:72]


SIDES = (((0, 1), (1, 0)), ((ROWS - 1, ROWS - 2), (0, 1)))


def pick_halo(info, side, outer, inner):
    take = info[0] == side
    return lambda *at: jnp.where(take, outer[at], inner[at])


def send(info, outer, inner, tops, bottoms):
    at_top = info[0] == 0
    for r, (top, bottom) in enumerate(zip(tops, bottoms)):
        outer[r] = jnp.where(at_top, top, bottom)
        inner[r] = jnp.where(at_top, bottom, top)


def old_edge_kernel(uo, ui, lv, d12, dc12, n1i, si, r0i, e0i, n1, s, r0, e0, outer, inner):
    info = Position()
    for side, (rows, order) in enumerate(SIDES):
        halo = pick_halo(info, side, uo, ui)
        us = [[halo(m, r) for m in range(3)] for r in order]
        p0 = beside(*[mixed(MIX0, v) for v in us])
        ps = beside(*[mixed(MIXS, v) for v in us])
        lumped = [lumped_halo(lv, v[0]) for v in us]
        c = beside(lumped[0][0], lumped[1][0])
        v = beside(lumped[0][1], lumped[1][1])
        for i, x in enumerate(rows):
            n1[x] = n1i[x] + d12[...] * p0[i]
            s[x] = si[x] + d12[...] * ps[i]
            r0[x] = r0i[x] + v[i] * (1.0 / 12.0)
            e0[x] = e0i[x] + dc12[...] * c[i]
    send(info, outer, inner, [n1[0], n1[1]], [n1[ROWS - 2], n1[ROWS - 1]])


def mid_kernel(n1, s, wfr, wc, d12, dc12, n2, r1, e1, c1, n1s, v1s, c1s):
    for x in (0, 1, ROWS + 2, ROWS + 3):
        n1s[x], v1s[x], c1s[x] = zeros(SP), zeros(CP), zeros(CP)

    def terms(xs):
        for x in xs:
            n = n1[x]
            y = dot(wfr[...], stacked(n, n * n))
            n2[x] = n + HALF * ((y[:SP] + y[SP : 2 * SP]) + d12[...] * lap_y(n)) + s[x]
            r, c, v = restricted(y[2 * SP :])
            r1[x] = r + lap_y(v) * (1.0 / 12.0)
            y = dot(wc[...], stacked(c, c * c))
            e1[x] = (y[:CP] + y[CP:]) + dc12[...] * lap_y(c)
            n1s[x + 2], v1s[x + 2], c1s[x + 2], c1[x] = n, v, c, c

    blocks(ROWS, terms)

    def laps(xs):
        for x in xs:
            n2[x] += (HALF * d12[...]) * lap_rows(n1s, x + 2)
            r1[x] += lap_rows(v1s, x + 2) * (1.0 / 12.0)
            e1[x] += dc12[...] * lap_rows(c1s, x + 2)

    blocks(ROWS, laps)


def lumped_old(first, c0, e0):
    return jnp.where(first, c0, -HALF * e0)


AB_ROWS, EXT_ROWS = 2 * ROWS + 4, 2 * ROWS + 20
A0, B0 = 2, ROWS + 4
XA0, XB0 = 6, ROWS + 16


def mid_edge_kernel(no, ni, lv, wr, d12, dc12, r0, e0, c0, n2i, r1i, e1i, n2, r1, e1, ab, c2, outer, inner, v2s, gs):
    info = Position()
    first = info[1] == 0
    for side, (rows, order) in enumerate(SIDES):
        halo = pick_halo(info, side, no, ni)
        ns = [halo(r) for r in order]
        lumped = [lumped_halo(lv, v) for v in ns]
        c = beside(lumped[0][0], lumped[1][0])
        v = beside(lumped[0][1], lumped[1][1])
        n = beside(*ns)
        for i, x in enumerate(rows):
            n2[x] = n2i[x] + (HALF * d12[...]) * n[i]
            r1[x] = r1i[x] + v[i] * (1.0 / 12.0)
            e1[x] = e1i[x] + dc12[...] * c[i]
    for x in (0, 1, ROWS + 2, ROWS + 3):
        v2s[x] = zeros(CP)

    def lumped(x, value):
        gs[x], c2[x], v2s[x + 2] = restricted(dot(wr[...], stacked(value, value * value)))

    def pieces(x, mid, late):
        v = v2s[x + 2]
        g2 = gs[x] + (lap_y(v) + lap_rows(v2s, x + 2)) * (1.0 / 12.0)
        ab[x + XA0] = mixed(MIX0, (r0[x], mid, g2)) + lumped_old(first, c0[x], e0[x])
        ab[x + XB0] = mixed([STEP * w for w in W1], (r0[x], mid, g2)) - HALF * late

    edges = (0, 1, ROWS - 2, ROWS - 1)
    for x in edges:
        lumped(x, n2[x])
    blocks(ROWS - 4, lambda xs: [lumped(x + 2, n2i[x + 2]) for x in xs], ROWS - 4)
    for x in edges:
        pieces(x, r1[x], e1[x])
    blocks(ROWS - 4, lambda xs: [pieces(x + 2, r1i[x + 2], e1i[x + 2]) for x in xs], ROWS - 4)
    top = [ab[x + XA0] for x in range(6)] + [ab[x + XB0] for x in range(4)] + [v2s[x + 2] for x in range(2)]
    bottom = [ab[x + XA0] for x in range(ROWS - 6, ROWS)] + [ab[x + XB0] for x in range(ROWS - 4, ROWS)]
    send(info, outer, inner, top, bottom + [v2s[x] for x in range(ROWS, ROWS + 2)])


def last_edge_kernel(mo, mi, ho, hi, abi, ab, short):
    info = Position()
    ka, kb = STEP * W0[2] / 12.0, STEP * W1[2] / 12.0
    done = {}
    for side, (rows, order) in enumerate(SIDES):
        inside = info[2] > 0 if side == 0 else info[2] < SLABS - 1
        own, halo = pick_halo(info, side, mo, mi), pick_halo(info, side, ho, hi)
        fix = beside(*[halo(10 + r) for r in order])
        theirs = beside(*[own(10 + r) for r in order[::-1]])
        for i, x in enumerate(rows):
            done[x + XA0] = abi[x + XA0] + ka * fix[i]
            done[x + XB0] = abi[x + XB0] + kb * fix[i]
        for depth, at, to, factor in ((6, 0, XA0, ka), (4, 6, XB0, kb)):
            for i in range(depth):
                x = -1 - i if side == 0 else ROWS + i
                value = halo(at + (depth - 1 - i if side == 0 else i))
                if i < 2:
                    value = value + factor * theirs[i]
                done[x + to] = jnp.where(inside, value, 0.0)
    for at, value in done.items():
        ab[at] = value
    for x in range(-2, ROWS + 2):
        short[x + A0] = done[x + XA0] if x + XA0 in done else abi[x + XA0]
    for x in range(ROWS):
        short[x + B0] = done[x + XB0] if x + XB0 in done else abi[x + XB0]


def sweep(info, z, z0, add, add0, out, out0, low, rows, wc, dc12):
    size = rows // 2

    def body(xs):
        zr = [z[xs[0] + (low + z0 + k)] for k in range(-2, size + 2)]
        for k in range(size):
            x, value = xs[k] + low, zr[k + 2]
            y = dot(wc[...], stacked(value, value * value))
            lap = lap_y(value) + 16.0 * (zr[k + 1] + zr[k + 3]) - (zr[k] + zr[k + 4])
            value = value + HALF * ((y[:CP] + y[CP:]) + dc12[...] * lap) + add[x + add0]
            if low < 0:
                inside = ((x >= 0) | (info[2] > 0)) & ((x < ROWS) | (info[2] < SLABS - 1))
                value = jnp.where(inside, value, 0.0)
            out[x + out0] = value

    blocks(rows, body, size)


def begin(info, z0, zo, zi, depth, zs):
    top, bottom = pick_halo(info, 0, zo, zi), pick_halo(info, 1, zo, zi)
    for r in range(depth):
        zs[r], zs[depth + ROWS + r] = top(r), bottom(r)

    def body(xs):
        for x in xs:
            zs[depth + x] = z0[x]

    blocks(ROWS, body)


def give(info, depth, outer, inner, value):
    send(info, outer, inner, [value(x) for x in range(depth)], [value(x) for x in range(ROWS - depth, ROWS)])


def hosting(info, hosts):
    return info[1] == jnp.where(info[0] == 0, hosts[0], hosts[1])


def start_kernel(hosts, ab, wc, dc12, result, unused, message, outer, inner):
    info = Position()

    @pl.when(hosting(info, hosts))
    def _():
        sweep(info, ab, A0, ab, B0, message, 0, 0, ROWS, wc, dc12)
        give(info, 8, outer, inner, lambda x: message[x])

        def body(xs):
            for x in xs:
                result[x], result[ROWS + x], result[2 * ROWS + x] = zeros(CP), ab[x + A0], message[x]

        blocks(ROWS, body)


def pair_kernel(
    slices, hosts, depth, z0, zo, zi, mine, short, long, wc, dc12, message, outer, inner, za, zb, zc, zs
):
    info = Position()

    def sweeps(one, two):
        begin(info, z0, zo, zi, 8, zs)
        sweep(info, zs, 8, one, XA0, za, 6, -6, ROWS + 12, wc, dc12)
        sweep(info, za, 6, one, XB0, zb, 4, -4, ROWS + 8, wc, dc12)
        if two is mine:
            sweep(info, zb, 4, two, XA0, zc, 2, -2, ROWS + 4, wc, dc12)
            sweep(info, zc, 2, two, XB0, message, 0, 0, ROWS, wc, dc12)
        else:
            sweep(info, zb, 4, two, A0, zc, 2, -2, ROWS + 4, wc, dc12)
            sweep(info, zc, 2, two, B0, message, 0, 0, ROWS, wc, dc12)
        give(info, depth, outer, inner, lambda x: message[x])

    for host in sorted(set(hosts)):
        one = mine if host == slices[0] else long
        two = mine if host == slices[1] else short
        pl.when(hosting(info, hosts) & (info[1] == host))(functools.partial(sweeps, one, two))


def gather(z0, za, zb, zc, z2, one, two):
    def body(xs):
        for x in xs:
            one[x], one[ROWS + x], one[2 * ROWS + x] = z0[x], za[x + 6], zb[x + 4]
            two[x], two[ROWS + x], two[2 * ROWS + x] = zb[x + 4], zc[x + 2], z2[x]

    blocks(ROWS, body)


def gather_kernel(slices, hosts, z0, za, zb, zc, z2, home_in, away_in, home, away):
    info = Position()
    active, second = hosting(info, hosts), info[1] == slices[1]
    pl.when(active & ~second)(lambda: gather(z0, za, zb, zc, z2, home, away))
    pl.when(active & second)(lambda: gather(z0, za, zb, zc, z2, away, home))


def base_kernel(n1, n2, c1, c2, pro, share, b1, b2):
    def body(xs):
        for x in xs:
            for n, c, b in ((n1, c1, b1), (n2, c2, b2)):
                value = thirds(jnp.concatenate([share[...] * c[x], zeros(8)], axis=0))
                b[:, x, :] = (n[x] - dot(pro[...], value))[:SPECIES]

    blocks(ROWS, body)


def out_kernel(
    where, u, b0, late, b1, b2, share, z0, zo, zi, ab, wc, dc12, home, one, other, out, z, za, zs, spread, node, sem
):
    info = Position()
    last = info[1] == SLICES - 1
    at_home = hosting(info, GROUPS[0][1])
    for slices, hosts in GROUPS[1:-1]:
        at_home = at_home | (hosting(info, hosts) & ((info[1] == slices[0]) | (info[1] == slices[1])))
    first = info[1] == GROUPS[1][0][0]
    for here, result in ((at_home, home), (first & ~at_home, one), (~at_home & ~first & ~last, other)):

        @pl.when(here)
        def _():

            def body(xs):
                for x in xs:
                    z[x] = result[x]

            blocks(3 * ROWS, body)

    @pl.when(last)
    def _():
        begin(info, z0, zo, zi, 4, zs)

        def body(xs):
            for x in xs:
                z[x] = z0[x]

        blocks(ROWS, body)

    def finish(m, base):
        def body(xs):
            for x in xs:
                spread[m, :, x, :] = share[...] * z[m * ROWS + x]

        blocks(ROWS, body, ROWS)

        def add(s):
            node[m, s] = base(s) + spread[m, where[s]]

        blocks(SPECIES, lambda at: [add(s) for s in at], 13)
        add(SPECIES - 1)
        copy = pltpu.make_async_copy(node.at[m], out.at[m], sem.at[m])
        copy.start()
        return copy

    first = info[1] == 0
    copies = [finish(0, lambda s: jnp.where(first, u[0, s], b0[s] + late[s]))]

    @pl.when(last)
    def _():
        sweep(info, zs, 4, ab, A0, za, 2, -2, ROWS + 4, wc, dc12)
        sweep(info, za, 2, ab, B0, z.at[pl.ds(2 * ROWS, ROWS)], 0, 0, ROWS, wc, dc12)

        def body(xs):
            for x in xs:
                z[ROWS + x] = za[x + 2]

        blocks(ROWS, body)

    copies += [finish(1, lambda s: b1[s]), finish(2, lambda s: b2[s])]
    for copy in copies:
        copy.wait()


def field(*shape):
    return jax.ShapeDtypeStruct(shape + (COLS,), F32)


SMEM = pl.BlockSpec(memory_space=pltpu.SMEM)
VMEM = pl.BlockSpec(memory_space=pltpu.VMEM)
ANY = pl.BlockSpec(memory_space=pl.ANY)


def call(kernel, name, outs, *args, scratch=(), alias=None, out_specs=None, specs=None):
    specs = specs or [SMEM if a.dtype == jnp.int32 and a.ndim == 1 else VMEM for a in args]
    return pl.pallas_call(
        kernel,
        out_shape=outs,
        in_specs=specs,
        **({"out_specs": out_specs} if out_specs else {}),
        scratch_shapes=[pltpu.VMEM(f.shape, f.dtype) if isinstance(f, jax.ShapeDtypeStruct) else f for f in scratch],
        input_output_aliases=alias or {},
        compiler_params=pltpu.CompilerParams(vmem_limit_bytes=VMEM_LIMIT),
        name=name,
    )(*args)


AXES = ("tm", "space")
OUTER = [(s, s + 1) for s in range(1, SLABS - 1, 2)] + [(s + 1, s) for s in range(1, SLABS - 1, 2)]
INNER = [(s, s ^ 1) for s in range(SLABS)]
SAME = [(s, s) for s in range(SLABS)]


def moved(value, *routes):
    pairs = [
        (source[s % 2] * SLABS + s, target[t % 2] * SLABS + t) for source, target, slabs in routes for s, t in slabs
    ]
    return lax.ppermute(value, AXES, pairs)


def both(p):
    return (p, p)


def swap(outer, inner):
    got_inner = moved(inner, *[(both(p), both(p), INNER) for p in range(SLICES)])
    got_outer = moved(outer, *[(both(p), both(p), OUTER) for p in range(SLICES)])
    return got_outer, got_inner


def hop(message, outer, inner, source, target):
    parts = ((outer, OUTER), (inner, INNER), (message, SAME))
    zo, zi, z = [moved(value, (source, target, slabs)) for value, slabs in parts]
    return [z, zo, zi]


def after(value, other):
    return lax.optimization_barrier((value, other))[0]


def local(fine_nodes, fine_rates, fine_pairs, fine_diff, coarse_rates, coarse_pairs, coarse_diff, species_map):
    nodes = fine_nodes[0]
    fine, coarse = field(ROWS, SP), field(ROWS, CP)
    message = field(3, 2, SP)
    def bf16(*shape):
        return jax.ShapeDtypeStruct(shape, BF16)

    raw = sum(
        jnp.pad(v.astype(F32), ((at, RAW - at - v.shape[0]), (0, 128 - v.shape[1])))
        for at, v in (
            (RATES, fine_rates),
            (PAIRS, fine_pairs),
            (CRATES, coarse_rates),
            (CPAIRS, coarse_pairs),
            (DIFF, fine_diff.reshape(1, SPECIES)),
            (CDIFF, coarse_diff.reshape(1, COARSE)),
            (MAP, species_map.reshape(1, SPECIES)),
        )
    )
    wf, wr, wfr, lv, wc, pro, d12, dc12, share = call(
        prep_kernel,
        "prep",
        [bf16(2 * SP, 256), bf16(128, 256), bf16(2 * SP + 128, 256), bf16(80, 128), bf16(2 * CP, 128), bf16(SP, 96)]
        + [field(SP), field(CP), field(CP)],
        raw,
    )
    outer, inner = call(first_kernel, "first", [message, message], nodes, wc)
    uo, ui = swap(outer, inner)

    n1, s, r0, e0, c0 = call(
        old_kernel,
        "old",
        [fine, fine, coarse, coarse, coarse],
        *(nodes, wf, wr, wc, d12, dc12),
        scratch=[field(4, 3, SP), field(ROWS + 4, SP), field(ROWS + 4, SP), field(ROWS + 4, CP), field(ROWS + 4, CP)],
    )
    two, twelve, eight = field(2, SP), field(12, CP), field(8, CP)
    n1, s, r0, e0, outer, inner = call(
        old_edge_kernel,
        "old_edge",
        [fine, fine, coarse, coarse, two, two],
        *(uo, ui, lv, d12, dc12, n1, s, r0, e0),
        alias={5: 0, 6: 1, 7: 2, 8: 3},
    )
    no, ni = swap(outer, inner)
    n2, r1, e1, c1 = call(
        mid_kernel, "mid", [fine, coarse, coarse, coarse], n1, s, wfr, wc, d12, dc12, scratch=[field(ROWS + 4, SP), field(ROWS + 4, CP), field(ROWS + 4, CP)]
    )
    extended, short = field(EXT_ROWS, CP), field(AB_ROWS, CP)
    n2, r1, e1, abx, c2, outer, inner = call(
        mid_edge_kernel,
        "mid_edge",
        [fine, coarse, coarse, extended, coarse, twelve, twelve],
        *(no, ni, lv, wr, d12, dc12, r0, e0, c0, n2, r1, e1),
        alias={9: 0, 10: 1, 11: 2},
        scratch=[field(ROWS + 4, CP), coarse],
    )
    ho, hi = swap(outer, inner)
    b1, b2 = call(base_kernel, "base", [field(SPECIES, ROWS)] * 2, n1, n2, c1, c2, pro, share)
    abx, ab = call(last_edge_kernel, "last_edge", [extended, short], outer, inner, ho, hi, abx, alias={4: 0})

    ab, abx = after(ab, b1), after(abx, b1)
    result = field(3 * ROWS, CP)
    pairs = [(slices, hosts) for slices, hosts in GROUPS if len(slices) == 2]
    short, long, back, first = [], [], [], []
    for slices, hosts in pairs:
        for core, host in enumerate(hosts):
            slabs = [(t, t) for t in range(core, SLABS, 2)]
            if host != slices[0]:
                long.append((both(slices[0]), both(host), slabs))
            if host != slices[1]:
                short.append((both(slices[1]), both(host), slabs))
            back.append((both(host), both(slices[0] if host == slices[1] else slices[1]), slabs))
            if host not in slices:
                first.append((both(host), both(slices[0]), slabs))
    short, long = moved(ab, *short), moved(abx, *long)
    forward = [(both(p), both(p + 1), SAME) for p in range(SLICES - 1)]
    home, away, *sent = call(
        functools.partial(start_kernel, GROUPS[0][1]), "start", [result, result, coarse, eight, eight], ab, wc, dc12
    )
    for at, (slices, hosts) in enumerate(GROUPS[1:], 1):
        z = hop(*sent, GROUPS[at - 1][1], hosts)
        if at == 1:
            z = list(lax.optimization_barrier(tuple(z)))
            b0 = moved(after(b2, z[0]), forward[2], forward[6])
            *z, short, long = lax.optimization_barrier((*z, short, long))
            late = moved(after(b2, z[0]), *forward[:2], *forward[3:6])
        elif at == 2:
            *z, b0 = lax.optimization_barrier((*z, b0))
        elif at == 3:
            *z, late, home, away = lax.optimization_barrier((*z, late, home, away))
        else:
            other, one = moved(away, *back), moved(home, *first)
            *z, other, one, home = lax.optimization_barrier((*z, other, one, home))
        if len(slices) == 2:
            depth = 4 * len(GROUPS[at + 1][0])
            *sent, za, zb, zc = call(
                functools.partial(pair_kernel, slices, hosts, depth),
                "pair",
                [coarse, field(depth, CP), field(depth, CP), field(ROWS + 12, CP), field(ROWS + 8, CP), field(ROWS + 4, CP)],
                *(*z, abx, short, long, wc, dc12),
                scratch=[field(ROWS + 16, CP)],
            )
            home, away = call(
                functools.partial(gather_kernel, slices, hosts),
                "gather",
                [result, result],
                *(z[0], za, zb, zc, sent[0], home, away),
                alias={5: 0, 6: 1},
            )
    out = call(
        out_kernel,
        "out",
        field(3, SPECIES, ROWS),
        *(species_map[:, 0], nodes, b0, late, b1, b2, share, *z, ab, wc, dc12, home, one, other),
        out_specs=ANY,
        scratch=[result, field(ROWS + 4, CP), field(ROWS + 8, CP), field(3, CP, ROWS), field(3, SPECIES, ROWS), pltpu.SemaphoreType.DMA((3,))],
    )
    return out[None]


def solution(mesh):
    in_specs = (P("tm", None, None, "space", None), P(), P(), P(), P(), P(), P(), P())
    out_specs = P("tm", None, None, "space", None)
    return jax.shard_map(local, mesh=mesh, in_specs=in_specs, out_specs=out_specs, check_vma=False)
```

```python
import functools

import jax
import jax.numpy as jnp
from jax import lax
from jax.experimental import pallas as pl
from jax.experimental.pallas import tpu as pltpu
from jax.sharding import PartitionSpec as P

SPECIES, COARSE = 53, 21
SP, CP = 56, 24
ROWS, COLS = 16, 256
SLICES, SLABS = 8, 16
STEP, HALF, RELAX = 0.1, 0.05, 3.0
W0 = (5.0 / 24.0, 1.0 / 3.0, -1.0 / 24.0)
W1 = (-1.0 / 24.0, 1.0 / 3.0, 5.0 / 24.0)
F32, BF16 = jnp.float32, jnp.bfloat16
GROUPS = (((0,), (0, 0)), ((1, 2), (1, 1)), ((3, 4), (3, 4)), ((5, 6), (5, 6)), ((7,), (7, 7)))
VMEM_LIMIT = 24 * 1024 * 1024


def split(x):
    hi = x.astype(BF16)
    lo = (x - hi.astype(F32)).astype(BF16)
    return jnp.concatenate([hi, lo], axis=0)


def thirds(x):
    hi = x.astype(BF16)
    rest = x - hi.astype(F32)
    mid = rest.astype(BF16)
    return jnp.concatenate([hi, mid, (rest - mid.astype(F32)).astype(BF16)], axis=0)


def zeros(rows):
    return jnp.zeros((rows, COLS), F32)


def dot(w, x):
    return jnp.dot(w, x, preferred_element_type=F32)


def stacked(x, squares):
    return split(jnp.concatenate([x, squares, zeros(16)], axis=0))


def lap_y(x):
    near = pltpu.roll(x, 1, 1) + pltpu.roll(x, COLS - 1, 1)
    far = pltpu.roll(x, 2, 1) + pltpu.roll(x, COLS - 2, 1)
    return 16.0 * near - far - 60.0 * x


def lap_rows(ref, x):
    return 16.0 * (ref[x - 1] + ref[x + 1]) - (ref[x - 2] + ref[x + 2])


def beside(near, far):
    return 16.0 * near - far, -near


RATES, PAIRS, CRATES, CPAIRS, DIFF, CDIFF, MAP, RAW = 0, 56, 112, 136, 160, 161, 162, 168


def prep_kernel(raw, wf, wr, wfr, lv, wc, pro, d12, dc12, share):
    row = lax.broadcasted_iota(jnp.int32, (SP, 128), 0)
    lane = lax.broadcasted_iota(jnp.int32, (SP, 128), 1)

    def halves(x):
        hi = x.astype(BF16).astype(F32)
        return hi, (x - hi).astype(BF16).astype(F32)

    def column(values, height):
        return jnp.sum(jnp.where(row == lane, values, 0.0), axis=1, keepdims=True)[:height]

    eye = jnp.where(row == lane, RELAX, 0.0)
    fine = raw[RATES : RATES + SP, :] - jnp.where(row < SPECIES, eye, 0.0)
    fine = fine + pltpu.roll(raw[PAIRS : PAIRS + SP, :], SP, 1)
    coarse = raw[CRATES : CRATES + CP, :] - jnp.where(row < COARSE, eye, 0.0)[:CP]
    coarse = coarse + pltpu.roll(raw[CPAIRS : CPAIRS + CP, :], CP, 1)
    vectors = raw[DIFF : DIFF + 8, :]
    diff_row = vectors[0:1]
    d12[...] = jnp.broadcast_to(column(diff_row, SP) / 12.0, (SP, COLS))
    dc12[...] = jnp.broadcast_to(column(vectors[1:2], CP) / 12.0, (CP, COLS))
    map_row = jnp.where(lane[0:1] < SPECIES, vectors[2:3].astype(jnp.int32), -1)
    map_column = jnp.sum(jnp.where(row == lane, map_row, 0), axis=1, keepdims=True)
    map_column = jnp.where(row[:, 0:1] < SPECIES, map_column, -1)
    lum = jnp.where((map_row == row[:CP]) & (lane[:CP] < SPECIES), 1.0, 0.0)
    counts = jnp.sum(lum, axis=1, keepdims=True)
    share[...] = jnp.broadcast_to(1.0 / jnp.maximum(counts, 1.0), (CP, COLS))
    lumped = jnp.dot(lum[:, :SP], fine, precision=lax.Precision.HIGHEST, preferred_element_type=F32)
    fh, fl = halves(fine)
    rh, rl = halves(lumped)
    dh, dl = halves(lum * diff_row)
    ch, cl = halves(coarse)
    f = jnp.concatenate([fh, fl], axis=0).astype(BF16)
    r = jnp.concatenate([rh, rl, lum, dh, dl, jnp.zeros((8, 128), F32)], axis=0).astype(BF16)
    for at in (0, 128):
        wf[:, at : at + 128] = f
        wr[:, at : at + 128] = r
        wfr[: 2 * SP, at : at + 128] = f
        wfr[2 * SP :, at : at + 128] = r
    v = jnp.concatenate([lum, dh, dl, jnp.zeros((8, 128), F32)], axis=0)
    lv[...] = (v + pltpu.roll(v, 64, 1)).astype(BF16)
    c = jnp.concatenate([ch, cl], axis=0)
    wc[...] = (c + pltpu.roll(c, 64, 1)).astype(BF16)
    lane96 = lax.broadcasted_iota(jnp.int32, (SP, 96), 1)
    pro[...] = jnp.where(map_column == lane96 % 32, 1.0, 0.0).astype(BF16)


class Position:
    def __init__(self):
        self.slice_at, self.slab = lax.axis_index("tm"), lax.axis_index("space")

    def __getitem__(self, at):
        return (self.slab % 2, self.slice_at, self.slab)[at]


def blocks(rows, body, size=4):
    @pl.loop(0, rows // size)
    def _(i):
        body([size * i + k for k in range(size)])


def first_kernel(u, weights_made, outer, inner):
    info = Position()
    at_top = info[0] == 0
    for m in range(3):
        for r in range(2):
            first, last = u[m, :, r, :], u[m, :, ROWS - 2 + r, :]
            for out, value in ((outer, jnp.where(at_top, first, last)), (inner, jnp.where(at_top, last, first))):
                out[m, r, SP - 8 :, :] = zeros(8)
                out[m, r, :SPECIES, :] = value


def restricted(y):
    return y[0:24] + y[24:48], y[48:72], y[72:96] + y[96:120]


MIX0 = [STEP * w for w in W0]
MIXS = [STEP * W1[0], STEP * W1[1] - HALF, STEP * W1[2]]


def mixed(factors, values):
    return factors[0] * values[0] + factors[1] * values[1] + factors[2] * values[2]


def old_kernel(u, wf, wr, wc, d12, dc12, n1, s, r0, e0, c0, ut, p0s, pss, v0s, c0s):
    for k in range(4):
        for m in range(3):
            ut[k, m, SP - 8 :, :] = zeros(8)
    for x in (0, 1, ROWS + 2, ROWS + 3):
        p0s[x], pss[x], v0s[x], c0s[x] = zeros(SP), zeros(SP), zeros(CP), zeros(CP)

    def terms(xs):
        for k, x in enumerate(xs):
            for m in range(3):
                ut[k, m, :SPECIES, :] = u[m, :, x, :]
        for k, x in enumerate(xs):
            us = [ut[k, m] for m in range(3)]
            qs = [v * v for v in us]
            p0, ps = mixed(MIX0, us), mixed(MIXS, us)
            y = dot(wf[...], stacked(p0, mixed(MIX0, qs)))
            n1[x] = us[0] + (y[:SP] + y[SP:]) + d12[...] * lap_y(p0)
            y = dot(wf[...], stacked(ps, mixed(MIXS, qs)))
            s[x] = (y[:SP] + y[SP:]) + d12[...] * lap_y(ps)
            r, c, v = restricted(dot(wr[...], stacked(us[0], qs[0])))
            r0[x] = r + lap_y(v) * (1.0 / 12.0)
            y = dot(wc[...], stacked(c, c * c))
            e0[x] = (y[:CP] + y[CP:]) + dc12[...] * lap_y(c)
            p0s[x + 2], pss[x + 2], v0s[x + 2], c0s[x + 2], c0[x] = p0, ps, v, c, c

    blocks(ROWS, terms)

    def laps(xs):
        for x in xs:
            n1[x] += d12[...] * lap_rows(p0s, x + 2)
            s[x] += d12[...] * lap_rows(pss, x + 2)
            r0[x] += lap_rows(v0s, x + 2) * (1.0 / 12.0)
            e0[x] += dc12[...] * lap_rows(c0s, x + 2)

    blocks(ROWS, laps)


def lumped_halo(lv, row):
    y = dot(lv[...], split(jnp.concatenate([row, zeros(8)], axis=0)))
    return y[0:24], y[24:48] + y[48:72]


SIDES = (((0, 1), (1, 0)), ((ROWS - 1, ROWS - 2), (0, 1)))


def pick_halo(info, side, outer, inner):
    take = info[0] == side
    return lambda *at: jnp.where(take, outer[at], inner[at])


def send(info, outer, inner, tops, bottoms):
    at_top = info[0] == 0
    for r, (top, bottom) in enumerate(zip(tops, bottoms)):
        outer[r] = jnp.where(at_top, top, bottom)
        inner[r] = jnp.where(at_top, bottom, top)


def old_edge_kernel(uo, ui, lv, d12, dc12, n1i, si, r0i, e0i, n1, s, r0, e0, outer, inner):
    info = Position()
    for side, (rows, order) in enumerate(SIDES):
        halo = pick_halo(info, side, uo, ui)
        us = [[halo(m, r) for m in range(3)] for r in order]
        p0 = beside(*[mixed(MIX0, v) for v in us])
        ps = beside(*[mixed(MIXS, v) for v in us])
        lumped = [lumped_halo(lv, v[0]) for v in us]
        c = beside(lumped[0][0], lumped[1][0])
        v = beside(lumped[0][1], lumped[1][1])
        for i, x in enumerate(rows):
            n1[x] = n1i[x] + d12[...] * p0[i]
            s[x] = si[x] + d12[...] * ps[i]
            r0[x] = r0i[x] + v[i] * (1.0 / 12.0)
            e0[x] = e0i[x] + dc12[...] * c[i]
    send(info, outer, inner, [n1[0], n1[1]], [n1[ROWS - 2], n1[ROWS - 1]])


def mid_kernel(n1, s, wfr, wc, d12, dc12, n2, r1, e1, c1, n1s, v1s, c1s):
    for x in (0, 1, ROWS + 2, ROWS + 3):
        n1s[x], v1s[x], c1s[x] = zeros(SP), zeros(CP), zeros(CP)

    def terms(xs):
        for x in xs:
            n = n1[x]
            y = dot(wfr[...], stacked(n, n * n))
            n2[x] = n + HALF * ((y[:SP] + y[SP : 2 * SP]) + d12[...] * lap_y(n)) + s[x]
            r, c, v = restricted(y[2 * SP :])
            r1[x] = r + lap_y(v) * (1.0 / 12.0)
            y = dot(wc[...], stacked(c, c * c))
            e1[x] = (y[:CP] + y[CP:]) + dc12[...] * lap_y(c)
            n1s[x + 2], v1s[x + 2], c1s[x + 2], c1[x] = n, v, c, c

    blocks(ROWS, terms, 8)

    def laps(xs):
        for x in xs:
            n2[x] += (HALF * d12[...]) * lap_rows(n1s, x + 2)
            r1[x] += lap_rows(v1s, x + 2) * (1.0 / 12.0)
            e1[x] += dc12[...] * lap_rows(c1s, x + 2)

    blocks(ROWS, laps, 8)


def lumped_old(first, c0, e0):
    return jnp.where(first, c0, -HALF * e0)


AB_ROWS, EXT_ROWS = 2 * ROWS + 4, 2 * ROWS + 20
A0, B0 = 2, ROWS + 4
XA0, XB0 = 6, ROWS + 16


def mid_edge_kernel(no, ni, lv, wr, d12, dc12, r0, e0, c0, n2i, r1i, e1i, n2, r1, e1, ab, c2, outer, inner, v2s, gs):
    info = Position()
    first = info[1] == 0
    for side, (rows, order) in enumerate(SIDES):
        halo = pick_halo(info, side, no, ni)
        ns = [halo(r) for r in order]
        lumped = [lumped_halo(lv, v) for v in ns]
        c = beside(lumped[0][0], lumped[1][0])
        v = beside(lumped[0][1], lumped[1][1])
        n = beside(*ns)
        for i, x in enumerate(rows):
            n2[x] = n2i[x] + (HALF * d12[...]) * n[i]
            r1[x] = r1i[x] + v[i] * (1.0 / 12.0)
            e1[x] = e1i[x] + dc12[...] * c[i]
    for x in (0, 1, ROWS + 2, ROWS + 3):
        v2s[x] = zeros(CP)

    def lumped(x, value):
        gs[x], c2[x], v2s[x + 2] = restricted(dot(wr[...], stacked(value, value * value)))

    def pieces(x, mid, late):
        v = v2s[x + 2]
        g2 = gs[x] + (lap_y(v) + lap_rows(v2s, x + 2)) * (1.0 / 12.0)
        ab[x + XA0] = mixed(MIX0, (r0[x], mid, g2)) + lumped_old(first, c0[x], e0[x])
        ab[x + XB0] = mixed([STEP * w for w in W1], (r0[x], mid, g2)) - HALF * late

    edges = (0, 1, ROWS - 2, ROWS - 1)
    for x in edges:
        lumped(x, n2[x])
    blocks(ROWS - 4, lambda xs: [lumped(x + 2, n2i[x + 2]) for x in xs], ROWS - 4)
    for x in edges:
        pieces(x, r1[x], e1[x])
    blocks(ROWS - 4, lambda xs: [pieces(x + 2, r1i[x + 2], e1i[x + 2]) for x in xs], ROWS - 4)
    top = [ab[x + XA0] for x in range(6)] + [ab[x + XB0] for x in range(4)] + [v2s[x + 2] for x in range(2)]
    bottom = [ab[x + XA0] for x in range(ROWS - 6, ROWS)] + [ab[x + XB0] for x in range(ROWS - 4, ROWS)]
    send(info, outer, inner, top, bottom + [v2s[x] for x in range(ROWS, ROWS + 2)])


def last_edge_kernel(mo, mi, ho, hi, abi, ab, short):
    info = Position()
    ka, kb = STEP * W0[2] / 12.0, STEP * W1[2] / 12.0
    done = {}
    for side, (rows, order) in enumerate(SIDES):
        inside = info[2] > 0 if side == 0 else info[2] < SLABS - 1
        own, halo = pick_halo(info, side, mo, mi), pick_halo(info, side, ho, hi)
        fix = beside(*[halo(10 + r) for r in order])
        theirs = beside(*[own(10 + r) for r in order[::-1]])
        for i, x in enumerate(rows):
            done[x + XA0] = abi[x + XA0] + ka * fix[i]
            done[x + XB0] = abi[x + XB0] + kb * fix[i]
        for depth, at, to, factor in ((6, 0, XA0, ka), (4, 6, XB0, kb)):
            for i in range(depth):
                x = -1 - i if side == 0 else ROWS + i
                value = halo(at + (depth - 1 - i if side == 0 else i))
                if i < 2:
                    value = value + factor * theirs[i]
                done[x + to] = jnp.where(inside, value, 0.0)
    for at, value in done.items():
        ab[at] = value
    for x in range(-2, ROWS + 2):
        short[x + A0] = done[x + XA0] if x + XA0 in done else abi[x + XA0]
    for x in range(ROWS):
        short[x + B0] = done[x + XB0] if x + XB0 in done else abi[x + XB0]


def sweep(info, z, z0, add, add0, out, out0, low, rows, wc, dc12):
    size = rows // 2

    def body(xs):
        zr = [z[xs[0] + (low + z0 + k)] for k in range(-2, size + 2)]
        for k in range(size):
            x, value = xs[k] + low, zr[k + 2]
            y = dot(wc[...], stacked(value, value * value))
            lap = lap_y(value) + 16.0 * (zr[k + 1] + zr[k + 3]) - (zr[k] + zr[k + 4])
            value = value + HALF * ((y[:CP] + y[CP:]) + dc12[...] * lap) + add[x + add0]
            if low < 0:
                inside = ((x >= 0) | (info[2] > 0)) & ((x < ROWS) | (info[2] < SLABS - 1))
                value = jnp.where(inside, value, 0.0)
            out[x + out0] = value

    blocks(rows, body, size)


def begin(info, z0, zo, zi, depth, zs):
    top, bottom = pick_halo(info, 0, zo, zi), pick_halo(info, 1, zo, zi)
    for r in range(depth):
        zs[r], zs[depth + ROWS + r] = top(r), bottom(r)

    def body(xs):
        for x in xs:
            zs[depth + x] = z0[x]

    blocks(ROWS, body)


def give(info, depth, outer, inner, value):
    send(info, outer, inner, [value(x) for x in range(depth)], [value(x) for x in range(ROWS - depth, ROWS)])


def hosting(info, hosts):
    return info[1] == jnp.where(info[0] == 0, hosts[0], hosts[1])


def start_kernel(hosts, ab, wc, dc12, result, unused, message, outer, inner):
    info = Position()

    @pl.when(hosting(info, hosts))
    def _():
        sweep(info, ab, A0, ab, B0, message, 0, 0, ROWS, wc, dc12)
        give(info, 8, outer, inner, lambda x: message[x])

        def body(xs):
            for x in xs:
                result[x], result[ROWS + x], result[2 * ROWS + x] = zeros(CP), ab[x + A0], message[x]

        blocks(ROWS, body)


def pair_kernel(
    slices, hosts, depth, z0, zo, zi, mine, short, long, wc, dc12, message, outer, inner, za, zb, zc, zs
):
    info = Position()

    def sweeps(one, two):
        begin(info, z0, zo, zi, 8, zs)
        sweep(info, zs, 8, one, XA0, za, 6, -6, ROWS + 12, wc, dc12)
        sweep(info, za, 6, one, XB0, zb, 4, -4, ROWS + 8, wc, dc12)
        if two is mine:
            sweep(info, zb, 4, two, XA0, zc, 2, -2, ROWS + 4, wc, dc12)
            sweep(info, zc, 2, two, XB0, message, 0, 0, ROWS, wc, dc12)
        else:
            sweep(info, zb, 4, two, A0, zc, 2, -2, ROWS + 4, wc, dc12)
            sweep(info, zc, 2, two, B0, message, 0, 0, ROWS, wc, dc12)
        give(info, depth, outer, inner, lambda x: message[x])

    for host in sorted(set(hosts)):
        one = mine if host == slices[0] else long
        two = mine if host == slices[1] else short
        pl.when(hosting(info, hosts) & (info[1] == host))(functools.partial(sweeps, one, two))


def inner_kernel(z, inner):
    info = Position()
    for r in range(8):
        inner[r] = jnp.where(info[0] == 0, z[ROWS - 8 + r], z[r])


def gather(z0, za, zb, zc, z2, one, two):
    def body(xs):
        for x in xs:
            one[x], one[ROWS + x], one[2 * ROWS + x] = z0[x], za[x + 6], zb[x + 4]
            two[x], two[ROWS + x], two[2 * ROWS + x] = zb[x + 4], zc[x + 2], z2[x]

    blocks(ROWS, body)


def gather_kernel(slices, hosts, z0, za, zb, zc, z2, home_in, away_in, home, away):
    info = Position()
    active, second = hosting(info, hosts), info[1] == slices[1]
    pl.when(active & ~second)(lambda: gather(z0, za, zb, zc, z2, home, away))
    pl.when(active & second)(lambda: gather(z0, za, zb, zc, z2, away, home))


def base_kernel(n1, n2, c1, c2, pro, share, b1, b2):
    def body(xs):
        for x in xs:
            for n, c, b in ((n1, c1, b1), (n2, c2, b2)):
                value = thirds(jnp.concatenate([share[...] * c[x], zeros(8)], axis=0))
                b[:, x, :] = (n[x] - dot(pro[...], value))[:SPECIES]

    blocks(ROWS, body)


PIECE, PIECES = 13, 4


def out_kernel(
    where, u, b0, late, fourth, b1, b2, share, z0, zo, zi, ab, wc, dc12, home, other, out, z, za, zs, spread, node, sem
):
    info = Position()
    last = info[1] == SLICES - 1
    at_home = hosting(info, GROUPS[0][1])
    for slices, hosts in GROUPS[1:-1]:
        at_home = at_home | (hosting(info, hosts) & ((info[1] == slices[0]) | (info[1] == slices[1])))
    for here, result in ((at_home, home), (~at_home & ~last, other)):

        @pl.when(here)
        def _():

            def body(xs):
                for x in xs:
                    z[x] = result[x]

            blocks(3 * ROWS, body)

    @pl.when(last)
    def _():
        begin(info, z0, zo, zi, 4, zs)

        def body(xs):
            for x in xs:
                z[x] = z0[x]

        blocks(ROWS, body)

    def finish(m, base):
        def body(xs):
            for x in xs:
                spread[m, :, x, :] = share[...] * z[m * ROWS + x]

        blocks(ROWS, body, ROWS)

        def add(s):
            node[m, s] = base(s) + spread[m, where[s]]

        @pl.loop(0, PIECES)
        def _(i):
            for k in range(PIECE):
                add(PIECE * i + k)
            written(m, i).start()

        add(SPECIES - 1)
        rest(m).start()

    def written(m, i):
        part = pl.ds(PIECE * i, PIECE)
        return pltpu.make_async_copy(node.at[m, part], out.at[m, part], sem.at[m, i])

    def rest(m):
        part = pl.ds(PIECE * PIECES, 1)
        return pltpu.make_async_copy(node.at[m, part], out.at[m, part], sem.at[m, PIECES])

    first = info[1] == 0
    finish(0, lambda s: jnp.where(first, u[0, s], b0[s] + late[s] + fourth[s]))

    @pl.when(last)
    def _():
        sweep(info, zs, 4, ab, A0, za, 2, -2, ROWS + 4, wc, dc12)
        sweep(info, za, 2, ab, B0, z.at[pl.ds(2 * ROWS, ROWS)], 0, 0, ROWS, wc, dc12)

        def body(xs):
            for x in xs:
                z[ROWS + x] = za[x + 2]

        blocks(ROWS, body)

    finish(1, lambda s: b1[s])
    finish(2, lambda s: b2[s])
    for m in range(3):

        @pl.loop(0, PIECES)
        def _(i):
            written(m, i).wait()

        rest(m).wait()


def field(*shape):
    return jax.ShapeDtypeStruct(shape + (COLS,), F32)


SMEM = pl.BlockSpec(memory_space=pltpu.SMEM)
VMEM = pl.BlockSpec(memory_space=pltpu.VMEM)
ANY = pl.BlockSpec(memory_space=pl.ANY)


def call(kernel, name, outs, *args, scratch=(), alias=None, out_specs=None, specs=None):
    specs = specs or [SMEM if a.dtype == jnp.int32 and a.ndim == 1 else VMEM for a in args]
    return pl.pallas_call(
        kernel,
        out_shape=outs,
        in_specs=specs,
        **({"out_specs": out_specs} if out_specs else {}),
        scratch_shapes=[pltpu.VMEM(f.shape, f.dtype) if isinstance(f, jax.ShapeDtypeStruct) else f for f in scratch],
        input_output_aliases=alias or {},
        compiler_params=pltpu.CompilerParams(vmem_limit_bytes=VMEM_LIMIT),
        name=name,
    )(*args)


AXES = ("tm", "space")
OUTER = [(s, s + 1) for s in range(1, SLABS - 1, 2)] + [(s + 1, s) for s in range(1, SLABS - 1, 2)]
INNER = [(s, s ^ 1) for s in range(SLABS)]
SAME = [(s, s) for s in range(SLABS)]


def moved(value, *routes):
    pairs = [
        (source[s % 2] * SLABS + s, target[t % 2] * SLABS + t) for source, target, slabs in routes for s, t in slabs
    ]
    return lax.ppermute(value, AXES, pairs)


def both(p):
    return (p, p)


def swap(outer, inner):
    got_inner = moved(inner, *[(both(p), both(p), INNER) for p in range(SLICES)])
    got_outer = moved(outer, *[(both(p), both(p), OUTER) for p in range(SLICES)])
    return got_outer, got_inner


def hop(message, outer, inner, source, target):
    parts = ((outer, OUTER), (inner, INNER), (message, SAME))
    zo, zi, z = [moved(value, (source, target, slabs)) for value, slabs in parts]
    return [z, zo, zi]


def after(value, other):
    return lax.optimization_barrier((value, other))[0]


def local(fine_nodes, fine_rates, fine_pairs, fine_diff, coarse_rates, coarse_pairs, coarse_diff, species_map):
    nodes = fine_nodes[0]
    fine, coarse = field(ROWS, SP), field(ROWS, CP)
    message = field(3, 2, SP)
    def bf16(*shape):
        return jax.ShapeDtypeStruct(shape, BF16)

    raw = sum(
        jnp.pad(v.astype(F32), ((at, RAW - at - v.shape[0]), (0, 128 - v.shape[1])))
        for at, v in (
            (RATES, fine_rates),
            (PAIRS, fine_pairs),
            (CRATES, coarse_rates),
            (CPAIRS, coarse_pairs),
            (DIFF, fine_diff.reshape(1, SPECIES)),
            (CDIFF, coarse_diff.reshape(1, COARSE)),
            (MAP, species_map.reshape(1, SPECIES)),
        )
    )
    wf, wr, wfr, lv, wc, pro, d12, dc12, share = call(
        prep_kernel,
        "prep",
        [bf16(2 * SP, 256), bf16(128, 256), bf16(2 * SP + 128, 256), bf16(80, 128), bf16(2 * CP, 128), bf16(SP, 96)]
        + [field(SP), field(CP), field(CP)],
        raw,
    )
    outer, inner = call(first_kernel, "first", [message, message], nodes, wc)
    uo, ui = swap(outer, inner)

    n1, s, r0, e0, c0 = call(
        old_kernel,
        "old",
        [fine, fine, coarse, coarse, coarse],
        *(nodes, wf, wr, wc, d12, dc12),
        scratch=[field(4, 3, SP), field(ROWS + 4, SP), field(ROWS + 4, SP), field(ROWS + 4, CP), field(ROWS + 4, CP)],
    )
    two, twelve, eight = field(2, SP), field(12, CP), field(8, CP)
    n1, s, r0, e0, outer, inner = call(
        old_edge_kernel,
        "old_edge",
        [fine, fine, coarse, coarse, two, two],
        *(uo, ui, lv, d12, dc12, n1, s, r0, e0),
        alias={5: 0, 6: 1, 7: 2, 8: 3},
    )
    no, ni = swap(outer, inner)
    n2, r1, e1, c1 = call(
        mid_kernel, "mid", [fine, coarse, coarse, coarse], n1, s, wfr, wc, d12, dc12, scratch=[field(ROWS + 4, SP), field(ROWS + 4, CP), field(ROWS + 4, CP)]
    )
    extended, short = field(EXT_ROWS, CP), field(AB_ROWS, CP)
    n2, r1, e1, abx, c2, outer, inner = call(
        mid_edge_kernel,
        "mid_edge",
        [fine, coarse, coarse, extended, coarse, twelve, twelve],
        *(no, ni, lv, wr, d12, dc12, r0, e0, c0, n2, r1, e1),
        alias={9: 0, 10: 1, 11: 2},
        scratch=[field(ROWS + 4, CP), coarse],
    )
    ho, hi = swap(outer, inner)
    b1, b2 = call(base_kernel, "base", [field(SPECIES, ROWS)] * 2, n1, n2, c1, c2, pro, share)
    abx, ab = call(last_edge_kernel, "last_edge", [extended, short], outer, inner, ho, hi, abx, alias={4: 0})

    forward = [(both(p), both(p + 1), SAME) for p in range(SLICES - 1)]
    ab, abx = after(ab, b1), after(abx, b1)
    result = field(3 * ROWS, CP)
    pairs = [(slices, hosts) for slices, hosts in GROUPS if len(slices) == 2]
    short, long, back = [], [], []
    for slices, hosts in pairs:
        for core, host in enumerate(hosts):
            slabs = [(t, t) for t in range(core, SLABS, 2)]
            if host != slices[0]:
                long.append((both(slices[0]), both(host), slabs))
            if host != slices[1]:
                short.append((both(slices[1]), both(host), slabs))
            back.append((both(host), both(slices[0] if host == slices[1] else slices[1]), slabs))
    short, long = moved(ab, *short), moved(abx, *long)
    home, away, *sent = call(
        functools.partial(start_kernel, GROUPS[0][1]), "start", [result, result, coarse, eight, eight], ab, wc, dc12
    )
    for at, (slices, hosts) in enumerate(GROUPS[1:], 1):
        if at > 1:
            z = hop(*sent, GROUPS[at - 1][1], hosts)
        if at == 1:
            zo, zm = lax.optimization_barrier(
                (moved(sent[1], (both(0), hosts, OUTER)), moved(sent[0], (both(0), hosts, SAME)))
            )
            zi = moved(call(inner_kernel, "inner", eight, zm), (hosts, hosts, INNER))
            z = list(lax.optimization_barrier((zm, zo, zi)))
            b0 = moved(after(b2, z[2]), forward[2], *forward[4:])
            *z, short, long = lax.optimization_barrier((*z, short, long))
            fourth = moved(after(b2, z[0]), forward[3])
        elif at == 2:
            *z, b0 = lax.optimization_barrier((*z, b0))
            late = moved(after(b2, z[0]), *forward[:2])
        elif at == 3:
            *z, late, fourth, home, away = lax.optimization_barrier((*z, late, fourth, home, away))
        else:
            other = moved(away, *back)
            *z, other, home = lax.optimization_barrier((*z, other, home))
        if len(slices) == 2:
            depth = 4 * len(GROUPS[at + 1][0])
            *sent, za, zb, zc = call(
                functools.partial(pair_kernel, slices, hosts, depth),
                "pair",
                [coarse, field(depth, CP), field(depth, CP), field(ROWS + 12, CP), field(ROWS + 8, CP), field(ROWS + 4, CP)],
                *(*z, abx, short, long, wc, dc12),
                scratch=[field(ROWS + 16, CP)],
            )
            home, away = call(
                functools.partial(gather_kernel, slices, hosts),
                "gather",
                [result, result],
                *(z[0], za, zb, zc, sent[0], home, away),
                alias={5: 0, 6: 1},
            )
    out = call(
        out_kernel,
        "out",
        field(3, SPECIES, ROWS),
        *(species_map[:, 0], nodes, b0, late, fourth, b1, b2, share, *z, ab, wc, dc12, home, other),
        out_specs=ANY,
        scratch=[result, field(ROWS + 4, CP), field(ROWS + 8, CP), field(3, CP, ROWS), field(3, SPECIES, ROWS), pltpu.SemaphoreType.DMA((3, PIECES + 1))],
    )
    return out[None]


def solution(mesh):
    in_specs = (P("tm", None, None, "space", None), P(), P(), P(), P(), P(), P(), P())
    out_specs = P("tm", None, None, "space", None)
    return jax.shard_map(local, mesh=mesh, in_specs=in_specs, out_specs=out_specs, check_vma=False)
```

```python
import functools

import jax
import jax.numpy as jnp
from jax import lax
from jax.experimental import pallas as pl
from jax.experimental.pallas import tpu as pltpu
from jax.sharding import PartitionSpec as P

SPECIES, COARSE = 53, 21
SP, CP = 56, 24
ROWS, COLS = 16, 256
SLICES, SLABS = 8, 16
STEP, HALF, RELAX = 0.1, 0.05, 3.0
W0 = (5.0 / 24.0, 1.0 / 3.0, -1.0 / 24.0)
W1 = (-1.0 / 24.0, 1.0 / 3.0, 5.0 / 24.0)
F32, BF16 = jnp.float32, jnp.bfloat16
GROUPS = (((0,), (0, 0)), ((1, 2), (1, 5)), ((3, 4), (3, 4)), ((5, 6), (5, 6)), ((7,), (7, 7)))
VMEM_LIMIT = 24 * 1024 * 1024


def split(x):
    hi = x.astype(BF16)
    lo = (x - hi.astype(F32)).astype(BF16)
    return jnp.concatenate([hi, lo], axis=0)


def thirds(x):
    hi = x.astype(BF16)
    rest = x - hi.astype(F32)
    mid = rest.astype(BF16)
    return jnp.concatenate([hi, mid, (rest - mid.astype(F32)).astype(BF16)], axis=0)


def zeros(rows):
    return jnp.zeros((rows, COLS), F32)


def dot(w, x):
    return jnp.dot(w, x, preferred_element_type=F32)


def two_terms(x):
    return jnp.concatenate([x, x - x.astype(BF16).astype(F32)], axis=0).astype(BF16)


def stacked(x, squares):
    return split(jnp.concatenate([x, squares], axis=0))


def lap_y(x):
    near = pltpu.roll(x, 1, 1) + pltpu.roll(x, COLS - 1, 1)
    far = pltpu.roll(x, 2, 1) + pltpu.roll(x, COLS - 2, 1)
    return 16.0 * near - far - 60.0 * x


def lap_rows(ref, x):
    return 16.0 * (ref[x - 1] + ref[x + 1]) - (ref[x - 2] + ref[x + 2])


def beside(near, far):
    return 16.0 * near - far, -near


RATES, PAIRS, CRATES, CPAIRS, DIFF, CDIFF, MAP, RAW = 0, 56, 112, 136, 160, 161, 162, 168


def prep_kernel(raw, wf, wr, wfr, lv, wc, ws, lapm, pro, d12, dc12, share):
    row = lax.broadcasted_iota(jnp.int32, (SP, 128), 0)
    lane = lax.broadcasted_iota(jnp.int32, (SP, 128), 1)

    def halves(x):
        hi = x.astype(BF16).astype(F32)
        return hi, (x - hi).astype(BF16).astype(F32)

    def column(values, height):
        return jnp.sum(jnp.where(row == lane, values, 0.0), axis=1, keepdims=True)[:height]

    eye = jnp.where(row == lane, RELAX, 0.0)
    fine = raw[RATES : RATES + SP, :] - jnp.where(row < SPECIES, eye, 0.0)
    fine = fine + pltpu.roll(raw[PAIRS : PAIRS + SP, :], SP, 1)
    coarse = raw[CRATES : CRATES + CP, :] - jnp.where(row < COARSE, eye, 0.0)[:CP]
    coarse = coarse + pltpu.roll(raw[CPAIRS : CPAIRS + CP, :], CP, 1)
    vectors = raw[DIFF : DIFF + 8, :]
    diff_row = vectors[0:1]
    d12[...] = jnp.broadcast_to(column(diff_row, SP) / 12.0, (SP, COLS))
    dc12[...] = jnp.broadcast_to(column(vectors[1:2], CP) / 12.0, (CP, COLS))
    map_row = jnp.where(lane[0:1] < SPECIES, vectors[2:3].astype(jnp.int32), -1)
    map_column = jnp.sum(jnp.where(row == lane, map_row, 0), axis=1, keepdims=True)
    map_column = jnp.where(row[:, 0:1] < SPECIES, map_column, -1)
    lum = jnp.where((map_row == row[:CP]) & (lane[:CP] < SPECIES), 1.0, 0.0)
    counts = jnp.sum(lum, axis=1, keepdims=True)
    share[...] = jnp.broadcast_to(1.0 / jnp.maximum(counts, 1.0), (CP, COLS))
    lumped = jnp.dot(lum[:, :SP], fine, precision=lax.Precision.HIGHEST, preferred_element_type=F32)
    fh, fl = halves(fine)
    rh, rl = halves(lumped)
    dh, dl = halves(lum * diff_row)
    ch, cl = halves(coarse)
    f = jnp.concatenate([fh, fl], axis=0)
    r = jnp.concatenate([rh, rl, lum, dh, dl, jnp.zeros((8, 128), F32)], axis=0)

    def twice(w, width):
        w = jnp.concatenate([w, jnp.zeros_like(w)], axis=1)
        return (w + pltpu.roll(w, width, 1))[:, : 2 * width].astype(BF16)

    wf[...] = twice(f, 2 * SP)
    wr[...] = twice(r, 2 * SP)
    wfr[: 2 * SP, :] = twice(f, 2 * SP)
    wfr[2 * SP :, :] = twice(r, 2 * SP)
    v = jnp.concatenate([lum, dh, dl, jnp.zeros((8, 128), F32)], axis=0)
    lv[...] = (v + pltpu.roll(v, 64, 1)).astype(BF16)
    c = jnp.concatenate([ch, cl], axis=0)
    wc[...] = twice(c, 2 * CP)
    linear, pairs = jnp.where(lane[: 2 * CP] < CP, c, 0.0), jnp.where(lane[: 2 * CP] < CP, 0.0, c)
    both_terms = linear + pltpu.roll(linear, CP, 1) + pltpu.roll(pairs, CP, 1) + pltpu.roll(pairs, 2 * CP, 1)
    ws[...] = both_terms[:, : 4 * CP].astype(BF16)
    far = lax.broadcasted_iota(jnp.int32, (COLS, COLS), 0) - lax.broadcasted_iota(jnp.int32, (COLS, COLS), 1)
    far = jnp.abs(far)
    far = jnp.minimum(far, COLS - far)
    lapm[...] = jnp.where(far == 0, -60.0, jnp.where(far == 1, 16.0, jnp.where(far == 2, -1.0, 0.0))).astype(BF16)
    lane96 = lax.broadcasted_iota(jnp.int32, (SP, 96), 1)
    pro[...] = jnp.where(map_column == lane96 % 32, 1.0, 0.0).astype(BF16)


class Position:
    def __init__(self):
        self.slice_at, self.slab = lax.axis_index("tm"), lax.axis_index("space")

    def __getitem__(self, at):
        return (self.slab % 2, self.slice_at, self.slab)[at]


def blocks(rows, body, size=4):
    @pl.loop(0, rows // size)
    def _(i):
        body([size * i + k for k in range(size)])


def first_kernel(u, weights_made, outer, inner):
    info = Position()
    at_top = info[0] == 0
    for m in range(3):
        for r in range(2):
            first, last = u[m, :, r, :], u[m, :, ROWS - 2 + r, :]
            for out, value in ((outer, jnp.where(at_top, first, last)), (inner, jnp.where(at_top, last, first))):
                out[m, r, SP - 8 :, :] = zeros(8)
                out[m, r, :SPECIES, :] = value


def restricted(y):
    return y[0:24] + y[24:48], y[48:72], y[72:96] + y[96:120]


MIX0 = [STEP * w for w in W0]
MIXS = [STEP * W1[0], STEP * W1[1] - HALF, STEP * W1[2]]


def mixed(factors, values):
    return factors[0] * values[0] + factors[1] * values[1] + factors[2] * values[2]


def old_kernel(u, wf, wr, wc, d12, dc12, n1, s, r0, e0, c0, ut, p0s, pss, v0s, c0s):
    for k in range(4):
        for m in range(3):
            ut[k, m, SP - 8 :, :] = zeros(8)
    for x in (0, 1, ROWS + 2, ROWS + 3):
        p0s[x], pss[x], v0s[x], c0s[x] = zeros(SP), zeros(SP), zeros(CP), zeros(CP)

    def terms(xs):
        for k, x in enumerate(xs):
            for m in range(3):
                ut[k, m, :SPECIES, :] = u[m, :, x, :]
        for k, x in enumerate(xs):
            us = [ut[k, m] for m in range(3)]
            qs = [v * v for v in us]
            p0, ps = mixed(MIX0, us), mixed(MIXS, us)
            y = dot(wf[...], stacked(p0, mixed(MIX0, qs)))
            n1[x] = us[0] + (y[:SP] + y[SP:]) + d12[...] * lap_y(p0)
            y = dot(wf[...], stacked(ps, mixed(MIXS, qs)))
            s[x] = (y[:SP] + y[SP:]) + d12[...] * lap_y(ps)
            r, c, v = restricted(dot(wr[...], stacked(us[0], qs[0])))
            r0[x] = r + lap_y(v) * (1.0 / 12.0)
            y = dot(wc[...], stacked(c, c * c))
            e0[x] = (y[:CP] + y[CP:]) + dc12[...] * lap_y(c)
            p0s[x + 2], pss[x + 2], v0s[x + 2], c0s[x + 2], c0[x] = p0, ps, v, c, c

    blocks(ROWS, terms)

    def laps(xs):
        for x in xs:
            n1[x] += d12[...] * lap_rows(p0s, x + 2)
            s[x] += d12[...] * lap_rows(pss, x + 2)
            r0[x] += lap_rows(v0s, x + 2) * (1.0 / 12.0)
            e0[x] += dc12[...] * lap_rows(c0s, x + 2)

    blocks(ROWS, laps)


def lumped_halo(lv, row):
    y = dot(lv[...], split(jnp.concatenate([row, zeros(8)], axis=0)))
    return y[0:24], y[24:48] + y[48:72]


SIDES = (((0, 1), (1, 0)), ((ROWS - 1, ROWS - 2), (0, 1)))


def pick_halo(info, side, outer, inner):
    take = info[0] == side
    return lambda *at: jnp.where(take, outer[at], inner[at])


def send(info, outer, inner, tops, bottoms):
    at_top = info[0] == 0
    for r, (top, bottom) in enumerate(zip(tops, bottoms)):
        outer[r] = jnp.where(at_top, top, bottom)
        inner[r] = jnp.where(at_top, bottom, top)


def old_edge_kernel(uo, ui, lv, d12, dc12, n1i, si, r0i, e0i, n1, s, r0, e0, outer, inner):
    info = Position()
    for side, (rows, order) in enumerate(SIDES):
        halo = pick_halo(info, side, uo, ui)
        us = [[halo(m, r) for m in range(3)] for r in order]
        p0 = beside(*[mixed(MIX0, v) for v in us])
        ps = beside(*[mixed(MIXS, v) for v in us])
        lumped = [lumped_halo(lv, v[0]) for v in us]
        c = beside(lumped[0][0], lumped[1][0])
        v = beside(lumped[0][1], lumped[1][1])
        for i, x in enumerate(rows):
            n1[x] = n1i[x] + d12[...] * p0[i]
            s[x] = si[x] + d12[...] * ps[i]
            r0[x] = r0i[x] + v[i] * (1.0 / 12.0)
            e0[x] = e0i[x] + dc12[...] * c[i]
    send(info, outer, inner, [n1[0], n1[1]], [n1[ROWS - 2], n1[ROWS - 1]])


def mid_kernel(n1, s, wfr, wc, d12, dc12, n2, r1, e1, c1, n1s, v1s, c1s):
    for x in (0, 1, ROWS + 2, ROWS + 3):
        n1s[x], v1s[x], c1s[x] = zeros(SP), zeros(CP), zeros(CP)

    def terms(xs):
        for x in xs:
            n = n1[x]
            y = dot(wfr[...], stacked(n, n * n))
            n2[x] = n + HALF * ((y[:SP] + y[SP : 2 * SP]) + d12[...] * lap_y(n)) + s[x]
            r, c, v = restricted(y[2 * SP :])
            r1[x] = r + lap_y(v) * (1.0 / 12.0)
            y = dot(wc[...], stacked(c, c * c))
            e1[x] = (y[:CP] + y[CP:]) + dc12[...] * lap_y(c)
            n1s[x + 2], v1s[x + 2], c1s[x + 2], c1[x] = n, v, c, c

    blocks(ROWS, terms, 8)

    def laps(xs):
        for x in xs:
            n2[x] += (HALF * d12[...]) * lap_rows(n1s, x + 2)
            r1[x] += lap_rows(v1s, x + 2) * (1.0 / 12.0)
            e1[x] += dc12[...] * lap_rows(c1s, x + 2)

    blocks(ROWS, laps, 8)


def lumped_old(first, c0, e0):
    return jnp.where(first, c0, -HALF * e0)


AB_ROWS, EXT_ROWS = 2 * ROWS + 4, 2 * ROWS + 20
A0, B0 = 2, ROWS + 4
XA0, XB0 = 6, ROWS + 16


def mid_edge_kernel(no, ni, lv, wr, d12, dc12, r0, e0, c0, n2i, r1i, e1i, n2, r1, e1, ab, c2, outer, inner, v2s, gs):
    info = Position()
    first = info[1] == 0
    for side, (rows, order) in enumerate(SIDES):
        halo = pick_halo(info, side, no, ni)
        ns = [halo(r) for r in order]
        lumped = [lumped_halo(lv, v) for v in ns]
        c = beside(lumped[0][0], lumped[1][0])
        v = beside(lumped[0][1], lumped[1][1])
        n = beside(*ns)
        for i, x in enumerate(rows):
            n2[x] = n2i[x] + (HALF * d12[...]) * n[i]
            r1[x] = r1i[x] + v[i] * (1.0 / 12.0)
            e1[x] = e1i[x] + dc12[...] * c[i]
    for x in (0, 1, ROWS + 2, ROWS + 3):
        v2s[x] = zeros(CP)

    def lumped(x, value):
        gs[x], c2[x], v2s[x + 2] = restricted(dot(wr[...], stacked(value, value * value)))

    def pieces(x, mid, late):
        v = v2s[x + 2]
        g2 = gs[x] + (lap_y(v) + lap_rows(v2s, x + 2)) * (1.0 / 12.0)
        ab[x + XA0] = mixed(MIX0, (r0[x], mid, g2)) + lumped_old(first, c0[x], e0[x])
        ab[x + XB0] = mixed([STEP * w for w in W1], (r0[x], mid, g2)) - HALF * late

    edges = (0, 1, ROWS - 2, ROWS - 1)
    for x in edges:
        lumped(x, n2[x])
    blocks(ROWS - 4, lambda xs: [lumped(x + 2, n2i[x + 2]) for x in xs], ROWS - 4)
    for x in edges:
        pieces(x, r1[x], e1[x])
    blocks(ROWS - 4, lambda xs: [pieces(x + 2, r1i[x + 2], e1i[x + 2]) for x in xs], ROWS - 4)
    top = [ab[x + XA0] for x in range(6)] + [ab[x + XB0] for x in range(4)] + [v2s[x + 2] for x in range(2)]
    bottom = [ab[x + XA0] for x in range(ROWS - 6, ROWS)] + [ab[x + XB0] for x in range(ROWS - 4, ROWS)]
    send(info, outer, inner, top, bottom + [v2s[x] for x in range(ROWS, ROWS + 2)])


def last_edge_kernel(mo, mi, ho, hi, abi, ab, short):
    info = Position()
    ka, kb = STEP * W0[2] / 12.0, STEP * W1[2] / 12.0
    done = {}
    for side, (rows, order) in enumerate(SIDES):
        inside = info[2] > 0 if side == 0 else info[2] < SLABS - 1
        own, halo = pick_halo(info, side, mo, mi), pick_halo(info, side, ho, hi)
        fix = beside(*[halo(10 + r) for r in order])
        theirs = beside(*[own(10 + r) for r in order[::-1]])
        for i, x in enumerate(rows):
            done[x + XA0] = abi[x + XA0] + ka * fix[i]
            done[x + XB0] = abi[x + XB0] + kb * fix[i]
        for depth, at, to, factor in ((6, 0, XA0, ka), (4, 6, XB0, kb)):
            for i in range(depth):
                x = -1 - i if side == 0 else ROWS + i
                value = halo(at + (depth - 1 - i if side == 0 else i))
                if i < 2:
                    value = value + factor * theirs[i]
                done[x + to] = jnp.where(inside, value, 0.0)
    for at, value in done.items():
        ab[at] = value
    for x in range(-2, ROWS + 2):
        short[x + A0] = done[x + XA0] if x + XA0 in done else abi[x + XA0]
    for x in range(ROWS):
        short[x + B0] = done[x + XB0] if x + XB0 in done else abi[x + XB0]


def sweep(info, z, z0, add, add0, out, out0, low, rows, ws, lapm, dc12):
    size = rows // 2

    def body(xs):
        zr = [z[xs[0] + (low + z0 + k)] for k in range(-2, size + 2)]
        terms = [two_terms(value) for value in zr[2:-2]]
        laps = dot(jnp.concatenate(terms, axis=0), lapm[...])
        for k in range(size):
            x, value = xs[k] + low, zr[k + 2]
            y = dot(ws[...], jnp.concatenate([terms[k], two_terms(value * value)], axis=0))
            lap = laps[2 * CP * k : 2 * CP * k + CP] + laps[2 * CP * k + CP : 2 * CP * (k + 1)]
            lap = lap + 16.0 * (zr[k + 1] + zr[k + 3]) - (zr[k] + zr[k + 4])
            value = value + HALF * ((y[:CP] + y[CP:]) + dc12[...] * lap) + add[x + add0]
            if low < 0:
                inside = ((x >= 0) | (info[2] > 0)) & ((x < ROWS) | (info[2] < SLABS - 1))
                value = jnp.where(inside, value, 0.0)
            out[x + out0] = value

    blocks(rows, body, size)


def begin(info, z0, zo, zi, depth, zs):
    top, bottom = pick_halo(info, 0, zo, zi), pick_halo(info, 1, zo, zi)
    for r in range(depth):
        zs[r], zs[depth + ROWS + r] = top(r), bottom(r)

    def body(xs):
        for x in xs:
            zs[depth + x] = z0[x]

    blocks(ROWS, body)


def give(info, depth, outer, inner, value):
    send(info, outer, inner, [value(x) for x in range(depth)], [value(x) for x in range(ROWS - depth, ROWS)])


def hosting(info, hosts):
    return info[1] == jnp.where(info[0] == 0, hosts[0], hosts[1])


def start_kernel(hosts, ab, ws, lapm, dc12, result, unused, message, outer, inner):
    info = Position()

    @pl.when(hosting(info, hosts))
    def _():
        sweep(info, ab, A0, ab, B0, message, 0, 0, ROWS, ws, lapm, dc12)
        give(info, 8, outer, inner, lambda x: message[x])

        def body(xs):
            for x in xs:
                result[x], result[ROWS + x], result[2 * ROWS + x] = zeros(CP), ab[x + A0], message[x]

        blocks(ROWS, body)


def pair_kernel(
    slices, hosts, depth, z0, zo, zi, mine, short, long, ws, lapm, dc12, message, outer, inner, za, zb, zc, zs
):
    info = Position()

    def sweeps(one, two):
        begin(info, z0, zo, zi, 8, zs)
        sweep(info, zs, 8, one, XA0, za, 6, -6, ROWS + 12, ws, lapm, dc12)
        sweep(info, za, 6, one, XB0, zb, 4, -4, ROWS + 8, ws, lapm, dc12)
        if two is mine:
            sweep(info, zb, 4, two, XA0, zc, 2, -2, ROWS + 4, ws, lapm, dc12)
            sweep(info, zc, 2, two, XB0, message, 0, 0, ROWS, ws, lapm, dc12)
        else:
            sweep(info, zb, 4, two, A0, zc, 2, -2, ROWS + 4, ws, lapm, dc12)
            sweep(info, zc, 2, two, B0, message, 0, 0, ROWS, ws, lapm, dc12)
        give(info, depth, outer, inner, lambda x: message[x])

    for host in sorted(set(hosts)):
        one = mine if host == slices[0] else long
        two = mine if host == slices[1] else short
        pl.when(hosting(info, hosts) & (info[1] == host))(functools.partial(sweeps, one, two))


def gather(z0, za, zb, zc, z2, one, two):
    def body(xs):
        for x in xs:
            one[x], one[ROWS + x], one[2 * ROWS + x] = z0[x], za[x + 6], zb[x + 4]
            two[x], two[ROWS + x], two[2 * ROWS + x] = zb[x + 4], zc[x + 2], z2[x]

    blocks(ROWS, body)


def gather_kernel(slices, hosts, z0, za, zb, zc, z2, home_in, away_in, home, away):
    info = Position()
    active, second = hosting(info, hosts), info[1] == slices[1]
    pl.when(active & ~second)(lambda: gather(z0, za, zb, zc, z2, home, away))
    pl.when(active & second)(lambda: gather(z0, za, zb, zc, z2, away, home))


def base_kernel(n1, n2, c1, c2, pro, share, b1, b2):
    def body(xs):
        for x in xs:
            for n, c, b in ((n1, c1, b1), (n2, c2, b2)):
                value = thirds(jnp.concatenate([share[...] * c[x], zeros(8)], axis=0))
                b[:, x, :] = (n[x] - dot(pro[...], value))[:SPECIES]

    blocks(ROWS, body)


def out_kernel(
    where, u, b0, late, b1, b2, share, z0, zo, zi, ab, ws, lapm, dc12, home, one, other, out, z, za, zs, spread, node, sem
):
    info = Position()
    last = info[1] == SLICES - 1
    at_home = hosting(info, GROUPS[0][1])
    for slices, hosts in GROUPS[1:-1]:
        at_home = at_home | (hosting(info, hosts) & ((info[1] == slices[0]) | (info[1] == slices[1])))
    first = info[1] == GROUPS[1][0][0]
    for here, result in ((at_home, home), (first & ~at_home, one), (~at_home & ~first & ~last, other)):

        @pl.when(here)
        def _():

            def body(xs):
                for x in xs:
                    z[x] = result[x]

            blocks(3 * ROWS, body)

    @pl.when(last)
    def _():
        begin(info, z0, zo, zi, 4, zs)

        def body(xs):
            for x in xs:
                z[x] = z0[x]

        blocks(ROWS, body)

    def finish(m, base):
        def body(xs):
            for x in xs:
                spread[m, :, x, :] = share[...] * z[m * ROWS + x]

        blocks(ROWS, body, ROWS)

        def add(s):
            node[m, s] = base(s) + spread[m, where[s]]

        blocks(SPECIES, lambda at: [add(s) for s in at], 13)
        add(SPECIES - 1)
        copy = pltpu.make_async_copy(node.at[m], out.at[m], sem.at[m])
        copy.start()
        return copy

    first = info[1] == 0
    copies = [finish(0, lambda s: jnp.where(first, u[0, s], b0[s] + late[s]))]

    @pl.when(last)
    def _():
        sweep(info, zs, 4, ab, A0, za, 2, -2, ROWS + 4, ws, lapm, dc12)
        sweep(info, za, 2, ab, B0, z.at[pl.ds(2 * ROWS, ROWS)], 0, 0, ROWS, ws, lapm, dc12)

        def body(xs):
            for x in xs:
                z[ROWS + x] = za[x + 2]

        blocks(ROWS, body)

    copies += [finish(1, lambda s: b1[s]), finish(2, lambda s: b2[s])]
    for copy in copies:
        copy.wait()


def field(*shape):
    return jax.ShapeDtypeStruct(shape + (COLS,), F32)


SMEM = pl.BlockSpec(memory_space=pltpu.SMEM)
VMEM = pl.BlockSpec(memory_space=pltpu.VMEM)
ANY = pl.BlockSpec(memory_space=pl.ANY)


def call(kernel, name, outs, *args, scratch=(), alias=None, out_specs=None, specs=None):
    specs = specs or [SMEM if a.dtype == jnp.int32 and a.ndim == 1 else VMEM for a in args]
    return pl.pallas_call(
        kernel,
        out_shape=outs,
        in_specs=specs,
        **({"out_specs": out_specs} if out_specs else {}),
        scratch_shapes=[pltpu.VMEM(f.shape, f.dtype) if isinstance(f, jax.ShapeDtypeStruct) else f for f in scratch],
        input_output_aliases=alias or {},
        compiler_params=pltpu.CompilerParams(vmem_limit_bytes=VMEM_LIMIT),
        name=name,
    )(*args)


AXES = ("tm", "space")
OUTER = [(s, s + 1) for s in range(1, SLABS - 1, 2)] + [(s + 1, s) for s in range(1, SLABS - 1, 2)]
INNER = [(s, s ^ 1) for s in range(SLABS)]
SAME = [(s, s) for s in range(SLABS)]


def moved(value, *routes):
    pairs = [
        (source[s % 2] * SLABS + s, target[t % 2] * SLABS + t) for source, target, slabs in routes for s, t in slabs
    ]
    return lax.ppermute(value, AXES, pairs)


def both(p):
    return (p, p)


def swap(outer, inner):
    got_inner = moved(inner, *[(both(p), both(p), INNER) for p in range(SLICES)])
    got_outer = moved(outer, *[(both(p), both(p), OUTER) for p in range(SLICES)])
    return got_outer, got_inner


def hop(message, outer, inner, source, target):
    parts = ((outer, OUTER), (inner, INNER), (message, SAME))
    zo, zi, z = [moved(value, (source, target, slabs)) for value, slabs in parts]
    return [z, zo, zi]


def after(value, other):
    return lax.optimization_barrier((value, other))[0]


def local(fine_nodes, fine_rates, fine_pairs, fine_diff, coarse_rates, coarse_pairs, coarse_diff, species_map):
    nodes = fine_nodes[0]
    fine, coarse = field(ROWS, SP), field(ROWS, CP)
    message = field(3, 2, SP)
    def bf16(*shape):
        return jax.ShapeDtypeStruct(shape, BF16)

    raw = sum(
        jnp.pad(v.astype(F32), ((at, RAW - at - v.shape[0]), (0, 128 - v.shape[1])))
        for at, v in (
            (RATES, fine_rates),
            (PAIRS, fine_pairs),
            (CRATES, coarse_rates),
            (CPAIRS, coarse_pairs),
            (DIFF, fine_diff.reshape(1, SPECIES)),
            (CDIFF, coarse_diff.reshape(1, COARSE)),
            (MAP, species_map.reshape(1, SPECIES)),
        )
    )
    wf, wr, wfr, lv, wc, ws, lapm, pro, d12, dc12, share = call(
        prep_kernel,
        "prep",
        [bf16(2 * SP, 4 * SP), bf16(128, 4 * SP), bf16(2 * SP + 128, 4 * SP), bf16(80, 128), bf16(2 * CP, 4 * CP), bf16(2 * CP, 4 * CP)]
        + [bf16(COLS, COLS), bf16(SP, 96)]
        + [field(SP), field(CP), field(CP)],
        raw,
    )
    outer, inner = call(first_kernel, "first", [message, message], nodes, wc)
    uo, ui = swap(outer, inner)

    n1, s, r0, e0, c0 = call(
        old_kernel,
        "old",
        [fine, fine, coarse, coarse, coarse],
        *(nodes, wf, wr, wc, d12, dc12),
        scratch=[field(4, 3, SP), field(ROWS + 4, SP), field(ROWS + 4, SP), field(ROWS + 4, CP), field(ROWS + 4, CP)],
    )
    two, twelve, eight = field(2, SP), field(12, CP), field(8, CP)
    n1, s, r0, e0, outer, inner = call(
        old_edge_kernel,
        "old_edge",
        [fine, fine, coarse, coarse, two, two],
        *(uo, ui, lv, d12, dc12, n1, s, r0, e0),
        alias={5: 0, 6: 1, 7: 2, 8: 3},
    )
    no, ni = swap(outer, inner)
    n2, r1, e1, c1 = call(
        mid_kernel, "mid", [fine, coarse, coarse, coarse], n1, s, wfr, wc, d12, dc12, scratch=[field(ROWS + 4, SP), field(ROWS + 4, CP), field(ROWS + 4, CP)]
    )
    extended, short = field(EXT_ROWS, CP), field(AB_ROWS, CP)
    n2, r1, e1, abx, c2, outer, inner = call(
        mid_edge_kernel,
        "mid_edge",
        [fine, coarse, coarse, extended, coarse, twelve, twelve],
        *(no, ni, lv, wr, d12, dc12, r0, e0, c0, n2, r1, e1),
        alias={9: 0, 10: 1, 11: 2},
        scratch=[field(ROWS + 4, CP), coarse],
    )
    ho, hi = swap(outer, inner)
    b1, b2 = call(base_kernel, "base", [field(SPECIES, ROWS)] * 2, n1, n2, c1, c2, pro, share)
    abx, ab = call(last_edge_kernel, "last_edge", [extended, short], outer, inner, ho, hi, abx, alias={4: 0})

    ab, abx = after(ab, b1), after(abx, b1)
    result = field(3 * ROWS, CP)
    pairs = [(slices, hosts) for slices, hosts in GROUPS if len(slices) == 2]
    short, long, back, first = [], [], [], []
    for slices, hosts in pairs:
        for core, host in enumerate(hosts):
            slabs = [(t, t) for t in range(core, SLABS, 2)]
            if host != slices[0]:
                long.append((both(slices[0]), both(host), slabs))
            if host != slices[1]:
                short.append((both(slices[1]), both(host), slabs))
            back.append((both(host), both(slices[0] if host == slices[1] else slices[1]), slabs))
            if host not in slices:
                first.append((both(host), both(slices[0]), slabs))
    short, long = moved(ab, *short), moved(abx, *long)
    forward = [(both(p), both(p + 1), SAME) for p in range(SLICES - 1)]
    home, away, *sent = call(
        functools.partial(start_kernel, GROUPS[0][1]), "start", [result, result, coarse, eight, eight], ab, ws, lapm, dc12
    )
    for at, (slices, hosts) in enumerate(GROUPS[1:], 1):
        z = hop(*sent, GROUPS[at - 1][1], hosts)
        if at == 1:
            z = list(lax.optimization_barrier(tuple(z)))
            b0 = moved(after(b2, z[0]), forward[2], forward[6])
            *z, short, long = lax.optimization_barrier((*z, short, long))
            late = moved(after(b2, z[0]), *forward[:2], *forward[3:6])
        elif at == 2:
            *z, b0 = lax.optimization_barrier((*z, b0))
        elif at == 3:
            *z, late, home, away = lax.optimization_barrier((*z, late, home, away))
        else:
            other, one = moved(away, *back), moved(home, *first)
            *z, other, one, home = lax.optimization_barrier((*z, other, one, home))
        if len(slices) == 2:
            depth = 4 * len(GROUPS[at + 1][0])
            *sent, za, zb, zc = call(
                functools.partial(pair_kernel, slices, hosts, depth),
                "pair",
                [coarse, field(depth, CP), field(depth, CP), field(ROWS + 12, CP), field(ROWS + 8, CP), field(ROWS + 4, CP)],
                *(*z, abx, short, long, ws, lapm, dc12),
                scratch=[field(ROWS + 16, CP)],
            )
            home, away = call(
                functools.partial(gather_kernel, slices, hosts),
                "gather",
                [result, result],
                *(z[0], za, zb, zc, sent[0], home, away),
                alias={5: 0, 6: 1},
            )
    out = call(
        out_kernel,
        "out",
        field(3, SPECIES, ROWS),
        *(species_map[:, 0], nodes, b0, late, b1, b2, share, *z, ab, ws, lapm, dc12, home, one, other),
        out_specs=ANY,
        scratch=[result, field(ROWS + 4, CP), field(ROWS + 8, CP), field(3, CP, ROWS), field(3, SPECIES, ROWS), pltpu.SemaphoreType.DMA((3,))],
    )
    return out[None]


def solution(mesh):
    in_specs = (P("tm", None, None, "space", None), P(), P(), P(), P(), P(), P(), P())
    out_specs = P("tm", None, None, "space", None)
    return jax.shard_map(local, mesh=mesh, in_specs=in_specs, out_specs=out_specs, check_vma=False)
```

```python
import functools

import jax
import jax.numpy as jnp
from jax import lax
from jax.experimental import pallas as pl
from jax.experimental.pallas import tpu as pltpu
from jax.sharding import PartitionSpec as P

SPECIES, COARSE = 53, 21
SP, CP = 56, 24
ROWS, COLS = 16, 256
SLICES, SLABS = 8, 16
STEP, HALF, RELAX = 0.1, 0.05, 3.0
W0 = (5.0 / 24.0, 1.0 / 3.0, -1.0 / 24.0)
W1 = (-1.0 / 24.0, 1.0 / 3.0, 5.0 / 24.0)
F32, BF16 = jnp.float32, jnp.bfloat16
GROUPS = (((0,), (0, 0)), ((1, 2), (1, 5)), ((3, 4), (3, 4)), ((5, 6), (5, 6)), ((7,), (7, 7)))
VMEM_LIMIT = 24 * 1024 * 1024


def split(x):
    hi = x.astype(BF16)
    lo = (x - hi.astype(F32)).astype(BF16)
    return jnp.concatenate([hi, lo], axis=0)


def thirds(x):
    hi = x.astype(BF16)
    rest = x - hi.astype(F32)
    mid = rest.astype(BF16)
    return jnp.concatenate([hi, mid, (rest - mid.astype(F32)).astype(BF16)], axis=0)


def zeros(rows):
    return jnp.zeros((rows, COLS), F32)


def dot(w, x):
    return jnp.dot(w, x, preferred_element_type=F32)


def two_terms(x):
    return jnp.concatenate([x, x - x.astype(BF16).astype(F32)], axis=0).astype(BF16)


def stacked(x, squares):
    return split(jnp.concatenate([x, squares], axis=0))


def lap_y(x):
    near = pltpu.roll(x, 1, 1) + pltpu.roll(x, COLS - 1, 1)
    far = pltpu.roll(x, 2, 1) + pltpu.roll(x, COLS - 2, 1)
    return 16.0 * near - far - 60.0 * x


def lap_rows(ref, x):
    return 16.0 * (ref[x - 1] + ref[x + 1]) - (ref[x - 2] + ref[x + 2])


def beside(near, far):
    return 16.0 * near - far, -near


RATES, PAIRS, CRATES, CPAIRS, DIFF, CDIFF, MAP, RAW = 0, 56, 112, 136, 160, 161, 162, 168


def prep_kernel(raw, wf, wr, wfr, lv, wc, ws, lapm, pro, d12, dc12, share):
    row = lax.broadcasted_iota(jnp.int32, (SP, 128), 0)
    lane = lax.broadcasted_iota(jnp.int32, (SP, 128), 1)

    def halves(x):
        hi = x.astype(BF16).astype(F32)
        return hi, (x - hi).astype(BF16).astype(F32)

    def column(values, height):
        return jnp.sum(jnp.where(row == lane, values, 0.0), axis=1, keepdims=True)[:height]

    eye = jnp.where(row == lane, RELAX, 0.0)
    fine = raw[RATES : RATES + SP, :] - jnp.where(row < SPECIES, eye, 0.0)
    fine = fine + pltpu.roll(raw[PAIRS : PAIRS + SP, :], SP, 1)
    coarse = raw[CRATES : CRATES + CP, :] - jnp.where(row < COARSE, eye, 0.0)[:CP]
    coarse = coarse + pltpu.roll(raw[CPAIRS : CPAIRS + CP, :], CP, 1)
    vectors = raw[DIFF : DIFF + 8, :]
    diff_row = vectors[0:1]
    d12[...] = jnp.broadcast_to(column(diff_row, SP) / 12.0, (SP, COLS))
    dc12[...] = jnp.broadcast_to(column(vectors[1:2], CP) / 12.0, (CP, COLS))
    map_row = jnp.where(lane[0:1] < SPECIES, vectors[2:3].astype(jnp.int32), -1)
    map_column = jnp.sum(jnp.where(row == lane, map_row, 0), axis=1, keepdims=True)
    map_column = jnp.where(row[:, 0:1] < SPECIES, map_column, -1)
    lum = jnp.where((map_row == row[:CP]) & (lane[:CP] < SPECIES), 1.0, 0.0)
    counts = jnp.sum(lum, axis=1, keepdims=True)
    share[...] = jnp.broadcast_to(1.0 / jnp.maximum(counts, 1.0), (CP, COLS))
    lumped = jnp.dot(lum[:, :SP], fine, precision=lax.Precision.HIGHEST, preferred_element_type=F32)
    fh, fl = halves(fine)
    rh, rl = halves(lumped)
    dh, dl = halves(lum * diff_row)
    ch, cl = halves(coarse)
    f = jnp.concatenate([fh, fl], axis=0)
    r = jnp.concatenate([rh, rl, lum, dh, dl, jnp.zeros((8, 128), F32)], axis=0)

    def twice(w, width):
        w = jnp.concatenate([w, jnp.zeros_like(w)], axis=1)
        return (w + pltpu.roll(w, width, 1))[:, : 2 * width].astype(BF16)

    wf[...] = twice(f, 2 * SP)
    wr[...] = twice(r, 2 * SP)
    wfr[: 2 * SP, :] = twice(f, 2 * SP)
    wfr[2 * SP :, :] = twice(r, 2 * SP)
    v = jnp.concatenate([lum, dh, dl, jnp.zeros((8, 128), F32)], axis=0)
    lv[...] = (v + pltpu.roll(v, 64, 1)).astype(BF16)
    c = jnp.concatenate([ch, cl], axis=0)
    wc[...] = twice(c, 2 * CP)
    linear, pairs = jnp.where(lane[: 2 * CP] < CP, c, 0.0), jnp.where(lane[: 2 * CP] < CP, 0.0, c)
    both_terms = linear + pltpu.roll(linear, CP, 1) + pltpu.roll(pairs, CP, 1) + pltpu.roll(pairs, 2 * CP, 1)
    ws[...] = both_terms[:, : 4 * CP].astype(BF16)
    far = lax.broadcasted_iota(jnp.int32, (COLS, COLS), 0) - lax.broadcasted_iota(jnp.int32, (COLS, COLS), 1)
    far = jnp.abs(far)
    far = jnp.minimum(far, COLS - far)
    lapm[...] = jnp.where(far == 0, -60.0, jnp.where(far == 1, 16.0, jnp.where(far == 2, -1.0, 0.0))).astype(BF16)
    lane96 = lax.broadcasted_iota(jnp.int32, (SP, 96), 1)
    pro[...] = jnp.where(map_column == lane96 % 32, 1.0, 0.0).astype(BF16)


class Position:
    def __init__(self):
        self.slice_at, self.slab = lax.axis_index("tm"), lax.axis_index("space")

    def __getitem__(self, at):
        return (self.slab % 2, self.slice_at, self.slab)[at]


def blocks(rows, body, size=4):
    @pl.loop(0, rows // size)
    def _(i):
        body([size * i + k for k in range(size)])


def first_kernel(u, weights_made, outer, inner):
    info = Position()
    at_top = info[0] == 0
    for m in range(3):
        for r in range(2):
            first, last = u[m, :, r, :], u[m, :, ROWS - 2 + r, :]
            for out, value in ((outer, jnp.where(at_top, first, last)), (inner, jnp.where(at_top, last, first))):
                out[m, r, SP - 8 :, :] = zeros(8)
                out[m, r, :SPECIES, :] = value


def restricted(y):
    return y[0:24] + y[24:48], y[48:72], y[72:96] + y[96:120]


MIX0 = [STEP * w for w in W0]
MIXS = [STEP * W1[0], STEP * W1[1] - HALF, STEP * W1[2]]


def mixed(factors, values):
    return factors[0] * values[0] + factors[1] * values[1] + factors[2] * values[2]


def old_kernel(u, wf, wr, wc, d12, dc12, n1, s, r0, e0, c0, ut, p0s, pss, v0s, c0s):
    for k in range(4):
        for m in range(3):
            ut[k, m, SP - 8 :, :] = zeros(8)
    for x in (0, 1, ROWS + 2, ROWS + 3):
        p0s[x], pss[x], v0s[x], c0s[x] = zeros(SP), zeros(SP), zeros(CP), zeros(CP)

    def terms(xs):
        for k, x in enumerate(xs):
            for m in range(3):
                ut[k, m, :SPECIES, :] = u[m, :, x, :]
        for k, x in enumerate(xs):
            us = [ut[k, m] for m in range(3)]
            qs = [v * v for v in us]
            p0, ps = mixed(MIX0, us), mixed(MIXS, us)
            y = dot(wf[...], stacked(p0, mixed(MIX0, qs)))
            n1[x] = us[0] + (y[:SP] + y[SP:]) + d12[...] * lap_y(p0)
            y = dot(wf[...], stacked(ps, mixed(MIXS, qs)))
            s[x] = (y[:SP] + y[SP:]) + d12[...] * lap_y(ps)
            r, c, v = restricted(dot(wr[...], stacked(us[0], qs[0])))
            r0[x] = r + lap_y(v) * (1.0 / 12.0)
            y = dot(wc[...], stacked(c, c * c))
            e0[x] = (y[:CP] + y[CP:]) + dc12[...] * lap_y(c)
            p0s[x + 2], pss[x + 2], v0s[x + 2], c0s[x + 2], c0[x] = p0, ps, v, c, c

    blocks(ROWS, terms)

    def laps(xs):
        for x in xs:
            n1[x] += d12[...] * lap_rows(p0s, x + 2)
            s[x] += d12[...] * lap_rows(pss, x + 2)
            r0[x] += lap_rows(v0s, x + 2) * (1.0 / 12.0)
            e0[x] += dc12[...] * lap_rows(c0s, x + 2)

    blocks(ROWS, laps)


def lumped_halo(lv, row):
    y = dot(lv[...], split(jnp.concatenate([row, zeros(8)], axis=0)))
    return y[0:24], y[24:48] + y[48:72]


SIDES = (((0, 1), (1, 0)), ((ROWS - 1, ROWS - 2), (0, 1)))


def packed_rows(rows):
    return (COARSE * (rows - 1) + CP + 7) // 8 * 8


def get(ref, r):
    return ref[COARSE * r : COARSE * r + CP, :]


def put(ref, r, value):
    ref[COARSE * r : COARSE * r + CP, :] = value


def pick_packed(info, side, outer, inner):
    take = info[0] == side
    return lambda r: jnp.where(take, get(outer, r), get(inner, r))


def send_packed(info, outer, inner, tops, bottoms):
    at_top = info[0] == 0
    for r, (top, bottom) in enumerate(zip(tops, bottoms)):
        put(outer, r, jnp.where(at_top, top, bottom))
        put(inner, r, jnp.where(at_top, bottom, top))


def pick_halo(info, side, outer, inner):
    take = info[0] == side
    return lambda *at: jnp.where(take, outer[at], inner[at])


def send(info, outer, inner, tops, bottoms):
    at_top = info[0] == 0
    for r, (top, bottom) in enumerate(zip(tops, bottoms)):
        outer[r] = jnp.where(at_top, top, bottom)
        inner[r] = jnp.where(at_top, bottom, top)


def old_edge_kernel(uo, ui, lv, d12, dc12, n1i, si, r0i, e0i, n1, s, r0, e0, outer, inner):
    info = Position()
    for side, (rows, order) in enumerate(SIDES):
        halo = pick_halo(info, side, uo, ui)
        us = [[halo(m, r) for m in range(3)] for r in order]
        p0 = beside(*[mixed(MIX0, v) for v in us])
        ps = beside(*[mixed(MIXS, v) for v in us])
        lumped = [lumped_halo(lv, v[0]) for v in us]
        c = beside(lumped[0][0], lumped[1][0])
        v = beside(lumped[0][1], lumped[1][1])
        for i, x in enumerate(rows):
            n1[x] = n1i[x] + d12[...] * p0[i]
            s[x] = si[x] + d12[...] * ps[i]
            r0[x] = r0i[x] + v[i] * (1.0 / 12.0)
            e0[x] = e0i[x] + dc12[...] * c[i]
    send(info, outer, inner, [n1[0], n1[1]], [n1[ROWS - 2], n1[ROWS - 1]])


def mid_kernel(n1, s, wfr, wc, d12, dc12, n2, r1, e1, c1, n1s, v1s, c1s):
    for x in (0, 1, ROWS + 2, ROWS + 3):
        n1s[x], v1s[x], c1s[x] = zeros(SP), zeros(CP), zeros(CP)

    def terms(xs):
        for x in xs:
            n = n1[x]
            y = dot(wfr[...], stacked(n, n * n))
            n2[x] = n + HALF * ((y[:SP] + y[SP : 2 * SP]) + d12[...] * lap_y(n)) + s[x]
            r, c, v = restricted(y[2 * SP :])
            r1[x] = r + lap_y(v) * (1.0 / 12.0)
            y = dot(wc[...], stacked(c, c * c))
            e1[x] = (y[:CP] + y[CP:]) + dc12[...] * lap_y(c)
            n1s[x + 2], v1s[x + 2], c1s[x + 2], c1[x] = n, v, c, c

    blocks(ROWS, terms, 8)

    def laps(xs):
        for x in xs:
            n2[x] += (HALF * d12[...]) * lap_rows(n1s, x + 2)
            r1[x] += lap_rows(v1s, x + 2) * (1.0 / 12.0)
            e1[x] += dc12[...] * lap_rows(c1s, x + 2)

    blocks(ROWS, laps, 8)


def lumped_old(first, c0, e0):
    return jnp.where(first, c0, -HALF * e0)


AB_ROWS, EXT_ROWS = 2 * ROWS + 4, 2 * ROWS + 20
A0, B0 = 2, ROWS + 4
XA0, XB0 = 6, ROWS + 16


def mid_edge_kernel(no, ni, lv, wr, d12, dc12, r0, e0, c0, n2i, r1i, e1i, n2, r1, e1, ab, c2, outer, inner, v2s, gs):
    info = Position()
    first = info[1] == 0
    for side, (rows, order) in enumerate(SIDES):
        halo = pick_halo(info, side, no, ni)
        ns = [halo(r) for r in order]
        lumped = [lumped_halo(lv, v) for v in ns]
        c = beside(lumped[0][0], lumped[1][0])
        v = beside(lumped[0][1], lumped[1][1])
        n = beside(*ns)
        for i, x in enumerate(rows):
            n2[x] = n2i[x] + (HALF * d12[...]) * n[i]
            r1[x] = r1i[x] + v[i] * (1.0 / 12.0)
            e1[x] = e1i[x] + dc12[...] * c[i]
    for x in (0, 1, ROWS + 2, ROWS + 3):
        v2s[x] = zeros(CP)

    def lumped(x, value):
        gs[x], c2[x], v2s[x + 2] = restricted(dot(wr[...], stacked(value, value * value)))

    def pieces(x, mid, late):
        v = v2s[x + 2]
        g2 = gs[x] + (lap_y(v) + lap_rows(v2s, x + 2)) * (1.0 / 12.0)
        ab[x + XA0] = mixed(MIX0, (r0[x], mid, g2)) + lumped_old(first, c0[x], e0[x])
        ab[x + XB0] = mixed([STEP * w for w in W1], (r0[x], mid, g2)) - HALF * late

    edges = (0, 1, ROWS - 2, ROWS - 1)
    for x in edges:
        lumped(x, n2[x])
    blocks(ROWS - 4, lambda xs: [lumped(x + 2, n2i[x + 2]) for x in xs], ROWS - 4)
    for x in edges:
        pieces(x, r1[x], e1[x])
    blocks(ROWS - 4, lambda xs: [pieces(x + 2, r1i[x + 2], e1i[x + 2]) for x in xs], ROWS - 4)
    top = [ab[x + XA0] for x in range(6)] + [ab[x + XB0] for x in range(4)] + [v2s[x + 2] for x in range(2)]
    bottom = [ab[x + XA0] for x in range(ROWS - 6, ROWS)] + [ab[x + XB0] for x in range(ROWS - 4, ROWS)]
    send_packed(info, outer, inner, top, bottom + [v2s[x] for x in range(ROWS, ROWS + 2)])


def last_edge_kernel(mo, mi, ho, hi, abi, ab, short):
    info = Position()
    ka, kb = STEP * W0[2] / 12.0, STEP * W1[2] / 12.0
    done = {}
    for side, (rows, order) in enumerate(SIDES):
        inside = info[2] > 0 if side == 0 else info[2] < SLABS - 1
        own, halo = pick_packed(info, side, mo, mi), pick_packed(info, side, ho, hi)
        fix = beside(*[halo(10 + r) for r in order])
        theirs = beside(*[own(10 + r) for r in order[::-1]])
        for i, x in enumerate(rows):
            done[x + XA0] = abi[x + XA0] + ka * fix[i]
            done[x + XB0] = abi[x + XB0] + kb * fix[i]
        for depth, at, to, factor in ((6, 0, XA0, ka), (4, 6, XB0, kb)):
            for i in range(depth):
                x = -1 - i if side == 0 else ROWS + i
                value = halo(at + (depth - 1 - i if side == 0 else i))
                if i < 2:
                    value = value + factor * theirs[i]
                done[x + to] = jnp.where(inside, value, 0.0)
    for at, value in done.items():
        ab[at] = value
    for x in range(-2, ROWS + 2):
        short[x + A0] = done[x + XA0] if x + XA0 in done else abi[x + XA0]
    for x in range(ROWS):
        short[x + B0] = done[x + XB0] if x + XB0 in done else abi[x + XB0]


def sweep(info, z, z0, add, add0, out, out0, low, rows, ws, lapm, dc12):
    size = rows // 2

    def body(xs):
        zr = [z[xs[0] + (low + z0 + k)] for k in range(-2, size + 2)]
        terms = [two_terms(value) for value in zr[2:-2]]
        laps = dot(jnp.concatenate(terms, axis=0), lapm[...])
        for k in range(size):
            x, value = xs[k] + low, zr[k + 2]
            y = dot(ws[...], jnp.concatenate([terms[k], two_terms(value * value)], axis=0))
            lap = laps[2 * CP * k : 2 * CP * k + CP] + laps[2 * CP * k + CP : 2 * CP * (k + 1)]
            lap = lap + 16.0 * (zr[k + 1] + zr[k + 3]) - (zr[k] + zr[k + 4])
            value = value + HALF * ((y[:CP] + y[CP:]) + dc12[...] * lap) + add[x + add0]
            if low < 0:
                inside = ((x >= 0) | (info[2] > 0)) & ((x < ROWS) | (info[2] < SLABS - 1))
                value = jnp.where(inside, value, 0.0)
            out[x + out0] = value

    blocks(rows, body, size)


def begin(info, z0, zo, zi, depth, zs):
    top, bottom = pick_packed(info, 0, zo, zi), pick_packed(info, 1, zo, zi)
    for r in range(depth):
        zs[r], zs[depth + ROWS + r] = top(r), bottom(r)
    for x in range(ROWS):
        zs[depth + x] = get(z0, x)


def give(info, depth, message, packed, outer, inner):
    for x in range(ROWS):
        put(packed, x, message[x])
    ends = [message[x] for x in range(depth)], [message[x] for x in range(ROWS - depth, ROWS)]
    send_packed(info, outer, inner, *ends)


def hosting(info, hosts):
    return info[1] == jnp.where(info[0] == 0, hosts[0], hosts[1])


def start_kernel(hosts, ab, ws, lapm, dc12, result, unused, packed, outer, inner, message):
    info = Position()

    @pl.when(hosting(info, hosts))
    def _():
        sweep(info, ab, A0, ab, B0, message, 0, 0, ROWS, ws, lapm, dc12)
        give(info, 8, message, packed, outer, inner)

        def body(xs):
            for x in xs:
                result[x], result[ROWS + x], result[2 * ROWS + x] = zeros(CP), ab[x + A0], message[x]

        blocks(ROWS, body)


def pair_kernel(
    slices, hosts, depth, z0, zo, zi, mine, short, long, ws, lapm, dc12, packed, outer, inner, za, zb, zc, message, zs
):
    info = Position()

    def sweeps(one, two):
        begin(info, z0, zo, zi, 8, zs)
        sweep(info, zs, 8, one, XA0, za, 6, -6, ROWS + 12, ws, lapm, dc12)
        sweep(info, za, 6, one, XB0, zb, 4, -4, ROWS + 8, ws, lapm, dc12)
        if two is mine:
            sweep(info, zb, 4, two, XA0, zc, 2, -2, ROWS + 4, ws, lapm, dc12)
            sweep(info, zc, 2, two, XB0, message, 0, 0, ROWS, ws, lapm, dc12)
        else:
            sweep(info, zb, 4, two, A0, zc, 2, -2, ROWS + 4, ws, lapm, dc12)
            sweep(info, zc, 2, two, B0, message, 0, 0, ROWS, ws, lapm, dc12)
        give(info, depth, message, packed, outer, inner)

    for host in sorted(set(hosts)):
        one = mine if host == slices[0] else long
        two = mine if host == slices[1] else short
        pl.when(hosting(info, hosts) & (info[1] == host))(functools.partial(sweeps, one, two))


def gather(zs, za, zb, zc, z2, one, two, away):
    for at, result in ((0, one), (1, two)):
        values = [lambda x: zs[x + 8], lambda x: za[x + 6], lambda x: zb[x + 4], lambda x: zc[x + 2], lambda x: z2[x]]
        for part, value in enumerate(values[2 * at : 2 * at + 3]):
            for x in range(ROWS):
                if at == away:
                    put(result, part * ROWS + x, value(x))
                else:
                    result[part * ROWS + x] = value(x)


def gather_kernel(slices, hosts, zs, za, zb, zc, z2, home_in, away_in, home, away):
    info = Position()
    active, second = hosting(info, hosts), info[1] == slices[1]
    pl.when(active & ~second)(lambda: gather(zs, za, zb, zc, z2, home, away, 1))
    if slices[1] in hosts:
        pl.when(active & second)(lambda: gather(zs, za, zb, zc, z2, away, home, 0))


def base_kernel(n1, n2, c1, c2, pro, share, b1, b2):
    def body(xs):
        for x in xs:
            for n, c, b in ((n1, c1, b1), (n2, c2, b2)):
                value = thirds(jnp.concatenate([share[...] * c[x], zeros(8)], axis=0))
                b[:, x, :] = (n[x] - dot(pro[...], value))[:SPECIES]

    blocks(ROWS, body)


def out_kernel(
    where, u, b0, late, b1, b2, share, z0, zo, zi, ab, ws, lapm, dc12, home, one, other, out, z, za, zs, spread, node, sem
):
    info = Position()
    last = info[1] == SLICES - 1
    at_home = hosting(info, GROUPS[0][1])
    for slices, hosts in GROUPS[1:-1]:
        at_home = at_home | (hosting(info, hosts) & ((info[1] == slices[0]) | (info[1] == slices[1])))
    first = info[1] == GROUPS[1][0][0]
    for here, result in ((at_home, home), (first & ~at_home, one)):

        @pl.when(here)
        def _():

            def body(xs):
                for x in xs:
                    z[x] = result[x]

            blocks(3 * ROWS, body)

    @pl.when(~at_home & ~first & ~last)
    def _():
        for x in range(3 * ROWS):
            z[x] = get(other, x)

    @pl.when(last)
    def _():
        begin(info, z0, zo, zi, 4, zs)

        def body(xs):
            for x in xs:
                z[x] = zs[x + 4]

        blocks(ROWS, body)

    def finish(m, base):
        def body(xs):
            for x in xs:
                spread[m, :, x, :] = share[...] * z[m * ROWS + x]

        blocks(ROWS, body, ROWS)

        def add(s):
            node[m, s] = base(s) + spread[m, where[s]]

        blocks(SPECIES, lambda at: [add(s) for s in at], 13)
        add(SPECIES - 1)
        copy = pltpu.make_async_copy(node.at[m], out.at[m], sem.at[m])
        copy.start()
        return copy

    first = info[1] == 0
    copies = [finish(0, lambda s: jnp.where(first, u[0, s], b0[s] + late[s]))]

    @pl.when(last)
    def _():
        sweep(info, zs, 4, ab, A0, za, 2, -2, ROWS + 4, ws, lapm, dc12)
        sweep(info, za, 2, ab, B0, z.at[pl.ds(2 * ROWS, ROWS)], 0, 0, ROWS, ws, lapm, dc12)

        def body(xs):
            for x in xs:
                z[ROWS + x] = za[x + 2]

        blocks(ROWS, body)

    copies += [finish(1, lambda s: b1[s]), finish(2, lambda s: b2[s])]
    for copy in copies:
        copy.wait()


def field(*shape):
    return jax.ShapeDtypeStruct(shape + (COLS,), F32)


SMEM = pl.BlockSpec(memory_space=pltpu.SMEM)
VMEM = pl.BlockSpec(memory_space=pltpu.VMEM)
ANY = pl.BlockSpec(memory_space=pl.ANY)


def call(kernel, name, outs, *args, scratch=(), alias=None, out_specs=None, specs=None):
    specs = specs or [SMEM if a.dtype == jnp.int32 and a.ndim == 1 else VMEM for a in args]
    return pl.pallas_call(
        kernel,
        out_shape=outs,
        in_specs=specs,
        **({"out_specs": out_specs} if out_specs else {}),
        scratch_shapes=[pltpu.VMEM(f.shape, f.dtype) if isinstance(f, jax.ShapeDtypeStruct) else f for f in scratch],
        input_output_aliases=alias or {},
        compiler_params=pltpu.CompilerParams(vmem_limit_bytes=VMEM_LIMIT),
        name=name,
    )(*args)


AXES = ("tm", "space")
OUTER = [(s, s + 1) for s in range(1, SLABS - 1, 2)] + [(s + 1, s) for s in range(1, SLABS - 1, 2)]
INNER = [(s, s ^ 1) for s in range(SLABS)]
SAME = [(s, s) for s in range(SLABS)]


def moved(value, *routes):
    pairs = [
        (source[s % 2] * SLABS + s, target[t % 2] * SLABS + t) for source, target, slabs in routes for s, t in slabs
    ]
    return lax.ppermute(value, AXES, pairs)


def both(p):
    return (p, p)


def swap(outer, inner):
    got_inner = moved(inner, *[(both(p), both(p), INNER) for p in range(SLICES)])
    got_outer = moved(outer, *[(both(p), both(p), OUTER) for p in range(SLICES)])
    return got_outer, got_inner


def hop(message, outer, inner, source, target):
    parts = ((outer, OUTER), (inner, INNER), (message, SAME))
    zo, zi, z = [moved(value, (source, target, slabs)) for value, slabs in parts]
    return [z, zo, zi]


def after(value, other):
    return lax.optimization_barrier((value, other))[0]


def local(fine_nodes, fine_rates, fine_pairs, fine_diff, coarse_rates, coarse_pairs, coarse_diff, species_map):
    nodes = fine_nodes[0]
    fine, coarse = field(ROWS, SP), field(ROWS, CP)
    message = field(3, 2, SP)
    def bf16(*shape):
        return jax.ShapeDtypeStruct(shape, BF16)

    raw = sum(
        jnp.pad(v.astype(F32), ((at, RAW - at - v.shape[0]), (0, 128 - v.shape[1])))
        for at, v in (
            (RATES, fine_rates),
            (PAIRS, fine_pairs),
            (CRATES, coarse_rates),
            (CPAIRS, coarse_pairs),
            (DIFF, fine_diff.reshape(1, SPECIES)),
            (CDIFF, coarse_diff.reshape(1, COARSE)),
            (MAP, species_map.reshape(1, SPECIES)),
        )
    )
    wf, wr, wfr, lv, wc, ws, lapm, pro, d12, dc12, share = call(
        prep_kernel,
        "prep",
        [bf16(2 * SP, 4 * SP), bf16(128, 4 * SP), bf16(2 * SP + 128, 4 * SP), bf16(80, 128), bf16(2 * CP, 4 * CP), bf16(2 * CP, 4 * CP)]
        + [bf16(COLS, COLS), bf16(SP, 96)]
        + [field(SP), field(CP), field(CP)],
        raw,
    )
    outer, inner = call(first_kernel, "first", [message, message], nodes, wc)
    uo, ui = swap(outer, inner)

    n1, s, r0, e0, c0 = call(
        old_kernel,
        "old",
        [fine, fine, coarse, coarse, coarse],
        *(nodes, wf, wr, wc, d12, dc12),
        scratch=[field(4, 3, SP), field(ROWS + 4, SP), field(ROWS + 4, SP), field(ROWS + 4, CP), field(ROWS + 4, CP)],
    )
    two, twelve = field(2, SP), field(packed_rows(12))
    n1, s, r0, e0, outer, inner = call(
        old_edge_kernel,
        "old_edge",
        [fine, fine, coarse, coarse, two, two],
        *(uo, ui, lv, d12, dc12, n1, s, r0, e0),
        alias={5: 0, 6: 1, 7: 2, 8: 3},
    )
    no, ni = swap(outer, inner)
    n2, r1, e1, c1 = call(
        mid_kernel, "mid", [fine, coarse, coarse, coarse], n1, s, wfr, wc, d12, dc12, scratch=[field(ROWS + 4, SP), field(ROWS + 4, CP), field(ROWS + 4, CP)]
    )
    extended, short = field(EXT_ROWS, CP), field(AB_ROWS, CP)
    n2, r1, e1, abx, c2, outer, inner = call(
        mid_edge_kernel,
        "mid_edge",
        [fine, coarse, coarse, extended, coarse, twelve, twelve],
        *(no, ni, lv, wr, d12, dc12, r0, e0, c0, n2, r1, e1),
        alias={9: 0, 10: 1, 11: 2},
        scratch=[field(ROWS + 4, CP), coarse],
    )
    ho, hi = swap(outer, inner)
    b1, b2 = call(base_kernel, "base", [field(SPECIES, ROWS)] * 2, n1, n2, c1, c2, pro, share)
    abx, ab = call(last_edge_kernel, "last_edge", [extended, short], outer, inner, ho, hi, abx, alias={4: 0})

    ab, abx = after(ab, b1), after(abx, b1)
    result, away_result = field(3 * ROWS, CP), field(packed_rows(3 * ROWS))
    bulk, ends = field(packed_rows(ROWS)), field(packed_rows(8))
    pairs = [(slices, hosts) for slices, hosts in GROUPS if len(slices) == 2]
    short, long, back, first = [], [], [], []
    for slices, hosts in pairs:
        for core, host in enumerate(hosts):
            slabs = [(t, t) for t in range(core, SLABS, 2)]
            if host != slices[0]:
                long.append((both(slices[0]), both(host), slabs))
            if host != slices[1]:
                short.append((both(slices[1]), both(host), slabs))
            back.append((both(host), both(slices[0] if host == slices[1] else slices[1]), slabs))
            if host not in slices:
                first.append((both(host), both(slices[0]), slabs))
    short, long = moved(ab, *short), moved(abx, *long)
    forward = [(both(p), both(p + 1), SAME) for p in range(SLICES - 1)]
    home, away, *sent = call(
        functools.partial(start_kernel, GROUPS[0][1]), "start", [result, away_result, bulk, ends, ends], ab, ws, lapm, dc12, scratch=[coarse]
    )
    for at, (slices, hosts) in enumerate(GROUPS[1:], 1):
        z = hop(*sent, GROUPS[at - 1][1], hosts)
        if at == 1:
            z = list(lax.optimization_barrier(tuple(z)))
            b0 = moved(after(b2, z[0]), forward[2], forward[6])
            *z, short, long = lax.optimization_barrier((*z, short, long))
            late = moved(after(b2, z[0]), *forward[:2], *forward[3:6])
        elif at == 2:
            *z, b0 = lax.optimization_barrier((*z, b0))
        elif at == 3:
            *z, late, home, away = lax.optimization_barrier((*z, late, home, away))
        else:
            other, one = moved(away, *back), moved(home, *first)
            *z, other, one, home = lax.optimization_barrier((*z, other, one, home))
        if len(slices) == 2:
            depth = 4 * len(GROUPS[at + 1][0])
            ends = field(packed_rows(depth))
            *sent, za, zb, zc, z2, zs = call(
                functools.partial(pair_kernel, slices, hosts, depth),
                "pair",
                [bulk, ends, ends, field(ROWS + 12, CP), field(ROWS + 8, CP), field(ROWS + 4, CP), coarse, field(ROWS + 16, CP)],
                *(*z, abx, short, long, ws, lapm, dc12),
            )
            home, away = call(
                functools.partial(gather_kernel, slices, hosts),
                "gather",
                [result, away_result],
                *(zs, za, zb, zc, z2, home, away),
                alias={5: 0, 6: 1},
            )
    out = call(
        out_kernel,
        "out",
        field(3, SPECIES, ROWS),
        *(species_map[:, 0], nodes, b0, late, b1, b2, share, *z, ab, ws, lapm, dc12, home, one, other),
        out_specs=ANY,
        scratch=[result, field(ROWS + 4, CP), field(ROWS + 8, CP), field(3, CP, ROWS), field(3, SPECIES, ROWS), pltpu.SemaphoreType.DMA((3,))],
    )
    return out[None]


def solution(mesh):
    in_specs = (P("tm", None, None, "space", None), P(), P(), P(), P(), P(), P(), P())
    out_specs = P("tm", None, None, "space", None)
    return jax.shard_map(local, mesh=mesh, in_specs=in_specs, out_specs=out_specs, check_vma=False)
```

```python
import functools

import jax
import jax.numpy as jnp
from jax import lax
from jax.experimental import pallas as pl
from jax.experimental.pallas import tpu as pltpu
from jax.sharding import PartitionSpec as P

SPECIES, COARSE = 53, 21
SP, CP = 56, 24
ROWS, COLS = 16, 256
SLICES, SLABS = 8, 16
STEP, HALF, RELAX = 0.1, 0.05, 3.0
W0 = (5.0 / 24.0, 1.0 / 3.0, -1.0 / 24.0)
W1 = (-1.0 / 24.0, 1.0 / 3.0, 5.0 / 24.0)
F32, BF16 = jnp.float32, jnp.bfloat16
GROUPS = (((0,), (0, 0)), ((1, 2), (1, 5)), ((3, 4), (3, 4)), ((5, 6), (5, 6)), ((7,), (7, 7)))
VMEM_LIMIT = 24 * 1024 * 1024


def split(x):
    hi = x.astype(BF16)
    lo = (x - hi.astype(F32)).astype(BF16)
    return jnp.concatenate([hi, lo], axis=0)


def thirds(x):
    hi = x.astype(BF16)
    rest = x - hi.astype(F32)
    mid = rest.astype(BF16)
    return jnp.concatenate([hi, mid, (rest - mid.astype(F32)).astype(BF16)], axis=0)


def zeros(rows):
    return jnp.zeros((rows, COLS), F32)


def dot(w, x):
    return jnp.dot(w, x, preferred_element_type=F32)


def two_terms(x):
    return jnp.concatenate([x, x - x.astype(BF16).astype(F32)], axis=0).astype(BF16)


def stacked(x, squares):
    return split(jnp.concatenate([x, squares], axis=0))


def lap_y(x):
    near = pltpu.roll(x, 1, 1) + pltpu.roll(x, COLS - 1, 1)
    far = pltpu.roll(x, 2, 1) + pltpu.roll(x, COLS - 2, 1)
    return 16.0 * near - far - 60.0 * x


def lap_rows(ref, x):
    return 16.0 * (ref[x - 1] + ref[x + 1]) - (ref[x - 2] + ref[x + 2])


def beside(near, far):
    return 16.0 * near - far, -near


RATES, PAIRS, CRATES, CPAIRS, DIFF, CDIFF, MAP, RAW = 0, 56, 112, 136, 160, 161, 162, 168


def prep_kernel(raw, wf, wr, wfr, lv, wc, ws, lapm, pro, d12, dc12, share):
    row = lax.broadcasted_iota(jnp.int32, (SP, 128), 0)
    lane = lax.broadcasted_iota(jnp.int32, (SP, 128), 1)

    def halves(x):
        hi = x.astype(BF16).astype(F32)
        return hi, (x - hi).astype(BF16).astype(F32)

    def column(values, height):
        return jnp.sum(jnp.where(row == lane, values, 0.0), axis=1, keepdims=True)[:height]

    eye = jnp.where(row == lane, RELAX, 0.0)
    fine = raw[RATES : RATES + SP, :] - jnp.where(row < SPECIES, eye, 0.0)
    fine = fine + pltpu.roll(raw[PAIRS : PAIRS + SP, :], SP, 1)
    coarse = raw[CRATES : CRATES + CP, :] - jnp.where(row < COARSE, eye, 0.0)[:CP]
    coarse = coarse + pltpu.roll(raw[CPAIRS : CPAIRS + CP, :], CP, 1)
    vectors = raw[DIFF : DIFF + 8, :]
    diff_row = vectors[0:1]
    d12[...] = jnp.broadcast_to(column(diff_row, SP) / 12.0, (SP, COLS))
    dc12[...] = jnp.broadcast_to(column(vectors[1:2], CP) / 12.0, (CP, COLS))
    map_row = jnp.where(lane[0:1] < SPECIES, vectors[2:3].astype(jnp.int32), -1)
    map_column = jnp.sum(jnp.where(row == lane, map_row, 0), axis=1, keepdims=True)
    map_column = jnp.where(row[:, 0:1] < SPECIES, map_column, -1)
    lum = jnp.where((map_row == row[:CP]) & (lane[:CP] < SPECIES), 1.0, 0.0)
    counts = jnp.sum(lum, axis=1, keepdims=True)
    share[...] = jnp.broadcast_to(1.0 / jnp.maximum(counts, 1.0), (CP, COLS))
    lumped = jnp.dot(lum[:, :SP], fine, precision=lax.Precision.HIGHEST, preferred_element_type=F32)
    fh, fl = halves(fine)
    rh, rl = halves(lumped)
    dh, dl = halves(lum * diff_row)
    ch, cl = halves(coarse)
    f = jnp.concatenate([fh, fl], axis=0)
    r = jnp.concatenate([rh, rl, lum, dh, dl, jnp.zeros((8, 128), F32)], axis=0)

    def twice(w, width):
        w = jnp.concatenate([w, jnp.zeros_like(w)], axis=1)
        return (w + pltpu.roll(w, width, 1))[:, : 2 * width].astype(BF16)

    wf[...] = twice(f, 2 * SP)
    wr[...] = twice(r, 2 * SP)
    wfr[: 2 * SP, :] = twice(f, 2 * SP)
    wfr[2 * SP :, :] = twice(r, 2 * SP)
    v = jnp.concatenate([lum, dh, dl, jnp.zeros((8, 128), F32)], axis=0)
    lv[...] = (v + pltpu.roll(v, 64, 1)).astype(BF16)
    c = jnp.concatenate([ch, cl], axis=0)
    wc[...] = twice(c, 2 * CP)
    linear, pairs = jnp.where(lane[: 2 * CP] < CP, c, 0.0), jnp.where(lane[: 2 * CP] < CP, 0.0, c)
    both_terms = linear + pltpu.roll(linear, CP, 1) + pltpu.roll(pairs, CP, 1) + pltpu.roll(pairs, 2 * CP, 1)
    ws[...] = both_terms[:, : 4 * CP].astype(BF16)
    far = lax.broadcasted_iota(jnp.int32, (COLS, COLS), 0) - lax.broadcasted_iota(jnp.int32, (COLS, COLS), 1)
    far = jnp.abs(far)
    far = jnp.minimum(far, COLS - far)
    lapm[...] = jnp.where(far == 0, -60.0, jnp.where(far == 1, 16.0, jnp.where(far == 2, -1.0, 0.0))).astype(BF16)
    lane96 = lax.broadcasted_iota(jnp.int32, (SP, 96), 1)
    pro[...] = jnp.where(map_column == lane96 % 32, 1.0, 0.0).astype(BF16)


class Position:
    def __init__(self):
        self.slice_at, self.slab = lax.axis_index("tm"), lax.axis_index("space")

    def __getitem__(self, at):
        return (self.slab % 2, self.slice_at, self.slab)[at]


def blocks(rows, body, size=4):
    @pl.loop(0, rows // size)
    def _(i):
        body([size * i + k for k in range(size)])


FIRST_ROWS = 328


def first_kernel(u, weights_made, outer, inner):
    info = Position()
    at_top = info[0] == 0
    for out in (outer, inner):
        out[FIRST_ROWS - 16 :, :] = zeros(16)
    for m in range(3):
        for r in range(2):
            first, last = u[m, :, r, :], u[m, :, ROWS - 2 + r, :]
            at = SPECIES * (2 * m + r)
            outer[at : at + SPECIES, :] = jnp.where(at_top, first, last)
            inner[at : at + SPECIES, :] = jnp.where(at_top, last, first)


def restricted(y):
    return y[0:24] + y[24:48], y[48:72], y[72:96] + y[96:120]


MIX0 = [STEP * w for w in W0]
MIXS = [STEP * W1[0], STEP * W1[1] - HALF, STEP * W1[2]]


def mixed(factors, values):
    return factors[0] * values[0] + factors[1] * values[1] + factors[2] * values[2]


def old_kernel(u, wf, wr, wc, d12, dc12, n1, s, r0, e0, c0, ut, p0s, pss, v0s, c0s):
    for k in range(4):
        for m in range(3):
            ut[k, m, SP - 8 :, :] = zeros(8)
    for x in (0, 1, ROWS + 2, ROWS + 3):
        p0s[x], pss[x], v0s[x], c0s[x] = zeros(SP), zeros(SP), zeros(CP), zeros(CP)

    def terms(xs):
        for k, x in enumerate(xs):
            for m in range(3):
                ut[k, m, :SPECIES, :] = u[m, :, x, :]
        for k, x in enumerate(xs):
            us = [ut[k, m] for m in range(3)]
            qs = [v * v for v in us]
            p0, ps = mixed(MIX0, us), mixed(MIXS, us)
            y = dot(wf[...], stacked(p0, mixed(MIX0, qs)))
            n1[x] = us[0] + (y[:SP] + y[SP:]) + d12[...] * lap_y(p0)
            y = dot(wf[...], stacked(ps, mixed(MIXS, qs)))
            s[x] = (y[:SP] + y[SP:]) + d12[...] * lap_y(ps)
            r, c, v = restricted(dot(wr[...], stacked(us[0], qs[0])))
            r0[x] = r + lap_y(v) * (1.0 / 12.0)
            y = dot(wc[...], stacked(c, c * c))
            e0[x] = (y[:CP] + y[CP:]) + dc12[...] * lap_y(c)
            p0s[x + 2], pss[x + 2], v0s[x + 2], c0s[x + 2], c0[x] = p0, ps, v, c, c

    blocks(ROWS, terms)

    def laps(xs):
        for x in xs:
            n1[x] += d12[...] * lap_rows(p0s, x + 2)
            s[x] += d12[...] * lap_rows(pss, x + 2)
            r0[x] += lap_rows(v0s, x + 2) * (1.0 / 12.0)
            e0[x] += dc12[...] * lap_rows(c0s, x + 2)

    blocks(ROWS, laps)


def lumped_halo(lv, row):
    y = dot(lv[...], split(jnp.concatenate([row, zeros(8)], axis=0)))
    return y[0:24], y[24:48] + y[48:72]


SIDES = (((0, 1), (1, 0)), ((ROWS - 1, ROWS - 2), (0, 1)))


def packed_rows(rows):
    return (COARSE * (rows - 1) + CP + 7) // 8 * 8


def get(ref, r):
    return ref[COARSE * r : COARSE * r + CP, :]


def put(ref, r, value):
    ref[COARSE * r : COARSE * r + CP, :] = value


def pick_packed(info, side, outer, inner):
    take = info[0] == side
    return lambda r: jnp.where(take, get(outer, r), get(inner, r))


def send_packed(info, outer, inner, tops, bottoms):
    at_top = info[0] == 0
    for r, (top, bottom) in enumerate(zip(tops, bottoms)):
        put(outer, r, jnp.where(at_top, top, bottom))
        put(inner, r, jnp.where(at_top, bottom, top))


def pick_halo(info, side, outer, inner):
    take = info[0] == side
    return lambda *at: jnp.where(take, outer[at], inner[at])


def send(info, outer, inner, tops, bottoms):
    at_top = info[0] == 0
    for r, (top, bottom) in enumerate(zip(tops, bottoms)):
        outer[r] = jnp.where(at_top, top, bottom)
        inner[r] = jnp.where(at_top, bottom, top)


def old_edge_kernel(uo, ui, lv, d12, dc12, n1i, si, r0i, e0i, n1, s, r0, e0, outer, inner):
    info = Position()
    for side, (rows, order) in enumerate(SIDES):
        halo = pick_halo(info, side, uo, ui)
        us = [[halo(pl.ds(SPECIES * (2 * m + r), SP)) for m in range(3)] for r in order]
        p0 = beside(*[mixed(MIX0, v) for v in us])
        ps = beside(*[mixed(MIXS, v) for v in us])
        lumped = [lumped_halo(lv, v[0]) for v in us]
        c = beside(lumped[0][0], lumped[1][0])
        v = beside(lumped[0][1], lumped[1][1])
        for i, x in enumerate(rows):
            n1[x] = n1i[x] + d12[...] * p0[i]
            s[x] = si[x] + d12[...] * ps[i]
            r0[x] = r0i[x] + v[i] * (1.0 / 12.0)
            e0[x] = e0i[x] + dc12[...] * c[i]
    send(info, outer, inner, [n1[0], n1[1]], [n1[ROWS - 2], n1[ROWS - 1]])


def mid_kernel(n1, s, wfr, wc, d12, dc12, n2, r1, e1, c1, n1s, v1s, c1s):
    for x in (0, 1, ROWS + 2, ROWS + 3):
        n1s[x], v1s[x], c1s[x] = zeros(SP), zeros(CP), zeros(CP)

    def terms(xs):
        for x in xs:
            n = n1[x]
            y = dot(wfr[...], stacked(n, n * n))
            n2[x] = n + HALF * ((y[:SP] + y[SP : 2 * SP]) + d12[...] * lap_y(n)) + s[x]
            r, c, v = restricted(y[2 * SP :])
            r1[x] = r + lap_y(v) * (1.0 / 12.0)
            y = dot(wc[...], stacked(c, c * c))
            e1[x] = (y[:CP] + y[CP:]) + dc12[...] * lap_y(c)
            n1s[x + 2], v1s[x + 2], c1s[x + 2], c1[x] = n, v, c, c

    blocks(ROWS, terms, ROWS)

    def laps(xs):
        for x in xs:
            n2[x] += (HALF * d12[...]) * lap_rows(n1s, x + 2)
            r1[x] += lap_rows(v1s, x + 2) * (1.0 / 12.0)
            e1[x] += dc12[...] * lap_rows(c1s, x + 2)

    blocks(ROWS, laps, ROWS)


def lumped_old(first, c0, e0):
    return jnp.where(first, c0, -HALF * e0)


AB_ROWS, EXT_ROWS = 2 * ROWS + 4, 2 * ROWS + 20
A0, B0 = 2, ROWS + 4
XA0, XB0 = 6, ROWS + 16


def mid_edge_kernel(no, ni, lv, wr, d12, dc12, r0, e0, c0, n2i, r1i, e1i, n2, r1, e1, ab, c2, outer, inner, v2s, gs):
    info = Position()
    first = info[1] == 0
    for side, (rows, order) in enumerate(SIDES):
        halo = pick_halo(info, side, no, ni)
        ns = [halo(r) for r in order]
        lumped = [lumped_halo(lv, v) for v in ns]
        c = beside(lumped[0][0], lumped[1][0])
        v = beside(lumped[0][1], lumped[1][1])
        n = beside(*ns)
        for i, x in enumerate(rows):
            n2[x] = n2i[x] + (HALF * d12[...]) * n[i]
            r1[x] = r1i[x] + v[i] * (1.0 / 12.0)
            e1[x] = e1i[x] + dc12[...] * c[i]
    for x in (0, 1, ROWS + 2, ROWS + 3):
        v2s[x] = zeros(CP)

    def lumped(x, value):
        gs[x], c2[x], v2s[x + 2] = restricted(dot(wr[...], stacked(value, value * value)))

    def pieces(x, mid, late):
        v = v2s[x + 2]
        g2 = gs[x] + (lap_y(v) + lap_rows(v2s, x + 2)) * (1.0 / 12.0)
        ab[x + XA0] = mixed(MIX0, (r0[x], mid, g2)) + lumped_old(first, c0[x], e0[x])
        ab[x + XB0] = mixed([STEP * w for w in W1], (r0[x], mid, g2)) - HALF * late

    edges = (0, 1, ROWS - 2, ROWS - 1)
    for x in edges:
        lumped(x, n2[x])
    blocks(ROWS - 4, lambda xs: [lumped(x + 2, n2i[x + 2]) for x in xs], ROWS - 4)
    for x in edges:
        pieces(x, r1[x], e1[x])
    blocks(ROWS - 4, lambda xs: [pieces(x + 2, r1i[x + 2], e1i[x + 2]) for x in xs], ROWS - 4)
    top = [ab[x + XA0] for x in range(6)] + [ab[x + XB0] for x in range(4)] + [v2s[x + 2] for x in range(2)]
    bottom = [ab[x + XA0] for x in range(ROWS - 6, ROWS)] + [ab[x + XB0] for x in range(ROWS - 4, ROWS)]
    send_packed(info, outer, inner, top, bottom + [v2s[x] for x in range(ROWS, ROWS + 2)])


def last_edge_kernel(mo, mi, ho, hi, abi, ab, short):
    info = Position()
    ka, kb = STEP * W0[2] / 12.0, STEP * W1[2] / 12.0
    done = {}
    for side, (rows, order) in enumerate(SIDES):
        inside = info[2] > 0 if side == 0 else info[2] < SLABS - 1
        own, halo = pick_packed(info, side, mo, mi), pick_packed(info, side, ho, hi)
        fix = beside(*[halo(10 + r) for r in order])
        theirs = beside(*[own(10 + r) for r in order[::-1]])
        for i, x in enumerate(rows):
            done[x + XA0] = abi[x + XA0] + ka * fix[i]
            done[x + XB0] = abi[x + XB0] + kb * fix[i]
        for depth, at, to, factor in ((6, 0, XA0, ka), (4, 6, XB0, kb)):
            for i in range(depth):
                x = -1 - i if side == 0 else ROWS + i
                value = halo(at + (depth - 1 - i if side == 0 else i))
                if i < 2:
                    value = value + factor * theirs[i]
                done[x + to] = jnp.where(inside, value, 0.0)
    for at, value in done.items():
        ab[at] = value
    for x in range(-2, ROWS + 2):
        short[x + A0] = done[x + XA0] if x + XA0 in done else abi[x + XA0]
    for x in range(ROWS):
        short[x + B0] = done[x + XB0] if x + XB0 in done else abi[x + XB0]


def sweep(info, z, z0, add, add0, out, out0, low, rows, ws, lapm, dc12):
    size = rows // 2

    def body(xs):
        zr = [z[xs[0] + (low + z0 + k)] for k in range(-2, size + 2)]
        terms = [two_terms(value) for value in zr[2:-2]]
        laps = dot(jnp.concatenate(terms, axis=0), lapm[...])
        for k in range(size):
            x, value = xs[k] + low, zr[k + 2]
            y = dot(ws[...], jnp.concatenate([terms[k], two_terms(value * value)], axis=0))
            lap = laps[2 * CP * k : 2 * CP * k + CP] + laps[2 * CP * k + CP : 2 * CP * (k + 1)]
            lap = lap + 16.0 * (zr[k + 1] + zr[k + 3]) - (zr[k] + zr[k + 4])
            value = value + HALF * ((y[:CP] + y[CP:]) + dc12[...] * lap) + add[x + add0]
            if low < 0:
                inside = ((x >= 0) | (info[2] > 0)) & ((x < ROWS) | (info[2] < SLABS - 1))
                value = jnp.where(inside, value, 0.0)
            out[x + out0] = value

    blocks(rows, body, size)


def begin(info, z0, zo, zi, depth, zs):
    top, bottom = pick_packed(info, 0, zo, zi), pick_packed(info, 1, zo, zi)
    for r in range(depth):
        zs[r], zs[depth + ROWS + r] = top(r), bottom(r)
    for x in range(ROWS):
        zs[depth + x] = get(z0, x)


def give(info, depth, message, packed, outer, inner):
    for x in range(ROWS):
        put(packed, x, message[x])
    ends = [message[x] for x in range(depth)], [message[x] for x in range(ROWS - depth, ROWS)]
    send_packed(info, outer, inner, *ends)


def hosting(info, hosts):
    return info[1] == jnp.where(info[0] == 0, hosts[0], hosts[1])


def start_kernel(hosts, ab, ws, lapm, dc12, result, unused, packed, outer, inner, message):
    info = Position()

    @pl.when(hosting(info, hosts))
    def _():
        sweep(info, ab, A0, ab, B0, message, 0, 0, ROWS, ws, lapm, dc12)
        give(info, 8, message, packed, outer, inner)

        def body(xs):
            for x in xs:
                result[x], result[ROWS + x], result[2 * ROWS + x] = zeros(CP), ab[x + A0], message[x]

        blocks(ROWS, body)


def pair_kernel(
    slices, hosts, depth, z0, zo, zi, mine, short, long, ws, lapm, dc12, packed, outer, inner, za, zb, zc, message, zs
):
    info = Position()

    def sweeps(one, two):
        begin(info, z0, zo, zi, 8, zs)
        sweep(info, zs, 8, one, XA0, za, 6, -6, ROWS + 12, ws, lapm, dc12)
        sweep(info, za, 6, one, XB0, zb, 4, -4, ROWS + 8, ws, lapm, dc12)
        if two is mine:
            sweep(info, zb, 4, two, XA0, zc, 2, -2, ROWS + 4, ws, lapm, dc12)
            sweep(info, zc, 2, two, XB0, message, 0, 0, ROWS, ws, lapm, dc12)
        else:
            sweep(info, zb, 4, two, A0, zc, 2, -2, ROWS + 4, ws, lapm, dc12)
            sweep(info, zc, 2, two, B0, message, 0, 0, ROWS, ws, lapm, dc12)
        give(info, depth, message, packed, outer, inner)

    for host in sorted(set(hosts)):
        one = mine if host == slices[0] else long
        two = mine if host == slices[1] else short
        pl.when(hosting(info, hosts) & (info[1] == host))(functools.partial(sweeps, one, two))


def gather(zs, za, zb, zc, z2, one, two, away):
    for at, result in ((0, one), (1, two)):
        values = [lambda x: zs[x + 8], lambda x: za[x + 6], lambda x: zb[x + 4], lambda x: zc[x + 2], lambda x: z2[x]]
        for part, value in enumerate(values[2 * at : 2 * at + 3]):
            for x in range(ROWS):
                if at == away:
                    put(result, part * ROWS + x, value(x))
                else:
                    result[part * ROWS + x] = value(x)


def gather_kernel(slices, hosts, zs, za, zb, zc, z2, home_in, away_in, home, away):
    info = Position()
    active, second = hosting(info, hosts), info[1] == slices[1]
    pl.when(active & ~second)(lambda: gather(zs, za, zb, zc, z2, home, away, 1))
    if slices[1] in hosts:
        pl.when(active & second)(lambda: gather(zs, za, zb, zc, z2, away, home, 0))


def base_kernel(n1, n2, c1, c2, pro, share, b1, b2):
    def body(xs):
        for x in xs:
            for n, c, b in ((n1, c1, b1), (n2, c2, b2)):
                value = thirds(jnp.concatenate([share[...] * c[x], zeros(8)], axis=0))
                b[:, x, :] = (n[x] - dot(pro[...], value))[:SPECIES]

    blocks(ROWS, body)


def out_kernel(
    where, u, b0, late, early, b1, b2, share, z0, zo, zi, ab, ws, lapm, dc12, home, one, other, out, z, za, zs, spread, node, sem
):
    info = Position()
    last = info[1] == SLICES - 1
    at_home = hosting(info, GROUPS[0][1])
    for slices, hosts in GROUPS[1:-1]:
        at_home = at_home | (hosting(info, hosts) & ((info[1] == slices[0]) | (info[1] == slices[1])))
    first = info[1] == GROUPS[1][0][0]
    for here, result in ((at_home, home), (first & ~at_home, one)):

        @pl.when(here)
        def _():

            def body(xs):
                for x in xs:
                    z[x] = result[x]

            blocks(3 * ROWS, body)

    @pl.when(~at_home & ~first & ~last)
    def _():
        for x in range(3 * ROWS):
            z[x] = get(other, x)

    @pl.when(last)
    def _():
        begin(info, z0, zo, zi, 4, zs)

        def body(xs):
            for x in xs:
                z[x] = zs[x + 4]

        blocks(ROWS, body)

    def finish(m, base):
        def body(xs):
            for x in xs:
                spread[m, :, x, :] = share[...] * z[m * ROWS + x]

        blocks(ROWS, body, ROWS)

        def add(s):
            node[m, s] = base(s) + spread[m, where[s]]

        blocks(SPECIES, lambda at: [add(s) for s in at], 13)
        add(SPECIES - 1)
        copy = pltpu.make_async_copy(node.at[m], out.at[m], sem.at[m])
        copy.start()
        return copy

    first = info[1] == 0
    copies = [finish(0, lambda s: jnp.where(first, u[0, s], b0[s] + late[s] + early[s]))]

    @pl.when(last)
    def _():
        sweep(info, zs, 4, ab, A0, za, 2, -2, ROWS + 4, ws, lapm, dc12)
        sweep(info, za, 2, ab, B0, z.at[pl.ds(2 * ROWS, ROWS)], 0, 0, ROWS, ws, lapm, dc12)

        def body(xs):
            for x in xs:
                z[ROWS + x] = za[x + 2]

        blocks(ROWS, body)

    copies += [finish(1, lambda s: b1[s]), finish(2, lambda s: b2[s])]
    for copy in copies:
        copy.wait()


def field(*shape):
    return jax.ShapeDtypeStruct(shape + (COLS,), F32)


SMEM = pl.BlockSpec(memory_space=pltpu.SMEM)
VMEM = pl.BlockSpec(memory_space=pltpu.VMEM)
ANY = pl.BlockSpec(memory_space=pl.ANY)


def call(kernel, name, outs, *args, scratch=(), alias=None, out_specs=None, specs=None):
    specs = specs or [SMEM if a.dtype == jnp.int32 and a.ndim == 1 else VMEM for a in args]
    return pl.pallas_call(
        kernel,
        out_shape=outs,
        in_specs=specs,
        **({"out_specs": out_specs} if out_specs else {}),
        scratch_shapes=[pltpu.VMEM(f.shape, f.dtype) if isinstance(f, jax.ShapeDtypeStruct) else f for f in scratch],
        input_output_aliases=alias or {},
        compiler_params=pltpu.CompilerParams(vmem_limit_bytes=VMEM_LIMIT),
        name=name,
    )(*args)


AXES = ("tm", "space")
OUTER = [(s, s + 1) for s in range(1, SLABS - 1, 2)] + [(s + 1, s) for s in range(1, SLABS - 1, 2)]
INNER = [(s, s ^ 1) for s in range(SLABS)]
SAME = [(s, s) for s in range(SLABS)]


def moved(value, *routes):
    pairs = [
        (source[s % 2] * SLABS + s, target[t % 2] * SLABS + t) for source, target, slabs in routes for s, t in slabs
    ]
    return lax.ppermute(value, AXES, pairs)


def both(p):
    return (p, p)


def swap(outer, inner):
    got_inner = moved(inner, *[(both(p), both(p), INNER) for p in range(SLICES)])
    got_outer = moved(outer, *[(both(p), both(p), OUTER) for p in range(SLICES)])
    return got_outer, got_inner


def hop(message, outer, inner, source, target):
    parts = ((outer, OUTER), (inner, INNER), (message, SAME))
    zo, zi, z = [moved(value, (source, target, slabs)) for value, slabs in parts]
    return [z, zo, zi]


def after(value, other):
    return lax.optimization_barrier((value, other))[0]


def local(fine_nodes, fine_rates, fine_pairs, fine_diff, coarse_rates, coarse_pairs, coarse_diff, species_map):
    nodes = fine_nodes[0]
    fine, coarse = field(ROWS, SP), field(ROWS, CP)
    message = field(FIRST_ROWS)
    def bf16(*shape):
        return jax.ShapeDtypeStruct(shape, BF16)

    raw = sum(
        jnp.pad(v.astype(F32), ((at, RAW - at - v.shape[0]), (0, 128 - v.shape[1])))
        for at, v in (
            (RATES, fine_rates),
            (PAIRS, fine_pairs),
            (CRATES, coarse_rates),
            (CPAIRS, coarse_pairs),
            (DIFF, fine_diff.reshape(1, SPECIES)),
            (CDIFF, coarse_diff.reshape(1, COARSE)),
            (MAP, species_map.reshape(1, SPECIES)),
        )
    )
    wf, wr, wfr, lv, wc, ws, lapm, pro, d12, dc12, share = call(
        prep_kernel,
        "prep",
        [bf16(2 * SP, 4 * SP), bf16(128, 4 * SP), bf16(2 * SP + 128, 4 * SP), bf16(80, 128), bf16(2 * CP, 4 * CP), bf16(2 * CP, 4 * CP)]
        + [bf16(COLS, COLS), bf16(SP, 96)]
        + [field(SP), field(CP), field(CP)],
        raw,
    )
    outer, inner = call(first_kernel, "first", [message, message], nodes, wc)
    uo, ui = swap(outer, inner)

    n1, s, r0, e0, c0 = call(
        old_kernel,
        "old",
        [fine, fine, coarse, coarse, coarse],
        *(nodes, wf, wr, wc, d12, dc12),
        scratch=[field(4, 3, SP), field(ROWS + 4, SP), field(ROWS + 4, SP), field(ROWS + 4, CP), field(ROWS + 4, CP)],
    )
    two, twelve = field(2, SP), field(packed_rows(12))
    n1, s, r0, e0, outer, inner = call(
        old_edge_kernel,
        "old_edge",
        [fine, fine, coarse, coarse, two, two],
        *(uo, ui, lv, d12, dc12, n1, s, r0, e0),
        alias={5: 0, 6: 1, 7: 2, 8: 3},
    )
    no, ni = swap(outer, inner)
    n2, r1, e1, c1 = call(
        mid_kernel, "mid", [fine, coarse, coarse, coarse], n1, s, wfr, wc, d12, dc12, scratch=[field(ROWS + 4, SP), field(ROWS + 4, CP), field(ROWS + 4, CP)]
    )
    extended, short = field(EXT_ROWS, CP), field(AB_ROWS, CP)
    n2, r1, e1, abx, c2, outer, inner = call(
        mid_edge_kernel,
        "mid_edge",
        [fine, coarse, coarse, extended, coarse, twelve, twelve],
        *(no, ni, lv, wr, d12, dc12, r0, e0, c0, n2, r1, e1),
        alias={9: 0, 10: 1, 11: 2},
        scratch=[field(ROWS + 4, CP), coarse],
    )
    ho, hi = swap(outer, inner)
    b1, b2 = call(base_kernel, "base", [field(SPECIES, ROWS)] * 2, n1, n2, c1, c2, pro, share)
    abx, ab = call(last_edge_kernel, "last_edge", [extended, short], outer, inner, ho, hi, abx, alias={4: 0})

    ab, abx = after(ab, b1), after(abx, b1)
    result, away_result = field(3 * ROWS, CP), field(packed_rows(3 * ROWS))
    bulk, ends = field(packed_rows(ROWS)), field(packed_rows(8))
    pairs = [(slices, hosts) for slices, hosts in GROUPS if len(slices) == 2]
    short, long, back, first = [], [], [], []
    for slices, hosts in pairs:
        for core, host in enumerate(hosts):
            slabs = [(t, t) for t in range(core, SLABS, 2)]
            if host != slices[0]:
                long.append((both(slices[0]), both(host), slabs))
            if host != slices[1]:
                short.append((both(slices[1]), both(host), slabs))
            back.append((both(host), both(slices[0] if host == slices[1] else slices[1]), slabs))
            if host not in slices:
                first.append((both(host), both(slices[0]), slabs))
    short, long = moved(ab, *short), moved(abx, *long)
    forward = [(both(p), both(p + 1), SAME) for p in range(SLICES - 1)]
    home, away, *sent = call(
        functools.partial(start_kernel, GROUPS[0][1]), "start", [result, away_result, bulk, ends, ends], ab, ws, lapm, dc12, scratch=[coarse]
    )
    for at, (slices, hosts) in enumerate(GROUPS[1:], 1):
        z = hop(*sent, GROUPS[at - 1][1], hosts)
        if at == 1:
            z = list(lax.optimization_barrier(tuple(z)))
            b0 = moved(after(b2, z[0]), forward[2], forward[6])
            *z, short, long = lax.optimization_barrier((*z, short, long))
            late = moved(after(b2, z[0]), *forward[3:6])
        elif at == 2:
            *z, b0 = lax.optimization_barrier((*z, b0))
            early = moved(after(b2, z[0]), *forward[:2])
        elif at == 3:
            *z, late, early, home, away = lax.optimization_barrier((*z, late, early, home, away))
        else:
            other, one = moved(away, *back), moved(home, *first)
            *z, other, one, home = lax.optimization_barrier((*z, other, one, home))
        if len(slices) == 2:
            depth = 4 * len(GROUPS[at + 1][0])
            ends = field(packed_rows(depth))
            *sent, za, zb, zc, z2, zs = call(
                functools.partial(pair_kernel, slices, hosts, depth),
                "pair",
                [bulk, ends, ends, field(ROWS + 12, CP), field(ROWS + 8, CP), field(ROWS + 4, CP), coarse, field(ROWS + 16, CP)],
                *(*z, abx, short, long, ws, lapm, dc12),
            )
            home, away = call(
                functools.partial(gather_kernel, slices, hosts),
                "gather",
                [result, away_result],
                *(zs, za, zb, zc, z2, home, away),
                alias={5: 0, 6: 1},
            )
    out = call(
        out_kernel,
        "out",
        field(3, SPECIES, ROWS),
        *(species_map[:, 0], nodes, b0, late, early, b1, b2, share, *z, ab, ws, lapm, dc12, home, one, other),
        out_specs=ANY,
        scratch=[result, field(ROWS + 4, CP), field(ROWS + 8, CP), field(3, CP, ROWS), field(3, SPECIES, ROWS), pltpu.SemaphoreType.DMA((3,))],
    )
    return out[None]


def solution(mesh):
    in_specs = (P("tm", None, None, "space", None), P(), P(), P(), P(), P(), P(), P())
    out_specs = P("tm", None, None, "space", None)
    return jax.shard_map(local, mesh=mesh, in_specs=in_specs, out_specs=out_specs, check_vma=False)
```

```python
import functools

import jax
import jax.numpy as jnp
from jax import lax
from jax.experimental import pallas as pl
from jax.experimental.pallas import tpu as pltpu
from jax.sharding import PartitionSpec as P

SPECIES, COARSE = 53, 21
SP, CP = 56, 24
ROWS, COLS = 16, 256
SLICES, SLABS = 8, 16
STEP, HALF, RELAX = 0.1, 0.05, 3.0
W0 = (5.0 / 24.0, 1.0 / 3.0, -1.0 / 24.0)
W1 = (-1.0 / 24.0, 1.0 / 3.0, 5.0 / 24.0)
F32, BF16 = jnp.float32, jnp.bfloat16
GROUPS = (((0,), (0, 0)), ((1, 2), (1, 5)), ((3, 4), (3, 4)), ((5, 6), (5, 6)), ((7,), (7, 7)))
VMEM_LIMIT = 24 * 1024 * 1024


def split(x):
    hi = x.astype(BF16)
    lo = (x - hi.astype(F32)).astype(BF16)
    return jnp.concatenate([hi, lo], axis=0)


def thirds(x):
    hi = x.astype(BF16)
    rest = x - hi.astype(F32)
    mid = rest.astype(BF16)
    return jnp.concatenate([hi, mid, (rest - mid.astype(F32)).astype(BF16)], axis=0)


def zeros(rows):
    return jnp.zeros((rows, COLS), F32)


def dot(w, x):
    return jnp.dot(w, x, preferred_element_type=F32)


def two_terms(x):
    return jnp.concatenate([x, x - x.astype(BF16).astype(F32)], axis=0).astype(BF16)


def stacked(x, squares):
    return split(jnp.concatenate([x, squares], axis=0))


def lap_y(x):
    near = pltpu.roll(x, 1, 1) + pltpu.roll(x, COLS - 1, 1)
    far = pltpu.roll(x, 2, 1) + pltpu.roll(x, COLS - 2, 1)
    return 16.0 * near - far - 60.0 * x


def lap_rows(ref, x):
    return 16.0 * (ref[x - 1] + ref[x + 1]) - (ref[x - 2] + ref[x + 2])


def beside(near, far):
    return 16.0 * near - far, -near


RATES, PAIRS, CRATES, CPAIRS, DIFF, CDIFF, MAP, RAW = 0, 56, 112, 136, 160, 161, 162, 168


def prep_kernel(raw, wf, wr, wfr, lv, wc, ws, lapm, pro, d12, dc12, share):
    row = lax.broadcasted_iota(jnp.int32, (SP, 128), 0)
    lane = lax.broadcasted_iota(jnp.int32, (SP, 128), 1)

    def halves(x):
        hi = x.astype(BF16).astype(F32)
        return hi, (x - hi).astype(BF16).astype(F32)

    def column(values, height):
        return jnp.sum(jnp.where(row == lane, values, 0.0), axis=1, keepdims=True)[:height]

    eye = jnp.where(row == lane, RELAX, 0.0)
    fine = raw[RATES : RATES + SP, :] - jnp.where(row < SPECIES, eye, 0.0)
    fine = fine + pltpu.roll(raw[PAIRS : PAIRS + SP, :], SP, 1)
    coarse = raw[CRATES : CRATES + CP, :] - jnp.where(row < COARSE, eye, 0.0)[:CP]
    coarse = coarse + pltpu.roll(raw[CPAIRS : CPAIRS + CP, :], CP, 1)
    vectors = raw[DIFF : DIFF + 8, :]
    diff_row = vectors[0:1]
    d12[...] = jnp.broadcast_to(column(diff_row, SP) / 12.0, (SP, COLS))
    dc12[...] = jnp.broadcast_to(column(vectors[1:2], CP) / 12.0, (CP, COLS))
    map_row = jnp.where(lane[0:1] < SPECIES, vectors[2:3].astype(jnp.int32), -1)
    map_column = jnp.sum(jnp.where(row == lane, map_row, 0), axis=1, keepdims=True)
    map_column = jnp.where(row[:, 0:1] < SPECIES, map_column, -1)
    lum = jnp.where((map_row == row[:CP]) & (lane[:CP] < SPECIES), 1.0, 0.0)
    counts = jnp.sum(lum, axis=1, keepdims=True)
    share[...] = jnp.broadcast_to(1.0 / jnp.maximum(counts, 1.0), (CP, COLS))
    lumped = jnp.dot(lum[:, :SP], fine, precision=lax.Precision.HIGHEST, preferred_element_type=F32)
    fh, fl = halves(fine)
    rh, rl = halves(lumped)
    dh, dl = halves(lum * diff_row)
    ch, cl = halves(coarse)
    f = jnp.concatenate([fh, fl], axis=0)
    r = jnp.concatenate([rh, rl, lum, dh, dl, jnp.zeros((8, 128), F32)], axis=0)

    def twice(w, width):
        w = jnp.concatenate([w, jnp.zeros_like(w)], axis=1)
        return (w + pltpu.roll(w, width, 1))[:, : 2 * width].astype(BF16)

    wf[...] = twice(f, 2 * SP)
    wr[...] = twice(r, 2 * SP)
    wfr[: 2 * SP, :] = twice(f, 2 * SP)
    wfr[2 * SP :, :] = twice(r, 2 * SP)
    v = jnp.concatenate([lum, dh, dl, jnp.zeros((8, 128), F32)], axis=0)
    lv[...] = (v + pltpu.roll(v, 64, 1)).astype(BF16)
    c = jnp.concatenate([ch, cl], axis=0)
    wc[...] = twice(c, 2 * CP)
    linear, pairs = jnp.where(lane[: 2 * CP] < CP, c, 0.0), jnp.where(lane[: 2 * CP] < CP, 0.0, c)
    both_terms = linear + pltpu.roll(linear, CP, 1) + pltpu.roll(pairs, CP, 1) + pltpu.roll(pairs, 2 * CP, 1)
    ws[...] = both_terms[:, : 4 * CP].astype(BF16)
    far = lax.broadcasted_iota(jnp.int32, (COLS, COLS), 0) - lax.broadcasted_iota(jnp.int32, (COLS, COLS), 1)
    far = jnp.abs(far)
    far = jnp.minimum(far, COLS - far)
    lapm[...] = jnp.where(far == 0, -60.0, jnp.where(far == 1, 16.0, jnp.where(far == 2, -1.0, 0.0))).astype(BF16)
    lane96 = lax.broadcasted_iota(jnp.int32, (SP, 96), 1)
    pro[...] = jnp.where(map_column == lane96 % 32, 1.0, 0.0).astype(BF16)


class Position:
    def __init__(self):
        self.slice_at, self.slab = lax.axis_index("tm"), lax.axis_index("space")

    def __getitem__(self, at):
        return (self.slab % 2, self.slice_at, self.slab)[at]


def blocks(rows, body, size=4):
    @pl.loop(0, rows // size)
    def _(i):
        body([size * i + k for k in range(size)])


FIRST_ROWS = 328


def first_kernel(u, weights_made, outer, inner):
    info = Position()
    at_top = info[0] == 0
    for out in (outer, inner):
        out[FIRST_ROWS - 16 :, :] = zeros(16)
    for m in range(3):
        for r in range(2):
            first, last = u[m, :, r, :], u[m, :, ROWS - 2 + r, :]
            at = SPECIES * (2 * m + r)
            outer[at : at + SPECIES, :] = jnp.where(at_top, first, last)
            inner[at : at + SPECIES, :] = jnp.where(at_top, last, first)


def restricted(y):
    return y[0:24] + y[24:48], y[48:72], y[72:96] + y[96:120]


MIX0 = [STEP * w for w in W0]
MIXS = [STEP * W1[0], STEP * W1[1] - HALF, STEP * W1[2]]


def mixed(factors, values):
    return factors[0] * values[0] + factors[1] * values[1] + factors[2] * values[2]


def old_kernel(u, wf, wr, wc, d12, dc12, n1, s, r0, e0, c0, ut, p0s, pss, v0s, c0s):
    for k in range(4):
        for m in range(3):
            ut[k, m, SP - 8 :, :] = zeros(8)
    for x in (0, 1, ROWS + 2, ROWS + 3):
        p0s[x], pss[x], v0s[x], c0s[x] = zeros(SP), zeros(SP), zeros(CP), zeros(CP)

    def terms(xs):
        for k, x in enumerate(xs):
            for m in range(3):
                ut[k, m, :SPECIES, :] = u[m, :, x, :]
        for k, x in enumerate(xs):
            us = [ut[k, m] for m in range(3)]
            qs = [v * v for v in us]
            p0, ps = mixed(MIX0, us), mixed(MIXS, us)
            y = dot(wf[...], stacked(p0, mixed(MIX0, qs)))
            n1[x] = us[0] + (y[:SP] + y[SP:]) + d12[...] * lap_y(p0)
            y = dot(wf[...], stacked(ps, mixed(MIXS, qs)))
            s[x] = (y[:SP] + y[SP:]) + d12[...] * lap_y(ps)
            r, c, v = restricted(dot(wr[...], stacked(us[0], qs[0])))
            r0[x] = r + lap_y(v) * (1.0 / 12.0)
            y = dot(wc[...], stacked(c, c * c))
            e0[x] = (y[:CP] + y[CP:]) + dc12[...] * lap_y(c)
            p0s[x + 2], pss[x + 2], v0s[x + 2], c0s[x + 2], c0[x] = p0, ps, v, c, c

    blocks(ROWS, terms)

    def laps(xs):
        for x in xs:
            n1[x] += d12[...] * lap_rows(p0s, x + 2)
            s[x] += d12[...] * lap_rows(pss, x + 2)
            r0[x] += lap_rows(v0s, x + 2) * (1.0 / 12.0)
            e0[x] += dc12[...] * lap_rows(c0s, x + 2)

    blocks(ROWS, laps)


def lumped_halo(lv, row):
    y = dot(lv[...], split(jnp.concatenate([row, zeros(8)], axis=0)))
    return y[0:24], y[24:48] + y[48:72]


SIDES = (((0, 1), (1, 0)), ((ROWS - 1, ROWS - 2), (0, 1)))


def packed_rows(rows):
    return (COARSE * (rows - 1) + CP + 7) // 8 * 8


def get(ref, r):
    return ref[COARSE * r : COARSE * r + CP, :]


def put(ref, r, value):
    ref[COARSE * r : COARSE * r + CP, :] = value


def pick_packed(info, side, outer, inner):
    take = info[0] == side
    return lambda r: jnp.where(take, get(outer, r), get(inner, r))


def send_packed(info, outer, inner, tops, bottoms):
    at_top = info[0] == 0
    for r, (top, bottom) in enumerate(zip(tops, bottoms)):
        put(outer, r, jnp.where(at_top, top, bottom))
        put(inner, r, jnp.where(at_top, bottom, top))


def pick_halo(info, side, outer, inner):
    take = info[0] == side
    return lambda *at: jnp.where(take, outer[at], inner[at])


def send(info, outer, inner, tops, bottoms):
    at_top = info[0] == 0
    for r, (top, bottom) in enumerate(zip(tops, bottoms)):
        outer[r] = jnp.where(at_top, top, bottom)
        inner[r] = jnp.where(at_top, bottom, top)


def old_edge_kernel(uo, ui, lv, d12, dc12, n1i, si, r0i, e0i, n1, s, r0, e0, outer, inner):
    info = Position()
    for side, (rows, order) in enumerate(SIDES):
        halo = pick_halo(info, side, uo, ui)
        us = [[halo(pl.ds(SPECIES * (2 * m + r), SP)) for m in range(3)] for r in order]
        p0 = beside(*[mixed(MIX0, v) for v in us])
        ps = beside(*[mixed(MIXS, v) for v in us])
        lumped = [lumped_halo(lv, v[0]) for v in us]
        c = beside(lumped[0][0], lumped[1][0])
        v = beside(lumped[0][1], lumped[1][1])
        for i, x in enumerate(rows):
            n1[x] = n1i[x] + d12[...] * p0[i]
            s[x] = si[x] + d12[...] * ps[i]
            r0[x] = r0i[x] + v[i] * (1.0 / 12.0)
            e0[x] = e0i[x] + dc12[...] * c[i]
    send(info, outer, inner, [n1[0], n1[1]], [n1[ROWS - 2], n1[ROWS - 1]])


def mid_kernel(n1, s, wfr, wc, d12, dc12, n2, r1, e1, c1, n1s, v1s, c1s):
    for x in (0, 1, ROWS + 2, ROWS + 3):
        n1s[x], v1s[x], c1s[x] = zeros(SP), zeros(CP), zeros(CP)

    def terms(xs):
        for x in xs:
            n = n1[x]
            y = dot(wfr[...], stacked(n, n * n))
            n2[x] = n + HALF * ((y[:SP] + y[SP : 2 * SP]) + d12[...] * lap_y(n)) + s[x]
            r, c, v = restricted(y[2 * SP :])
            r1[x] = r + lap_y(v) * (1.0 / 12.0)
            y = dot(wc[...], stacked(c, c * c))
            e1[x] = (y[:CP] + y[CP:]) + dc12[...] * lap_y(c)
            n1s[x + 2], v1s[x + 2], c1s[x + 2], c1[x] = n, v, c, c

    blocks(ROWS, terms, ROWS)

    def laps(xs):
        for x in xs:
            n2[x] += (HALF * d12[...]) * lap_rows(n1s, x + 2)
            r1[x] += lap_rows(v1s, x + 2) * (1.0 / 12.0)
            e1[x] += dc12[...] * lap_rows(c1s, x + 2)

    blocks(ROWS, laps, ROWS)


def lumped_old(first, c0, e0):
    return jnp.where(first, c0, -HALF * e0)


AB_ROWS, EXT_ROWS = 2 * ROWS + 4, 2 * ROWS + 20
A0, B0 = 2, ROWS + 4
XA0, XB0 = 6, ROWS + 16


def mid_edge_kernel(no, ni, lv, wr, d12, dc12, r0, e0, c0, n2i, r1i, e1i, n2, r1, e1, ab, c2, outer, inner, v2s, gs):
    info = Position()
    first = info[1] == 0
    for side, (rows, order) in enumerate(SIDES):
        halo = pick_halo(info, side, no, ni)
        ns = [halo(r) for r in order]
        lumped = [lumped_halo(lv, v) for v in ns]
        c = beside(lumped[0][0], lumped[1][0])
        v = beside(lumped[0][1], lumped[1][1])
        n = beside(*ns)
        for i, x in enumerate(rows):
            n2[x] = n2i[x] + (HALF * d12[...]) * n[i]
            r1[x] = r1i[x] + v[i] * (1.0 / 12.0)
            e1[x] = e1i[x] + dc12[...] * c[i]
    for x in (0, 1, ROWS + 2, ROWS + 3):
        v2s[x] = zeros(CP)

    def lumped(x, value):
        gs[x], c2[x], v2s[x + 2] = restricted(dot(wr[...], stacked(value, value * value)))

    def pieces(x, mid, late):
        v = v2s[x + 2]
        g2 = gs[x] + (lap_y(v) + lap_rows(v2s, x + 2)) * (1.0 / 12.0)
        ab[x + XA0] = mixed(MIX0, (r0[x], mid, g2)) + lumped_old(first, c0[x], e0[x])
        ab[x + XB0] = mixed([STEP * w for w in W1], (r0[x], mid, g2)) - HALF * late

    edges = (0, 1, ROWS - 2, ROWS - 1)
    for x in edges:
        lumped(x, n2[x])
    blocks(ROWS - 4, lambda xs: [lumped(x + 2, n2i[x + 2]) for x in xs], ROWS - 4)
    for x in edges:
        pieces(x, r1[x], e1[x])
    blocks(ROWS - 4, lambda xs: [pieces(x + 2, r1i[x + 2], e1i[x + 2]) for x in xs], ROWS - 4)
    top = [ab[x + XA0] for x in range(6)] + [ab[x + XB0] for x in range(4)] + [v2s[x + 2] for x in range(2)]
    bottom = [ab[x + XA0] for x in range(ROWS - 6, ROWS)] + [ab[x + XB0] for x in range(ROWS - 4, ROWS)]
    send_packed(info, outer, inner, top, bottom + [v2s[x] for x in range(ROWS, ROWS + 2)])


def last_edge_kernel(mo, mi, ho, hi, abi, ab, short):
    info = Position()
    ka, kb = STEP * W0[2] / 12.0, STEP * W1[2] / 12.0
    done = {}
    for side, (rows, order) in enumerate(SIDES):
        inside = info[2] > 0 if side == 0 else info[2] < SLABS - 1
        own, halo = pick_packed(info, side, mo, mi), pick_packed(info, side, ho, hi)
        fix = beside(*[halo(10 + r) for r in order])
        theirs = beside(*[own(10 + r) for r in order[::-1]])
        for i, x in enumerate(rows):
            done[x + XA0] = abi[x + XA0] + ka * fix[i]
            done[x + XB0] = abi[x + XB0] + kb * fix[i]
        for depth, at, to, factor in ((6, 0, XA0, ka), (4, 6, XB0, kb)):
            for i in range(depth):
                x = -1 - i if side == 0 else ROWS + i
                value = halo(at + (depth - 1 - i if side == 0 else i))
                if i < 2:
                    value = value + factor * theirs[i]
                done[x + to] = jnp.where(inside, value, 0.0)
    for at, value in done.items():
        ab[at] = value
    for x in range(-2, ROWS + 2):
        short[x + A0] = done[x + XA0] if x + XA0 in done else abi[x + XA0]
    for x in range(ROWS):
        short[x + B0] = done[x + XB0] if x + XB0 in done else abi[x + XB0]


def sweep(info, z, z0, add, add0, out, out0, low, rows, ws, lapm, dc12):
    size = rows // 2

    def body(xs):
        zr = [z[xs[0] + (low + z0 + k)] for k in range(-2, size + 2)]
        terms = [two_terms(value) for value in zr[2:-2]]
        laps = dot(jnp.concatenate(terms, axis=0), lapm[...])
        for k in range(size):
            x, value = xs[k] + low, zr[k + 2]
            y = dot(ws[...], jnp.concatenate([terms[k], two_terms(value * value)], axis=0))
            lap = laps[2 * CP * k : 2 * CP * k + CP] + laps[2 * CP * k + CP : 2 * CP * (k + 1)]
            lap = lap + 16.0 * (zr[k + 1] + zr[k + 3]) - (zr[k] + zr[k + 4])
            value = value + HALF * ((y[:CP] + y[CP:]) + dc12[...] * lap) + add[x + add0]
            if low < 0:
                inside = ((x >= 0) | (info[2] > 0)) & ((x < ROWS) | (info[2] < SLABS - 1))
                value = jnp.where(inside, value, 0.0)
            out[x + out0] = value

    blocks(rows, body, size)


def begin(info, z0, zo, zi, depth, zs):
    top, bottom = pick_packed(info, 0, zo, zi), pick_packed(info, 1, zo, zi)
    for r in range(depth):
        zs[r], zs[depth + ROWS + r] = top(r), bottom(r)
    for x in range(ROWS):
        zs[depth + x] = get(z0, x)


def give(info, depth, message, packed, outer, inner):
    for x in range(ROWS):
        put(packed, x, message[x])
    ends = [message[x] for x in range(depth)], [message[x] for x in range(ROWS - depth, ROWS)]
    send_packed(info, outer, inner, *ends)


def hosting(info, hosts):
    return info[1] == jnp.where(info[0] == 0, hosts[0], hosts[1])


def start_kernel(hosts, ab, ws, lapm, dc12, result, unused, packed, outer, inner, message):
    info = Position()

    @pl.when(hosting(info, hosts))
    def _():
        sweep(info, ab, A0, ab, B0, message, 0, 0, ROWS, ws, lapm, dc12)
        give(info, 8, message, packed, outer, inner)

        for part, value in enumerate((lambda x: zeros(CP), lambda x: ab[x + A0], lambda x: message[x])):
            for x in range(ROWS):
                put(result, part * ROWS + x, value(x))


def pair_kernel(
    slices, hosts, depth, z0, zo, zi, mine, short, long, ws, lapm, dc12, packed, outer, inner, za, zb, zc, message, zs
):
    info = Position()

    def sweeps(one, two):
        begin(info, z0, zo, zi, 8, zs)
        sweep(info, zs, 8, one, XA0, za, 6, -6, ROWS + 12, ws, lapm, dc12)
        sweep(info, za, 6, one, XB0, zb, 4, -4, ROWS + 8, ws, lapm, dc12)
        if two is mine:
            sweep(info, zb, 4, two, XA0, zc, 2, -2, ROWS + 4, ws, lapm, dc12)
            sweep(info, zc, 2, two, XB0, message, 0, 0, ROWS, ws, lapm, dc12)
        else:
            sweep(info, zb, 4, two, A0, zc, 2, -2, ROWS + 4, ws, lapm, dc12)
            sweep(info, zc, 2, two, B0, message, 0, 0, ROWS, ws, lapm, dc12)
        give(info, depth, message, packed, outer, inner)

    for host in sorted(set(hosts)):
        one = mine if host == slices[0] else long
        two = mine if host == slices[1] else short
        pl.when(hosting(info, hosts) & (info[1] == host))(functools.partial(sweeps, one, two))


def gather(zs, za, zb, zc, z2, one, two):
    values = [lambda x: zs[x + 8], lambda x: za[x + 6], lambda x: zb[x + 4], lambda x: zc[x + 2], lambda x: z2[x]]
    for result, parts in ((one, values[:3]), (two, values[2:])):
        for part, value in enumerate(parts):
            for x in range(ROWS):
                put(result, part * ROWS + x, value(x))


def gather_kernel(slices, hosts, zs, za, zb, zc, z2, home_in, away_in, home, away):
    info = Position()
    active, second = hosting(info, hosts), info[1] == slices[1]
    pl.when(active & ~second)(lambda: gather(zs, za, zb, zc, z2, home, away))
    if slices[1] in hosts:
        pl.when(active & second)(lambda: gather(zs, za, zb, zc, z2, away, home))


def base_kernel(n1, n2, c1, c2, pro, share, b1, b2):
    def body(xs):
        for x in xs:
            for n, c, b in ((n1, c1, b1), (n2, c2, b2)):
                value = thirds(jnp.concatenate([share[...] * c[x], zeros(8)], axis=0))
                b[:, x, :] = (n[x] - dot(pro[...], value))[:SPECIES]

    blocks(ROWS, body)


def out_kernel(
    where, u, b0, late, b1, b2, share, z0, zo, zi, ab, ws, lapm, dc12, home, one, other, out, z, za, zs, spread, node, sem
):
    info = Position()
    last = info[1] == SLICES - 1
    at_home = hosting(info, GROUPS[0][1])
    for slices, hosts in GROUPS[1:-1]:
        at_home = at_home | (hosting(info, hosts) & ((info[1] == slices[0]) | (info[1] == slices[1])))
    first = info[1] == GROUPS[1][0][0]
    for here, result in ((at_home, home), (first & ~at_home, one), (~at_home & ~first & ~last, other)):

        @pl.when(here)
        def _():
            for x in range(3 * ROWS):
                z[x] = get(result, x)

    @pl.when(last)
    def _():
        begin(info, z0, zo, zi, 4, zs)

        def body(xs):
            for x in xs:
                z[x] = zs[x + 4]

        blocks(ROWS, body)

    def finish(m, base):
        def body(xs):
            for x in xs:
                spread[m, :, x, :] = share[...] * z[m * ROWS + x]

        blocks(ROWS, body, ROWS)

        def add(s):
            node[m, s] = base(s) + spread[m, where[s]]

        blocks(SPECIES, lambda at: [add(s) for s in at], 13)
        add(SPECIES - 1)
        copy = pltpu.make_async_copy(node.at[m], out.at[m], sem.at[m])
        copy.start()
        return copy

    first = info[1] == 0
    copies = [finish(0, lambda s: jnp.where(first, u[0, s], b0[s] + late[s]))]

    @pl.when(last)
    def _():
        sweep(info, zs, 4, ab, A0, za, 2, -2, ROWS + 4, ws, lapm, dc12)
        sweep(info, za, 2, ab, B0, z.at[pl.ds(2 * ROWS, ROWS)], 0, 0, ROWS, ws, lapm, dc12)

        def body(xs):
            for x in xs:
                z[ROWS + x] = za[x + 2]

        blocks(ROWS, body)

    copies += [finish(1, lambda s: b1[s]), finish(2, lambda s: b2[s])]
    for copy in copies:
        copy.wait()


def field(*shape):
    return jax.ShapeDtypeStruct(shape + (COLS,), F32)


SMEM = pl.BlockSpec(memory_space=pltpu.SMEM)
VMEM = pl.BlockSpec(memory_space=pltpu.VMEM)
ANY = pl.BlockSpec(memory_space=pl.ANY)


def call(kernel, name, outs, *args, scratch=(), alias=None, out_specs=None, specs=None):
    specs = specs or [SMEM if a.dtype == jnp.int32 and a.ndim == 1 else VMEM for a in args]
    return pl.pallas_call(
        kernel,
        out_shape=outs,
        in_specs=specs,
        **({"out_specs": out_specs} if out_specs else {}),
        scratch_shapes=[pltpu.VMEM(f.shape, f.dtype) if isinstance(f, jax.ShapeDtypeStruct) else f for f in scratch],
        input_output_aliases=alias or {},
        compiler_params=pltpu.CompilerParams(vmem_limit_bytes=VMEM_LIMIT),
        name=name,
    )(*args)


AXES = ("tm", "space")
OUTER = [(s, s + 1) for s in range(1, SLABS - 1, 2)] + [(s + 1, s) for s in range(1, SLABS - 1, 2)]
INNER = [(s, s ^ 1) for s in range(SLABS)]
SAME = [(s, s) for s in range(SLABS)]


def moved(value, *routes):
    pairs = [
        (source[s % 2] * SLABS + s, target[t % 2] * SLABS + t) for source, target, slabs in routes for s, t in slabs
    ]
    return lax.ppermute(value, AXES, pairs)


def both(p):
    return (p, p)


def swap(outer, inner):
    got_inner = moved(inner, *[(both(p), both(p), INNER) for p in range(SLICES)])
    got_outer = moved(outer, *[(both(p), both(p), OUTER) for p in range(SLICES)])
    return got_outer, got_inner


def hop(message, outer, inner, source, target):
    parts = ((outer, OUTER), (inner, INNER), (message, SAME))
    zo, zi, z = [moved(value, (source, target, slabs)) for value, slabs in parts]
    return [z, zo, zi]


def after(value, other):
    return lax.optimization_barrier((value, other))[0]


def local(fine_nodes, fine_rates, fine_pairs, fine_diff, coarse_rates, coarse_pairs, coarse_diff, species_map):
    nodes = fine_nodes[0]
    fine, coarse = field(ROWS, SP), field(ROWS, CP)
    message = field(FIRST_ROWS)
    def bf16(*shape):
        return jax.ShapeDtypeStruct(shape, BF16)

    raw = sum(
        jnp.pad(v.astype(F32), ((at, RAW - at - v.shape[0]), (0, 128 - v.shape[1])))
        for at, v in (
            (RATES, fine_rates),
            (PAIRS, fine_pairs),
            (CRATES, coarse_rates),
            (CPAIRS, coarse_pairs),
            (DIFF, fine_diff.reshape(1, SPECIES)),
            (CDIFF, coarse_diff.reshape(1, COARSE)),
            (MAP, species_map.reshape(1, SPECIES)),
        )
    )
    wf, wr, wfr, lv, wc, ws, lapm, pro, d12, dc12, share = call(
        prep_kernel,
        "prep",
        [bf16(2 * SP, 4 * SP), bf16(128, 4 * SP), bf16(2 * SP + 128, 4 * SP), bf16(80, 128), bf16(2 * CP, 4 * CP), bf16(2 * CP, 4 * CP)]
        + [bf16(COLS, COLS), bf16(SP, 96)]
        + [field(SP), field(CP), field(CP)],
        raw,
    )
    outer, inner = call(first_kernel, "first", [message, message], nodes, wc)
    uo, ui = swap(outer, inner)

    n1, s, r0, e0, c0 = call(
        old_kernel,
        "old",
        [fine, fine, coarse, coarse, coarse],
        *(nodes, wf, wr, wc, d12, dc12),
        scratch=[field(4, 3, SP), field(ROWS + 4, SP), field(ROWS + 4, SP), field(ROWS + 4, CP), field(ROWS + 4, CP)],
    )
    two, twelve = field(2, SP), field(packed_rows(12))
    n1, s, r0, e0, outer, inner = call(
        old_edge_kernel,
        "old_edge",
        [fine, fine, coarse, coarse, two, two],
        *(uo, ui, lv, d12, dc12, n1, s, r0, e0),
        alias={5: 0, 6: 1, 7: 2, 8: 3},
    )
    no, ni = swap(outer, inner)
    n2, r1, e1, c1 = call(
        mid_kernel, "mid", [fine, coarse, coarse, coarse], n1, s, wfr, wc, d12, dc12, scratch=[field(ROWS + 4, SP), field(ROWS + 4, CP), field(ROWS + 4, CP)]
    )
    extended, short = field(EXT_ROWS, CP), field(AB_ROWS, CP)
    n2, r1, e1, abx, c2, outer, inner = call(
        mid_edge_kernel,
        "mid_edge",
        [fine, coarse, coarse, extended, coarse, twelve, twelve],
        *(no, ni, lv, wr, d12, dc12, r0, e0, c0, n2, r1, e1),
        alias={9: 0, 10: 1, 11: 2},
        scratch=[field(ROWS + 4, CP), coarse],
    )
    ho, hi = swap(outer, inner)
    b1, b2 = call(base_kernel, "base", [field(SPECIES, ROWS)] * 2, n1, n2, c1, c2, pro, share)
    abx, ab = call(last_edge_kernel, "last_edge", [extended, short], outer, inner, ho, hi, abx, alias={4: 0})

    ab, abx = after(ab, b1), after(abx, b1)
    packed = field(packed_rows(3 * ROWS))
    bulk, ends = field(packed_rows(ROWS)), field(packed_rows(8))
    pairs = [(slices, hosts) for slices, hosts in GROUPS if len(slices) == 2]
    short, long, back, first = [], [], [], []
    for slices, hosts in pairs:
        for core, host in enumerate(hosts):
            slabs = [(t, t) for t in range(core, SLABS, 2)]
            if host != slices[0]:
                long.append((both(slices[0]), both(host), slabs))
            if host != slices[1]:
                short.append((both(slices[1]), both(host), slabs))
            back.append((both(host), both(slices[0] if host == slices[1] else slices[1]), slabs))
            if host not in slices:
                first.append((both(host), both(slices[0]), slabs))
    short, long = moved(ab, *short), moved(abx, *long)
    forward = [(both(p), both(p + 1), SAME) for p in range(SLICES - 1)]
    home, away, *sent = call(
        functools.partial(start_kernel, GROUPS[0][1]), "start", [packed, packed, bulk, ends, ends], ab, ws, lapm, dc12, scratch=[coarse]
    )
    for at, (slices, hosts) in enumerate(GROUPS[1:], 1):
        z = hop(*sent, GROUPS[at - 1][1], hosts)
        if at == 1:
            z = list(lax.optimization_barrier(tuple(z)))
            b0 = moved(after(b2, z[0]), forward[2], forward[6])
            *z, short, long = lax.optimization_barrier((*z, short, long))
            late = moved(after(b2, z[0]), *forward[:2], *forward[3:6])
        elif at == 2:
            *z, b0 = lax.optimization_barrier((*z, b0))
        elif at == 3:
            *z, late, home, away = lax.optimization_barrier((*z, late, home, away))
        else:
            other, one = moved(away, *back), moved(home, *first)
            *z, other, one, home = lax.optimization_barrier((*z, other, one, home))
        if len(slices) == 2:
            depth = 4 * len(GROUPS[at + 1][0])
            ends = field(packed_rows(depth))
            *sent, za, zb, zc, z2, zs = call(
                functools.partial(pair_kernel, slices, hosts, depth),
                "pair",
                [bulk, ends, ends, field(ROWS + 12, CP), field(ROWS + 8, CP), field(ROWS + 4, CP), coarse, field(ROWS + 16, CP)],
                *(*z, abx, short, long, ws, lapm, dc12),
            )
            home, away = call(
                functools.partial(gather_kernel, slices, hosts),
                "gather",
                [packed, packed],
                *(zs, za, zb, zc, z2, home, away),
                alias={5: 0, 6: 1},
            )
    out = call(
        out_kernel,
        "out",
        field(3, SPECIES, ROWS),
        *(species_map[:, 0], nodes, b0, late, b1, b2, share, *z, ab, ws, lapm, dc12, home, one, other),
        out_specs=ANY,
        scratch=[field(3 * ROWS, CP), field(ROWS + 4, CP), field(ROWS + 8, CP), field(3, CP, ROWS), field(3, SPECIES, ROWS), pltpu.SemaphoreType.DMA((3,))],
    )
    return out[None]


def solution(mesh):
    in_specs = (P("tm", None, None, "space", None), P(), P(), P(), P(), P(), P(), P())
    out_specs = P("tm", None, None, "space", None)
    return jax.shard_map(local, mesh=mesh, in_specs=in_specs, out_specs=out_specs, check_vma=False)
```

```python
import functools

import jax
import jax.numpy as jnp
from jax import lax
from jax.experimental import pallas as pl
from jax.experimental.pallas import tpu as pltpu
from jax.sharding import PartitionSpec as P

SPECIES, COARSE = 53, 21
SP, CP = 56, 24
ROWS, COLS = 16, 256
SLICES, SLABS = 8, 16
STEP, HALF, RELAX = 0.1, 0.05, 3.0
W0 = (5.0 / 24.0, 1.0 / 3.0, -1.0 / 24.0)
W1 = (-1.0 / 24.0, 1.0 / 3.0, 5.0 / 24.0)
F32, BF16 = jnp.float32, jnp.bfloat16
GROUPS = (((0,), (0, 0)), ((1, 2), (1, 5)), ((3, 4), (3, 4)), ((5, 6), (5, 6)), ((7,), (7, 7)))
VMEM_LIMIT = 24 * 1024 * 1024


def split(x):
    hi = x.astype(BF16)
    lo = (x - hi.astype(F32)).astype(BF16)
    return jnp.concatenate([hi, lo], axis=0)


def thirds(x):
    hi = x.astype(BF16)
    rest = x - hi.astype(F32)
    mid = rest.astype(BF16)
    return jnp.concatenate([hi, mid, (rest - mid.astype(F32)).astype(BF16)], axis=0)


def zeros(rows):
    return jnp.zeros((rows, COLS), F32)


def dot(w, x):
    return jnp.dot(w, x, preferred_element_type=F32)


def two_terms(x):
    return jnp.concatenate([x, x - x.astype(BF16).astype(F32)], axis=0).astype(BF16)


def stacked(x, squares):
    return split(jnp.concatenate([x, squares], axis=0))


def lap_y(x):
    near = pltpu.roll(x, 1, 1) + pltpu.roll(x, COLS - 1, 1)
    far = pltpu.roll(x, 2, 1) + pltpu.roll(x, COLS - 2, 1)
    return 16.0 * near - far - 60.0 * x


def lap_rows(ref, x):
    return 16.0 * (ref[x - 1] + ref[x + 1]) - (ref[x - 2] + ref[x + 2])


def beside(near, far):
    return 16.0 * near - far, -near


RATES, PAIRS, CRATES, CPAIRS, DIFF, CDIFF, MAP, RAW = 0, 56, 112, 136, 160, 161, 162, 168


def prep_kernel(raw, wf, wr, wfr, lv, wc, ws, lapm, pro, d12, dc12, share):
    row = lax.broadcasted_iota(jnp.int32, (SP, 128), 0)
    lane = lax.broadcasted_iota(jnp.int32, (SP, 128), 1)

    def halves(x):
        hi = x.astype(BF16).astype(F32)
        return hi, (x - hi).astype(BF16).astype(F32)

    def column(values, height):
        return jnp.sum(jnp.where(row == lane, values, 0.0), axis=1, keepdims=True)[:height]

    eye = jnp.where(row == lane, RELAX, 0.0)
    fine = raw[RATES : RATES + SP, :] - jnp.where(row < SPECIES, eye, 0.0)
    fine = fine + pltpu.roll(raw[PAIRS : PAIRS + SP, :], SP, 1)
    coarse = raw[CRATES : CRATES + CP, :] - jnp.where(row < COARSE, eye, 0.0)[:CP]
    coarse = coarse + pltpu.roll(raw[CPAIRS : CPAIRS + CP, :], CP, 1)
    vectors = raw[DIFF : DIFF + 8, :]
    diff_row = vectors[0:1]
    d12[...] = jnp.broadcast_to(column(diff_row, SP) / 12.0, (SP, COLS))
    dc12[...] = jnp.broadcast_to(column(vectors[1:2], CP) / 12.0, (CP, COLS))
    map_row = jnp.where(lane[0:1] < SPECIES, vectors[2:3].astype(jnp.int32), -1)
    map_column = jnp.sum(jnp.where(row == lane, map_row, 0), axis=1, keepdims=True)
    map_column = jnp.where(row[:, 0:1] < SPECIES, map_column, -1)
    lum = jnp.where((map_row == row[:CP]) & (lane[:CP] < SPECIES), 1.0, 0.0)
    counts = jnp.sum(lum, axis=1, keepdims=True)
    share[...] = jnp.broadcast_to(1.0 / jnp.maximum(counts, 1.0), (CP, COLS))
    lumped = jnp.dot(lum[:, :SP], fine, precision=lax.Precision.HIGHEST, preferred_element_type=F32)
    fh, fl = halves(fine)
    rh, rl = halves(lumped)
    dh, dl = halves(lum * diff_row)
    ch, cl = halves(coarse)
    f = jnp.concatenate([fh, fl], axis=0)
    r = jnp.concatenate([rh, rl, lum, dh, dl, jnp.zeros((8, 128), F32)], axis=0)

    def twice(w, width):
        w = jnp.concatenate([w, jnp.zeros_like(w)], axis=1)
        return (w + pltpu.roll(w, width, 1))[:, : 2 * width].astype(BF16)

    wf[...] = twice(f, 2 * SP)
    wr[...] = twice(r, 2 * SP)
    wfr[: 2 * SP, :] = twice(f, 2 * SP)
    wfr[2 * SP :, :] = twice(r, 2 * SP)
    v = jnp.concatenate([lum, dh, dl, jnp.zeros((8, 128), F32)], axis=0)
    lv[...] = (v + pltpu.roll(v, 64, 1)).astype(BF16)
    c = jnp.concatenate([ch, cl], axis=0)
    wc[...] = twice(c, 2 * CP)
    linear, pairs = jnp.where(lane[: 2 * CP] < CP, c, 0.0), jnp.where(lane[: 2 * CP] < CP, 0.0, c)
    both_terms = linear + pltpu.roll(linear, CP, 1) + pltpu.roll(pairs, CP, 1) + pltpu.roll(pairs, 2 * CP, 1)
    ws[...] = both_terms[:, : 4 * CP].astype(BF16)
    far = lax.broadcasted_iota(jnp.int32, (COLS, COLS), 0) - lax.broadcasted_iota(jnp.int32, (COLS, COLS), 1)
    far = jnp.abs(far)
    far = jnp.minimum(far, COLS - far)
    lapm[...] = jnp.where(far == 0, -60.0, jnp.where(far == 1, 16.0, jnp.where(far == 2, -1.0, 0.0))).astype(BF16)
    lane96 = lax.broadcasted_iota(jnp.int32, (SP, 96), 1)
    pro[...] = jnp.where(map_column == lane96 % 32, 1.0, 0.0).astype(BF16)


class Position:
    def __init__(self):
        self.slice_at, self.slab = lax.axis_index("tm"), lax.axis_index("space")

    def __getitem__(self, at):
        return (self.slab % 2, self.slice_at, self.slab)[at]


def blocks(rows, body, size=4):
    @pl.loop(0, rows // size)
    def _(i):
        body([size * i + k for k in range(size)])


FIRST_ROWS = 328


def first_kernel(u, weights_made, outer, inner):
    info = Position()
    at_top = info[0] == 0
    for out in (outer, inner):
        out[FIRST_ROWS - 16 :, :] = zeros(16)
    for m in range(3):
        for r in range(2):
            first, last = u[m, :, r, :], u[m, :, ROWS - 2 + r, :]
            at = SPECIES * (2 * m + r)
            outer[at : at + SPECIES, :] = jnp.where(at_top, first, last)
            inner[at : at + SPECIES, :] = jnp.where(at_top, last, first)


def restricted(y):
    return y[0:24] + y[24:48], y[48:72], y[72:96] + y[96:120]


MIX0 = [STEP * w for w in W0]
MIXS = [STEP * W1[0], STEP * W1[1] - HALF, STEP * W1[2]]


def mixed(factors, values):
    return factors[0] * values[0] + factors[1] * values[1] + factors[2] * values[2]


def old_kernel(u, wf, wr, wc, d12, dc12, n1, s, r0, e0, c0, ut, p0s, pss, v0s, c0s):
    for k in range(4):
        for m in range(3):
            ut[k, m, SP - 8 :, :] = zeros(8)
    for x in (0, 1, ROWS + 2, ROWS + 3):
        p0s[x], pss[x], v0s[x], c0s[x] = zeros(SP), zeros(SP), zeros(CP), zeros(CP)

    def terms(xs):
        for k, x in enumerate(xs):
            for m in range(3):
                ut[k, m, :SPECIES, :] = u[m, :, x, :]
        for k, x in enumerate(xs):
            us = [ut[k, m] for m in range(3)]
            qs = [v * v for v in us]
            p0, ps = mixed(MIX0, us), mixed(MIXS, us)
            y = dot(wf[...], stacked(p0, mixed(MIX0, qs)))
            n1[x] = us[0] + (y[:SP] + y[SP:]) + d12[...] * lap_y(p0)
            y = dot(wf[...], stacked(ps, mixed(MIXS, qs)))
            s[x] = (y[:SP] + y[SP:]) + d12[...] * lap_y(ps)
            r, c, v = restricted(dot(wr[...], stacked(us[0], qs[0])))
            r0[x] = r + lap_y(v) * (1.0 / 12.0)
            y = dot(wc[...], stacked(c, c * c))
            e0[x] = (y[:CP] + y[CP:]) + dc12[...] * lap_y(c)
            p0s[x + 2], pss[x + 2], v0s[x + 2], c0s[x + 2], c0[x] = p0, ps, v, c, c

    blocks(ROWS, terms)

    def laps(xs):
        for x in xs:
            n1[x] += d12[...] * lap_rows(p0s, x + 2)
            s[x] += d12[...] * lap_rows(pss, x + 2)
            r0[x] += lap_rows(v0s, x + 2) * (1.0 / 12.0)
            e0[x] += dc12[...] * lap_rows(c0s, x + 2)

    blocks(ROWS, laps)


def lumped_halo(lv, row):
    y = dot(lv[...], split(jnp.concatenate([row, zeros(8)], axis=0)))
    return y[0:24], y[24:48] + y[48:72]


SIDES = (((0, 1), (1, 0)), ((ROWS - 1, ROWS - 2), (0, 1)))


def packed_rows(rows):
    return (COARSE * (rows - 1) + CP + 7) // 8 * 8


def get(ref, r):
    return ref[COARSE * r : COARSE * r + CP, :]


def put(ref, r, value):
    ref[COARSE * r : COARSE * r + CP, :] = value


def pick_packed(info, side, outer, inner):
    take = info[0] == side
    return lambda r: jnp.where(take, get(outer, r), get(inner, r))


def send_packed(info, outer, inner, tops, bottoms):
    at_top = info[0] == 0
    for r, (top, bottom) in enumerate(zip(tops, bottoms)):
        put(outer, r, jnp.where(at_top, top, bottom))
        put(inner, r, jnp.where(at_top, bottom, top))


def pick_halo(info, side, outer, inner):
    take = info[0] == side
    return lambda *at: jnp.where(take, outer[at], inner[at])


def send(info, outer, inner, tops, bottoms):
    at_top = info[0] == 0
    for r, (top, bottom) in enumerate(zip(tops, bottoms)):
        outer[r] = jnp.where(at_top, top, bottom)
        inner[r] = jnp.where(at_top, bottom, top)


def old_edge_kernel(uo, ui, lv, d12, dc12, n1i, si, r0i, e0i, n1, s, r0, e0, outer, inner):
    info = Position()
    for side, (rows, order) in enumerate(SIDES):
        halo = pick_halo(info, side, uo, ui)
        us = [[halo(pl.ds(SPECIES * (2 * m + r), SP)) for m in range(3)] for r in order]
        p0 = beside(*[mixed(MIX0, v) for v in us])
        ps = beside(*[mixed(MIXS, v) for v in us])
        lumped = [lumped_halo(lv, v[0]) for v in us]
        c = beside(lumped[0][0], lumped[1][0])
        v = beside(lumped[0][1], lumped[1][1])
        for i, x in enumerate(rows):
            n1[x] = n1i[x] + d12[...] * p0[i]
            s[x] = si[x] + d12[...] * ps[i]
            r0[x] = r0i[x] + v[i] * (1.0 / 12.0)
            e0[x] = e0i[x] + dc12[...] * c[i]
    send(info, outer, inner, [n1[0], n1[1]], [n1[ROWS - 2], n1[ROWS - 1]])


def mid_kernel(n1, s, wfr, wc, d12, dc12, n2, r1, e1, c1, n1s, v1s, c1s):
    for x in (0, 1, ROWS + 2, ROWS + 3):
        n1s[x], v1s[x], c1s[x] = zeros(SP), zeros(CP), zeros(CP)

    def terms(xs):
        for x in xs:
            n = n1[x]
            y = dot(wfr[...], stacked(n, n * n))
            n2[x] = n + HALF * ((y[:SP] + y[SP : 2 * SP]) + d12[...] * lap_y(n)) + s[x]
            r, c, v = restricted(y[2 * SP :])
            r1[x] = r + lap_y(v) * (1.0 / 12.0)
            y = dot(wc[...], stacked(c, c * c))
            e1[x] = (y[:CP] + y[CP:]) + dc12[...] * lap_y(c)
            n1s[x + 2], v1s[x + 2], c1s[x + 2], c1[x] = n, v, c, c

    blocks(ROWS, terms, ROWS)

    def laps(xs):
        for x in xs:
            n2[x] += (HALF * d12[...]) * lap_rows(n1s, x + 2)
            r1[x] += lap_rows(v1s, x + 2) * (1.0 / 12.0)
            e1[x] += dc12[...] * lap_rows(c1s, x + 2)

    blocks(ROWS, laps, ROWS)


def lumped_old(first, c0, e0):
    return jnp.where(first, c0, -HALF * e0)


AB_ROWS, EXT_ROWS = 2 * ROWS + 4, 2 * ROWS + 20
A0, B0 = 2, ROWS + 4
XA0, XB0 = 6, ROWS + 16


def mid_edge_kernel(no, ni, lv, wr, d12, dc12, r0, e0, c0, n2i, r1i, e1i, n2, r1, e1, ab, c2, outer, inner, v2s, gs):
    info = Position()
    first = info[1] == 0
    for side, (rows, order) in enumerate(SIDES):
        halo = pick_halo(info, side, no, ni)
        ns = [halo(r) for r in order]
        lumped = [lumped_halo(lv, v) for v in ns]
        c = beside(lumped[0][0], lumped[1][0])
        v = beside(lumped[0][1], lumped[1][1])
        n = beside(*ns)
        for i, x in enumerate(rows):
            n2[x] = n2i[x] + (HALF * d12[...]) * n[i]
            r1[x] = r1i[x] + v[i] * (1.0 / 12.0)
            e1[x] = e1i[x] + dc12[...] * c[i]
    for x in (0, 1, ROWS + 2, ROWS + 3):
        v2s[x] = zeros(CP)

    def lumped(x, value):
        gs[x], c2[x], v2s[x + 2] = restricted(dot(wr[...], stacked(value, value * value)))

    def pieces(x, mid, late):
        v = v2s[x + 2]
        g2 = gs[x] + (lap_y(v) + lap_rows(v2s, x + 2)) * (1.0 / 12.0)
        ab[x + XA0] = mixed(MIX0, (r0[x], mid, g2)) + lumped_old(first, c0[x], e0[x])
        ab[x + XB0] = mixed([STEP * w for w in W1], (r0[x], mid, g2)) - HALF * late

    edges = (0, 1, ROWS - 2, ROWS - 1)
    for x in edges:
        lumped(x, n2[x])
    blocks(ROWS - 4, lambda xs: [lumped(x + 2, n2i[x + 2]) for x in xs], ROWS - 4)
    for x in edges:
        pieces(x, r1[x], e1[x])
    blocks(ROWS - 4, lambda xs: [pieces(x + 2, r1i[x + 2], e1i[x + 2]) for x in xs], ROWS - 4)
    top = [ab[x + XA0] for x in range(6)] + [ab[x + XB0] for x in range(4)] + [v2s[x + 2] for x in range(2)]
    bottom = [ab[x + XA0] for x in range(ROWS - 6, ROWS)] + [ab[x + XB0] for x in range(ROWS - 4, ROWS)]
    send_packed(info, outer, inner, top, bottom + [v2s[x] for x in range(ROWS, ROWS + 2)])


def last_edge_kernel(mo, mi, ho, hi, abi, ab, short):
    info = Position()
    ka, kb = STEP * W0[2] / 12.0, STEP * W1[2] / 12.0
    done = {}
    for side, (rows, order) in enumerate(SIDES):
        inside = info[2] > 0 if side == 0 else info[2] < SLABS - 1
        own, halo = pick_packed(info, side, mo, mi), pick_packed(info, side, ho, hi)
        fix = beside(*[halo(10 + r) for r in order])
        theirs = beside(*[own(10 + r) for r in order[::-1]])
        for i, x in enumerate(rows):
            done[x + XA0] = abi[x + XA0] + ka * fix[i]
            done[x + XB0] = abi[x + XB0] + kb * fix[i]
        for depth, at, to, factor in ((6, 0, XA0, ka), (4, 6, XB0, kb)):
            for i in range(depth):
                x = -1 - i if side == 0 else ROWS + i
                value = halo(at + (depth - 1 - i if side == 0 else i))
                if i < 2:
                    value = value + factor * theirs[i]
                done[x + to] = jnp.where(inside, value, 0.0)
    for at, value in done.items():
        ab[at] = value
    for x in range(-2, ROWS + 2):
        short[x + A0] = done[x + XA0] if x + XA0 in done else abi[x + XA0]
    for x in range(ROWS):
        short[x + B0] = done[x + XB0] if x + XB0 in done else abi[x + XB0]


def sweep(info, z, z0, add, add0, out, out0, low, rows, ws, lapm, dc12):
    size = rows // 2

    def body(xs):
        zr = [z[xs[0] + (low + z0 + k)] for k in range(-2, size + 2)]
        terms = [two_terms(value) for value in zr[2:-2]]
        laps = dot(jnp.concatenate(terms, axis=0), lapm[...])
        for k in range(size):
            x, value = xs[k] + low, zr[k + 2]
            y = dot(ws[...], jnp.concatenate([terms[k], two_terms(value * value)], axis=0))
            lap = laps[2 * CP * k : 2 * CP * k + CP] + laps[2 * CP * k + CP : 2 * CP * (k + 1)]
            lap = lap + 16.0 * (zr[k + 1] + zr[k + 3]) - (zr[k] + zr[k + 4])
            value = value + HALF * ((y[:CP] + y[CP:]) + dc12[...] * lap) + add[x + add0]
            if low < 0:
                inside = ((x >= 0) | (info[2] > 0)) & ((x < ROWS) | (info[2] < SLABS - 1))
                value = jnp.where(inside, value, 0.0)
            out[x + out0] = value

    blocks(rows, body, size)


def begin(info, z0, zo, zi, depth, zs):
    top, bottom = pick_packed(info, 0, zo, zi), pick_packed(info, 1, zo, zi)
    for r in range(depth):
        zs[r], zs[depth + ROWS + r] = top(r), bottom(r)
    for x in range(ROWS):
        zs[depth + x] = get(z0, x)


def give(info, depth, message, packed, outer, inner):
    for x in range(ROWS):
        put(packed, x, message[x])
    ends = [message[x] for x in range(depth)], [message[x] for x in range(ROWS - depth, ROWS)]
    send_packed(info, outer, inner, *ends)


def hosting(info, hosts):
    return info[1] == jnp.where(info[0] == 0, hosts[0], hosts[1])


def start_kernel(hosts, ab, ws, lapm, dc12, result, unused, packed, outer, inner, message):
    info = Position()

    @pl.when(hosting(info, hosts))
    def _():
        sweep(info, ab, A0, ab, B0, message, 0, 0, ROWS, ws, lapm, dc12)
        give(info, 8, message, packed, outer, inner)

        def body(xs):
            for x in xs:
                result[x], result[ROWS + x], result[2 * ROWS + x] = zeros(CP), ab[x + A0], message[x]

        blocks(ROWS, body)


def pair_kernel(
    slices, hosts, depth, z0, zo, zi, mine, short, long, ws, lapm, dc12, packed, outer, inner, za, zb, zc, message, zs
):
    info = Position()

    def sweeps(one, two):
        begin(info, z0, zo, zi, 8, zs)
        sweep(info, zs, 8, one, XA0, za, 6, -6, ROWS + 12, ws, lapm, dc12)
        sweep(info, za, 6, one, XB0, zb, 4, -4, ROWS + 8, ws, lapm, dc12)
        if two is mine:
            sweep(info, zb, 4, two, XA0, zc, 2, -2, ROWS + 4, ws, lapm, dc12)
            sweep(info, zc, 2, two, XB0, message, 0, 0, ROWS, ws, lapm, dc12)
        else:
            sweep(info, zb, 4, two, A0, zc, 2, -2, ROWS + 4, ws, lapm, dc12)
            sweep(info, zc, 2, two, B0, message, 0, 0, ROWS, ws, lapm, dc12)
        give(info, depth, message, packed, outer, inner)

    for host in sorted(set(hosts)):
        one = mine if host == slices[0] else long
        two = mine if host == slices[1] else short
        pl.when(hosting(info, hosts) & (info[1] == host))(functools.partial(sweeps, one, two))


def gather(zs, za, zb, zc, z2, one, two, away):
    for at, result in ((0, one), (1, two)):
        values = [lambda x: zs[x + 8], lambda x: za[x + 6], lambda x: zb[x + 4], lambda x: zc[x + 2], lambda x: z2[x]]
        for part, value in enumerate(values[2 * at : 2 * at + 3]):
            for x in range(ROWS):
                if at == away:
                    put(result, part * ROWS + x, value(x))
                else:
                    result[part * ROWS + x] = value(x)


def gather_kernel(slices, hosts, zs, za, zb, zc, z2, home_in, away_in, home, away):
    info = Position()
    active, second = hosting(info, hosts), info[1] == slices[1]
    pl.when(active & ~second)(lambda: gather(zs, za, zb, zc, z2, home, away, 1))
    if slices[1] in hosts:
        pl.when(active & second)(lambda: gather(zs, za, zb, zc, z2, away, home, 0))


def base_kernel(n1, n2, c1, c2, pro, share, b1, b2):
    def body(xs):
        for x in xs:
            for n, c, b in ((n1, c1, b1), (n2, c2, b2)):
                value = thirds(jnp.concatenate([share[...] * c[x], zeros(8)], axis=0))
                b[:, x, :] = (n[x] - dot(pro[...], value))[:SPECIES]

    blocks(ROWS, body)


def out_kernel(
    where, u, b0, late, b1, b2, share, z0, zo, zi, ab, ws, lapm, dc12, home, one, other, out, z, za, zs, spread, node, sem
):
    info = Position()
    last = info[1] == SLICES - 1
    at_home = hosting(info, GROUPS[0][1])
    for slices, hosts in GROUPS[1:-1]:
        at_home = at_home | (hosting(info, hosts) & ((info[1] == slices[0]) | (info[1] == slices[1])))
    first = info[1] == GROUPS[1][0][0]
    for here, result in ((at_home, home), (first & ~at_home, one)):

        @pl.when(here)
        def _():

            def body(xs):
                for x in xs:
                    z[x] = result[x]

            blocks(3 * ROWS, body)

    @pl.when(~at_home & ~first & ~last)
    def _():
        for x in range(3 * ROWS):
            z[x] = get(other, x)

    @pl.when(last)
    def _():
        begin(info, z0, zo, zi, 4, zs)

        def body(xs):
            for x in xs:
                z[x] = zs[x + 4]

        blocks(ROWS, body)

    def finish(m, base):
        def body(xs):
            for x in xs:
                spread[m, :, x, :] = share[...] * z[m * ROWS + x]

        blocks(ROWS, body, ROWS)

        def add(s):
            node[m, s] = base(s) + spread[m, where[s]]

        blocks(SPECIES, lambda at: [add(s) for s in at], 13)
        add(SPECIES - 1)
        copy = pltpu.make_async_copy(node.at[m], out.at[m], sem.at[m])
        copy.start()
        return copy

    first = info[1] == 0
    copies = [finish(0, lambda s: jnp.where(first, u[0, s], b0[s] + late[s]))]

    @pl.when(last)
    def _():
        sweep(info, zs, 4, ab, A0, za, 2, -2, ROWS + 4, ws, lapm, dc12)
        sweep(info, za, 2, ab, B0, z.at[pl.ds(2 * ROWS, ROWS)], 0, 0, ROWS, ws, lapm, dc12)

        def body(xs):
            for x in xs:
                z[ROWS + x] = za[x + 2]

        blocks(ROWS, body)

    copies += [finish(1, lambda s: b1[s]), finish(2, lambda s: b2[s])]
    for copy in copies:
        copy.wait()


def field(*shape):
    return jax.ShapeDtypeStruct(shape + (COLS,), F32)


SMEM = pl.BlockSpec(memory_space=pltpu.SMEM)
VMEM = pl.BlockSpec(memory_space=pltpu.VMEM)
ANY = pl.BlockSpec(memory_space=pl.ANY)


def call(kernel, name, outs, *args, scratch=(), alias=None, out_specs=None, specs=None):
    specs = specs or [SMEM if a.dtype == jnp.int32 and a.ndim == 1 else VMEM for a in args]
    return pl.pallas_call(
        kernel,
        out_shape=outs,
        in_specs=specs,
        **({"out_specs": out_specs} if out_specs else {}),
        scratch_shapes=[pltpu.VMEM(f.shape, f.dtype) if isinstance(f, jax.ShapeDtypeStruct) else f for f in scratch],
        input_output_aliases=alias or {},
        compiler_params=pltpu.CompilerParams(vmem_limit_bytes=VMEM_LIMIT),
        name=name,
    )(*args)


AXES = ("tm", "space")
OUTER = [(s, s + 1) for s in range(1, SLABS - 1, 2)] + [(s + 1, s) for s in range(1, SLABS - 1, 2)]
INNER = [(s, s ^ 1) for s in range(SLABS)]
SAME = [(s, s) for s in range(SLABS)]


def moved(value, *routes):
    pairs = [
        (source[s % 2] * SLABS + s, target[t % 2] * SLABS + t) for source, target, slabs in routes for s, t in slabs
    ]
    return lax.ppermute(value, AXES, pairs)


def both(p):
    return (p, p)


def swap(outer, inner):
    got_inner = moved(inner, *[(both(p), both(p), INNER) for p in range(SLICES)])
    got_outer = moved(outer, *[(both(p), both(p), OUTER) for p in range(SLICES)])
    return got_outer, got_inner


def hop(message, outer, inner, source, target):
    parts = ((outer, OUTER), (inner, INNER), (message, SAME))
    zo, zi, z = [moved(value, (source, target, slabs)) for value, slabs in parts]
    return [z, zo, zi]


def after(value, other):
    return lax.optimization_barrier((value, other))[0]


def local(fine_nodes, fine_rates, fine_pairs, fine_diff, coarse_rates, coarse_pairs, coarse_diff, species_map):
    nodes = fine_nodes[0]
    fine, coarse = field(ROWS, SP), field(ROWS, CP)
    message = field(FIRST_ROWS)
    def bf16(*shape):
        return jax.ShapeDtypeStruct(shape, BF16)

    raw = sum(
        jnp.pad(v.astype(F32), ((at, RAW - at - v.shape[0]), (0, 128 - v.shape[1])))
        for at, v in (
            (RATES, fine_rates),
            (PAIRS, fine_pairs),
            (CRATES, coarse_rates),
            (CPAIRS, coarse_pairs),
            (DIFF, fine_diff.reshape(1, SPECIES)),
            (CDIFF, coarse_diff.reshape(1, COARSE)),
            (MAP, species_map.reshape(1, SPECIES)),
        )
    )
    wf, wr, wfr, lv, wc, ws, lapm, pro, d12, dc12, share = call(
        prep_kernel,
        "prep",
        [bf16(2 * SP, 4 * SP), bf16(128, 4 * SP), bf16(2 * SP + 128, 4 * SP), bf16(80, 128), bf16(2 * CP, 4 * CP), bf16(2 * CP, 4 * CP)]
        + [bf16(COLS, COLS), bf16(SP, 96)]
        + [field(SP), field(CP), field(CP)],
        raw,
    )
    outer, inner = call(first_kernel, "first", [message, message], nodes, wc)
    uo, ui = swap(outer, inner)

    n1, s, r0, e0, c0 = call(
        old_kernel,
        "old",
        [fine, fine, coarse, coarse, coarse],
        *(nodes, wf, wr, wc, d12, dc12),
        scratch=[field(4, 3, SP), field(ROWS + 4, SP), field(ROWS + 4, SP), field(ROWS + 4, CP), field(ROWS + 4, CP)],
    )
    two, twelve = field(2, SP), field(packed_rows(12))
    n1, s, r0, e0, outer, inner = call(
        old_edge_kernel,
        "old_edge",
        [fine, fine, coarse, coarse, two, two],
        *(uo, ui, lv, d12, dc12, n1, s, r0, e0),
        alias={5: 0, 6: 1, 7: 2, 8: 3},
    )
    no, ni = swap(outer, inner)
    n2, r1, e1, c1 = call(
        mid_kernel, "mid", [fine, coarse, coarse, coarse], n1, s, wfr, wc, d12, dc12, scratch=[field(ROWS + 4, SP), field(ROWS + 4, CP), field(ROWS + 4, CP)]
    )
    extended, short = field(EXT_ROWS, CP), field(AB_ROWS, CP)
    n2, r1, e1, abx, c2, outer, inner = call(
        mid_edge_kernel,
        "mid_edge",
        [fine, coarse, coarse, extended, coarse, twelve, twelve],
        *(no, ni, lv, wr, d12, dc12, r0, e0, c0, n2, r1, e1),
        alias={9: 0, 10: 1, 11: 2},
        scratch=[field(ROWS + 4, CP), coarse],
    )
    ho, hi = swap(outer, inner)
    b1, b2 = call(base_kernel, "base", [field(SPECIES, ROWS)] * 2, n1, n2, c1, c2, pro, share)
    abx, ab = call(last_edge_kernel, "last_edge", [extended, short], outer, inner, ho, hi, abx, alias={4: 0})

    ab, abx = after(ab, b1), after(abx, b1)
    result, away_result = field(3 * ROWS, CP), field(packed_rows(3 * ROWS))
    bulk, ends = field(packed_rows(ROWS)), field(packed_rows(8))
    pairs = [(slices, hosts) for slices, hosts in GROUPS if len(slices) == 2]
    short, long, back, first = [], [], [], []
    for slices, hosts in pairs:
        for core, host in enumerate(hosts):
            slabs = [(t, t) for t in range(core, SLABS, 2)]
            if host != slices[0]:
                long.append((both(slices[0]), both(host), slabs))
            if host != slices[1]:
                short.append((both(slices[1]), both(host), slabs))
            back.append((both(host), both(slices[0] if host == slices[1] else slices[1]), slabs))
            if host not in slices:
                first.append((both(host), both(slices[0]), slabs))
    short, long = moved(ab, *short), moved(abx, *long)
    forward = [(both(p), both(p + 1), SAME) for p in range(SLICES - 1)]
    home, away, *sent = call(
        functools.partial(start_kernel, GROUPS[0][1]), "start", [result, away_result, bulk, ends, ends], ab, ws, lapm, dc12, scratch=[coarse]
    )
    for at, (slices, hosts) in enumerate(GROUPS[1:], 1):
        z = hop(*sent, GROUPS[at - 1][1], hosts)
        if at == 1:
            z = list(lax.optimization_barrier(tuple(z)))
            b0 = moved(after(b2, z[0]), forward[2], forward[6])
            *z, short, long = lax.optimization_barrier((*z, short, long))
            late = moved(after(b2, z[0]), *forward[:2], *forward[3:6])
        elif at == 2:
            *z, b0 = lax.optimization_barrier((*z, b0))
        elif at == 3:
            *z, late, home, away = lax.optimization_barrier((*z, late, home, away))
        else:
            other, one = moved(away, *back), moved(home, *first)
            *z, other, one, home = lax.optimization_barrier((*z, other, one, home))
        if len(slices) == 2:
            depth = 4 * len(GROUPS[at + 1][0])
            ends = field(packed_rows(depth))
            *sent, za, zb, zc, z2, zs = call(
                functools.partial(pair_kernel, slices, hosts, depth),
                "pair",
                [bulk, ends, ends, field(ROWS + 12, CP), field(ROWS + 8, CP), field(ROWS + 4, CP), coarse, field(ROWS + 16, CP)],
                *(*z, abx, short, long, ws, lapm, dc12),
            )
            home, away = call(
                functools.partial(gather_kernel, slices, hosts),
                "gather",
                [result, away_result],
                *(zs, za, zb, zc, z2, home, away),
                alias={5: 0, 6: 1},
            )
    out = call(
        out_kernel,
        "out",
        field(3, SPECIES, ROWS),
        *(species_map[:, 0], nodes, b0, late, b1, b2, share, *z, ab, ws, lapm, dc12, home, one, other),
        out_specs=ANY,
        scratch=[result, field(ROWS + 4, CP), field(ROWS + 8, CP), field(3, CP, ROWS), field(3, SPECIES, ROWS), pltpu.SemaphoreType.DMA((3,))],
    )
    return out[None]


def solution(mesh):
    in_specs = (P("tm", None, None, "space", None), P(), P(), P(), P(), P(), P(), P())
    out_specs = P("tm", None, None, "space", None)
    return jax.shard_map(local, mesh=mesh, in_specs=in_specs, out_specs=out_specs, check_vma=False)
```
